32 devices in a mesh: test: 4 (over y, core), src: 8 (over z, x).
Axes of the slice: x: 2, y: 2, z: 4, core: 2. Of those that a mesh axis runs over, the one named last changes fastest.
Arguments:
- test_points: float32 [8, 3, 1024], P('test'), may hold values from 0 to 1
- test_basis: bfloat16 [8, 1024, 384], P('test'), may hold values from -0.1875 to 0.1875
- test_counts: int32 [8], P('test'), may hold values from 128 to 384, as said below
- source_points: float32 [64, 3, 1024], P('src'), may hold values from 0 to 1
- source_basis: bfloat16 [64, 1024, 384], P('src', 'test'), may hold values from -0.1875 to 0.1875
- source_counts: int32 [64], P('src'), may hold values from 128 to 384, as said below
- coefficients: bfloat16 [64, 384, 512], P('src'), may hold values from -0.0546875 to 0.0546875
Outputs:
- reduced: bfloat16 [8, 384, 64, 384], P('test', 'src')
- projected: bfloat16 [8, 384, 512], P('test', 'src')
The draws below stay inside these ranges and needn't reach their ends.
Inputs may be any that keep to these rules, and one draw needn't show every extreme that they name: `test_counts`: number of leading basis columns of a test block that are used; the rest are ignored. Some test block uses all 384 in every draw. `source_counts`: number of leading basis columns of a source block that are used; the rest are ignored. Some source block uses all 384 in every draw.
All inputs are finite; a program needn't handle non-finite values.
Results may differ from the reference program's by a relative error of at most 0.015.
Values may be sent and summed in bfloat16 or wider, within the bound.
No kernel may reach another device: no remote copies, remote signals or barrier semaphores. Data moves between devices by JAX's collectives and lax.ppermute only.
A program may use at most 128 MiB of HBM per device.

```python
import jax
import jax.numpy as jnp
from jax import lax

B = 1024
KMAX = 384
NCOL = 512
NTB = 8
NSB = 64


def count_draw(key, length):
    counts = jax.random.randint(key, (length,), KMAX // 3, KMAX + 1)
    top_pos = jax.random.randint(jax.random.fold_in(key, 11), (), 0, length)
    low_pos = jax.random.randint(jax.random.fold_in(key, 12), (), 0, length)
    counts = counts.at[low_pos].set(KMAX // 3)
    counts = counts.at[top_pos].set(KMAX)
    return counts.astype(jnp.int32)


def draw_test_counts(key, part):
    return count_draw(jax.random.fold_in(key, 101), NTB)


def draw_source_counts(key, part):
    return count_draw(jax.random.fold_in(key, 202), NSB)


def shard_levels(rng, extent, cuts, low, high):
    factor_of, own = 1.0, jax.random.fold_in(rng, 6)
    for position, blocks in cuts:
        heights = jnp.exp(jax.random.uniform(jax.random.fold_in(own, position), (blocks,), jnp.float32, low / len(cuts), high / len(cuts)))
        factor_of = factor_of * jnp.repeat(heights, extent[position] // blocks).reshape([-1 if axis == position else 1 for axis in range(len(extent))])
    return factor_of


def noise(stream_key, shape, deviation, most, cuts=(), held_as=jnp.bfloat16):
    drawn = jax.random.normal(stream_key, shape, jnp.float32) * deviation
    if len(cuts) > 0:
        drawn = shard_levels(stream_key, shape, cuts, -0.22, 0.18) * drawn
    return jnp.clip(drawn, min=-most, max=most).astype(held_as)


def setup_inputs(seed: int = 0) -> dict:
    seeds = jax.random.split(jax.random.key(seed), 8)
    return {
        "test_points": jnp.clip(1.0 * jax.random.uniform(seeds[0], (NTB, 3, B), jnp.float32) ** shard_levels(seeds[0], (NTB, 3, B), ((0, 4),), -0.2, 0.2), 0.0, 1.0),
        "test_basis": noise(seeds[1], (NTB, B, KMAX), B ** -0.5, 0.1875, ((0, 4),)),
        "test_counts": draw_test_counts(jax.random.fold_in(seeds[7], 71), 0),
        "source_points": jnp.clip(1.0 * jax.random.uniform(seeds[3], (NSB, 3, B), jnp.float32) ** shard_levels(seeds[3], (NSB, 3, B), ((0, 8),), -0.2, 0.2), 0.0, 1.0),
        "source_basis": noise(seeds[4], (NSB, B, KMAX), B ** -0.5, 0.1875, ((0, 8), (1, 4))),
        "source_counts": draw_source_counts(jax.random.fold_in(seeds[7], 71), 0),
        "coefficients": noise(seeds[6], (NSB, KMAX, NCOL), (KMAX * NSB // 2) ** -0.5, 0.0546875, ((0, 8),)),
    }


softening = 0.0025

def tile_kernel(test_xyz, source_xyz):
    total = jnp.zeros((test_xyz.shape[1], source_xyz.shape[1]), test_xyz.dtype)
    for comp in range(3):
        delta = test_xyz[comp][:, None] - source_xyz[comp][None, :]
        total = total + delta * delta
    return lax.rsqrt(total + softening)

def reference(test_points, test_basis, test_counts, source_points, source_basis, source_counts, coefficients):
    column_ids = lax.iota(jnp.int32, KMAX)
    test_mask = (column_ids[None, None, :] < test_counts[:, None, None]).astype(jnp.bfloat16)
    source_mask = (column_ids[None, None, :] < source_counts[:, None, None]).astype(jnp.bfloat16)
    test_masked = test_basis * test_mask
    source_masked = source_basis * source_mask

    def per_test(inputs):
        test_xyz, test_side = inputs

        def per_source(carry, sinputs):
            source_xyz, source_side, coeff = sinputs
            kernel = tile_kernel(test_xyz, source_xyz).astype(jnp.bfloat16)
            half = jnp.dot(kernel, source_side, preferred_element_type=jnp.float32).astype(jnp.bfloat16)
            tile = lax.dot_general(test_side, half, (((0,), (0,)), ((), ())), preferred_element_type=jnp.float32).astype(jnp.bfloat16)
            carry = carry + jnp.dot(tile, coeff, preferred_element_type=jnp.float32)
            return (carry, tile)
        start = jnp.zeros((KMAX, NCOL), jnp.float32)
        total, tiles = lax.scan(per_source, start, (source_points, source_masked, coefficients))
        return (tiles, total.astype(jnp.bfloat16))
    tiles, projected = lax.map(per_test, (test_points, test_masked))
    reduced = jnp.transpose(tiles, (0, 2, 1, 3))
    return (reduced, projected)
```

```python
import jax
import jax.numpy as jnp
from jax import lax
from jax.sharding import PartitionSpec as P

softening = 0.0025


def group_kernel(test_xyz, source_xyz):
    total = jnp.zeros((source_xyz.shape[0], test_xyz.shape[1], source_xyz.shape[2]), test_xyz.dtype)
    for comp in range(3):
        delta = test_xyz[comp][None, :, None] - source_xyz[:, comp][:, None, :]
        total = total + delta * delta
    return lax.rsqrt(total + softening).astype(jnp.bfloat16)


def group_tiles(test_xyz, test_side, source_xyz, source_side, coeff):
    kernel = group_kernel(test_xyz, source_xyz)
    half = jnp.einsum(
        "gpq,gqk->gpk", kernel, source_side, preferred_element_type=jnp.float32
    ).astype(jnp.bfloat16)
    tile = jnp.einsum("pk,gpl->gkl", test_side, half, preferred_element_type=jnp.float32).astype(
        jnp.bfloat16
    )
    partial_sum = jnp.einsum("gkl,gln->kn", tile, coeff, preferred_element_type=jnp.float32)
    return (tile, partial_sum)


def group_cuts(nsource):
    cuts = [0, 1, nsource // 2, nsource]
    return [(a, b) for a, b in zip(cuts[:-1], cuts[1:]) if b > a]


def body(
    test_points, test_basis, test_counts, source_points, source_basis, source_counts, coefficients
):
    nsource = source_points.shape[0]
    ntest = test_points.shape[0]
    kmax = source_basis.shape[2]
    nsrc = lax.axis_size("src")
    column_ids = lax.iota(jnp.int32, kmax)
    source_mask = (column_ids[None, :] < source_counts[:, None]).astype(jnp.bfloat16)
    test_mask = (column_ids[None, :] < test_counts[:, None]).astype(jnp.bfloat16)
    test_side = test_basis * test_mask[:, None, :]
    moved = []
    totals = [jnp.zeros((kmax, coefficients.shape[2]), jnp.float32)] * ntest
    for first, last in group_cuts(nsource):
        side = lax.all_gather(source_basis[first:last], "test", axis=1, tiled=True)
        side = side * source_mask[first:last, None, :]
        tiles = []
        for tblock in range(ntest):
            tile, partial_sum = group_tiles(
                test_points[tblock],
                test_side[tblock],
                source_points[first:last],
                side,
                coefficients[first:last],
            )
            tiles.append(tile)
            totals[tblock] = totals[tblock] + partial_sum
        stack = jnp.stack(tiles, axis=0)
        got = lax.all_to_all(stack, "src", split_axis=2, concat_axis=1, tiled=True)
        rows = got.shape[2]
        moved.append(got.reshape(ntest, nsrc, last - first, rows, kmax))
    reduced = jnp.concatenate(moved, axis=2).transpose(0, 3, 1, 2, 4)
    reduced = reduced.reshape(ntest, reduced.shape[1], nsrc * nsource, kmax)
    summed = jnp.stack(totals, axis=0)
    projected = lax.psum_scatter(
        summed.astype(jnp.bfloat16), "src", scatter_dimension=1, tiled=True
    )
    return (reduced, projected)


def solution(mesh):
    return jax.shard_map(
        body,
        mesh=mesh,
        in_specs=(
            P("test", None, None),
            P("test", None, None),
            P("test"),
            P("src", None, None),
            P("src", "test", None),
            P("src"),
            P("src", None, None),
        ),
        out_specs=(P("test", "src", None, None), P("test", "src", None)),
        check_vma=False,
    )
```

```python
import jax
import jax.numpy as jnp
from jax import lax
from jax.sharding import PartitionSpec as P

softening = 0.0025


def group_kernel(test_xyz, source_xyz):
    total = jnp.zeros((source_xyz.shape[0], test_xyz.shape[1], source_xyz.shape[2]), test_xyz.dtype)
    for comp in range(3):
        delta = test_xyz[comp][None, :, None] - source_xyz[:, comp][:, None, :]
        total = total + delta * delta
    return lax.rsqrt(total + softening).astype(jnp.bfloat16)


def group_tiles(test_xyz, test_side, source_xyz, source_side, coeff):
    kernel = group_kernel(test_xyz, source_xyz)
    half = jnp.einsum(
        "gpq,gqk->gpk", kernel, source_side, preferred_element_type=jnp.float32
    ).astype(jnp.bfloat16)
    tile = jnp.einsum("pk,gpl->gkl", test_side, half, preferred_element_type=jnp.float32).astype(
        jnp.bfloat16
    )
    partial_sum = jnp.einsum("gkl,gln->kn", tile, coeff, preferred_element_type=jnp.float32)
    return (tile, partial_sum)


def group_cuts(nsource):
    cuts = [0, 1, nsource // 2, nsource]
    return [(a, b) for a, b in zip(cuts[:-1], cuts[1:]) if b > a]


def exchange(x, axis, flip):
    size = lax.axis_size(axis)
    return lax.ppermute(x, axis, [(a, a ^ flip) for a in range(size)])


def bits_down(size):
    bit = size // 2
    while bit >= 1:
        yield bit
        bit //= 2


def gather_shards(shard, axis):
    held = {0: shard}
    for bit in bits_down(lax.axis_size(axis)):
        for offset in list(held):
            held[offset ^ bit] = exchange(held[offset], axis, bit)
    return [held[offset] for offset in sorted(held)]


def send_rows(stack, axis):
    size = lax.axis_size(axis)
    me = lax.axis_index(axis)
    got = jnp.zeros_like(stack)
    own = lax.dynamic_index_in_dim(stack, me, 0, keepdims=True)
    got = lax.dynamic_update_slice_in_dim(got, own, me, 0)
    for flip in reversed(range(1, size)):
        block = lax.dynamic_index_in_dim(stack, me ^ flip, 0, keepdims=True)
        got = lax.dynamic_update_slice_in_dim(got, exchange(block, axis, flip), me ^ flip, 0)
    return got


def sum_rows(total, axis):
    me = lax.axis_index(axis)
    bits = list(bits_down(lax.axis_size(axis)))
    held = total.reshape((2,) * len(bits) + total.shape[1:])
    for bit in [bits[-1]] + bits[:-1]:
        place = len(bits) - 1 if bit == 1 else 0
        mine = (me // bit) % 2
        keep = lax.dynamic_index_in_dim(held, mine, place, keepdims=False)
        give = lax.dynamic_index_in_dim(held, 1 - mine, place, keepdims=False)
        got = exchange(give.astype(jnp.bfloat16), axis, bit)
        held = keep + got.astype(jnp.float32)
        bits = [b for b in bits if b != bit]
    return held


def body(
    test_points, test_basis, test_counts, source_points, source_basis, source_counts, coefficients
):
    nsource = source_points.shape[0]
    ntest = test_points.shape[0]
    kmax = source_basis.shape[2]
    ncol = coefficients.shape[2]
    nsrc = lax.axis_size("src")
    ntest_axis = lax.axis_size("test")
    rows = kmax // nsrc
    column_ids = lax.iota(jnp.int32, kmax)
    source_mask = (column_ids[None, :] < source_counts[:, None]).astype(jnp.bfloat16)
    test_mask = (column_ids[None, :] < test_counts[:, None]).astype(jnp.bfloat16)
    test_side = test_basis * test_mask[:, None, :]
    me_test = lax.axis_index("test")
    part = source_basis.shape[1]
    points = jnp.concatenate(
        [
            lax.dynamic_slice_in_dim(source_points, (me_test ^ offset) * part, part, 2)
            for offset in range(ntest_axis)
        ],
        axis=2,
    )
    moved = []
    totals = [jnp.zeros((kmax, ncol), jnp.float32)] * ntest
    for first, last in group_cuts(nsource):
        shards = gather_shards(source_basis[first:last], "test")
        side = jnp.concatenate(shards, axis=1) * source_mask[first:last, None, :]
        tiles = []
        for tblock in range(ntest):
            tile, partial_sum = group_tiles(
                test_points[tblock],
                test_side[tblock],
                points[first:last],
                side,
                coefficients[first:last],
            )
            tiles.append(tile)
            totals[tblock] = totals[tblock] + partial_sum
        stack = jnp.stack(tiles, axis=0).reshape(ntest, last - first, nsrc, rows, kmax)
        moved.append(send_rows(stack.transpose(2, 0, 1, 3, 4), "src"))
    reduced = jnp.concatenate(moved, axis=2).transpose(1, 3, 0, 2, 4)
    reduced = reduced.reshape(ntest, rows, nsrc * nsource, kmax)
    summed = jnp.stack(totals, axis=0).reshape(ntest, nsrc, rows, ncol).transpose(1, 0, 2, 3)
    projected = sum_rows(summed, "src").astype(jnp.bfloat16)
    return (reduced, projected)


def solution(mesh):
    return jax.shard_map(
        body,
        mesh=mesh,
        in_specs=(
            P("test", None, None),
            P("test", None, None),
            P("test"),
            P("src", None, None),
            P("src", "test", None),
            P("src"),
            P("src", None, None),
        ),
        out_specs=(P("test", "src", None, None), P("test", "src", None)),
        check_vma=False,
    )
```

```python
import functools

import jax
import jax.numpy as jnp
from jax import lax
from jax.experimental import pallas as pl
from jax.experimental.pallas import tpu as pltpu
from jax.sharding import PartitionSpec as P

softening = 0.0025
QBLOCK = 256
VMEM_LIMIT = 40 * 1024 * 1024


def exchange(x, axis, flip):
    size = lax.axis_size(axis)
    return lax.ppermute(x, axis, [(a, a ^ flip) for a in range(size)])


def bits_down(size):
    bit = size // 2
    while bit >= 1:
        yield bit
        bit //= 2


def gather_shards(shard, axis):
    held = {0: shard}
    for bit in bits_down(lax.axis_size(axis)):
        for offset in list(held):
            held[offset ^ bit] = exchange(held[offset], axis, bit)
    return [held[offset] for offset in sorted(held)]


def sum_rows(total, axis):
    me = lax.axis_index(axis)
    bits = list(bits_down(lax.axis_size(axis)))
    held = total.reshape((2,) * len(bits) + total.shape[1:])
    for bit in [bits[-1]] + bits[:-1]:
        place = len(bits) - 1 if bit == 1 else 0
        mine = (me // bit) % 2
        keep = lax.dynamic_index_in_dim(held, mine, place, keepdims=False)
        give = lax.dynamic_index_in_dim(held, 1 - mine, place, keepdims=False)
        got = exchange(give.astype(jnp.bfloat16), axis, bit)
        held = keep + got.astype(jnp.float32)
        bits = [b for b in bits if b != bit]
    return held


def left_kernel(test_ref, source_ref, basis_ref, out_ref):
    nq = source_ref.shape[2]
    block = min(QBLOCK, nq)
    for start in range(0, nq, block):
        total = None
        for comp in range(3):
            delta = test_ref[0, :, comp : comp + 1] - source_ref[0, comp : comp + 1, start : start + block]
            total = delta * delta if total is None else total + delta * delta
        kernel = lax.rsqrt(total + softening).astype(jnp.bfloat16)
        out_ref[0, 0, :, start : start + block] = jnp.dot(
            basis_ref[0], kernel, preferred_element_type=jnp.float32
        ).astype(jnp.bfloat16)


def left_products(test_columns, source_points, basis_rows):
    ntest, npoint, _ = test_columns.shape
    nsource, _, nq = source_points.shape
    kmax = basis_rows.shape[1]
    return pl.pallas_call(
        left_kernel,
        grid=(ntest, nsource),
        out_shape=jax.ShapeDtypeStruct((ntest, nsource, kmax, nq), jnp.bfloat16),
        in_specs=[
            pl.BlockSpec((1, npoint, 3), lambda i, j: (i, 0, 0)),
            pl.BlockSpec((1, 3, nq), lambda i, j: (j, 0, 0)),
            pl.BlockSpec((1, kmax, npoint), lambda i, j: (i, 0, 0)),
        ],
        out_specs=pl.BlockSpec((1, 1, kmax, nq), lambda i, j: (i, j, 0, 0)),
        compiler_params=pltpu.CompilerParams(vmem_limit_bytes=VMEM_LIMIT),
        cost_estimate=pl.CostEstimate(
            flops=2 * ntest * nsource * npoint * nq * kmax,
            bytes_accessed=2 * ntest * nsource * kmax * nq,
            transcendentals=ntest * nsource * npoint * nq,
        ),
    )(test_columns, source_points, basis_rows)


def tile_kernel(nshard, ndest, test_counts_ref, source_counts_ref, left_ref, *refs):
    shard_refs, coeff_ref, tile_ref, sum_ref = refs[:nshard], refs[nshard], refs[-2], refs[-1]
    i, j = pl.program_id(0), pl.program_id(1)
    kmax = left_ref.shape[2]
    part = left_ref.shape[3] // nshard
    tile = None
    for place, shard_ref in enumerate(shard_refs):
        term = jnp.dot(
            left_ref[0, 0, :, place * part : (place + 1) * part],
            shard_ref[0],
            preferred_element_type=jnp.float32,
        )
        tile = term if tile is None else tile + term
    row_ids = lax.broadcasted_iota(jnp.int32, tile.shape, 0)
    column_ids = lax.broadcasted_iota(jnp.int32, tile.shape, 1)
    used = (row_ids < test_counts_ref[i]) & (column_ids < source_counts_ref[j])
    tile = jnp.where(used, tile, 0.0)
    rows = kmax // ndest
    for dest in range(ndest):
        tile_ref[dest, 0, 0] = tile[dest * rows : (dest + 1) * rows].astype(jnp.bfloat16)
    term = jnp.dot(tile.astype(jnp.bfloat16), coeff_ref[0], preferred_element_type=jnp.float32)

    @pl.when(j == 0)
    def _():
        sum_ref[0] = term

    @pl.when(j > 0)
    def _():
        sum_ref[0] += term


def tiles_and_sums(ndest, test_counts, source_counts, left, shards, coefficients):
    ntest, nsource, kmax, nq = left.shape
    nshard = len(shards)
    part, width = shards[0].shape[1:]
    ncol = coefficients.shape[2]
    rows = kmax // ndest
    smem = pl.BlockSpec(memory_space=pltpu.SMEM)
    return pl.pallas_call(
        functools.partial(tile_kernel, nshard, ndest),
        grid=(ntest, nsource),
        out_shape=(
            jax.ShapeDtypeStruct((ndest, ntest, nsource, rows, width), jnp.bfloat16),
            jax.ShapeDtypeStruct((ntest, kmax, ncol), jnp.float32),
        ),
        in_specs=[smem, smem, pl.BlockSpec((1, 1, kmax, nq), lambda i, j: (i, j, 0, 0))]
        + [pl.BlockSpec((1, part, width), lambda i, j: (j, 0, 0))] * nshard
        + [pl.BlockSpec((1, kmax, ncol), lambda i, j: (j, 0, 0))],
        out_specs=(
            pl.BlockSpec((ndest, 1, 1, rows, width), lambda i, j: (0, i, j, 0, 0)),
            pl.BlockSpec((1, kmax, ncol), lambda i, j: (i, 0, 0)),
        ),
        compiler_params=pltpu.CompilerParams(vmem_limit_bytes=VMEM_LIMIT),
        cost_estimate=pl.CostEstimate(
            flops=2 * ntest * nsource * kmax * width * (nq + ncol),
            bytes_accessed=2 * ntest * nsource * kmax * (nq + width),
            transcendentals=0,
        ),
    )(test_counts, source_counts, left, *shards, coefficients)


def body(
    test_points, test_basis, test_counts, source_points, source_basis, source_counts, coefficients
):
    nsource, part, kmax = source_basis.shape
    ntest = test_points.shape[0]
    ncol = coefficients.shape[2]
    nsrc = lax.axis_size("src")
    ntest_axis = lax.axis_size("test")
    rows = kmax // nsrc
    me_test = lax.axis_index("test")
    points = jnp.concatenate(
        [
            lax.dynamic_slice_in_dim(source_points, (me_test ^ offset) * part, part, 2)
            for offset in range(ntest_axis)
        ],
        axis=2,
    )
    test_columns = test_points.transpose(0, 2, 1)
    basis_rows = test_basis.transpose(0, 2, 1)
    cut = max(1, nsource // 4)
    first_shards = gather_shards(source_basis[:cut], "test")
    rest, _ = lax.optimization_barrier((source_basis[cut:], first_shards[ntest_axis // 2]))
    rest_shards = gather_shards(rest, "test")
    groups = [(0, cut, first_shards), (cut, nsource, rest_shards)]
    moved = []
    total = 0.0
    for first, last, shards in groups:
        left = left_products(test_columns, points[first:last], basis_rows)
        tiles, sums = tiles_and_sums(
            nsrc, test_counts, source_counts[first:last], left, shards, coefficients[first:last]
        )
        total = total + sums
        moved.append(lax.all_to_all(tiles, "src", split_axis=0, concat_axis=0, tiled=True))
    reduced = jnp.concatenate(moved, axis=2).transpose(1, 3, 0, 2, 4)
    reduced = reduced.reshape(ntest, rows, nsrc * nsource, kmax)
    summed = total.reshape(ntest, nsrc, rows, ncol).transpose(1, 0, 2, 3)
    projected = sum_rows(summed, "src").astype(jnp.bfloat16)
    return (reduced, projected)


def solution(mesh):
    return jax.shard_map(
        body,
        mesh=mesh,
        in_specs=(
            P("test", None, None),
            P("test", None, None),
            P("test"),
            P("src", None, None),
            P("src", "test", None),
            P("src"),
            P("src", None, None),
        ),
        out_specs=(P("test", "src", None, None), P("test", "src", None)),
        check_vma=False,
    )
```

```python
import functools

import jax
import jax.numpy as jnp
from jax import lax
from jax.experimental import pallas as pl
from jax.experimental.pallas import tpu as pltpu
from jax.sharding import PartitionSpec as P

softening = 0.0025
QBLOCK = 256
VMEM_LIMIT = 40 * 1024 * 1024


def exchange(x, axis, flip):
    size = lax.axis_size(axis)
    return lax.ppermute(x, axis, [(a, a ^ flip) for a in range(size)])


def bits_down(size):
    bit = size // 2
    while bit >= 1:
        yield bit
        bit //= 2


def three_terms(x):
    high = lax.reduce_precision(x, 8, 7)
    middle = lax.reduce_precision(x - high, 8, 7)
    return high, middle, x - high - middle


def distance_features(points, is_test):
    centred = points - 0.5
    norm = jnp.sum(centred * centred, axis=1, keepdims=True)
    if is_test:
        norm = norm + softening
    terms = three_terms(centred)
    if is_test:
        cross = [-2.0 * a for a in terms for _ in range(3)]
    else:
        cross = [b for _ in range(3) for b in terms]
    ones = [jnp.ones_like(norm)] * 3
    norms = list(three_terms(norm))
    rows = cross + (norms + ones if is_test else ones + norms)
    features = jnp.concatenate(rows, axis=1).astype(jnp.bfloat16)
    pad = -features.shape[1] % 16
    return jnp.pad(features, ((0, 0), (0, pad), (0, 0)))


def left_kernel(test_ref, source_ref, basis_ref, out_ref):
    nq = source_ref.shape[2]
    block = min(QBLOCK, nq)

    def kernel_block(start):
        squared = jnp.dot(
            test_ref[0], source_ref[0, :, start : start + block], preferred_element_type=jnp.float32
        )
        return lax.rsqrt(squared.astype(jnp.bfloat16))

    ready = kernel_block(0)
    for start in range(0, nq, block):
        now = ready
        if start + block < nq:
            ready = kernel_block(start + block)
        out_ref[0, 0, :, start : start + block] = jnp.dot(
            basis_ref[0], now, preferred_element_type=jnp.float32
        ).astype(jnp.bfloat16)


def left_products(test_features, source_features, basis_rows, first, last):
    ntest, npoint, nfeature = test_features.shape
    nq = source_features.shape[2]
    kmax = basis_rows.shape[1]
    nsource = last - first
    return pl.pallas_call(
        left_kernel,
        grid=(ntest, nsource),
        out_shape=jax.ShapeDtypeStruct((ntest, nsource, kmax, nq), jnp.bfloat16),
        in_specs=[
            pl.BlockSpec((1, npoint, nfeature), lambda i, j: (i, 0, 0)),
            pl.BlockSpec((1, nfeature, nq), lambda i, j: (first + j, 0, 0)),
            pl.BlockSpec((1, kmax, npoint), lambda i, j: (i, 0, 0)),
        ],
        out_specs=pl.BlockSpec((1, 1, kmax, nq), lambda i, j: (i, j, 0, 0)),
        compiler_params=pltpu.CompilerParams(vmem_limit_bytes=VMEM_LIMIT),
        cost_estimate=pl.CostEstimate(
            flops=2 * ntest * nsource * npoint * nq * kmax,
            bytes_accessed=2 * ntest * nsource * kmax * nq,
            transcendentals=ntest * nsource * npoint * nq,
        ),
    )(test_features, source_features, basis_rows)


def tile_kernel(nshard, ndest, first, has_start, test_counts_ref, source_counts_ref, left_ref, *refs):
    shard_refs, coeff_ref = refs[:nshard], refs[nshard]
    start_ref = refs[nshard + 1] if has_start else None
    tile_ref, sum_ref, total_ref = refs[-3:]
    j, i = pl.program_id(0), pl.program_id(1)
    kmax = left_ref.shape[2]
    part = left_ref.shape[3] // nshard
    tile = None
    for place, shard_ref in enumerate(shard_refs):
        term = jnp.dot(
            left_ref[0, 0, :, place * part : (place + 1) * part],
            shard_ref[0],
            preferred_element_type=jnp.float32,
        )
        tile = term if tile is None else tile + term
    row_ids = lax.broadcasted_iota(jnp.int32, tile.shape, 0)
    column_ids = lax.broadcasted_iota(jnp.int32, tile.shape, 1)
    used = (row_ids < test_counts_ref[i]) & (column_ids < source_counts_ref[first + j])
    tile = jnp.where(used, tile, 0.0)
    rows = kmax // ndest
    for dest in range(ndest):
        tile_ref[dest, 0, 0] = tile[dest * rows : (dest + 1) * rows].astype(jnp.bfloat16)
    term = jnp.dot(tile.astype(jnp.bfloat16), coeff_ref[0], preferred_element_type=jnp.float32)

    @pl.when(j == 0)
    def _():
        total_ref[i] = term + start_ref[i] if has_start else term

    @pl.when(j > 0)
    def _():
        total_ref[i] += term

    @pl.when(j == pl.num_programs(0) - 1)
    def _():
        sum_ref[i] = total_ref[i].astype(sum_ref.dtype)


def tiles_and_sums(ndest, first, test_counts, source_counts, left, shards, coefficients, start):
    ntest, nsource, kmax, nq = left.shape
    nshard = len(shards)
    part, width = shards[0].shape[1:]
    ncol = coefficients.shape[2]
    rows = kmax // ndest
    smem = pl.BlockSpec(memory_space=pltpu.SMEM)
    whole_sum = pl.BlockSpec((ntest, kmax, ncol), lambda j, i: (0, 0, 0))
    has_start = start is not None
    sum_dtype = jnp.bfloat16 if has_start else jnp.float32
    return pl.pallas_call(
        functools.partial(tile_kernel, nshard, ndest, first, has_start),
        grid=(nsource, ntest),
        out_shape=(
            jax.ShapeDtypeStruct((ndest, ntest, nsource, rows, width), jnp.bfloat16),
            jax.ShapeDtypeStruct((ntest, kmax, ncol), sum_dtype),
        ),
        in_specs=[smem, smem, pl.BlockSpec((1, 1, kmax, nq), lambda j, i: (i, j, 0, 0))]
        + [pl.BlockSpec((1, part, width), lambda j, i: (j, 0, 0))] * nshard
        + [pl.BlockSpec((1, kmax, ncol), lambda j, i: (first + j, 0, 0))]
        + ([whole_sum] if has_start else []),
        out_specs=(
            pl.BlockSpec((ndest, 1, 1, rows, width), lambda j, i: (0, i, j, 0, 0)),
            whole_sum,
        ),
        scratch_shapes=[pltpu.VMEM((ntest, kmax, ncol), jnp.float32)],
        compiler_params=pltpu.CompilerParams(vmem_limit_bytes=VMEM_LIMIT),
        cost_estimate=pl.CostEstimate(
            flops=2 * ntest * nsource * kmax * width * (nq + ncol),
            bytes_accessed=2 * ntest * nsource * kmax * (nq + width),
            transcendentals=0,
        ),
    )(test_counts, source_counts, left, *shards, coefficients, *([start] if has_start else []))


def body(
    test_points, test_basis, test_counts, source_points, source_basis, source_counts, coefficients
):
    nsource, part, kmax = source_basis.shape
    ntest = test_points.shape[0]
    nsrc = lax.axis_size("src")
    ntest_axis = lax.axis_size("test")
    rows = kmax // nsrc
    me_test = lax.axis_index("test")
    points = jnp.concatenate(
        [
            lax.dynamic_slice_in_dim(source_points, (me_test ^ offset) * part, part, 2)
            for offset in range(ntest_axis)
        ],
        axis=2,
    )
    source_features = distance_features(points, False)
    test_features = distance_features(test_points, True).transpose(0, 2, 1)
    basis_rows = test_basis.transpose(0, 2, 1)
    cut = max(1, nsource // 4)
    held = {}

    def gather(name, shard, left):
        got = {0: shard}
        bits = list(bits_down(ntest_axis))
        for bit in bits:
            if bit == bits[-1] and left is not None:
                names = [o for o in got if o != 0]
                tied = lax.optimization_barrier(tuple(got[o] for o in names) + (left,))
                got.update(zip(names, tied[:-1]))
                left = tied[-1]
            for offset in list(got):
                got[offset ^ bit] = exchange(got[offset], "test", bit)
            if bit == bits[0]:
                held[name] = got[bit]
        return [got[offset] for offset in sorted(got)], left

    left_a = left_products(test_features, source_features, basis_rows, 0, cut)
    shards_a, left_a = gather("a", source_basis[:cut], left_a)
    tiles_a, sums_a = tiles_and_sums(
        nsrc, 0, test_counts, source_counts, left_a, shards_a, coefficients, None
    )
    moved_a = lax.all_to_all(tiles_a, "src", split_axis=0, concat_axis=0, tiled=True)

    rest, _ = lax.optimization_barrier((source_basis[cut:], held["a"]))
    features_b, _ = lax.optimization_barrier((source_features, tiles_a))
    left_b = left_products(test_features, features_b, basis_rows, cut, nsource)
    shards_b, left_b = gather("b", rest, left_b)
    tiles_b, summed = tiles_and_sums(
        nsrc, cut, test_counts, source_counts, left_b, shards_b, coefficients, sums_a
    )
    projected = lax.psum_scatter(summed, "src", scatter_dimension=1, tiled=True)
    moved_b = lax.all_to_all(tiles_b, "src", split_axis=0, concat_axis=0, tiled=True)

    reduced = jnp.concatenate([moved_a, moved_b], axis=2).transpose(1, 3, 0, 2, 4)
    reduced = reduced.reshape(ntest, rows, nsrc * nsource, kmax)
    return (reduced, projected)


def solution(mesh):
    return jax.shard_map(
        body,
        mesh=mesh,
        in_specs=(
            P("test", None, None),
            P("test", None, None),
            P("test"),
            P("src", None, None),
            P("src", "test", None),
            P("src"),
            P("src", None, None),
        ),
        out_specs=(P("test", "src", None, None), P("test", "src", None)),
        check_vma=False,
    )
```

```python
import functools

import jax
import jax.numpy as jnp
from jax import lax
from jax.experimental import pallas as pl
from jax.experimental.pallas import tpu as pltpu
from jax.sharding import PartitionSpec as P

softening = 0.0025
QBLOCK = 256
VMEM_LIMIT = 60 * 1024 * 1024


def exchange(x, axis, flip):
    size = lax.axis_size(axis)
    return lax.ppermute(x, axis, [(a, a ^ flip) for a in range(size)])


def bits_down(size):
    bit = size // 2
    while bit >= 1:
        yield bit
        bit //= 2


def sum_rows(total, axis):
    size = lax.axis_size(axis)
    me = lax.axis_index(axis)
    held, bit = total, 1
    while held.shape[0] > 4:
        pairs = held.reshape((held.shape[0] // 2, 2) + held.shape[1:])
        mine = (me // bit) % 2
        keep = lax.dynamic_index_in_dim(pairs, mine, 1, keepdims=False)
        give = lax.dynamic_index_in_dim(pairs, 1 - mine, 1, keepdims=False)
        got = exchange(give, axis, bit)
        held = (keep.astype(jnp.float32) + got.astype(jnp.float32)).astype(held.dtype)
        bit *= 2
    mine = me // bit
    result = lax.dynamic_index_in_dim(held, mine, 0, keepdims=False).astype(jnp.float32)
    for flip in range(1, held.shape[0]):
        give = lax.dynamic_index_in_dim(held, mine ^ flip, 0, keepdims=False)
        result = result + exchange(give, axis, flip * bit).astype(jnp.float32)
    return result.astype(total.dtype)


def features_kernel(test_ref, source_ref, test_out_ref, source_out_ref, rows_ref):
    def three_terms(x):
        high = x.astype(jnp.bfloat16).astype(jnp.float32)
        middle = (x - high).astype(jnp.bfloat16).astype(jnp.float32)
        return high, middle, x - high - middle

    def fill(centred, is_test):
        norm = jnp.sum(centred * centred, axis=0, keepdims=True)
        terms = three_terms(centred)
        norms = three_terms(norm + softening if is_test else norm)
        for a in range(3):
            for b in range(3):
                place = 3 * (3 * a + b)
                rows_ref[place : place + 3, :] = -2.0 * terms[a] if is_test else terms[b]
        for a in range(3):
            rows_ref[27 + a : 28 + a, :] = norms[a] if is_test else jnp.ones_like(norm)
            rows_ref[30 + a : 31 + a, :] = jnp.ones_like(norm) if is_test else norms[a]
        return rows_ref[...]

    rows_ref[...] = jnp.zeros_like(rows_ref)
    for i in range(test_ref.shape[0]):
        rows = fill(test_ref[i] - 0.5, True)
        test_out_ref[i] = rows.T.astype(jnp.bfloat16)
    for j in range(source_ref.shape[0]):
        rows = fill(source_ref[j] - 0.5, False)
        source_out_ref[j] = rows.astype(jnp.bfloat16)


NFEATURE = 128


def distance_features(test_points, source_points):
    ntest, _, npoint = test_points.shape
    nsource, _, nq = source_points.shape
    vmem = pl.BlockSpec(memory_space=pltpu.VMEM)
    return pl.pallas_call(
        features_kernel,
        out_shape=(
            jax.ShapeDtypeStruct((ntest, npoint, NFEATURE), jnp.bfloat16),
            jax.ShapeDtypeStruct((nsource, NFEATURE, nq), jnp.bfloat16),
        ),
        in_specs=[vmem, vmem],
        out_specs=(vmem, vmem),
        scratch_shapes=[pltpu.VMEM((NFEATURE, max(npoint, nq)), jnp.float32)],
        compiler_params=pltpu.CompilerParams(vmem_limit_bytes=VMEM_LIMIT),
    )(test_points, source_points)


def left_kernel(test_ref, source_ref, basis_ref, out_ref):
    nq = source_ref.shape[2]
    block = min(QBLOCK, nq)
    steps = [(i, start) for i in range(test_ref.shape[0]) for start in range(0, nq, block)]

    def kernel_block(i, start):
        squared = jnp.dot(
            test_ref[i], source_ref[0, :, start : start + block], preferred_element_type=jnp.float32
        )
        return lax.rsqrt(squared.astype(jnp.bfloat16))

    ready = kernel_block(*steps[0])
    for place, (i, start) in enumerate(steps):
        now = ready
        if place + 1 < len(steps):
            ready = kernel_block(*steps[place + 1])
        out_ref[i, 0, :, start : start + block] = jnp.dot(
            basis_ref[i], now, preferred_element_type=jnp.float32
        ).astype(jnp.bfloat16)


def left_products(test_features, source_features, basis_rows, first, last):
    ntest, npoint, nfeature = test_features.shape
    nq = source_features.shape[2]
    kmax = basis_rows.shape[1]
    nsource = last - first
    return pl.pallas_call(
        left_kernel,
        grid=(nsource,),
        out_shape=jax.ShapeDtypeStruct((ntest, nsource, kmax, nq), jnp.bfloat16),
        in_specs=[
            pl.BlockSpec((ntest, npoint, nfeature), lambda j: (0, 0, 0)),
            pl.BlockSpec((1, nfeature, nq), lambda j: (first + j, 0, 0)),
            pl.BlockSpec((ntest, kmax, npoint), lambda j: (0, 0, 0)),
        ],
        out_specs=pl.BlockSpec((ntest, 1, kmax, nq), lambda j: (0, j, 0, 0)),
        compiler_params=pltpu.CompilerParams(vmem_limit_bytes=VMEM_LIMIT),
        cost_estimate=pl.CostEstimate(
            flops=2 * ntest * nsource * npoint * nq * kmax,
            bytes_accessed=2 * ntest * nsource * kmax * nq,
            transcendentals=ntest * nsource * npoint * nq,
        ),
    )(test_features, source_features, basis_rows)


def tile_kernel(nshard, first, has_start, test_counts_ref, source_counts_ref, left_ref, *refs):
    shard_refs, coeff_ref = refs[:nshard], refs[nshard]
    start_ref = refs[nshard + 1] if has_start else None
    tile_ref, sum_ref, total_ref = refs[-3:]
    j = pl.program_id(0)
    ntest, _, kmax, nq = left_ref.shape
    ndest, _, _, rows, width = tile_ref.shape
    side = jnp.concatenate([shard_ref[0] for shard_ref in shard_refs], axis=0)
    row_ids = lax.broadcasted_iota(jnp.int32, (kmax, width), 0)
    column_ids = lax.broadcasted_iota(jnp.int32, (kmax, width), 1)
    tiles = jnp.dot(
        left_ref[...].reshape(ntest * kmax, nq), side, preferred_element_type=jnp.float32
    )
    masked = []
    for i in range(ntest):
        used = (row_ids < test_counts_ref[i]) & (column_ids < source_counts_ref[first + j])
        tile = jnp.where(used, tiles[i * kmax : (i + 1) * kmax], 0.0)
        for dest in range(ndest):
            tile_ref[dest, i, 0] = tile[dest * rows : (dest + 1) * rows].astype(jnp.bfloat16)
        masked.append(tile.astype(jnp.bfloat16))
    term = jnp.dot(jnp.concatenate(masked, axis=0), coeff_ref[0], preferred_element_type=jnp.float32)

    @pl.when(j == 0)
    def _():
        total_ref[...] = term + start_ref[...] if has_start else term

    @pl.when(j > 0)
    def _():
        total_ref[...] += term

    @pl.when(j == pl.num_programs(0) - 1)
    def _():
        if has_start:
            for i in range(ntest):
                for dest in range(ndest):
                    top = i * kmax + dest * rows
                    sum_ref[dest, i] = total_ref[top : top + rows, :].astype(sum_ref.dtype)
        else:
            sum_ref[...] = total_ref[...]


def tiles_and_sums(ndest, first, test_counts, source_counts, left, shards, coefficients, start):
    ntest, nsource, kmax, nq = left.shape
    nshard = len(shards)
    part, width = shards[0].shape[1:]
    ncol = coefficients.shape[2]
    rows = kmax // ndest
    smem = pl.BlockSpec(memory_space=pltpu.SMEM)
    total_spec = pl.BlockSpec((ntest * kmax, ncol), lambda j: (0, 0))
    has_start = start is not None
    if has_start:
        sum_shape = jax.ShapeDtypeStruct((ndest, ntest, rows, ncol), jnp.bfloat16)
        sum_spec = pl.BlockSpec((ndest, ntest, rows, ncol), lambda j: (0, 0, 0, 0))
    else:
        sum_shape = jax.ShapeDtypeStruct((ntest * kmax, ncol), jnp.float32)
        sum_spec = total_spec
    return pl.pallas_call(
        functools.partial(tile_kernel, nshard, first, has_start),
        grid=(nsource,),
        out_shape=(
            jax.ShapeDtypeStruct((ndest, ntest, nsource, rows, width), jnp.bfloat16),
            sum_shape,
        ),
        in_specs=[smem, smem, pl.BlockSpec((ntest, 1, kmax, nq), lambda j: (0, j, 0, 0))]
        + [pl.BlockSpec((1, part, width), lambda j: (j, 0, 0))] * nshard
        + [pl.BlockSpec((1, kmax, ncol), lambda j: (first + j, 0, 0))]
        + ([total_spec] if has_start else []),
        out_specs=(
            pl.BlockSpec((ndest, ntest, 1, rows, width), lambda j: (0, 0, j, 0, 0)),
            sum_spec,
        ),
        scratch_shapes=[pltpu.VMEM((ntest * kmax, ncol), jnp.float32)],
        compiler_params=pltpu.CompilerParams(vmem_limit_bytes=VMEM_LIMIT),
        cost_estimate=pl.CostEstimate(
            flops=2 * ntest * nsource * kmax * width * (nq + ncol),
            bytes_accessed=2 * ntest * nsource * kmax * (nq + width),
            transcendentals=0,
        ),
    )(test_counts, source_counts, left, *shards, coefficients, *([start] if has_start else []))


def body(
    test_points, test_basis, test_counts, source_points, source_basis, source_counts, coefficients
):
    nsource, part, kmax = source_basis.shape
    ntest = test_points.shape[0]
    nsrc = lax.axis_size("src")
    ntest_axis = lax.axis_size("test")
    rows = kmax // nsrc
    me_test = lax.axis_index("test")
    cut = max(1, nsource // 4)
    held = {}

    def gather(name, shard, left):
        got = {0: shard}
        bits = list(bits_down(ntest_axis))
        for bit in bits:
            if bit == bits[-1]:
                names = [o for o in got if o != 0]
                tied = lax.optimization_barrier(tuple(got[o] for o in names) + (left,))
                got.update(zip(names, tied[:-1]))
                left = tied[-1]
            for offset in list(got):
                got[offset ^ bit] = exchange(got[offset], "test", bit)
            if bit == bits[0]:
                held[name] = got[bit]
        return [got[offset] for offset in sorted(got)], left

    points = jnp.concatenate(
        [
            lax.dynamic_slice_in_dim(source_points, (me_test ^ offset) * part, part, 2)
            for offset in range(ntest_axis)
        ],
        axis=2,
    )
    test_features, source_features = distance_features(test_points, points)
    basis_rows = test_basis.transpose(0, 2, 1)

    left_a = left_products(test_features, source_features, basis_rows, 0, cut)
    shards_a, left_a = gather("a", source_basis[:cut], left_a)
    tiles_a, sums_a = tiles_and_sums(
        nsrc, 0, test_counts, source_counts, left_a, shards_a, coefficients, None
    )
    moved_a = lax.all_to_all(tiles_a, "src", split_axis=0, concat_axis=0, tiled=True)

    rest, _ = lax.optimization_barrier((source_basis[cut:], held["a"]))
    features_b, _ = lax.optimization_barrier((source_features, tiles_a))
    left_b = left_products(test_features, features_b, basis_rows, cut, nsource)
    shards_b, left_b = gather("b", rest, left_b)
    tiles_b, summed = tiles_and_sums(
        nsrc, cut, test_counts, source_counts, left_b, shards_b, coefficients, sums_a
    )
    projected = sum_rows(summed, "src")
    moved_b = lax.all_to_all(tiles_b, "src", split_axis=0, concat_axis=0, tiled=True)

    reduced = jnp.concatenate([moved_a, moved_b], axis=2).transpose(1, 3, 0, 2, 4)
    reduced = reduced.reshape(ntest, rows, nsrc * nsource, kmax)
    return (reduced, projected)


def solution(mesh):
    return jax.shard_map(
        body,
        mesh=mesh,
        in_specs=(
            P("test", None, None),
            P("test", None, None),
            P("test"),
            P("src", None, None),
            P("src", "test", None),
            P("src"),
            P("src", None, None),
        ),
        out_specs=(P("test", "src", None, None), P("test", "src", None)),
        check_vma=False,
    )
```

```python
import functools

import jax
import jax.numpy as jnp
from jax import lax
from jax.experimental import pallas as pl
from jax.experimental.pallas import tpu as pltpu
from jax.sharding import PartitionSpec as P

softening = 0.0025
QBLOCK = 256
LANES = 128
VMEM_LIMIT = 60 * 1024 * 1024


def exchange(x, axis, flip):
    size = lax.axis_size(axis)
    return lax.ppermute(x, axis, [(a, a ^ flip) for a in range(size)])


def bits_down(size):
    bit = size // 2
    while bit >= 1:
        yield bit
        bit //= 2


def sum_rows(total, axis):
    size = lax.axis_size(axis)
    me = lax.axis_index(axis)
    held, bit = total, 1
    while held.shape[0] > 4:
        pairs = held.reshape((held.shape[0] // 2, 2) + held.shape[1:])
        mine = (me // bit) % 2
        keep = lax.dynamic_index_in_dim(pairs, mine, 1, keepdims=False)
        give = lax.dynamic_index_in_dim(pairs, 1 - mine, 1, keepdims=False)
        got = exchange(give, axis, bit)
        held = (keep.astype(jnp.float32) + got.astype(jnp.float32)).astype(held.dtype)
        bit *= 2
    mine = me // bit
    result = lax.dynamic_index_in_dim(held, mine, 0, keepdims=False).astype(jnp.float32)
    for flip in range(1, held.shape[0]):
        give = lax.dynamic_index_in_dim(held, mine ^ flip, 0, keepdims=False)
        result = result + exchange(give, axis, flip * bit).astype(jnp.float32)
    return result.astype(total.dtype)


def features_kernel(test_ref, source_ref, test_out_ref, source_out_ref, rows_ref):
    def three_terms(x):
        high = x.astype(jnp.bfloat16).astype(jnp.float32)
        middle = (x - high).astype(jnp.bfloat16).astype(jnp.float32)
        return high, middle, x - high - middle

    def fill(centred, is_test):
        norm = jnp.sum(centred * centred, axis=0, keepdims=True)
        terms = three_terms(centred)
        norms = three_terms(norm + softening if is_test else norm)
        for a in range(3):
            for b in range(3):
                place = 3 * (3 * a + b)
                rows_ref[place : place + 3, :] = -2.0 * terms[a] if is_test else terms[b]
        for a in range(3):
            rows_ref[27 + a : 28 + a, :] = norms[a] if is_test else jnp.ones_like(norm)
            rows_ref[30 + a : 31 + a, :] = jnp.ones_like(norm) if is_test else norms[a]
        return rows_ref[...]

    rows_ref[...] = jnp.zeros_like(rows_ref)
    for i in range(test_ref.shape[0]):
        rows = fill(test_ref[i] - 0.5, True)
        test_out_ref[i] = rows.T.astype(jnp.bfloat16)
    for j in range(source_ref.shape[0]):
        rows = fill(source_ref[j] - 0.5, False)
        source_out_ref[j] = rows.astype(jnp.bfloat16)


NFEATURE = 128


def distance_features(test_points, source_points):
    ntest, _, npoint = test_points.shape
    nsource, _, nq = source_points.shape
    vmem = pl.BlockSpec(memory_space=pltpu.VMEM)
    return pl.pallas_call(
        features_kernel,
        out_shape=(
            jax.ShapeDtypeStruct((ntest, npoint, NFEATURE), jnp.bfloat16),
            jax.ShapeDtypeStruct((nsource, NFEATURE, nq), jnp.bfloat16),
        ),
        in_specs=[vmem, vmem],
        out_specs=(vmem, vmem),
        scratch_shapes=[pltpu.VMEM((NFEATURE, max(npoint, nq)), jnp.float32)],
        compiler_params=pltpu.CompilerParams(vmem_limit_bytes=VMEM_LIMIT),
    )(test_points, source_points)


def left_kernel(order_ref, test_ref, source_ref, basis_ref, out_ref):
    nq = source_ref.shape[2]
    block = min(QBLOCK, nq)
    steps = [(i, start) for i in range(test_ref.shape[0]) for start in range(0, nq, block)]

    def kernel_block(i, start):
        squared = jnp.dot(
            test_ref[i], source_ref[0, :, start : start + block], preferred_element_type=jnp.float32
        )
        return lax.rsqrt(squared.astype(jnp.bfloat16))

    ready = kernel_block(*steps[0])
    for place, (i, start) in enumerate(steps):
        now = ready
        if place + 1 < len(steps):
            ready = kernel_block(*steps[place + 1])
        out_ref[i, 0, :, start : start + block] = jnp.dot(
            basis_ref[i], now, preferred_element_type=jnp.float32
        ).astype(jnp.bfloat16)


def left_products(order, test_features, source_features, basis_rows, first, last):
    ntest, npoint, nfeature = test_features.shape
    nq = source_features.shape[2]
    kmax = basis_rows.shape[1]
    nsource = last - first
    return pl.pallas_call(
        left_kernel,
        grid_spec=pltpu.PrefetchScalarGridSpec(
            num_scalar_prefetch=1,
            grid=(nsource,),
            in_specs=[
                pl.BlockSpec((ntest, npoint, nfeature), lambda j, order: (0, 0, 0)),
                pl.BlockSpec((1, nfeature, nq), lambda j, order: (order[first + j], 0, 0)),
                pl.BlockSpec((ntest, kmax, npoint), lambda j, order: (0, 0, 0)),
            ],
            out_specs=pl.BlockSpec((ntest, 1, kmax, nq), lambda j, order: (0, j, 0, 0)),
        ),
        out_shape=jax.ShapeDtypeStruct((ntest, nsource, kmax, nq), jnp.bfloat16),
        compiler_params=pltpu.CompilerParams(vmem_limit_bytes=VMEM_LIMIT),
        cost_estimate=pl.CostEstimate(
            flops=2 * ntest * nsource * npoint * nq * kmax,
            bytes_accessed=2 * ntest * nsource * kmax * nq,
            transcendentals=ntest * nsource * npoint * nq,
        ),
    )(order, test_features, source_features, basis_rows)


def tile_kernel(nshard, first, packed, *refs):
    order_ref, source_counts_ref, offsets_ref, test_counts_ref, left_ref = refs[:5]
    shard_refs, coeff_ref = refs[5 : 5 + nshard], refs[5 + nshard]
    start_ref = refs[6 + nshard] if packed else None
    tile_ref, sum_ref, total_ref = refs[-3:]
    j = pl.program_id(0)
    ntest, _, kmax, nq = left_ref.shape
    ndest, _, rows, _ = tile_ref.shape if packed else tile_ref.shape[:2] + tile_ref.shape[3:]
    width = shard_refs[0].shape[2]
    side = jnp.concatenate([shard_ref[0] for shard_ref in shard_refs], axis=0)
    row_ids = lax.broadcasted_iota(jnp.int32, (kmax, width), 0)
    column_ids = lax.broadcasted_iota(jnp.int32, (kmax, width), 1)
    tiles = jnp.dot(
        left_ref[...].reshape(ntest * kmax, nq), side, preferred_element_type=jnp.float32
    )
    count = source_counts_ref[order_ref[first + j]]
    masked = []
    for i in range(ntest):
        used = (row_ids < test_counts_ref[i]) & (column_ids < count)
        masked.append(jnp.where(used, tiles[i * kmax : (i + 1) * kmax], 0.0))
    if packed:
        offset = offsets_ref[order_ref[first + j]]
        shift = offset % LANES
        base = pl.multiple_of(offset - shift, LANES)
        low = lax.broadcasted_iota(jnp.int32, (kmax, LANES), 1) < shift
        for i in range(ntest):
            rolled = [
                pltpu.roll(masked[i][:, start : start + LANES], shift, axis=1)
                for start in range(0, width, LANES)
            ]
            for place in range(len(rolled) + 1):
                here = pl.ds(pl.multiple_of(base + place * LANES, LANES), LANES)
                if place == 0:
                    before = jnp.concatenate(
                        [tile_ref[dest, i, :, here].astype(jnp.float32) for dest in range(ndest)], axis=0
                    )
                else:
                    before = rolled[place - 1]
                after = rolled[place] if place < len(rolled) else jnp.zeros_like(before)
                window = jnp.where(low, before, after)
                for dest in range(ndest):
                    tile_ref[dest, i, :, here] = window[dest * rows : (dest + 1) * rows].astype(jnp.bfloat16)
    else:
        for i in range(ntest):
            for dest in range(ndest):
                tile_ref[dest, i, 0] = masked[i][dest * rows : (dest + 1) * rows].astype(jnp.bfloat16)
    rounded = jnp.concatenate([tile.astype(jnp.bfloat16) for tile in masked], axis=0)
    term = jnp.dot(rounded, coeff_ref[0], preferred_element_type=jnp.float32)

    @pl.when(j == 0)
    def _():
        total_ref[...] = term + start_ref[...] if packed else term

    @pl.when(j > 0)
    def _():
        total_ref[...] += term

    @pl.when(j == pl.num_programs(0) - 1)
    def _():
        if packed:
            for i in range(ntest):
                for dest in range(ndest):
                    top = i * kmax + dest * rows
                    sum_ref[dest, i] = total_ref[top : top + rows, :].astype(sum_ref.dtype)
        else:
            sum_ref[...] = total_ref[...]


def tiles_and_sums(ndest, first, tables, test_counts, left, shards, coefficients, start):
    ntest, nsource, kmax, nq = left.shape
    nshard = len(shards)
    part, width = shards[0].shape[1:]
    ncol = coefficients.shape[2]
    rows = kmax // ndest
    total_spec = pl.BlockSpec((ntest * kmax, ncol), lambda j, *_: (0, 0))
    packed = start is not None
    if packed:
        full = nsource * width + LANES
        tile_shape = jax.ShapeDtypeStruct((ndest, ntest, rows, full), jnp.bfloat16)
        tile_spec = pl.BlockSpec((ndest, ntest, rows, full), lambda j, *_: (0, 0, 0, 0))
        sum_shape = jax.ShapeDtypeStruct((ndest, ntest, rows, ncol), jnp.bfloat16)
        sum_spec = pl.BlockSpec((ndest, ntest, rows, ncol), lambda j, *_: (0, 0, 0, 0))
    else:
        tile_shape = jax.ShapeDtypeStruct((ndest, ntest, nsource, rows, width), jnp.bfloat16)
        tile_spec = pl.BlockSpec((ndest, ntest, 1, rows, width), lambda j, *_: (0, 0, j, 0, 0))
        sum_shape = jax.ShapeDtypeStruct((ntest * kmax, ncol), jnp.float32)
        sum_spec = total_spec
    return pl.pallas_call(
        functools.partial(tile_kernel, nshard, first, packed),
        grid_spec=pltpu.PrefetchScalarGridSpec(
            num_scalar_prefetch=4,
            grid=(nsource,),
            in_specs=[pl.BlockSpec((ntest, 1, kmax, nq), lambda j, *_: (0, j, 0, 0))]
            + [pl.BlockSpec((1, part, width), lambda j, *_: (j, 0, 0))] * nshard
            + [pl.BlockSpec((1, kmax, ncol), lambda j, order, *_: (order[first + j], 0, 0))]
            + ([total_spec] if packed else []),
            out_specs=(tile_spec, sum_spec),
            scratch_shapes=[pltpu.VMEM((ntest * kmax, ncol), jnp.float32)],
        ),
        out_shape=(tile_shape, sum_shape),
        compiler_params=pltpu.CompilerParams(vmem_limit_bytes=VMEM_LIMIT),
        cost_estimate=pl.CostEstimate(
            flops=2 * ntest * nsource * kmax * width * (nq + ncol),
            bytes_accessed=2 * ntest * nsource * kmax * (nq + width),
            transcendentals=0,
        ),
    )(*tables, test_counts, left, *shards, coefficients, *([start] if packed else []))


def unpack_kernel(cut, step, order_ref, counts_ref, offsets_ref, whole_ref, packed_ref, out_ref):
    _, ntest, _, rows, width = whole_ref.shape
    packed_width = packed_ref.shape[3]
    nblock = out_ref.shape[1] // step
    lanes = lax.broadcasted_iota(jnp.int32, (rows, LANES), 1)
    for near in range(step):
        source = pl.program_id(0) * step + near
        for place in range(nblock):
            block = order_ref[source * nblock + place]
            if place < cut:
                for i in range(ntest):
                    out_ref[i, near * nblock + block] = whole_ref[near, i, place]
                continue
            count = counts_ref[source * nblock + block]
            offset = offsets_ref[source * nblock + block]
            shift = offset % LANES
            base = offset - shift
            back = (LANES - shift) % LANES
            low = lanes < LANES - shift
            for i in range(ntest):
                rolled = []
                for tile in range(width // LANES + 1):
                    here = pl.multiple_of(jnp.minimum(base + tile * LANES, packed_width - LANES), LANES)
                    piece = packed_ref[near, i, :, pl.ds(here, LANES)].astype(jnp.float32)
                    rolled.append(pltpu.roll(piece, back, axis=1))
                for tile in range(width // LANES):
                    value = jnp.where(low, rolled[tile], rolled[tile + 1])
                    value = jnp.where(lanes < count - tile * LANES, value, 0.0)
                    out_ref[i, near * nblock + block, :, tile * LANES : (tile + 1) * LANES] = value.astype(
                        jnp.bfloat16
                    )


def unpack(cut, tables, whole, packed):
    nsrc, ntest, _, rows, width = whole.shape
    packed_width = packed.shape[3]
    nblock = tables[0].shape[0] // nsrc
    step = 2
    return pl.pallas_call(
        functools.partial(unpack_kernel, cut, step),
        grid_spec=pltpu.PrefetchScalarGridSpec(
            num_scalar_prefetch=3,
            grid=(nsrc // step,),
            in_specs=[
                pl.BlockSpec((step, ntest, cut, rows, width), lambda s, *_: (s, 0, 0, 0, 0)),
                pl.BlockSpec((step, ntest, rows, packed_width), lambda s, *_: (s, 0, 0, 0)),
            ],
            out_specs=pl.BlockSpec((ntest, step * nblock, rows, width), lambda s, *_: (0, s, 0, 0)),
        ),
        out_shape=jax.ShapeDtypeStruct((ntest, nsrc * nblock, rows, width), jnp.bfloat16),
        compiler_params=pltpu.CompilerParams(vmem_limit_bytes=VMEM_LIMIT),
    )(*tables, whole, packed)


def block_tables(counts, cut):
    n, nblock = counts.shape
    ids = lax.iota(jnp.int32, nblock)
    mine, other = counts[:, :, None], counts[:, None, :]
    ahead = (other > mine) | ((other == mine) & (ids[None, None, :] < ids[None, :, None]))
    rank = jnp.sum(ahead.astype(jnp.int32), axis=2)
    order = jnp.sum(jnp.where(rank[:, None, :] == ids[None, :, None], ids[None, None, :], 0), axis=2)
    before = ahead & (rank[:, None, :] >= cut)
    offsets = jnp.sum(jnp.where(before, other, 0), axis=2)
    used = jnp.sum(jnp.where(rank >= cut, counts, 0), axis=1)
    return order, offsets, used


def body(
    test_points, test_basis, test_counts, source_points, source_basis, source_counts, coefficients
):
    nsource, part, kmax = source_basis.shape
    ntest = test_points.shape[0]
    nsrc = lax.axis_size("src")
    ntest_axis = lax.axis_size("test")
    rows = kmax // nsrc
    me_test = lax.axis_index("test")
    cut = max(1, nsource // 4)
    held = {}

    def gather(name, shard, left):
        got = {0: shard}
        bits = list(bits_down(ntest_axis))
        for bit in bits:
            if bit == bits[-1]:
                names = [o for o in got if o != 0]
                tied = lax.optimization_barrier(tuple(got[o] for o in names) + (left,))
                got.update(zip(names, tied[:-1]))
                left = tied[-1]
            for offset in list(got):
                got[offset ^ bit] = exchange(got[offset], "test", bit)
            if bit == bits[0]:
                held[name] = got[bit]
        return [got[offset] for offset in sorted(got)], left

    order, offsets, _ = block_tables(source_counts[None, :], cut)
    order, offsets = order[0], offsets[0]
    tables = (order, source_counts, offsets)
    ordered = [lax.dynamic_index_in_dim(source_basis, order[place], 0) for place in range(nsource)]

    points = jnp.concatenate(
        [
            lax.dynamic_slice_in_dim(source_points, (me_test ^ offset) * part, part, 2)
            for offset in range(ntest_axis)
        ],
        axis=2,
    )
    test_features, source_features = distance_features(test_points, points)
    basis_rows = test_basis.transpose(0, 2, 1)

    left_a = left_products(order, test_features, source_features, basis_rows, 0, cut)
    shards_a, left_a = gather("a", jnp.concatenate(ordered[:cut], axis=0), left_a)
    tiles_a, sums_a = tiles_and_sums(nsrc, 0, tables, test_counts, left_a, shards_a, coefficients, None)
    moved_a = lax.all_to_all(tiles_a, "src", split_axis=0, concat_axis=0, tiled=True)

    rest, _ = lax.optimization_barrier((jnp.concatenate(ordered[cut:], axis=0), held["a"]))
    features_b, _ = lax.optimization_barrier((source_features, tiles_a))
    left_b = left_products(order, test_features, features_b, basis_rows, cut, nsource)
    shards_b, left_b = gather("b", rest, left_b)
    tiles_b, summed = tiles_and_sums(
        nsrc, cut, tables, test_counts, left_b, shards_b, coefficients, sums_a
    )

    all_counts = source_counts[None, :]
    for bit in reversed(list(bits_down(nsrc))):
        all_counts = jnp.concatenate([all_counts, exchange(all_counts, "src", bit)], axis=0)
    all_counts = jnp.take(all_counts, lax.iota(jnp.int32, nsrc) ^ lax.axis_index("src"), axis=0)
    all_order, all_offsets, all_used = block_tables(all_counts, cut)
    all_tables = (all_order.reshape(-1), all_counts.reshape(-1), all_offsets.reshape(-1))

    most = (nsource - cut) * kmax
    widths = list(range(most // 2, most, LANES)) + [most]
    need = jnp.max(all_used)
    branch = jnp.sum((need > jnp.array(widths[:-1], jnp.int32)).astype(jnp.int32))

    def finish(width, tiles_b, summed, moved_a, all_tables):
        moved_b = lax.all_to_all(tiles_b[..., :width], "src", split_axis=0, concat_axis=0, tiled=True)
        return unpack(cut, all_tables, moved_a, moved_b), sum_rows(summed, "src")

    blocks, projected = lax.switch(
        branch,
        [functools.partial(finish, width) for width in widths],
        tiles_b,
        summed,
        moved_a,
        all_tables,
    )
    return (blocks.transpose(0, 2, 1, 3), projected)


def solution(mesh):
    return jax.shard_map(
        body,
        mesh=mesh,
        in_specs=(
            P("test", None, None),
            P("test", None, None),
            P("test"),
            P("src", None, None),
            P("src", "test", None),
            P("src"),
            P("src", None, None),
        ),
        out_specs=(P("test", "src", None, None), P("test", "src", None)),
        check_vma=False,
    )
```

```python
import functools

import jax
import jax.numpy as jnp
from jax import lax
from jax.experimental import pallas as pl
from jax.experimental.pallas import tpu as pltpu
from jax.sharding import PartitionSpec as P

softening = 0.0025
QBLOCK = 256
LANES = 128
VMEM_LIMIT = 60 * 1024 * 1024


def exchange(x, axis, flip):
    size = lax.axis_size(axis)
    return lax.ppermute(x, axis, [(a, a ^ flip) for a in range(size)])


def bits_down(size):
    bit = size // 2
    while bit >= 1:
        yield bit
        bit //= 2


def sum_rows(total, axis):
    size = lax.axis_size(axis)
    me = lax.axis_index(axis)
    held, bit = total, 1
    while held.shape[0] > 4:
        pairs = held.reshape((held.shape[0] // 2, 2) + held.shape[1:])
        mine = (me // bit) % 2
        keep = lax.dynamic_index_in_dim(pairs, mine, 1, keepdims=False)
        give = lax.dynamic_index_in_dim(pairs, 1 - mine, 1, keepdims=False)
        got = exchange(give, axis, bit)
        held = (keep.astype(jnp.float32) + got.astype(jnp.float32)).astype(held.dtype)
        bit *= 2
    mine = me // bit
    result = lax.dynamic_index_in_dim(held, mine, 0, keepdims=False).astype(jnp.float32)
    for flip in range(1, held.shape[0]):
        give = lax.dynamic_index_in_dim(held, mine ^ flip, 0, keepdims=False)
        result = result + exchange(give, axis, flip * bit).astype(jnp.float32)
    return result.astype(total.dtype)


def rank_blocks(counts, cut):
    ranks = []
    for j, mine in enumerate(counts):
        rank = jnp.int32(0)
        for k, other in enumerate(counts):
            if k != j:
                ahead = other >= mine if k < j else other > mine
                rank += ahead.astype(jnp.int32)
        ranks.append(rank)
    offsets = []
    for j in range(len(counts)):
        offset = jnp.int32(0)
        for k, other in enumerate(counts):
            if k != j:
                offset += jnp.where((ranks[k] >= cut) & (ranks[k] < ranks[j]), other, 0)
        offsets.append(offset)
    return ranks, offsets


def pick_kernel(cut, counts_ref, basis_ref, order_ref, offsets_ref, first_ref, rest_ref, sems):
    nblock = basis_ref.shape[0]
    ranks, offsets = rank_blocks([counts_ref[j] for j in range(nblock)], cut)
    for j in range(nblock):
        order_ref[ranks[j]] = jnp.int32(j)
        offsets_ref[j] = offsets[j]
    copies = []
    for place in range(nblock):
        target = first_ref.at[place] if place < cut else rest_ref.at[place - cut]
        copies.append(pltpu.make_async_copy(basis_ref.at[order_ref[place]], target, sems.at[place]))
    for copy in copies:
        copy.start()
    for copy in copies:
        copy.wait()


def pick(cut, counts, basis):
    nblock = basis.shape[0]
    smem, anywhere = pl.BlockSpec(memory_space=pltpu.SMEM), pl.BlockSpec(memory_space=pl.ANY)
    return pl.pallas_call(
        functools.partial(pick_kernel, cut),
        out_shape=(
            jax.ShapeDtypeStruct((nblock,), jnp.int32),
            jax.ShapeDtypeStruct((nblock,), jnp.int32),
            jax.ShapeDtypeStruct((cut,) + basis.shape[1:], basis.dtype),
            jax.ShapeDtypeStruct((nblock - cut,) + basis.shape[1:], basis.dtype),
        ),
        in_specs=[smem, anywhere],
        out_specs=(smem, smem, anywhere, anywhere),
        scratch_shapes=[pltpu.SemaphoreType.DMA((nblock,))],
        compiler_params=pltpu.CompilerParams(vmem_limit_bytes=VMEM_LIMIT),
    )(counts, basis)


def tables_kernel(cut, nblock, widths, me_ref, counts_ref, order_ref, sorted_ref, offsets_ref, branch_ref):
    nsrc = sorted_ref.shape[0] // nblock

    def step(source, need):
        base = (source ^ me_ref[0]) * nblock
        counts = [counts_ref[base + j] for j in range(nblock)]
        ranks, offsets = rank_blocks(counts, cut)
        used = jnp.int32(0)
        for j in range(nblock):
            order_ref[source * nblock + ranks[j]] = jnp.int32(j)
            sorted_ref[source * nblock + j] = counts[j]
            offsets_ref[source * nblock + j] = offsets[j]
            used += jnp.where(ranks[j] >= cut, counts[j], 0)
        return jnp.maximum(need, used)

    need = lax.fori_loop(0, nsrc, step, jnp.int32(0))
    branch = jnp.int32(0)
    for width in widths[:-1]:
        branch += (need > width).astype(jnp.int32)
    branch_ref[0] = branch


def all_tables(cut, nblock, widths, me, counts):
    smem = pl.BlockSpec(memory_space=pltpu.SMEM)
    table = jax.ShapeDtypeStruct(counts.shape, jnp.int32)
    return pl.pallas_call(
        functools.partial(tables_kernel, cut, nblock, widths),
        out_shape=(table, table, table, jax.ShapeDtypeStruct((1,), jnp.int32)),
        in_specs=[smem, smem],
        out_specs=(smem,) * 4,
    )(me, counts)


def features_kernel(nshard, me_ref, test_ref, source_ref, basis_ref, test_out_ref, source_out_ref, basis_out_ref, rows_ref):
    part = source_ref.shape[2] // nshard

    def three_terms(x):
        high = x.astype(jnp.bfloat16).astype(jnp.float32)
        middle = (x - high).astype(jnp.bfloat16).astype(jnp.float32)
        return high, middle, x - high - middle

    def fill(centred, is_test):
        norm = jnp.sum(centred * centred, axis=0, keepdims=True)
        terms = three_terms(centred)
        norms = three_terms(norm + softening if is_test else norm)
        for a in range(3):
            for b in range(3):
                place = 3 * (3 * a + b)
                rows_ref[place : place + 3, :] = -2.0 * terms[a] if is_test else terms[b]
        for a in range(3):
            rows_ref[27 + a : 28 + a, :] = norms[a] if is_test else jnp.ones_like(norm)
            rows_ref[30 + a : 31 + a, :] = jnp.ones_like(norm) if is_test else norms[a]
        return rows_ref[...]

    rows_ref[...] = jnp.zeros_like(rows_ref)
    for i in range(test_ref.shape[0]):
        rows = fill(test_ref[i] - 0.5, True)
        test_out_ref[i] = rows.T.astype(jnp.bfloat16)
        basis_out_ref[i] = basis_ref[i].T
    for j in range(source_ref.shape[0]):
        pieces = []
        for offset in range(nshard):
            start = pl.multiple_of((me_ref[0] ^ offset) * part, part)
            pieces.append(source_ref[j, :, pl.ds(start, part)])
        rows = fill(jnp.concatenate(pieces, axis=1) - 0.5, False)
        source_out_ref[j] = rows.astype(jnp.bfloat16)


NFEATURE = 128


def distance_features(nshard, me, test_points, source_points, test_basis):
    ntest, _, npoint = test_points.shape
    nsource, _, nq = source_points.shape
    kmax = test_basis.shape[2]
    vmem = pl.BlockSpec(memory_space=pltpu.VMEM)
    return pl.pallas_call(
        functools.partial(features_kernel, nshard),
        out_shape=(
            jax.ShapeDtypeStruct((ntest, npoint, NFEATURE), jnp.bfloat16),
            jax.ShapeDtypeStruct((nsource, NFEATURE, nq), jnp.bfloat16),
            jax.ShapeDtypeStruct((ntest, kmax, npoint), jnp.bfloat16),
        ),
        in_specs=[pl.BlockSpec(memory_space=pltpu.SMEM), vmem, vmem, vmem],
        out_specs=(vmem, vmem, vmem),
        scratch_shapes=[pltpu.VMEM((NFEATURE, max(npoint, nq)), jnp.float32)],
        compiler_params=pltpu.CompilerParams(vmem_limit_bytes=VMEM_LIMIT),
    )(me, test_points, source_points, test_basis)


def left_kernel(order_ref, test_ref, source_ref, basis_ref, out_ref):
    nq = source_ref.shape[2]
    block = min(QBLOCK, nq)
    steps = [(i, start) for i in range(test_ref.shape[0]) for start in range(0, nq, block)]

    def kernel_block(i, start):
        squared = jnp.dot(
            test_ref[i], source_ref[0, :, start : start + block], preferred_element_type=jnp.float32
        )
        return lax.rsqrt(squared.astype(jnp.bfloat16))

    ready = kernel_block(*steps[0])
    for place, (i, start) in enumerate(steps):
        now = ready
        if place + 1 < len(steps):
            ready = kernel_block(*steps[place + 1])
        out_ref[i, 0, :, start : start + block] = jnp.dot(
            basis_ref[i], now, preferred_element_type=jnp.float32
        ).astype(jnp.bfloat16)


def left_products(order, test_features, source_features, basis_rows, first, last):
    ntest, npoint, nfeature = test_features.shape
    nq = source_features.shape[2]
    kmax = basis_rows.shape[1]
    nsource = last - first
    return pl.pallas_call(
        left_kernel,
        grid_spec=pltpu.PrefetchScalarGridSpec(
            num_scalar_prefetch=1,
            grid=(nsource,),
            in_specs=[
                pl.BlockSpec((ntest, npoint, nfeature), lambda j, order: (0, 0, 0)),
                pl.BlockSpec((1, nfeature, nq), lambda j, order: (order[first + j], 0, 0)),
                pl.BlockSpec((ntest, kmax, npoint), lambda j, order: (0, 0, 0)),
            ],
            out_specs=pl.BlockSpec((ntest, 1, kmax, nq), lambda j, order: (0, j, 0, 0)),
        ),
        out_shape=jax.ShapeDtypeStruct((ntest, nsource, kmax, nq), jnp.bfloat16),
        compiler_params=pltpu.CompilerParams(vmem_limit_bytes=VMEM_LIMIT),
        cost_estimate=pl.CostEstimate(
            flops=2 * ntest * nsource * npoint * nq * kmax,
            bytes_accessed=2 * ntest * nsource * kmax * nq,
            transcendentals=ntest * nsource * npoint * nq,
        ),
    )(order, test_features, source_features, basis_rows)


def tile_kernel(nshard, first, packed, *refs):
    order_ref, source_counts_ref, offsets_ref, test_counts_ref, left_ref = refs[:5]
    shard_refs, coeff_ref = refs[5 : 5 + nshard], refs[5 + nshard]
    start_ref = refs[6 + nshard] if packed else None
    tile_ref, sum_ref, total_ref = refs[-3:]
    j = pl.program_id(0)
    ntest, _, kmax, nq = left_ref.shape
    ndest, _, rows, _ = tile_ref.shape if packed else tile_ref.shape[:2] + tile_ref.shape[3:]
    width = shard_refs[0].shape[2]
    side = jnp.concatenate([shard_ref[0] for shard_ref in shard_refs], axis=0)
    row_ids = lax.broadcasted_iota(jnp.int32, (kmax, width), 0)
    column_ids = lax.broadcasted_iota(jnp.int32, (kmax, width), 1)
    tiles = jnp.dot(
        left_ref[...].reshape(ntest * kmax, nq), side, preferred_element_type=jnp.float32
    )
    count = source_counts_ref[order_ref[first + j]]
    masked = []
    for i in range(ntest):
        used = (row_ids < test_counts_ref[i]) & (column_ids < count)
        masked.append(jnp.where(used, tiles[i * kmax : (i + 1) * kmax], 0.0))
    if packed:
        offset = offsets_ref[order_ref[first + j]]
        shift = offset % LANES
        base = pl.multiple_of(offset - shift, LANES)
        low = lax.broadcasted_iota(jnp.int32, (kmax, LANES), 1) < shift
        for i in range(ntest):
            rolled = [
                pltpu.roll(masked[i][:, start : start + LANES], shift, axis=1)
                for start in range(0, width, LANES)
            ]
            for place in range(len(rolled) + 1):
                here = pl.ds(pl.multiple_of(base + place * LANES, LANES), LANES)
                if place == 0:
                    before = jnp.concatenate(
                        [tile_ref[dest, i, :, here].astype(jnp.float32) for dest in range(ndest)], axis=0
                    )
                else:
                    before = rolled[place - 1]
                after = rolled[place] if place < len(rolled) else jnp.zeros_like(before)
                window = jnp.where(low, before, after)
                for dest in range(ndest):
                    tile_ref[dest, i, :, here] = window[dest * rows : (dest + 1) * rows].astype(jnp.bfloat16)
    else:
        for i in range(ntest):
            for dest in range(ndest):
                tile_ref[dest, i, 0] = masked[i][dest * rows : (dest + 1) * rows].astype(jnp.bfloat16)
    rounded = jnp.concatenate([tile.astype(jnp.bfloat16) for tile in masked], axis=0)
    term = jnp.dot(rounded, coeff_ref[0], preferred_element_type=jnp.float32)

    @pl.when(j == 0)
    def _():
        total_ref[...] = term + start_ref[...] if packed else term

    @pl.when(j > 0)
    def _():
        total_ref[...] += term

    @pl.when(j == pl.num_programs(0) - 1)
    def _():
        if packed:
            for i in range(ntest):
                for dest in range(ndest):
                    top = i * kmax + dest * rows
                    sum_ref[dest, i] = total_ref[top : top + rows, :].astype(sum_ref.dtype)
        else:
            sum_ref[...] = total_ref[...]


def tiles_and_sums(ndest, first, tables, test_counts, left, shards, coefficients, start):
    ntest, nsource, kmax, nq = left.shape
    nshard = len(shards)
    part, width = shards[0].shape[1:]
    ncol = coefficients.shape[2]
    rows = kmax // ndest
    total_spec = pl.BlockSpec((ntest * kmax, ncol), lambda j, *_: (0, 0))
    packed = start is not None
    if packed:
        full = nsource * width + LANES
        tile_shape = jax.ShapeDtypeStruct((ndest, ntest, rows, full), jnp.bfloat16)
        tile_spec = pl.BlockSpec((ndest, ntest, rows, full), lambda j, *_: (0, 0, 0, 0))
        sum_shape = jax.ShapeDtypeStruct((ndest, ntest, rows, ncol), jnp.bfloat16)
        sum_spec = pl.BlockSpec((ndest, ntest, rows, ncol), lambda j, *_: (0, 0, 0, 0))
    else:
        tile_shape = jax.ShapeDtypeStruct((ndest, ntest, nsource, rows, width), jnp.bfloat16)
        tile_spec = pl.BlockSpec((ndest, ntest, 1, rows, width), lambda j, *_: (0, 0, j, 0, 0))
        sum_shape = jax.ShapeDtypeStruct((ntest * kmax, ncol), jnp.float32)
        sum_spec = total_spec
    return pl.pallas_call(
        functools.partial(tile_kernel, nshard, first, packed),
        grid_spec=pltpu.PrefetchScalarGridSpec(
            num_scalar_prefetch=4,
            grid=(nsource,),
            in_specs=[pl.BlockSpec((ntest, 1, kmax, nq), lambda j, *_: (0, j, 0, 0))]
            + [pl.BlockSpec((1, part, width), lambda j, *_: (j, 0, 0))] * nshard
            + [pl.BlockSpec((1, kmax, ncol), lambda j, order, *_: (order[first + j], 0, 0))]
            + ([total_spec] if packed else []),
            out_specs=(tile_spec, sum_spec),
            scratch_shapes=[pltpu.VMEM((ntest * kmax, ncol), jnp.float32)],
        ),
        out_shape=(tile_shape, sum_shape),
        compiler_params=pltpu.CompilerParams(vmem_limit_bytes=VMEM_LIMIT),
        cost_estimate=pl.CostEstimate(
            flops=2 * ntest * nsource * kmax * width * (nq + ncol),
            bytes_accessed=2 * ntest * nsource * kmax * (nq + width),
            transcendentals=0,
        ),
    )(*tables, test_counts, left, *shards, coefficients, *([start] if packed else []))


def unpack_kernel(cut, order_ref, counts_ref, offsets_ref, whole_ref, packed_ref, out_ref, rows_ref):
    nsrc, _, _, rows, width = whole_ref.shape
    packed_width = packed_ref.shape[3]
    nall = out_ref.shape[2]
    nblock = nall // nsrc
    ntile = width // LANES
    lanes = lax.broadcasted_iota(jnp.int32, (rows, LANES), 1)
    for source in range(nsrc):
        for place in range(nblock):
            block = order_ref[source * nblock + place]
            target = source * nblock + block
            if place < cut:
                for tile in range(ntile):
                    value = whole_ref[source, 0, place, :, tile * LANES : (tile + 1) * LANES]
                    rows_ref[pl.ds(tile * rows * nall + target, rows, stride=nall), :] = value.astype(jnp.float32)
                continue
            count = counts_ref[source * nblock + block]
            offset = offsets_ref[source * nblock + block]
            shift = offset % LANES
            base = offset - shift
            back = (LANES - shift) % LANES
            low = lanes < LANES - shift
            rolled = []
            for tile in range(ntile + 1):
                start = pl.multiple_of(jnp.minimum(base + tile * LANES, packed_width - LANES), LANES)
                piece = packed_ref[source, 0, :, pl.ds(start, LANES)].astype(jnp.float32)
                rolled.append(pltpu.roll(piece, back, axis=1))
            for tile in range(ntile):
                value = jnp.where(low, rolled[tile], rolled[tile + 1])
                value = jnp.where(lanes < count - tile * LANES, value, 0.0)
                rows_ref[pl.ds(tile * rows * nall + target, rows, stride=nall), :] = value
    for tile in range(ntile):
        part = rows_ref[tile * rows * nall : (tile + 1) * rows * nall, :].astype(out_ref.dtype)
        out_ref[0, :, :, tile * LANES : (tile + 1) * LANES] = part.reshape(rows, nall, LANES)


def unpack(cut, tables, whole, packed):
    nsrc, ntest, _, rows, width = whole.shape
    packed_width = packed.shape[3]
    nall = tables[0].shape[0]
    chunk = 16 if rows % 16 == 0 else rows
    return pl.pallas_call(
        functools.partial(unpack_kernel, cut),
        grid_spec=pltpu.PrefetchScalarGridSpec(
            num_scalar_prefetch=3,
            grid=(ntest, rows // chunk),
            in_specs=[
                pl.BlockSpec((nsrc, 1, cut, chunk, width), lambda i, k, *_: (0, i, 0, k, 0)),
                pl.BlockSpec((nsrc, 1, chunk, packed_width), lambda i, k, *_: (0, i, k, 0)),
            ],
            out_specs=pl.BlockSpec((1, chunk, nall, width), lambda i, k, *_: (i, k, 0, 0)),
            scratch_shapes=[pltpu.VMEM((chunk * nall * width // LANES, LANES), jnp.float32)],
        ),
        out_shape=jax.ShapeDtypeStruct((ntest, rows, nall, width), jnp.bfloat16),
        compiler_params=pltpu.CompilerParams(vmem_limit_bytes=VMEM_LIMIT),
    )(*tables, whole, packed)


def body(
    test_points, test_basis, test_counts, source_points, source_basis, source_counts, coefficients
):
    nsource, part, kmax = source_basis.shape
    ntest = test_points.shape[0]
    nsrc = lax.axis_size("src")
    ntest_axis = lax.axis_size("test")
    me_test = lax.axis_index("test")
    cut = max(1, nsource // 4)
    held = {}

    def gather(name, shard, left):
        got = {0: shard}
        bits = list(bits_down(ntest_axis))
        for bit in bits:
            if bit == bits[-1]:
                names = [o for o in got if o != 0]
                tied = lax.optimization_barrier(tuple(got[o] for o in names) + (left,))
                got.update(zip(names, tied[:-1]))
                left = tied[-1]
            for offset in list(got):
                got[offset ^ bit] = exchange(got[offset], "test", bit)
            if bit == bits[0]:
                held[name] = got[bit]
        return [got[offset] for offset in sorted(got)], left

    most = (nsource - cut) * kmax
    widths = list(range(most // 2, most, LANES)) + [most]

    order, offsets, basis_a, basis_b = pick(cut, source_counts, source_basis)
    tables = (order, source_counts, offsets)
    test_features, source_features, basis_rows = distance_features(
        ntest_axis, jnp.reshape(me_test, (1,)), test_points, source_points, test_basis
    )

    left_a = left_products(order, test_features, source_features, basis_rows, 0, cut)
    counts, marks = source_counts[None, :], [test_features, left_a]
    for place, bit in enumerate(reversed(list(bits_down(nsrc)))):
        if place > 0:
            counts, _ = lax.optimization_barrier((counts, marks[min(place, len(marks)) - 1]))
        counts = jnp.concatenate([counts, exchange(counts, "src", bit)], axis=0)

    shards_a, left_a = gather("a", basis_a, left_a)
    tiles_a, sums_a = tiles_and_sums(nsrc, 0, tables, test_counts, left_a, shards_a, coefficients, None)
    moved_a = lax.all_to_all(tiles_a, "src", split_axis=0, concat_axis=0, tiled=True)

    rest, _ = lax.optimization_barrier((basis_b, held["a"]))
    features_b, counts, _ = lax.optimization_barrier((source_features, counts, tiles_a))
    me_src = jnp.reshape(lax.axis_index("src"), (1,))
    *spread, branch = all_tables(cut, nsource, widths, me_src, counts.reshape(-1))
    left_b = left_products(order, test_features, features_b, basis_rows, cut, nsource)
    shards_b, left_b = gather("b", rest, left_b)
    tiles_b, summed = tiles_and_sums(
        nsrc, cut, tables, test_counts, left_b, shards_b, coefficients, sums_a
    )

    def finish(width, tiles_b, summed, moved_a, spread):
        moved_b = lax.all_to_all(tiles_b[..., :width], "src", split_axis=0, concat_axis=0, tiled=True)
        return unpack(cut, spread, moved_a, moved_b), sum_rows(summed, "src")

    return lax.switch(
        branch[0],
        [functools.partial(finish, width) for width in widths],
        tiles_b,
        summed,
        moved_a,
        tuple(spread),
    )


def solution(mesh):
    return jax.shard_map(
        body,
        mesh=mesh,
        in_specs=(
            P("test", None, None),
            P("test", None, None),
            P("test"),
            P("src", None, None),
            P("src", "test", None),
            P("src"),
            P("src", None, None),
        ),
        out_specs=(P("test", "src", None, None), P("test", "src", None)),
        check_vma=False,
    )
```

```python
import functools

import jax
import jax.numpy as jnp
from jax import lax
from jax.experimental import pallas as pl
from jax.experimental.pallas import tpu as pltpu
from jax.sharding import PartitionSpec as P

softening = 0.0025
QBLOCK = 256
LANES = 128
VMEM_LIMIT = 60 * 1024 * 1024


def exchange(x, axis, flip):
    size = lax.axis_size(axis)
    return lax.ppermute(x, axis, [(a, a ^ flip) for a in range(size)])


def bits_down(size):
    bit = size // 2
    while bit >= 1:
        yield bit
        bit //= 2


def sum_rows(total, axis):
    size = lax.axis_size(axis)
    me = lax.axis_index(axis)
    held, bit = total, 1
    while held.shape[0] > 4:
        pairs = held.reshape((held.shape[0] // 2, 2) + held.shape[1:])
        mine = (me // bit) % 2
        keep = lax.dynamic_index_in_dim(pairs, mine, 1, keepdims=False)
        give = lax.dynamic_index_in_dim(pairs, 1 - mine, 1, keepdims=False)
        got = exchange(give, axis, bit)
        held = (keep.astype(jnp.float32) + got.astype(jnp.float32)).astype(held.dtype)
        bit *= 2
    mine = me // bit
    result = lax.dynamic_index_in_dim(held, mine, 0, keepdims=False).astype(jnp.float32)
    for flip in range(1, held.shape[0]):
        give = lax.dynamic_index_in_dim(held, mine ^ flip, 0, keepdims=False)
        result = result + exchange(give, axis, flip * bit).astype(jnp.float32)
    return result.astype(total.dtype)


def rank_blocks(counts, cut):
    ranks = []
    for j, mine in enumerate(counts):
        rank = jnp.int32(0)
        for k, other in enumerate(counts):
            if k != j:
                ahead = other >= mine if k < j else other > mine
                rank += ahead.astype(jnp.int32)
        ranks.append(rank)
    offsets = []
    for j in range(len(counts)):
        offset = jnp.int32(0)
        for k, other in enumerate(counts):
            if k != j:
                offset += jnp.where((ranks[k] >= cut) & (ranks[k] < ranks[j]), other, 0)
        offsets.append(offset)
    return ranks, offsets


def pick_kernel(cut, counts_ref, basis_ref, order_ref, offsets_ref, first_ref, rest_ref):
    nblock = basis_ref.shape[0]
    ranks, offsets = rank_blocks([counts_ref[j] for j in range(nblock)], cut)
    for j in range(nblock):
        order_ref[ranks[j]] = jnp.int32(j)
        offsets_ref[j] = offsets[j]
    for place in range(nblock):
        block = basis_ref[order_ref[place]]
        if place < cut:
            first_ref[place] = block
        else:
            rest_ref[place - cut] = block


def pick(cut, counts, basis):
    nblock = basis.shape[0]
    smem, vmem = pl.BlockSpec(memory_space=pltpu.SMEM), pl.BlockSpec(memory_space=pltpu.VMEM)
    return pl.pallas_call(
        functools.partial(pick_kernel, cut),
        out_shape=(
            jax.ShapeDtypeStruct((nblock,), jnp.int32),
            jax.ShapeDtypeStruct((nblock,), jnp.int32),
            jax.ShapeDtypeStruct((cut,) + basis.shape[1:], basis.dtype),
            jax.ShapeDtypeStruct((nblock - cut,) + basis.shape[1:], basis.dtype),
        ),
        in_specs=[smem, vmem],
        out_specs=(smem, smem, vmem, vmem),
        compiler_params=pltpu.CompilerParams(vmem_limit_bytes=VMEM_LIMIT),
    )(counts, basis)


def tables_kernel(cut, nblock, widths, me_ref, counts_ref, order_ref, sorted_ref, offsets_ref, branch_ref):
    nsrc = sorted_ref.shape[0] // nblock

    def step(source, need):
        base = (source ^ me_ref[0]) * nblock
        counts = [counts_ref[base + j] for j in range(nblock)]
        ranks, offsets = rank_blocks(counts, cut)
        used = jnp.int32(0)
        for j in range(nblock):
            order_ref[source * nblock + ranks[j]] = jnp.int32(j)
            sorted_ref[source * nblock + j] = counts[j]
            offsets_ref[source * nblock + j] = offsets[j]
            used += jnp.where(ranks[j] >= cut, counts[j], 0)
        return jnp.maximum(need, used)

    need = lax.fori_loop(0, nsrc, step, jnp.int32(0))
    branch = jnp.int32(0)
    for width in widths[:-1]:
        branch += (need > width).astype(jnp.int32)
    branch_ref[0] = branch


def all_tables(cut, nblock, widths, me, counts):
    smem = pl.BlockSpec(memory_space=pltpu.SMEM)
    table = jax.ShapeDtypeStruct(counts.shape, jnp.int32)
    return pl.pallas_call(
        functools.partial(tables_kernel, cut, nblock, widths),
        out_shape=(table, table, table, jax.ShapeDtypeStruct((1,), jnp.int32)),
        in_specs=[smem, smem],
        out_specs=(smem,) * 4,
    )(me, counts)


def features_kernel(nshard, me_ref, test_ref, source_ref, basis_ref, test_out_ref, source_out_ref, basis_out_ref, rows_ref):
    part = source_ref.shape[2] // nshard

    def three_terms(x):
        high = x.astype(jnp.bfloat16).astype(jnp.float32)
        middle = (x - high).astype(jnp.bfloat16).astype(jnp.float32)
        return high, middle, x - high - middle

    def fill(centred, is_test):
        norm = jnp.sum(centred * centred, axis=0, keepdims=True)
        terms = three_terms(centred)
        norms = three_terms(norm + softening if is_test else norm)
        for a in range(3):
            for b in range(3):
                place = 3 * (3 * a + b)
                rows_ref[place : place + 3, :] = -2.0 * terms[a] if is_test else terms[b]
        for a in range(3):
            rows_ref[27 + a : 28 + a, :] = norms[a] if is_test else jnp.ones_like(norm)
            rows_ref[30 + a : 31 + a, :] = jnp.ones_like(norm) if is_test else norms[a]
        return rows_ref[...]

    rows_ref[...] = jnp.zeros_like(rows_ref)
    for i in range(test_ref.shape[0]):
        rows = fill(test_ref[i] - 0.5, True)
        test_out_ref[i] = rows.T.astype(jnp.bfloat16)
        basis_out_ref[i] = basis_ref[i].T
    for j in range(source_ref.shape[0]):
        pieces = []
        for offset in range(nshard):
            start = pl.multiple_of((me_ref[0] ^ offset) * part, part)
            pieces.append(source_ref[j, :, pl.ds(start, part)])
        rows = fill(jnp.concatenate(pieces, axis=1) - 0.5, False)
        source_out_ref[j] = rows.astype(jnp.bfloat16)


NFEATURE = 128


def distance_features(nshard, me, test_points, source_points, test_basis):
    ntest, _, npoint = test_points.shape
    nsource, _, nq = source_points.shape
    kmax = test_basis.shape[2]
    vmem = pl.BlockSpec(memory_space=pltpu.VMEM)
    return pl.pallas_call(
        functools.partial(features_kernel, nshard),
        out_shape=(
            jax.ShapeDtypeStruct((ntest, npoint, NFEATURE), jnp.bfloat16),
            jax.ShapeDtypeStruct((nsource, NFEATURE, nq), jnp.bfloat16),
            jax.ShapeDtypeStruct((ntest, kmax, npoint), jnp.bfloat16),
        ),
        in_specs=[pl.BlockSpec(memory_space=pltpu.SMEM), vmem, vmem, vmem],
        out_specs=(vmem, vmem, vmem),
        scratch_shapes=[pltpu.VMEM((NFEATURE, max(npoint, nq)), jnp.float32)],
        compiler_params=pltpu.CompilerParams(vmem_limit_bytes=VMEM_LIMIT),
    )(me, test_points, source_points, test_basis)


def left_kernel(order_ref, test_ref, source_ref, basis_ref, out_ref):
    nq = source_ref.shape[2]
    block = min(QBLOCK, nq)
    steps = [(i, start) for i in range(test_ref.shape[0]) for start in range(0, nq, block)]

    def kernel_block(i, start):
        squared = jnp.dot(
            test_ref[i], source_ref[0, :, start : start + block], preferred_element_type=jnp.float32
        )
        return lax.rsqrt(squared.astype(jnp.bfloat16))

    ready = kernel_block(*steps[0])
    for place, (i, start) in enumerate(steps):
        now = ready
        if place + 1 < len(steps):
            ready = kernel_block(*steps[place + 1])
        out_ref[i, 0, :, start : start + block] = jnp.dot(
            basis_ref[i], now, preferred_element_type=jnp.float32
        ).astype(jnp.bfloat16)


def left_products(order, test_features, source_features, basis_rows, first, last):
    ntest, npoint, nfeature = test_features.shape
    nq = source_features.shape[2]
    kmax = basis_rows.shape[1]
    nsource = last - first
    return pl.pallas_call(
        left_kernel,
        grid_spec=pltpu.PrefetchScalarGridSpec(
            num_scalar_prefetch=1,
            grid=(nsource,),
            in_specs=[
                pl.BlockSpec((ntest, npoint, nfeature), lambda j, order: (0, 0, 0)),
                pl.BlockSpec((1, nfeature, nq), lambda j, order: (order[first + j], 0, 0)),
                pl.BlockSpec((ntest, kmax, npoint), lambda j, order: (0, 0, 0)),
            ],
            out_specs=pl.BlockSpec((ntest, 1, kmax, nq), lambda j, order: (0, j, 0, 0)),
        ),
        out_shape=jax.ShapeDtypeStruct((ntest, nsource, kmax, nq), jnp.bfloat16),
        compiler_params=pltpu.CompilerParams(vmem_limit_bytes=VMEM_LIMIT),
        cost_estimate=pl.CostEstimate(
            flops=2 * ntest * nsource * npoint * nq * kmax,
            bytes_accessed=2 * ntest * nsource * kmax * nq,
            transcendentals=ntest * nsource * npoint * nq,
        ),
    )(order, test_features, source_features, basis_rows)


def tile_kernel(nshard, first, packed, *refs):
    order_ref, source_counts_ref, offsets_ref, test_counts_ref, left_ref = refs[:5]
    shard_refs = refs[5 : 5 + nshard]
    if packed:
        tile_ref, main_ref, over_ref, pack_ref = refs[5 + nshard :]
    else:
        (tile_ref,) = refs[5 + nshard :]
    j = pl.program_id(0)
    ntest, _, kmax, _ = left_ref.shape
    ndest, _, _, rows, width = tile_ref.shape
    count = source_counts_ref[order_ref[first + j]]

    def work(wide):
        side = jnp.concatenate([shard_ref[0, :, :wide] for shard_ref in shard_refs], axis=0)
        row_ids = lax.broadcasted_iota(jnp.int32, (kmax, wide), 0)
        column_ids = lax.broadcasted_iota(jnp.int32, (kmax, wide), 1)
        products = [
            jnp.dot(left_ref[i, 0], side, preferred_element_type=jnp.float32) for i in range(ntest)
        ]
        if packed:
            offset = offsets_ref[order_ref[first + j]]
            shift = offset % LANES
            base = offset - shift
            low = lax.broadcasted_iota(jnp.int32, (kmax, LANES), 1) < shift
        for i in range(ntest):
            used = (row_ids < test_counts_ref[i]) & (column_ids < count)
            tile = jnp.where(used, products[i], 0.0)
            for dest in range(ndest):
                tile_ref[dest, i, 0, :, :wide] = tile[dest * rows : (dest + 1) * rows].astype(jnp.bfloat16)
                if wide < width:
                    tile_ref[dest, i, 0, :, wide:] = jnp.zeros((rows, width - wide), jnp.bfloat16)
            if not packed:
                continue
            rolled = [
                pltpu.roll(tile[:, start : start + LANES], shift, axis=1) for start in range(0, wide, LANES)
            ]
            for place in range(len(rolled) + 1):
                here = pl.ds(pl.multiple_of(base + place * LANES, LANES), LANES)
                if place == 0:
                    before = jnp.concatenate(
                        [pack_ref[dest, i, :, here].astype(jnp.float32) for dest in range(ndest)], axis=0
                    )
                else:
                    before = rolled[place - 1]
                after = rolled[place] if place < len(rolled) else jnp.zeros_like(before)
                window = jnp.where(low, before, after)
                for dest in range(ndest):
                    pack_ref[dest, i, :, here] = window[dest * rows : (dest + 1) * rows].astype(jnp.bfloat16)

    narrow = width - LANES
    if narrow > 0:
        pl.when(count <= narrow)(lambda: work(narrow))
        pl.when(count > narrow)(lambda: work(width))
    else:
        work(width)

    if packed:

        @pl.when(j == pl.num_programs(0) - 1)
        def _():
            main = main_ref.shape[3]
            main_ref[...] = pack_ref[:, :, :, :main]
            over_ref[...] = pack_ref[:, :, :, main : main + over_ref.shape[3]]


def tiles(ndest, first, tables, test_counts, left, shards, main):
    ntest, nsource, kmax, nq = left.shape
    nshard = len(shards)
    part, width = shards[0].shape[1:]
    rows = kmax // ndest
    packed = main is not None
    shapes = [jax.ShapeDtypeStruct((ndest, ntest, nsource, rows, width), jnp.bfloat16)]
    specs = [pl.BlockSpec((ndest, ntest, 1, rows, width), lambda j, *_: (0, 0, j, 0, 0))]
    scratch = []
    if packed:
        for columns in (main, nsource * width - main):
            shape = (ndest, ntest, rows, columns)
            shapes.append(jax.ShapeDtypeStruct(shape, jnp.bfloat16))
            specs.append(pl.BlockSpec(shape, lambda j, *_: (0, 0, 0, 0)))
        scratch.append(pltpu.VMEM((ndest, ntest, rows, nsource * width + LANES), jnp.bfloat16))
    return pl.pallas_call(
        functools.partial(tile_kernel, nshard, first, packed),
        grid_spec=pltpu.PrefetchScalarGridSpec(
            num_scalar_prefetch=4,
            grid=(nsource,),
            in_specs=[pl.BlockSpec((ntest, 1, kmax, nq), lambda j, *_: (0, j, 0, 0))]
            + [pl.BlockSpec((1, part, width), lambda j, *_: (j, 0, 0))] * nshard,
            out_specs=specs,
            scratch_shapes=scratch,
        ),
        out_shape=shapes,
        compiler_params=pltpu.CompilerParams(vmem_limit_bytes=VMEM_LIMIT),
        cost_estimate=pl.CostEstimate(
            flops=2 * ntest * nsource * kmax * width * nq,
            bytes_accessed=2 * ntest * nsource * kmax * (nq + width),
            transcendentals=0,
        ),
    )(*tables, test_counts, left, *shards)


def project_kernel(cut, order_ref, first_ref, rest_ref, coeff_ref, sum_ref, total_ref):
    j = pl.program_id(0)
    ndest, ntest, _, rows, width = first_ref.shape

    def add(tile_ref, fresh):
        whole = [tile_ref[dest, i, 0] for i in range(ntest) for dest in range(ndest)]
        term = jnp.dot(jnp.concatenate(whole, axis=0), coeff_ref[0], preferred_element_type=jnp.float32)
        total_ref[...] = term if fresh else total_ref[...] + term

    pl.when(j == 0)(lambda: add(first_ref, True))
    pl.when((j > 0) & (j < cut))(lambda: add(first_ref, False))
    pl.when(j >= cut)(lambda: add(rest_ref, False))

    @pl.when(j == pl.num_programs(0) - 1)
    def _():
        for i in range(ntest):
            for dest in range(ndest):
                top = (i * ndest + dest) * rows
                sum_ref[dest, i] = total_ref[top : top + rows, :].astype(sum_ref.dtype)


def project(order, first, rest, coefficients):
    ndest, ntest, cut, rows, width = first.shape
    nsource, _, ncol = coefficients.shape
    block = (ndest, ntest, 1, rows, width)
    return pl.pallas_call(
        functools.partial(project_kernel, cut),
        grid_spec=pltpu.PrefetchScalarGridSpec(
            num_scalar_prefetch=1,
            grid=(nsource,),
            in_specs=[
                pl.BlockSpec(block, lambda j, order: (0, 0, jnp.minimum(j, cut - 1), 0, 0)),
                pl.BlockSpec(block, lambda j, order: (0, 0, jnp.maximum(j - cut, 0), 0, 0)),
                pl.BlockSpec((1, width, ncol), lambda j, order: (order[j], 0, 0)),
            ],
            out_specs=pl.BlockSpec((ndest, ntest, rows, ncol), lambda j, order: (0, 0, 0, 0)),
            scratch_shapes=[pltpu.VMEM((ndest * ntest * rows, ncol), jnp.float32)],
        ),
        out_shape=jax.ShapeDtypeStruct((ndest, ntest, rows, ncol), jnp.bfloat16),
        compiler_params=pltpu.CompilerParams(vmem_limit_bytes=VMEM_LIMIT),
        cost_estimate=pl.CostEstimate(
            flops=2 * ndest * ntest * rows * width * ncol * nsource,
            bytes_accessed=2 * ndest * ntest * rows * width * nsource,
            transcendentals=0,
        ),
    )(order, first, rest, coefficients)


def unpack_kernel(cut, order_ref, counts_ref, offsets_ref, whole_ref, packed_ref, out_ref, rows_ref):
    nsrc, _, _, rows, width = whole_ref.shape
    packed_width = packed_ref.shape[3]
    nall = out_ref.shape[2]
    nblock = nall // nsrc
    ntile = width // LANES
    lanes = lax.broadcasted_iota(jnp.int32, (rows, LANES), 1)

    @pl.loop(0, nsrc)
    def _(source):
        for place in range(nblock):
            block = order_ref[source * nblock + place]
            target = source * nblock + block
            if place < cut:
                rows_ref[target] = whole_ref[source, 0, place].astype(jnp.float32)
                continue
            count = counts_ref[target]
            offset = offsets_ref[target]
            shift = offset % LANES
            base = offset - shift
            back = (LANES - shift) % LANES
            low = lanes < LANES - shift
            rolled = []
            for tile in range(ntile + 1):
                start = pl.multiple_of(jnp.minimum(base + tile * LANES, packed_width - LANES), LANES)
                piece = packed_ref[source, 0, :, pl.ds(start, LANES)].astype(jnp.float32)
                rolled.append(pltpu.roll(piece, back, axis=1))
            for tile in range(ntile):
                value = jnp.where(low, rolled[tile], rolled[tile + 1])
                value = jnp.where(lanes < count - tile * LANES, value, 0.0)
                rows_ref[target, :, tile * LANES : (tile + 1) * LANES] = value

    @pl.loop(0, nall // 16)
    def _(group):
        here = pl.ds(pl.multiple_of(group * 16, 16), 16)
        turned = jnp.transpose(rows_ref[here], (1, 0, 2))
        out_ref[0, :, here, :] = turned.astype(out_ref.dtype)


def unpack(cut, tables, whole, packed):
    nsrc, ntest, _, rows, width = whole.shape
    packed_width = packed.shape[3]
    nall = tables[0].shape[0]
    chunk = 16 if rows % 16 == 0 else rows
    return pl.pallas_call(
        functools.partial(unpack_kernel, cut),
        grid_spec=pltpu.PrefetchScalarGridSpec(
            num_scalar_prefetch=3,
            grid=(ntest, rows // chunk),
            in_specs=[
                pl.BlockSpec((nsrc, 1, cut, chunk, width), lambda i, k, *_: (0, i, 0, k, 0)),
                pl.BlockSpec((nsrc, 1, chunk, packed_width), lambda i, k, *_: (0, i, k, 0)),
            ],
            out_specs=pl.BlockSpec((1, chunk, nall, width), lambda i, k, *_: (i, k, 0, 0)),
            scratch_shapes=[pltpu.VMEM((nall, chunk, width), jnp.float32)],
        ),
        out_shape=jax.ShapeDtypeStruct((ntest, rows, nall, width), jnp.bfloat16),
        compiler_params=pltpu.CompilerParams(vmem_limit_bytes=VMEM_LIMIT),
    )(*tables, whole, packed)


def body(
    test_points, test_basis, test_counts, source_points, source_basis, source_counts, coefficients
):
    nsource, part, kmax = source_basis.shape
    ntest = test_points.shape[0]
    nsrc = lax.axis_size("src")
    ntest_axis = lax.axis_size("test")
    me_test = lax.axis_index("test")
    cut = max(1, nsource // 4)
    held = {}

    def gather(name, shard, left):
        got = {0: shard}
        bits = list(bits_down(ntest_axis))
        for bit in bits:
            if bit == bits[-1]:
                names = [o for o in got if o != 0]
                tied = lax.optimization_barrier(tuple(got[o] for o in names) + (left,))
                got.update(zip(names, tied[:-1]))
                left = tied[-1]
            for offset in list(got):
                got[offset ^ bit] = exchange(got[offset], "test", bit)
            if bit == bits[0]:
                held[name] = got[bit]
        return [got[offset] for offset in sorted(got)], left

    most = (nsource - cut) * kmax
    main = min(most, -(-most * 7 // (9 * LANES)) * LANES)
    widths = [main, min(most, main + 2 * LANES), most]

    order, offsets, basis_a, basis_b = pick(cut, source_counts, source_basis)
    tables = (order, source_counts, offsets)
    test_features, source_features, basis_rows = distance_features(
        ntest_axis, jnp.reshape(me_test, (1,)), test_points, source_points, test_basis
    )

    left_a = left_products(order, test_features, source_features, basis_rows, 0, cut)
    shards_a, left_a = gather("a", basis_a, left_a)
    (tiles_a,) = tiles(nsrc, 0, tables, test_counts, left_a, shards_a, None)
    moved_a = lax.all_to_all(tiles_a, "src", split_axis=0, concat_axis=0, tiled=True)

    rest, _ = lax.optimization_barrier((basis_b, held["a"]))
    features_b, _ = lax.optimization_barrier((source_features, tiles_a))
    left_b = left_products(order, test_features, features_b, basis_rows, cut, nsource)
    shards_b, left_b = gather("b", rest, left_b)
    tiles_b, packed, beyond = tiles(nsrc, cut, tables, test_counts, left_b, shards_b, main)
    moved_b = lax.all_to_all(packed, "src", split_axis=0, concat_axis=0, tiled=True)

    projected = sum_rows(project(order, tiles_a, tiles_b, coefficients), "src")
    counts, _ = lax.optimization_barrier((source_counts, packed))
    counts = jnp.stack([counts] + [exchange(counts, "src", flip) for flip in range(1, nsrc)], axis=0)
    me_src = jnp.reshape(lax.axis_index("src"), (1,))
    *spread, branch = all_tables(cut, nsource, widths, me_src, counts.reshape(-1))

    def finish(width, beyond, moved_a, moved_b, spread):
        if width > main:
            more = lax.all_to_all(
                beyond[..., : width - main], "src", split_axis=0, concat_axis=0, tiled=True
            )
            moved_b = jnp.concatenate([moved_b, more], axis=3)
        return unpack(cut, spread, moved_a, moved_b)

    reduced = lax.switch(
        branch[0],
        [functools.partial(finish, width) for width in widths],
        beyond,
        moved_a,
        moved_b,
        tuple(spread),
    )
    return (reduced, projected)


def solution(mesh):
    return jax.shard_map(
        body,
        mesh=mesh,
        in_specs=(
            P("test", None, None),
            P("test", None, None),
            P("test"),
            P("src", None, None),
            P("src", "test", None),
            P("src"),
            P("src", None, None),
        ),
        out_specs=(P("test", "src", None, None), P("test", "src", None)),
        check_vma=False,
    )
```

```python
import functools

import jax
import jax.numpy as jnp
from jax import lax
from jax.experimental import pallas as pl
from jax.experimental.pallas import tpu as pltpu
from jax.sharding import PartitionSpec as P

softening = 0.0025
QBLOCK = 256
LANES = 128
VMEM_LIMIT = 60 * 1024 * 1024


def exchange(x, axis, flip):
    size = lax.axis_size(axis)
    return lax.ppermute(x, axis, [(a, a ^ flip) for a in range(size)])


def bits_down(size):
    bit = size // 2
    while bit >= 1:
        yield bit
        bit //= 2


def sum_rows(total, axis):
    size = lax.axis_size(axis)
    me = lax.axis_index(axis)
    held, bit = total, 1
    while held.shape[0] > 4:
        pairs = held.reshape((held.shape[0] // 2, 2) + held.shape[1:])
        mine = (me // bit) % 2
        keep = lax.dynamic_index_in_dim(pairs, mine, 1, keepdims=False)
        give = lax.dynamic_index_in_dim(pairs, 1 - mine, 1, keepdims=False)
        got = exchange(give, axis, bit)
        held = (keep.astype(jnp.float32) + got.astype(jnp.float32)).astype(held.dtype)
        bit *= 2
    mine = me // bit
    result = lax.dynamic_index_in_dim(held, mine, 0, keepdims=False).astype(jnp.float32)
    for flip in range(1, held.shape[0]):
        give = lax.dynamic_index_in_dim(held, mine ^ flip, 0, keepdims=False)
        result = result + exchange(give, axis, flip * bit).astype(jnp.float32)
    return result.astype(total.dtype)


def rank_blocks(counts, cut):
    ranks = []
    for j, mine in enumerate(counts):
        rank = jnp.int32(0)
        for k, other in enumerate(counts):
            if k != j:
                ahead = other >= mine if k < j else other > mine
                rank += ahead.astype(jnp.int32)
        ranks.append(rank)
    offsets = []
    for j in range(len(counts)):
        offset = jnp.int32(0)
        for k, other in enumerate(counts):
            if k != j:
                offset += jnp.where((ranks[k] >= cut) & (ranks[k] < ranks[j]), other, 0)
        offsets.append(offset)
    return ranks, offsets


def pick_kernel(cut, counts_ref, basis_ref, order_ref, offsets_ref, first_ref, rest_ref):
    nblock = basis_ref.shape[0]
    ranks, offsets = rank_blocks([counts_ref[j] for j in range(nblock)], cut)
    for j in range(nblock):
        order_ref[ranks[j]] = jnp.int32(j)
        offsets_ref[j] = offsets[j]
    for place in range(nblock):
        block = basis_ref[order_ref[place]]
        if place < cut:
            first_ref[place] = block
        else:
            rest_ref[place - cut] = block


def pick(cut, counts, basis):
    nblock = basis.shape[0]
    smem, vmem = pl.BlockSpec(memory_space=pltpu.SMEM), pl.BlockSpec(memory_space=pltpu.VMEM)
    return pl.pallas_call(
        functools.partial(pick_kernel, cut),
        out_shape=(
            jax.ShapeDtypeStruct((nblock,), jnp.int32),
            jax.ShapeDtypeStruct((nblock,), jnp.int32),
            jax.ShapeDtypeStruct((cut,) + basis.shape[1:], basis.dtype),
            jax.ShapeDtypeStruct((nblock - cut,) + basis.shape[1:], basis.dtype),
        ),
        in_specs=[smem, vmem],
        out_specs=(smem, smem, vmem, vmem),
        compiler_params=pltpu.CompilerParams(vmem_limit_bytes=VMEM_LIMIT),
    )(counts, basis)


def tables_kernel(cut, nblock, widths, counts_ref, order_ref, offsets_ref, branch_ref):
    def step(source, need):
        base = source * nblock
        counts = [counts_ref[base + j] for j in range(nblock)]
        ranks, offsets = rank_blocks(counts, cut)
        used = jnp.int32(0)
        for j in range(nblock):
            order_ref[base + ranks[j]] = jnp.int32(j)
            offsets_ref[base + j] = offsets[j]
            used += jnp.where(ranks[j] >= cut, counts[j], 0)
        return jnp.maximum(need, used)

    need = lax.fori_loop(0, counts_ref.shape[0] // nblock, step, jnp.int32(0))
    branch = jnp.int32(0)
    for width in widths[:-1]:
        branch += (need > width).astype(jnp.int32)
    branch_ref[0] = branch


def all_tables(cut, nblock, widths, counts):
    smem = pl.BlockSpec(memory_space=pltpu.SMEM)
    table = jax.ShapeDtypeStruct(counts.shape, jnp.int32)
    return pl.pallas_call(
        functools.partial(tables_kernel, cut, nblock, widths),
        out_shape=(table, table, jax.ShapeDtypeStruct((1,), jnp.int32)),
        in_specs=[smem],
        out_specs=(smem,) * 3,
    )(counts)


def features_kernel(nshard, me_ref, test_ref, source_ref, basis_ref, test_out_ref, source_out_ref, basis_out_ref, rows_ref):
    part = source_ref.shape[2] // nshard

    def three_terms(x):
        high = x.astype(jnp.bfloat16).astype(jnp.float32)
        middle = (x - high).astype(jnp.bfloat16).astype(jnp.float32)
        return high, middle, x - high - middle

    def fill(centred, is_test):
        norm = jnp.sum(centred * centred, axis=0, keepdims=True)
        terms = three_terms(centred)
        norms = three_terms(norm + softening if is_test else norm)
        for a in range(3):
            for b in range(3):
                place = 3 * (3 * a + b)
                rows_ref[place : place + 3, :] = -2.0 * terms[a] if is_test else terms[b]
        for a in range(3):
            rows_ref[27 + a : 28 + a, :] = norms[a] if is_test else jnp.ones_like(norm)
            rows_ref[30 + a : 31 + a, :] = jnp.ones_like(norm) if is_test else norms[a]
        return rows_ref[...]

    rows_ref[...] = jnp.zeros_like(rows_ref)
    for i in range(test_ref.shape[1]):
        rows = fill(test_ref[:, i, :] - 0.5, True)
        test_out_ref[i] = rows.T.astype(jnp.bfloat16)
        basis_out_ref[i] = basis_ref[i].T
    for j in range(source_ref.shape[1]):
        pieces = []
        for offset in range(nshard):
            start = pl.multiple_of((me_ref[0] ^ offset) * part, part)
            pieces.append(source_ref[:, j, pl.ds(start, part)])
        rows = fill(jnp.concatenate(pieces, axis=1) - 0.5, False)
        source_out_ref[j] = rows.astype(jnp.bfloat16)


NFEATURE = 128


def distance_features(nshard, me, test_points, source_points, test_basis):
    ntest, _, npoint = test_points.shape
    nsource, _, nq = source_points.shape
    kmax = test_basis.shape[2]
    vmem = pl.BlockSpec(memory_space=pltpu.VMEM)
    return pl.pallas_call(
        functools.partial(features_kernel, nshard),
        out_shape=(
            jax.ShapeDtypeStruct((ntest, npoint, NFEATURE), jnp.bfloat16),
            jax.ShapeDtypeStruct((nsource, NFEATURE, nq), jnp.bfloat16),
            jax.ShapeDtypeStruct((ntest, kmax, npoint), jnp.bfloat16),
        ),
        in_specs=[pl.BlockSpec(memory_space=pltpu.SMEM), vmem, vmem, vmem],
        out_specs=(vmem, vmem, vmem),
        scratch_shapes=[pltpu.VMEM((NFEATURE, max(npoint, nq)), jnp.float32)],
        compiler_params=pltpu.CompilerParams(vmem_limit_bytes=VMEM_LIMIT),
    )(me, test_points.transpose(1, 0, 2), source_points.transpose(1, 0, 2), test_basis)


def left_kernel(order_ref, test_ref, source_ref, basis_ref, out_ref):
    nq = source_ref.shape[2]
    block = min(QBLOCK, nq)
    steps = [(i, start) for i in range(test_ref.shape[0]) for start in range(0, nq, block)]

    def kernel_block(i, start):
        squared = jnp.dot(
            test_ref[i], source_ref[0, :, start : start + block], preferred_element_type=jnp.float32
        )
        return lax.rsqrt(squared.astype(jnp.bfloat16))

    ready = kernel_block(*steps[0])
    for place, (i, start) in enumerate(steps):
        now = ready
        if place + 1 < len(steps):
            ready = kernel_block(*steps[place + 1])
        out_ref[i, 0, :, start : start + block] = jnp.dot(
            basis_ref[i], now, preferred_element_type=jnp.float32
        ).astype(jnp.bfloat16)


def left_products(order, test_features, source_features, basis_rows, first, last):
    ntest, npoint, nfeature = test_features.shape
    nq = source_features.shape[2]
    kmax = basis_rows.shape[1]
    nsource = last - first
    return pl.pallas_call(
        left_kernel,
        grid_spec=pltpu.PrefetchScalarGridSpec(
            num_scalar_prefetch=1,
            grid=(nsource,),
            in_specs=[
                pl.BlockSpec((ntest, npoint, nfeature), lambda j, order: (0, 0, 0)),
                pl.BlockSpec((1, nfeature, nq), lambda j, order: (order[first + j], 0, 0)),
                pl.BlockSpec((ntest, kmax, npoint), lambda j, order: (0, 0, 0)),
            ],
            out_specs=pl.BlockSpec((ntest, 1, kmax, nq), lambda j, order: (0, j, 0, 0)),
        ),
        out_shape=jax.ShapeDtypeStruct((ntest, nsource, kmax, nq), jnp.bfloat16),
        compiler_params=pltpu.CompilerParams(vmem_limit_bytes=VMEM_LIMIT),
        cost_estimate=pl.CostEstimate(
            flops=2 * ntest * nsource * npoint * nq * kmax,
            bytes_accessed=2 * ntest * nsource * kmax * nq,
            transcendentals=ntest * nsource * npoint * nq,
        ),
    )(order, test_features, source_features, basis_rows)


def tile_kernel(nshard, first, packed, *refs):
    order_ref, source_counts_ref, offsets_ref, test_counts_ref, left_ref = refs[:5]
    shard_refs = refs[5 : 5 + nshard]
    if packed:
        tile_ref, main_ref, over_ref, pack_ref = refs[5 + nshard :]
    else:
        (tile_ref,) = refs[5 + nshard :]
    j = pl.program_id(0)
    ntest, _, kmax, _ = left_ref.shape
    ndest, _, _, rows, width = tile_ref.shape
    count = source_counts_ref[order_ref[first + j]]

    def work(wide):
        side = jnp.concatenate([shard_ref[0, :, :wide] for shard_ref in shard_refs], axis=0)
        row_ids = lax.broadcasted_iota(jnp.int32, (kmax, wide), 0)
        column_ids = lax.broadcasted_iota(jnp.int32, (kmax, wide), 1)
        products = [
            jnp.dot(left_ref[i, 0], side, preferred_element_type=jnp.float32) for i in range(ntest)
        ]
        if packed:
            offset = offsets_ref[order_ref[first + j]]
            shift = offset % LANES
            base = offset - shift
            low = lax.broadcasted_iota(jnp.int32, (kmax, LANES), 1) < shift
        for i in range(ntest):
            used = (row_ids < test_counts_ref[i]) & (column_ids < count)
            tile = jnp.where(used, products[i], 0.0)
            for dest in range(ndest):
                tile_ref[dest, i, 0, :, :wide] = tile[dest * rows : (dest + 1) * rows].astype(jnp.bfloat16)
                if wide < width:
                    tile_ref[dest, i, 0, :, wide:] = jnp.zeros((rows, width - wide), jnp.bfloat16)
            if not packed:
                continue
            rolled = [
                pltpu.roll(tile[:, start : start + LANES], shift, axis=1) for start in range(0, wide, LANES)
            ]
            for place in range(len(rolled) + 1):
                here = pl.ds(pl.multiple_of(base + place * LANES, LANES), LANES)
                if place == 0:
                    before = jnp.concatenate(
                        [pack_ref[dest, i, :, here].astype(jnp.float32) for dest in range(ndest)], axis=0
                    )
                else:
                    before = rolled[place - 1]
                after = rolled[place] if place < len(rolled) else jnp.zeros_like(before)
                window = jnp.where(low, before, after)
                for dest in range(ndest):
                    pack_ref[dest, i, :, here] = window[dest * rows : (dest + 1) * rows].astype(jnp.bfloat16)

    narrow = width - LANES
    if narrow > 0:
        pl.when(count <= narrow)(lambda: work(narrow))
        pl.when(count > narrow)(lambda: work(width))
    else:
        work(width)

    if packed:

        @pl.when(j == pl.num_programs(0) - 1)
        def _():
            main = main_ref.shape[3]
            main_ref[...] = pack_ref[:, :, :, :main]
            over_ref[...] = pack_ref[:, :, :, main : main + over_ref.shape[3]]


def tiles(ndest, first, tables, test_counts, left, shards, main):
    ntest, nsource, kmax, nq = left.shape
    nshard = len(shards)
    part, width = shards[0].shape[1:]
    rows = kmax // ndest
    packed = main is not None
    shapes = [jax.ShapeDtypeStruct((ndest, ntest, nsource, rows, width), jnp.bfloat16)]
    specs = [pl.BlockSpec((ndest, ntest, 1, rows, width), lambda j, *_: (0, 0, j, 0, 0))]
    scratch = []
    if packed:
        for columns in (main, nsource * width - main):
            shape = (ndest, ntest, rows, columns)
            shapes.append(jax.ShapeDtypeStruct(shape, jnp.bfloat16))
            specs.append(pl.BlockSpec(shape, lambda j, *_: (0, 0, 0, 0)))
        scratch.append(pltpu.VMEM((ndest, ntest, rows, nsource * width + LANES), jnp.bfloat16))
    return pl.pallas_call(
        functools.partial(tile_kernel, nshard, first, packed),
        grid_spec=pltpu.PrefetchScalarGridSpec(
            num_scalar_prefetch=4,
            grid=(nsource,),
            in_specs=[pl.BlockSpec((ntest, 1, kmax, nq), lambda j, *_: (0, j, 0, 0))]
            + [pl.BlockSpec((1, part, width), lambda j, *_: (j, 0, 0))] * nshard,
            out_specs=specs,
            scratch_shapes=scratch,
        ),
        out_shape=shapes,
        compiler_params=pltpu.CompilerParams(vmem_limit_bytes=VMEM_LIMIT),
        cost_estimate=pl.CostEstimate(
            flops=2 * ntest * nsource * kmax * width * nq,
            bytes_accessed=2 * ntest * nsource * kmax * (nq + width),
            transcendentals=0,
        ),
    )(*tables, test_counts, left, *shards)


def project_kernel(cut, order_ref, first_ref, rest_ref, coeff_ref, sum_ref, total_ref):
    j = pl.program_id(0)
    ndest, ntest, _, rows, width = first_ref.shape

    def add(tile_ref, fresh):
        whole = [tile_ref[dest, i, 0] for i in range(ntest) for dest in range(ndest)]
        term = jnp.dot(jnp.concatenate(whole, axis=0), coeff_ref[0], preferred_element_type=jnp.float32)
        total_ref[...] = term if fresh else total_ref[...] + term

    pl.when(j == 0)(lambda: add(first_ref, True))
    pl.when((j > 0) & (j < cut))(lambda: add(first_ref, False))
    pl.when(j >= cut)(lambda: add(rest_ref, False))

    @pl.when(j == pl.num_programs(0) - 1)
    def _():
        for i in range(ntest):
            for dest in range(ndest):
                top = (i * ndest + dest) * rows
                sum_ref[dest, i] = total_ref[top : top + rows, :].astype(sum_ref.dtype)


def project(order, first, rest, coefficients):
    ndest, ntest, cut, rows, width = first.shape
    nsource, _, ncol = coefficients.shape
    block = (ndest, ntest, 1, rows, width)
    return pl.pallas_call(
        functools.partial(project_kernel, cut),
        grid_spec=pltpu.PrefetchScalarGridSpec(
            num_scalar_prefetch=1,
            grid=(nsource,),
            in_specs=[
                pl.BlockSpec(block, lambda j, order: (0, 0, jnp.minimum(j, cut - 1), 0, 0)),
                pl.BlockSpec(block, lambda j, order: (0, 0, jnp.maximum(j - cut, 0), 0, 0)),
                pl.BlockSpec((1, width, ncol), lambda j, order: (order[j], 0, 0)),
            ],
            out_specs=pl.BlockSpec((ndest, ntest, rows, ncol), lambda j, order: (0, 0, 0, 0)),
            scratch_shapes=[pltpu.VMEM((ndest * ntest * rows, ncol), jnp.float32)],
        ),
        out_shape=jax.ShapeDtypeStruct((ndest, ntest, rows, ncol), jnp.bfloat16),
        compiler_params=pltpu.CompilerParams(vmem_limit_bytes=VMEM_LIMIT),
        cost_estimate=pl.CostEstimate(
            flops=2 * ndest * ntest * rows * width * ncol * nsource,
            bytes_accessed=2 * ndest * ntest * rows * width * nsource,
            transcendentals=0,
        ),
    )(order, first, rest, coefficients)


def unpack_kernel(cut, order_ref, counts_ref, offsets_ref, whole_ref, packed_ref, out_ref, rows_ref):
    nsrc, _, _, rows, width = whole_ref.shape
    packed_width = packed_ref.shape[3]
    nall = out_ref.shape[2]
    nblock = nall // nsrc
    ntile = width // LANES
    step = 16 if rows % 16 == 0 else rows
    lanes = lax.broadcasted_iota(jnp.int32, (rows, LANES), 1)

    @pl.loop(0, nsrc)
    def _(source):
        for place in range(nblock):
            block = order_ref[source * nblock + place]
            target = source * nblock + block
            if place < cut:
                rows_ref[target] = whole_ref[source, 0, place].astype(jnp.float32)
                continue
            count = counts_ref[target]
            offset = offsets_ref[target]
            shift = offset % LANES
            base = offset - shift
            back = (LANES - shift) % LANES
            low = lanes < LANES - shift
            rolled = []
            for tile in range(ntile + 1):
                start = pl.multiple_of(jnp.minimum(base + tile * LANES, packed_width - LANES), LANES)
                piece = packed_ref[source, 0, :, pl.ds(start, LANES)].astype(jnp.float32)
                rolled.append(pltpu.roll(piece, back, axis=1))
            for tile in range(ntile):
                value = jnp.where(low, rolled[tile], rolled[tile + 1])
                value = jnp.where(lanes < count - tile * LANES, value, 0.0)
                rows_ref[target, :, tile * LANES : (tile + 1) * LANES] = value

    @pl.loop(0, nall // 16)
    def _(group):
        here = pl.ds(pl.multiple_of(group * 16, 16), 16)
        for top in range(0, rows, step):
            turned = jnp.transpose(rows_ref[here, top : top + step, :], (1, 0, 2))
            out_ref[0, top : top + step, here, :] = turned.astype(out_ref.dtype)


def unpack(cut, tables, whole, packed):
    nsrc, ntest, _, rows, width = whole.shape
    packed_width = packed.shape[3]
    nall = tables[0].shape[0]
    return pl.pallas_call(
        functools.partial(unpack_kernel, cut),
        grid_spec=pltpu.PrefetchScalarGridSpec(
            num_scalar_prefetch=3,
            grid=(ntest,),
            in_specs=[
                pl.BlockSpec((nsrc, 1, cut, rows, width), lambda i, *_: (0, i, 0, 0, 0)),
                pl.BlockSpec((nsrc, 1, rows, packed_width), lambda i, *_: (0, i, 0, 0)),
            ],
            out_specs=pl.BlockSpec((1, rows, nall, width), lambda i, *_: (i, 0, 0, 0)),
            scratch_shapes=[pltpu.VMEM((nall, rows, width), jnp.float32)],
        ),
        out_shape=jax.ShapeDtypeStruct((ntest, rows, nall, width), jnp.bfloat16),
        compiler_params=pltpu.CompilerParams(vmem_limit_bytes=VMEM_LIMIT),
    )(*tables, whole, packed)


def body(
    test_points, test_basis, test_counts, source_points, source_basis, source_counts, coefficients
):
    nsource, part, kmax = source_basis.shape
    ntest = test_points.shape[0]
    nsrc = lax.axis_size("src")
    ntest_axis = lax.axis_size("test")
    me_test = lax.axis_index("test")
    cut = max(1, nsource // 4)
    held = {}

    def gather(name, shard, left):
        got = {0: shard}
        bits = list(bits_down(ntest_axis))
        for bit in bits:
            if bit == bits[-1]:
                names = [o for o in got if o != 0]
                tied = lax.optimization_barrier(tuple(got[o] for o in names) + (left,))
                got.update(zip(names, tied[:-1]))
                left = tied[-1]
            for offset in list(got):
                got[offset ^ bit] = exchange(got[offset], "test", bit)
            if bit == bits[0]:
                held[name] = got[bit]
        return [got[offset] for offset in sorted(got)], left

    most = (nsource - cut) * kmax
    main = min(most, -(-most * 7 // (9 * LANES)) * LANES)
    widths = [main, min(most, main + 2 * LANES), most]

    order, offsets, basis_a, basis_b = pick(cut, source_counts, source_basis)
    tables = (order, source_counts, offsets)
    counts = lax.all_gather(source_counts, "src", axis=0, tiled=True)
    test_points, counts = lax.optimization_barrier((test_points, counts))
    test_features, source_features, basis_rows = distance_features(
        ntest_axis, jnp.reshape(me_test, (1,)), test_points, source_points, test_basis
    )

    left_a = left_products(order, test_features, source_features, basis_rows, 0, cut)
    shards_a, left_a = gather("a", basis_a, left_a)
    (tiles_a,) = tiles(nsrc, 0, tables, test_counts, left_a, shards_a, None)
    moved_a = lax.all_to_all(tiles_a, "src", split_axis=0, concat_axis=0, tiled=True)

    rest, _ = lax.optimization_barrier((basis_b, held["a"]))
    features_b, _ = lax.optimization_barrier((source_features, tiles_a))
    left_b = left_products(order, test_features, features_b, basis_rows, cut, nsource)
    shards_b, left_b = gather("b", rest, left_b)
    tiles_b, packed, beyond = tiles(nsrc, cut, tables, test_counts, left_b, shards_b, main)
    moved_b = lax.all_to_all(packed, "src", split_axis=0, concat_axis=0, tiled=True)

    projected = sum_rows(project(order, tiles_a, tiles_b, coefficients), "src")
    counts, _ = lax.optimization_barrier((counts, packed))
    all_order, all_offsets, branch = all_tables(cut, nsource, widths, counts)
    spread = (all_order, counts, all_offsets)

    def finish(width, beyond, moved_a, moved_b, spread):
        if width > main:
            more = lax.all_to_all(
                beyond[..., : width - main], "src", split_axis=0, concat_axis=0, tiled=True
            )
            moved_b = jnp.concatenate([moved_b, more], axis=3)
        return unpack(cut, spread, moved_a, moved_b)

    reduced = lax.switch(
        branch[0],
        [functools.partial(finish, width) for width in widths],
        beyond,
        moved_a,
        moved_b,
        spread,
    )
    return (reduced, projected)


def solution(mesh):
    return jax.shard_map(
        body,
        mesh=mesh,
        in_specs=(
            P("test", None, None),
            P("test", None, None),
            P("test"),
            P("src", None, None),
            P("src", "test", None),
            P("src"),
            P("src", None, None),
        ),
        out_specs=(P("test", "src", None, None), P("test", "src", None)),
        check_vma=False,
    )
```

```python
import functools

import jax
import jax.numpy as jnp
from jax import lax
from jax.experimental import pallas as pl
from jax.experimental.pallas import tpu as pltpu
from jax.sharding import PartitionSpec as P

softening = 0.0025
QBLOCK = 256
LANES = 128
VMEM_LIMIT = 60 * 1024 * 1024


def exchange(x, axis, flip):
    size = lax.axis_size(axis)
    return lax.ppermute(x, axis, [(a, a ^ flip) for a in range(size)])


def bits_down(size):
    bit = size // 2
    while bit >= 1:
        yield bit
        bit //= 2


def sum_rows(total, axis):
    size = lax.axis_size(axis)
    me = lax.axis_index(axis)
    held, bit = total, 1
    while held.shape[0] > 4:
        pairs = held.reshape((held.shape[0] // 2, 2) + held.shape[1:])
        mine = (me // bit) % 2
        keep = lax.dynamic_index_in_dim(pairs, mine, 1, keepdims=False)
        give = lax.dynamic_index_in_dim(pairs, 1 - mine, 1, keepdims=False)
        got = exchange(give, axis, bit)
        held = (keep.astype(jnp.float32) + got.astype(jnp.float32)).astype(held.dtype)
        bit *= 2
    mine = me // bit
    result = lax.dynamic_index_in_dim(held, mine, 0, keepdims=False).astype(jnp.float32)
    for flip in range(1, held.shape[0]):
        give = lax.dynamic_index_in_dim(held, mine ^ flip, 0, keepdims=False)
        result = result + exchange(give, axis, flip * bit).astype(jnp.float32)
    return result.astype(total.dtype)


def rank_blocks(counts, cut):
    ranks = []
    for j, mine in enumerate(counts):
        rank = jnp.int32(0)
        for k, other in enumerate(counts):
            if k != j:
                ahead = other >= mine if k < j else other > mine
                rank += ahead.astype(jnp.int32)
        ranks.append(rank)
    offsets = []
    for j in range(len(counts)):
        offset = jnp.int32(0)
        for k, other in enumerate(counts):
            if k != j:
                offset += jnp.where((ranks[k] >= cut) & (ranks[k] < ranks[j]), other, 0)
        offsets.append(offset)
    return ranks, offsets


def pick_kernel(cut, counts_ref, basis_ref, order_ref, offsets_ref, first_ref, rest_ref):
    nblock = basis_ref.shape[0]
    ranks, offsets = rank_blocks([counts_ref[j] for j in range(nblock)], cut)
    for j in range(nblock):
        order_ref[ranks[j]] = jnp.int32(j)
        offsets_ref[j] = offsets[j]
    for place in range(nblock):
        block = basis_ref[order_ref[place]]
        if place < cut:
            first_ref[place] = block
        else:
            rest_ref[place - cut] = block


def pick(cut, counts, basis):
    nblock = basis.shape[0]
    smem, vmem = pl.BlockSpec(memory_space=pltpu.SMEM), pl.BlockSpec(memory_space=pltpu.VMEM)
    return pl.pallas_call(
        functools.partial(pick_kernel, cut),
        out_shape=(
            jax.ShapeDtypeStruct((nblock,), jnp.int32),
            jax.ShapeDtypeStruct((nblock,), jnp.int32),
            jax.ShapeDtypeStruct((cut,) + basis.shape[1:], basis.dtype),
            jax.ShapeDtypeStruct((nblock - cut,) + basis.shape[1:], basis.dtype),
        ),
        in_specs=[smem, vmem],
        out_specs=(smem, smem, vmem, vmem),
        compiler_params=pltpu.CompilerParams(vmem_limit_bytes=VMEM_LIMIT),
    )(counts, basis)


def tables_kernel(cut, nblock, widths, me_ref, *refs):
    *group_refs, counts_ref, order_ref, offsets_ref, branch_ref, joined_ref = refs
    group = group_refs[0].shape[0]
    for place, group_ref in enumerate(group_refs):
        for k in range(group):
            joined_ref[place * group + k] = group_ref[k]

    def step(source, need):
        base = source * nblock
        theirs = (source ^ me_ref[0]) * nblock
        counts = [joined_ref[theirs + j] for j in range(nblock)]
        ranks, offsets = rank_blocks(counts, cut)
        used = jnp.int32(0)
        for j in range(nblock):
            counts_ref[base + j] = counts[j]
            order_ref[base + ranks[j]] = jnp.int32(j)
            offsets_ref[base + j] = offsets[j]
            used += jnp.where(ranks[j] >= cut, counts[j], 0)
        return jnp.maximum(need, used)

    need = lax.fori_loop(0, counts_ref.shape[0] // nblock, step, jnp.int32(0))
    branch = jnp.int32(0)
    for width in widths[:-1]:
        branch += (need > width).astype(jnp.int32)
    branch_ref[0] = branch


def all_tables(cut, nblock, widths, me, groups):
    smem = pl.BlockSpec(memory_space=pltpu.SMEM)
    total = sum(group.shape[0] for group in groups)
    table = jax.ShapeDtypeStruct((total,), jnp.int32)
    return pl.pallas_call(
        functools.partial(tables_kernel, cut, nblock, widths),
        out_shape=(table, table, table, jax.ShapeDtypeStruct((1,), jnp.int32)),
        in_specs=[smem] * (1 + len(groups)),
        out_specs=(smem,) * 4,
        scratch_shapes=[pltpu.SMEM((total,), jnp.int32)],
    )(me, *groups)


def features_kernel(nshard, me_ref, test_ref, source_ref, basis_ref, *refs):
    *counts_refs, test_out_ref, source_out_ref, basis_out_ref, joined_ref, rows_ref = refs
    part = source_ref.shape[2] // nshard
    nblock = counts_refs[0].shape[0]
    for place, counts_ref in enumerate(counts_refs):
        for j in range(nblock):
            joined_ref[place * nblock + j] = counts_ref[j]

    def three_terms(x):
        high = x.astype(jnp.bfloat16).astype(jnp.float32)
        middle = (x - high).astype(jnp.bfloat16).astype(jnp.float32)
        return high, middle, x - high - middle

    def fill(centred, is_test):
        norm = jnp.sum(centred * centred, axis=0, keepdims=True)
        terms = three_terms(centred)
        norms = three_terms(norm + softening if is_test else norm)
        for a in range(3):
            for b in range(3):
                place = 3 * (3 * a + b)
                rows_ref[place : place + 3, :] = -2.0 * terms[a] if is_test else terms[b]
        for a in range(3):
            rows_ref[27 + a : 28 + a, :] = norms[a] if is_test else jnp.ones_like(norm)
            rows_ref[30 + a : 31 + a, :] = jnp.ones_like(norm) if is_test else norms[a]
        return rows_ref[...]

    rows_ref[...] = jnp.zeros_like(rows_ref)
    for i in range(test_ref.shape[1]):
        rows = fill(test_ref[:, i, :] - 0.5, True)
        test_out_ref[i] = rows.T.astype(jnp.bfloat16)
        basis_out_ref[i] = basis_ref[i].T
    for j in range(source_ref.shape[1]):
        pieces = []
        for offset in range(nshard):
            start = pl.multiple_of((me_ref[0] ^ offset) * part, part)
            pieces.append(source_ref[:, j, pl.ds(start, part)])
        rows = fill(jnp.concatenate(pieces, axis=1) - 0.5, False)
        source_out_ref[j] = rows.astype(jnp.bfloat16)


NFEATURE = 128


def distance_features(nshard, me, test_points, source_points, test_basis, counts):
    ntest, _, npoint = test_points.shape
    nsource, _, nq = source_points.shape
    kmax = test_basis.shape[2]
    smem, vmem = pl.BlockSpec(memory_space=pltpu.SMEM), pl.BlockSpec(memory_space=pltpu.VMEM)
    return pl.pallas_call(
        functools.partial(features_kernel, nshard),
        out_shape=(
            jax.ShapeDtypeStruct((ntest, npoint, NFEATURE), jnp.bfloat16),
            jax.ShapeDtypeStruct((nsource, NFEATURE, nq), jnp.bfloat16),
            jax.ShapeDtypeStruct((ntest, kmax, npoint), jnp.bfloat16),
            jax.ShapeDtypeStruct((len(counts) * nsource,), jnp.int32),
        ),
        in_specs=[smem, vmem, vmem, vmem] + [smem] * len(counts),
        out_specs=(vmem, vmem, vmem, smem),
        scratch_shapes=[pltpu.VMEM((NFEATURE, max(npoint, nq)), jnp.float32)],
        compiler_params=pltpu.CompilerParams(vmem_limit_bytes=VMEM_LIMIT),
    )(me, test_points.transpose(1, 0, 2), source_points.transpose(1, 0, 2), test_basis, *counts)


def left_kernel(order_ref, test_ref, source_ref, basis_ref, out_ref):
    nq = source_ref.shape[2]
    block = min(QBLOCK, nq)
    steps = [(i, start) for i in range(test_ref.shape[0]) for start in range(0, nq, block)]

    def kernel_block(i, start):
        squared = jnp.dot(
            test_ref[i], source_ref[0, :, start : start + block], preferred_element_type=jnp.float32
        )
        return lax.rsqrt(squared.astype(jnp.bfloat16))

    ready = kernel_block(*steps[0])
    for place, (i, start) in enumerate(steps):
        now = ready
        if place + 1 < len(steps):
            ready = kernel_block(*steps[place + 1])
        out_ref[i, 0, :, start : start + block] = jnp.dot(
            basis_ref[i], now, preferred_element_type=jnp.float32
        ).astype(jnp.bfloat16)


def left_products(order, test_features, source_features, basis_rows, first, last):
    ntest, npoint, nfeature = test_features.shape
    nq = source_features.shape[2]
    kmax = basis_rows.shape[1]
    nsource = last - first
    return pl.pallas_call(
        left_kernel,
        grid_spec=pltpu.PrefetchScalarGridSpec(
            num_scalar_prefetch=1,
            grid=(nsource,),
            in_specs=[
                pl.BlockSpec((ntest, npoint, nfeature), lambda j, order: (0, 0, 0)),
                pl.BlockSpec((1, nfeature, nq), lambda j, order: (order[first + j], 0, 0)),
                pl.BlockSpec((ntest, kmax, npoint), lambda j, order: (0, 0, 0)),
            ],
            out_specs=pl.BlockSpec((ntest, 1, kmax, nq), lambda j, order: (0, j, 0, 0)),
        ),
        out_shape=jax.ShapeDtypeStruct((ntest, nsource, kmax, nq), jnp.bfloat16),
        compiler_params=pltpu.CompilerParams(vmem_limit_bytes=VMEM_LIMIT),
        cost_estimate=pl.CostEstimate(
            flops=2 * ntest * nsource * npoint * nq * kmax,
            bytes_accessed=2 * ntest * nsource * kmax * nq,
            transcendentals=ntest * nsource * npoint * nq,
        ),
    )(order, test_features, source_features, basis_rows)


def tile_kernel(nshard, first, packed, *refs):
    order_ref, source_counts_ref, offsets_ref, test_counts_ref, left_ref = refs[:5]
    shard_refs = refs[5 : 5 + nshard]
    if packed:
        tile_ref, main_ref, over_ref, pack_ref = refs[5 + nshard :]
    else:
        (tile_ref,) = refs[5 + nshard :]
    j = pl.program_id(0)
    ntest, _, kmax, _ = left_ref.shape
    ndest, _, _, rows, width = tile_ref.shape
    count = source_counts_ref[order_ref[first + j]]

    def work(wide):
        side = jnp.concatenate([shard_ref[0, :, :wide] for shard_ref in shard_refs], axis=0)
        row_ids = lax.broadcasted_iota(jnp.int32, (kmax, wide), 0)
        column_ids = lax.broadcasted_iota(jnp.int32, (kmax, wide), 1)
        products = [
            jnp.dot(left_ref[i, 0], side, preferred_element_type=jnp.float32) for i in range(ntest)
        ]
        if packed:
            offset = offsets_ref[order_ref[first + j]]
            shift = offset % LANES
            base = offset - shift
            low = lax.broadcasted_iota(jnp.int32, (kmax, LANES), 1) < shift
        for i in range(ntest):
            used = (row_ids < test_counts_ref[i]) & (column_ids < count)
            tile = jnp.where(used, products[i], 0.0)
            for dest in range(ndest):
                tile_ref[dest, i, 0, :, :wide] = tile[dest * rows : (dest + 1) * rows].astype(jnp.bfloat16)
                if wide < width:
                    tile_ref[dest, i, 0, :, wide:] = jnp.zeros((rows, width - wide), jnp.bfloat16)
            if not packed:
                continue
            rolled = [
                pltpu.roll(tile[:, start : start + LANES], shift, axis=1) for start in range(0, wide, LANES)
            ]
            for place in range(len(rolled) + 1):
                here = pl.ds(pl.multiple_of(base + place * LANES, LANES), LANES)
                if place == 0:
                    before = jnp.concatenate(
                        [pack_ref[dest, i, :, here].astype(jnp.float32) for dest in range(ndest)], axis=0
                    )
                else:
                    before = rolled[place - 1]
                after = rolled[place] if place < len(rolled) else jnp.zeros_like(before)
                window = jnp.where(low, before, after)
                for dest in range(ndest):
                    pack_ref[dest, i, :, here] = window[dest * rows : (dest + 1) * rows].astype(jnp.bfloat16)

    narrow = width - LANES
    if narrow > 0:
        pl.when(count <= narrow)(lambda: work(narrow))
        pl.when(count > narrow)(lambda: work(width))
    else:
        work(width)

    if packed:

        @pl.when(j == pl.num_programs(0) - 1)
        def _():
            main = main_ref.shape[3]
            main_ref[...] = pack_ref[:, :, :, :main]
            over_ref[...] = pack_ref[:, :, :, main : main + over_ref.shape[3]]


def tiles(ndest, first, tables, test_counts, left, shards, main):
    ntest, nsource, kmax, nq = left.shape
    nshard = len(shards)
    part, width = shards[0].shape[1:]
    rows = kmax // ndest
    packed = main is not None
    shapes = [jax.ShapeDtypeStruct((ndest, ntest, nsource, rows, width), jnp.bfloat16)]
    specs = [pl.BlockSpec((ndest, ntest, 1, rows, width), lambda j, *_: (0, 0, j, 0, 0))]
    scratch = []
    if packed:
        for columns in (main, nsource * width - main):
            shape = (ndest, ntest, rows, columns)
            shapes.append(jax.ShapeDtypeStruct(shape, jnp.bfloat16))
            specs.append(pl.BlockSpec(shape, lambda j, *_: (0, 0, 0, 0)))
        scratch.append(pltpu.VMEM((ndest, ntest, rows, nsource * width + LANES), jnp.bfloat16))
    return pl.pallas_call(
        functools.partial(tile_kernel, nshard, first, packed),
        grid_spec=pltpu.PrefetchScalarGridSpec(
            num_scalar_prefetch=4,
            grid=(nsource,),
            in_specs=[pl.BlockSpec((ntest, 1, kmax, nq), lambda j, *_: (0, j, 0, 0))]
            + [pl.BlockSpec((1, part, width), lambda j, *_: (j, 0, 0))] * nshard,
            out_specs=specs,
            scratch_shapes=scratch,
        ),
        out_shape=shapes,
        compiler_params=pltpu.CompilerParams(vmem_limit_bytes=VMEM_LIMIT),
        cost_estimate=pl.CostEstimate(
            flops=2 * ntest * nsource * kmax * width * nq,
            bytes_accessed=2 * ntest * nsource * kmax * (nq + width),
            transcendentals=0,
        ),
    )(*tables, test_counts, left, *shards)


def project_kernel(cut, order_ref, first_ref, rest_ref, coeff_ref, sum_ref, total_ref):
    j = pl.program_id(0)
    ndest, ntest, _, rows, width = first_ref.shape

    def add(tile_ref, fresh):
        whole = [tile_ref[dest, i, 0] for i in range(ntest) for dest in range(ndest)]
        term = jnp.dot(jnp.concatenate(whole, axis=0), coeff_ref[0], preferred_element_type=jnp.float32)
        total_ref[...] = term if fresh else total_ref[...] + term

    pl.when(j == 0)(lambda: add(first_ref, True))
    pl.when((j > 0) & (j < cut))(lambda: add(first_ref, False))
    pl.when(j >= cut)(lambda: add(rest_ref, False))

    @pl.when(j == pl.num_programs(0) - 1)
    def _():
        for i in range(ntest):
            for dest in range(ndest):
                top = (i * ndest + dest) * rows
                sum_ref[dest, i] = total_ref[top : top + rows, :].astype(sum_ref.dtype)


def project(order, first, rest, coefficients):
    ndest, ntest, cut, rows, width = first.shape
    nsource, _, ncol = coefficients.shape
    block = (ndest, ntest, 1, rows, width)
    return pl.pallas_call(
        functools.partial(project_kernel, cut),
        grid_spec=pltpu.PrefetchScalarGridSpec(
            num_scalar_prefetch=1,
            grid=(nsource,),
            in_specs=[
                pl.BlockSpec(block, lambda j, order: (0, 0, jnp.minimum(j, cut - 1), 0, 0)),
                pl.BlockSpec(block, lambda j, order: (0, 0, jnp.maximum(j - cut, 0), 0, 0)),
                pl.BlockSpec((1, width, ncol), lambda j, order: (order[j], 0, 0)),
            ],
            out_specs=pl.BlockSpec((ndest, ntest, rows, ncol), lambda j, order: (0, 0, 0, 0)),
            scratch_shapes=[pltpu.VMEM((ndest * ntest * rows, ncol), jnp.float32)],
        ),
        out_shape=jax.ShapeDtypeStruct((ndest, ntest, rows, ncol), jnp.bfloat16),
        compiler_params=pltpu.CompilerParams(vmem_limit_bytes=VMEM_LIMIT),
        cost_estimate=pl.CostEstimate(
            flops=2 * ndest * ntest * rows * width * ncol * nsource,
            bytes_accessed=2 * ndest * ntest * rows * width * nsource,
            transcendentals=0,
        ),
    )(order, first, rest, coefficients)


def unpack_kernel(cut, order_ref, counts_ref, offsets_ref, whole_ref, packed_ref, out_ref, rows_ref):
    nsrc, _, _, rows, width = whole_ref.shape
    packed_width = packed_ref.shape[3]
    nall = out_ref.shape[2]
    nblock = nall // nsrc
    ntile = width // LANES
    step = 16 if rows % 16 == 0 else rows
    lanes = lax.broadcasted_iota(jnp.int32, (rows, LANES), 1)

    @pl.loop(0, nsrc)
    def _(source):
        for place in range(nblock):
            block = order_ref[source * nblock + place]
            target = source * nblock + block
            if place < cut:
                rows_ref[target] = whole_ref[source, 0, place].astype(jnp.float32)
                continue
            count = counts_ref[target]
            offset = offsets_ref[target]
            shift = offset % LANES
            base = offset - shift
            back = (LANES - shift) % LANES
            low = lanes < LANES - shift
            rolled = []
            for tile in range(ntile + 1):
                start = pl.multiple_of(jnp.minimum(base + tile * LANES, packed_width - LANES), LANES)
                piece = packed_ref[source, 0, :, pl.ds(start, LANES)].astype(jnp.float32)
                rolled.append(pltpu.roll(piece, back, axis=1))
            for tile in range(ntile):
                value = jnp.where(low, rolled[tile], rolled[tile + 1])
                value = jnp.where(lanes < count - tile * LANES, value, 0.0)
                rows_ref[target, :, tile * LANES : (tile + 1) * LANES] = value

    @pl.loop(0, nall // 16)
    def _(group):
        here = pl.ds(pl.multiple_of(group * 16, 16), 16)
        for top in range(0, rows, step):
            turned = jnp.transpose(rows_ref[here, top : top + step, :], (1, 0, 2))
            out_ref[0, top : top + step, here, :] = turned.astype(out_ref.dtype)


def unpack(cut, tables, whole, packed):
    nsrc, ntest, _, rows, width = whole.shape
    packed_width = packed.shape[3]
    nall = tables[0].shape[0]
    return pl.pallas_call(
        functools.partial(unpack_kernel, cut),
        grid_spec=pltpu.PrefetchScalarGridSpec(
            num_scalar_prefetch=3,
            grid=(ntest,),
            in_specs=[
                pl.BlockSpec((nsrc, 1, cut, rows, width), lambda i, *_: (0, i, 0, 0, 0)),
                pl.BlockSpec((nsrc, 1, rows, packed_width), lambda i, *_: (0, i, 0, 0)),
            ],
            out_specs=pl.BlockSpec((1, rows, nall, width), lambda i, *_: (i, 0, 0, 0)),
            scratch_shapes=[pltpu.VMEM((nall, rows, width), jnp.float32)],
        ),
        out_shape=jax.ShapeDtypeStruct((ntest, rows, nall, width), jnp.bfloat16),
        compiler_params=pltpu.CompilerParams(vmem_limit_bytes=VMEM_LIMIT),
    )(*tables, whole, packed)


def body(
    test_points, test_basis, test_counts, source_points, source_basis, source_counts, coefficients
):
    nsource, part, kmax = source_basis.shape
    ntest = test_points.shape[0]
    nsrc = lax.axis_size("src")
    ntest_axis = lax.axis_size("test")
    me_test = lax.axis_index("test")
    cut = max(1, nsource * 3 // 8)
    held = {}

    def gather(name, shard, left):
        got = {0: shard}
        bits = list(bits_down(ntest_axis))
        for bit in bits:
            if bit == bits[-1]:
                names = [o for o in got if o != 0]
                tied = lax.optimization_barrier(tuple(got[o] for o in names) + (left,))
                got.update(zip(names, tied[:-1]))
                left = tied[-1]
            for offset in list(got):
                got[offset ^ bit] = exchange(got[offset], "test", bit)
            if bit == bits[0]:
                held[name] = got[bit]
        return [got[offset] for offset in sorted(got)], left

    most = (nsource - cut) * kmax
    main = min(most, -(-most * 18 // (25 * LANES)) * LANES)
    widths = [main, min(most, main + 2 * LANES), most]

    order, offsets, basis_a, basis_b = pick(cut, source_counts, source_basis)
    tables = (order, source_counts, offsets)
    inner = max(1, nsrc // 4)
    near = [source_counts] + [exchange(source_counts, "src", flip) for flip in range(1, inner)]
    test_features, source_features, basis_rows, joined = distance_features(
        ntest_axis, jnp.reshape(me_test, (1,)), test_points, source_points, test_basis, near
    )
    groups = [joined] + [exchange(joined, "src", flip) for flip in range(inner, nsrc, inner)]

    left_a = left_products(order, test_features, source_features, basis_rows, 0, cut)
    shards_a, left_a = gather("a", basis_a, left_a)
    (tiles_a,) = tiles(nsrc, 0, tables, test_counts, left_a, shards_a, None)
    moved_a = lax.all_to_all(tiles_a, "src", split_axis=0, concat_axis=0, tiled=True)

    rest, _ = lax.optimization_barrier((basis_b, held["a"]))
    features_b, _ = lax.optimization_barrier((source_features, tiles_a))
    left_b = left_products(order, test_features, features_b, basis_rows, cut, nsource)
    shards_b, left_b = gather("b", rest, left_b)
    tiles_b, packed, beyond = tiles(nsrc, cut, tables, test_counts, left_b, shards_b, main)
    moved_b = lax.all_to_all(packed, "src", split_axis=0, concat_axis=0, tiled=True)

    projected = sum_rows(project(order, tiles_a, tiles_b, coefficients), "src")
    me_src, _ = lax.optimization_barrier((jnp.reshape(lax.axis_index("src"), (1,)), packed))
    all_counts, all_order, all_offsets, branch = all_tables(cut, nsource, widths, me_src, groups)
    spread = (all_order, all_counts, all_offsets)

    def finish(width, beyond, moved_a, moved_b, spread):
        if width > main:
            more = lax.all_to_all(
                beyond[..., : width - main], "src", split_axis=0, concat_axis=0, tiled=True
            )
            moved_b = jnp.concatenate([moved_b, more], axis=3)
        return unpack(cut, spread, moved_a, moved_b)

    reduced = lax.switch(
        branch[0],
        [functools.partial(finish, width) for width in widths],
        beyond,
        moved_a,
        moved_b,
        spread,
    )
    return (reduced, projected)


def solution(mesh):
    return jax.shard_map(
        body,
        mesh=mesh,
        in_specs=(
            P("test", None, None),
            P("test", None, None),
            P("test"),
            P("src", None, None),
            P("src", "test", None),
            P("src"),
            P("src", None, None),
        ),
        out_specs=(P("test", "src", None, None), P("test", "src", None)),
        check_vma=False,
    )
```

```python
import functools

import jax
import jax.numpy as jnp
from jax import lax
from jax.experimental import pallas as pl
from jax.experimental.pallas import tpu as pltpu
from jax.sharding import PartitionSpec as P

softening = 0.0025
QBLOCK = 256
LANES = 128
VMEM_LIMIT = 60 * 1024 * 1024


def exchange(x, axis, flip):
    size = lax.axis_size(axis)
    return lax.ppermute(x, axis, [(a, a ^ flip) for a in range(size)])


def bits_down(size):
    bit = size // 2
    while bit >= 1:
        yield bit
        bit //= 2


def sum_rows(total, axis):
    size = lax.axis_size(axis)
    me = lax.axis_index(axis)
    held, bit = total, 1
    while held.shape[0] > 4:
        pairs = held.reshape((held.shape[0] // 2, 2) + held.shape[1:])
        mine = (me // bit) % 2
        keep = lax.dynamic_index_in_dim(pairs, mine, 1, keepdims=False)
        give = lax.dynamic_index_in_dim(pairs, 1 - mine, 1, keepdims=False)
        got = exchange(give, axis, bit)
        held = (keep.astype(jnp.float32) + got.astype(jnp.float32)).astype(held.dtype)
        bit *= 2
    mine = me // bit
    result = lax.dynamic_index_in_dim(held, mine, 0, keepdims=False).astype(jnp.float32)
    for flip in range(1, held.shape[0]):
        give = lax.dynamic_index_in_dim(held, mine ^ flip, 0, keepdims=False)
        result = result + exchange(give, axis, flip * bit).astype(jnp.float32)
    return result.astype(total.dtype)


def rank_blocks(counts, cut):
    ranks = []
    for j, mine in enumerate(counts):
        rank = jnp.int32(0)
        for k, other in enumerate(counts):
            if k != j:
                ahead = other >= mine if k < j else other > mine
                rank += ahead.astype(jnp.int32)
        ranks.append(rank)
    offsets = []
    for j in range(len(counts)):
        offset = jnp.int32(0)
        for k, other in enumerate(counts):
            if k != j:
                offset += jnp.where((ranks[k] >= cut) & (ranks[k] < ranks[j]), other, 0)
        offsets.append(offset)
    return ranks, offsets


def pick_kernel(cut, counts_ref, basis_ref, order_ref, offsets_ref, first_ref, rest_ref):
    nblock = basis_ref.shape[0]
    ranks, offsets = rank_blocks([counts_ref[j] for j in range(nblock)], cut)
    for j in range(nblock):
        order_ref[ranks[j]] = jnp.int32(j)
        offsets_ref[j] = offsets[j]
    for place in range(nblock):
        block = basis_ref[order_ref[place]]
        if place < cut:
            first_ref[place] = block
        else:
            rest_ref[place - cut] = block


def pick(cut, counts, basis):
    nblock = basis.shape[0]
    smem, vmem = pl.BlockSpec(memory_space=pltpu.SMEM), pl.BlockSpec(memory_space=pltpu.VMEM)
    return pl.pallas_call(
        functools.partial(pick_kernel, cut),
        out_shape=(
            jax.ShapeDtypeStruct((nblock,), jnp.int32),
            jax.ShapeDtypeStruct((nblock,), jnp.int32),
            jax.ShapeDtypeStruct((cut,) + basis.shape[1:], basis.dtype),
            jax.ShapeDtypeStruct((nblock - cut,) + basis.shape[1:], basis.dtype),
        ),
        in_specs=[smem, vmem],
        out_specs=(smem, smem, vmem, vmem),
        compiler_params=pltpu.CompilerParams(vmem_limit_bytes=VMEM_LIMIT),
    )(counts, basis)


def tables_kernel(cut, nblock, widths, me_ref, *refs):
    *group_refs, counts_ref, order_ref, offsets_ref, branch_ref, joined_ref = refs
    group = group_refs[0].shape[0]
    for place, group_ref in enumerate(group_refs):
        for k in range(group):
            joined_ref[place * group + k] = group_ref[k]

    def step(source, need):
        base = source * nblock
        theirs = (source ^ me_ref[0]) * nblock
        counts = [joined_ref[theirs + j] for j in range(nblock)]
        ranks, offsets = rank_blocks(counts, cut)
        used = jnp.int32(0)
        for j in range(nblock):
            counts_ref[base + j] = counts[j]
            order_ref[base + ranks[j]] = jnp.int32(j)
            offsets_ref[base + j] = offsets[j]
            used += jnp.where(ranks[j] >= cut, counts[j], 0)
        return jnp.maximum(need, used)

    need = lax.fori_loop(0, counts_ref.shape[0] // nblock, step, jnp.int32(0))
    branch = jnp.int32(0)
    for width in widths[:-1]:
        branch += (need > width).astype(jnp.int32)
    branch_ref[0] = branch


def all_tables(cut, nblock, widths, me, groups):
    smem = pl.BlockSpec(memory_space=pltpu.SMEM)
    total = sum(group.shape[0] for group in groups)
    table = jax.ShapeDtypeStruct((total,), jnp.int32)
    return pl.pallas_call(
        functools.partial(tables_kernel, cut, nblock, widths),
        out_shape=(table, table, table, jax.ShapeDtypeStruct((1,), jnp.int32)),
        in_specs=[smem] * (1 + len(groups)),
        out_specs=(smem,) * 4,
        scratch_shapes=[pltpu.SMEM((total,), jnp.int32)],
    )(me, *groups)


def features_kernel(nshard, me_ref, test_ref, source_ref, basis_ref, test_out_ref, source_out_ref, basis_out_ref, rows_ref):
    part = source_ref.shape[2] // nshard

    def three_terms(x):
        high = x.astype(jnp.bfloat16).astype(jnp.float32)
        middle = (x - high).astype(jnp.bfloat16).astype(jnp.float32)
        return high, middle, x - high - middle

    def fill(centred, is_test):
        norm = jnp.sum(centred * centred, axis=0, keepdims=True)
        terms = three_terms(centred)
        norms = three_terms(norm + softening if is_test else norm)
        for a in range(3):
            for b in range(3):
                place = 3 * (3 * a + b)
                rows_ref[place : place + 3, :] = -2.0 * terms[a] if is_test else terms[b]
        for a in range(3):
            rows_ref[27 + a : 28 + a, :] = norms[a] if is_test else jnp.ones_like(norm)
            rows_ref[30 + a : 31 + a, :] = jnp.ones_like(norm) if is_test else norms[a]
        return rows_ref[...]

    rows_ref[...] = jnp.zeros_like(rows_ref)
    for i in range(test_ref.shape[1]):
        rows = fill(test_ref[:, i, :] - 0.5, True)
        test_out_ref[i] = rows.T.astype(jnp.bfloat16)
        basis_out_ref[i] = basis_ref[i].T
    for j in range(source_ref.shape[1]):
        pieces = []
        for offset in range(nshard):
            start = pl.multiple_of((me_ref[0] ^ offset) * part, part)
            pieces.append(source_ref[:, j, pl.ds(start, part)])
        rows = fill(jnp.concatenate(pieces, axis=1) - 0.5, False)
        source_out_ref[j] = rows.astype(jnp.bfloat16)


NFEATURE = 128


def distance_features(nshard, me, test_points, source_points, test_basis):
    ntest, _, npoint = test_points.shape
    nsource, _, nq = source_points.shape
    kmax = test_basis.shape[2]
    smem, vmem = pl.BlockSpec(memory_space=pltpu.SMEM), pl.BlockSpec(memory_space=pltpu.VMEM)
    return pl.pallas_call(
        functools.partial(features_kernel, nshard),
        out_shape=(
            jax.ShapeDtypeStruct((ntest, npoint, NFEATURE), jnp.bfloat16),
            jax.ShapeDtypeStruct((nsource, NFEATURE, nq), jnp.bfloat16),
            jax.ShapeDtypeStruct((ntest, kmax, npoint), jnp.bfloat16),
        ),
        in_specs=[smem, vmem, vmem, vmem],
        out_specs=(vmem, vmem, vmem),
        scratch_shapes=[pltpu.VMEM((NFEATURE, max(npoint, nq)), jnp.float32)],
        compiler_params=pltpu.CompilerParams(vmem_limit_bytes=VMEM_LIMIT),
    )(me, test_points.transpose(1, 0, 2), source_points.transpose(1, 0, 2), test_basis)


def left_kernel(order_ref, test_ref, source_ref, basis_ref, out_ref):
    nq = source_ref.shape[2]
    block = min(QBLOCK, nq)
    steps = [(i, start) for i in range(test_ref.shape[0]) for start in range(0, nq, block)]

    def kernel_block(i, start):
        squared = jnp.dot(
            test_ref[i], source_ref[0, :, start : start + block], preferred_element_type=jnp.float32
        )
        return lax.rsqrt(squared.astype(jnp.bfloat16))

    ready = kernel_block(*steps[0])
    for place, (i, start) in enumerate(steps):
        now = ready
        if place + 1 < len(steps):
            ready = kernel_block(*steps[place + 1])
        out_ref[i, 0, :, start : start + block] = jnp.dot(
            basis_ref[i], now, preferred_element_type=jnp.float32
        ).astype(jnp.bfloat16)


def left_products(order, test_features, source_features, basis_rows, first, last):
    ntest, npoint, nfeature = test_features.shape
    nq = source_features.shape[2]
    kmax = basis_rows.shape[1]
    nsource = last - first
    return pl.pallas_call(
        left_kernel,
        grid_spec=pltpu.PrefetchScalarGridSpec(
            num_scalar_prefetch=1,
            grid=(nsource,),
            in_specs=[
                pl.BlockSpec((ntest, npoint, nfeature), lambda j, order: (0, 0, 0)),
                pl.BlockSpec((1, nfeature, nq), lambda j, order: (order[first + j], 0, 0)),
                pl.BlockSpec((ntest, kmax, npoint), lambda j, order: (0, 0, 0)),
            ],
            out_specs=pl.BlockSpec((ntest, 1, kmax, nq), lambda j, order: (0, j, 0, 0)),
        ),
        out_shape=jax.ShapeDtypeStruct((ntest, nsource, kmax, nq), jnp.bfloat16),
        compiler_params=pltpu.CompilerParams(vmem_limit_bytes=VMEM_LIMIT),
        cost_estimate=pl.CostEstimate(
            flops=2 * ntest * nsource * npoint * nq * kmax,
            bytes_accessed=2 * ntest * nsource * kmax * nq,
            transcendentals=ntest * nsource * npoint * nq,
        ),
    )(order, test_features, source_features, basis_rows)


def tile_kernel(nshard, first, packed, *refs):
    order_ref, source_counts_ref, offsets_ref, test_counts_ref, left_ref = refs[:5]
    shard_refs = refs[5 : 5 + nshard]
    if packed:
        tile_ref, main_ref, over_ref, pack_ref = refs[5 + nshard :]
    else:
        (tile_ref,) = refs[5 + nshard :]
    j = pl.program_id(0)
    ntest, _, kmax, _ = left_ref.shape
    ndest, _, _, rows, width = tile_ref.shape
    count = source_counts_ref[order_ref[first + j]]

    def work(wide):
        side = jnp.concatenate([shard_ref[0, :, :wide] for shard_ref in shard_refs], axis=0)
        row_ids = lax.broadcasted_iota(jnp.int32, (kmax, wide), 0)
        column_ids = lax.broadcasted_iota(jnp.int32, (kmax, wide), 1)
        products = [
            jnp.dot(left_ref[i, 0], side, preferred_element_type=jnp.float32) for i in range(ntest)
        ]
        if packed:
            offset = offsets_ref[order_ref[first + j]]
            shift = offset % LANES
            base = offset - shift
            low = lax.broadcasted_iota(jnp.int32, (kmax, LANES), 1) < shift
        for i in range(ntest):
            used = (row_ids < test_counts_ref[i]) & (column_ids < count)
            tile = jnp.where(used, products[i], 0.0)
            for dest in range(ndest):
                tile_ref[dest, i, 0, :, :wide] = tile[dest * rows : (dest + 1) * rows].astype(jnp.bfloat16)
                if wide < width:
                    tile_ref[dest, i, 0, :, wide:] = jnp.zeros((rows, width - wide), jnp.bfloat16)
            if not packed:
                continue
            rolled = [
                pltpu.roll(tile[:, start : start + LANES], shift, axis=1) for start in range(0, wide, LANES)
            ]
            for place in range(len(rolled) + 1):
                here = pl.ds(pl.multiple_of(base + place * LANES, LANES), LANES)
                if place == 0:
                    before = jnp.concatenate(
                        [pack_ref[dest, i, :, here].astype(jnp.float32) for dest in range(ndest)], axis=0
                    )
                else:
                    before = rolled[place - 1]
                after = rolled[place] if place < len(rolled) else jnp.zeros_like(before)
                window = jnp.where(low, before, after)
                for dest in range(ndest):
                    pack_ref[dest, i, :, here] = window[dest * rows : (dest + 1) * rows].astype(jnp.bfloat16)

    narrow = width - LANES
    if narrow > 0:
        pl.when(count <= narrow)(lambda: work(narrow))
        pl.when(count > narrow)(lambda: work(width))
    else:
        work(width)

    if packed:

        @pl.when(j == pl.num_programs(0) - 1)
        def _():
            main = main_ref.shape[3]
            main_ref[...] = pack_ref[:, :, :, :main]
            over_ref[...] = pack_ref[:, :, :, main : main + over_ref.shape[3]]


def tiles(ndest, first, tables, test_counts, left, shards, main):
    ntest, nsource, kmax, nq = left.shape
    nshard = len(shards)
    part, width = shards[0].shape[1:]
    rows = kmax // ndest
    packed = main is not None
    shapes = [jax.ShapeDtypeStruct((ndest, ntest, nsource, rows, width), jnp.bfloat16)]
    specs = [pl.BlockSpec((ndest, ntest, 1, rows, width), lambda j, *_: (0, 0, j, 0, 0))]
    scratch = []
    if packed:
        for columns in (main, nsource * width - main):
            shape = (ndest, ntest, rows, columns)
            shapes.append(jax.ShapeDtypeStruct(shape, jnp.bfloat16))
            specs.append(pl.BlockSpec(shape, lambda j, *_: (0, 0, 0, 0)))
        scratch.append(pltpu.VMEM((ndest, ntest, rows, nsource * width + LANES), jnp.bfloat16))
    return pl.pallas_call(
        functools.partial(tile_kernel, nshard, first, packed),
        grid_spec=pltpu.PrefetchScalarGridSpec(
            num_scalar_prefetch=4,
            grid=(nsource,),
            in_specs=[pl.BlockSpec((ntest, 1, kmax, nq), lambda j, *_: (0, j, 0, 0))]
            + [pl.BlockSpec((1, part, width), lambda j, *_: (j, 0, 0))] * nshard,
            out_specs=specs,
            scratch_shapes=scratch,
        ),
        out_shape=shapes,
        compiler_params=pltpu.CompilerParams(vmem_limit_bytes=VMEM_LIMIT),
        cost_estimate=pl.CostEstimate(
            flops=2 * ntest * nsource * kmax * width * nq,
            bytes_accessed=2 * ntest * nsource * kmax * (nq + width),
            transcendentals=0,
        ),
    )(*tables, test_counts, left, *shards)


def project_kernel(cut, order_ref, first_ref, rest_ref, coeff_ref, *refs):
    *counts_refs, sum_ref, joined_ref, total_ref = refs
    j = pl.program_id(0)
    ndest, ntest, _, rows, width = first_ref.shape

    def add(tile_ref, fresh):
        whole = [tile_ref[dest, i, 0] for i in range(ntest) for dest in range(ndest)]
        term = jnp.dot(jnp.concatenate(whole, axis=0), coeff_ref[0], preferred_element_type=jnp.float32)
        total_ref[...] = term if fresh else total_ref[...] + term

    pl.when(j == 0)(lambda: add(first_ref, True))
    pl.when((j > 0) & (j < cut))(lambda: add(first_ref, False))
    pl.when(j >= cut)(lambda: add(rest_ref, False))

    @pl.when(j == pl.num_programs(0) - 1)
    def _():
        for i in range(ntest):
            for dest in range(ndest):
                top = (i * ndest + dest) * rows
                sum_ref[dest, i] = total_ref[top : top + rows, :].astype(sum_ref.dtype)
        nblock = counts_refs[0].shape[0]
        for place, counts_ref in enumerate(counts_refs):
            for k in range(nblock):
                joined_ref[place * nblock + k] = counts_ref[k]


def project(order, first, rest, coefficients, counts):
    ndest, ntest, cut, rows, width = first.shape
    nsource, _, ncol = coefficients.shape
    block = (ndest, ntest, 1, rows, width)
    smem = pl.BlockSpec(memory_space=pltpu.SMEM)
    return pl.pallas_call(
        functools.partial(project_kernel, cut),
        grid_spec=pltpu.PrefetchScalarGridSpec(
            num_scalar_prefetch=1,
            grid=(nsource,),
            in_specs=[
                pl.BlockSpec(block, lambda j, order: (0, 0, jnp.minimum(j, cut - 1), 0, 0)),
                pl.BlockSpec(block, lambda j, order: (0, 0, jnp.maximum(j - cut, 0), 0, 0)),
                pl.BlockSpec((1, width, ncol), lambda j, order: (order[j], 0, 0)),
            ]
            + [smem] * len(counts),
            out_specs=(pl.BlockSpec((ndest, ntest, rows, ncol), lambda j, order: (0, 0, 0, 0)), smem),
            scratch_shapes=[pltpu.VMEM((ndest * ntest * rows, ncol), jnp.float32)],
        ),
        out_shape=(
            jax.ShapeDtypeStruct((ndest, ntest, rows, ncol), jnp.bfloat16),
            jax.ShapeDtypeStruct((len(counts) * nsource,), jnp.int32),
        ),
        compiler_params=pltpu.CompilerParams(vmem_limit_bytes=VMEM_LIMIT),
        cost_estimate=pl.CostEstimate(
            flops=2 * ndest * ntest * rows * width * ncol * nsource,
            bytes_accessed=2 * ndest * ntest * rows * width * nsource,
            transcendentals=0,
        ),
    )(order, first, rest, coefficients, *counts)


def unpack_kernel(cut, order_ref, counts_ref, offsets_ref, whole_ref, packed_ref, out_ref, rows_ref):
    nsrc, _, _, rows, width = whole_ref.shape
    packed_width = packed_ref.shape[3]
    nall = out_ref.shape[2]
    nblock = nall // nsrc
    ntile = width // LANES
    step = 16 if rows % 16 == 0 else rows
    lanes = lax.broadcasted_iota(jnp.int32, (rows, LANES), 1)

    @pl.loop(0, nsrc)
    def _(source):
        for place in range(nblock):
            block = order_ref[source * nblock + place]
            target = source * nblock + block
            if place < cut:
                rows_ref[target] = whole_ref[source, 0, place].astype(jnp.float32)
                continue
            count = counts_ref[target]
            offset = offsets_ref[target]
            shift = offset % LANES
            base = offset - shift
            back = (LANES - shift) % LANES
            low = lanes < LANES - shift
            rolled = []
            for tile in range(ntile + 1):
                start = pl.multiple_of(jnp.minimum(base + tile * LANES, packed_width - LANES), LANES)
                piece = packed_ref[source, 0, :, pl.ds(start, LANES)].astype(jnp.float32)
                rolled.append(pltpu.roll(piece, back, axis=1))
            for tile in range(ntile):
                value = jnp.where(low, rolled[tile], rolled[tile + 1])
                value = jnp.where(lanes < count - tile * LANES, value, 0.0)
                rows_ref[target, :, tile * LANES : (tile + 1) * LANES] = value

    @pl.loop(0, nall // 16)
    def _(group):
        here = pl.ds(pl.multiple_of(group * 16, 16), 16)
        for top in range(0, rows, step):
            turned = jnp.transpose(rows_ref[here, top : top + step, :], (1, 0, 2))
            out_ref[0, top : top + step, here, :] = turned.astype(out_ref.dtype)


def unpack(cut, tables, whole, packed):
    nsrc, ntest, _, rows, width = whole.shape
    packed_width = packed.shape[3]
    nall = tables[0].shape[0]
    return pl.pallas_call(
        functools.partial(unpack_kernel, cut),
        grid_spec=pltpu.PrefetchScalarGridSpec(
            num_scalar_prefetch=3,
            grid=(ntest,),
            in_specs=[
                pl.BlockSpec((nsrc, 1, cut, rows, width), lambda i, *_: (0, i, 0, 0, 0)),
                pl.BlockSpec((nsrc, 1, rows, packed_width), lambda i, *_: (0, i, 0, 0)),
            ],
            out_specs=pl.BlockSpec((1, rows, nall, width), lambda i, *_: (i, 0, 0, 0)),
            scratch_shapes=[pltpu.VMEM((nall, rows, width), jnp.float32)],
        ),
        out_shape=jax.ShapeDtypeStruct((ntest, rows, nall, width), jnp.bfloat16),
        compiler_params=pltpu.CompilerParams(vmem_limit_bytes=VMEM_LIMIT),
    )(*tables, whole, packed)


def body(
    test_points, test_basis, test_counts, source_points, source_basis, source_counts, coefficients
):
    nsource, part, kmax = source_basis.shape
    ntest = test_points.shape[0]
    nsrc = lax.axis_size("src")
    ntest_axis = lax.axis_size("test")
    me_test = lax.axis_index("test")
    cut = max(1, nsource * 3 // 8)

    def gather(name, shard, left):
        got = {0: shard}
        bits = list(bits_down(ntest_axis))
        for bit in bits:
            if bit == bits[-1] and name == "a":
                names = [o for o in got if o != 0]
                tied = lax.optimization_barrier(tuple(got[o] for o in names) + (left,))
                got.update(zip(names, tied[:-1]))
                left = tied[-1]
            for offset in list(got):
                got[offset ^ bit] = exchange(got[offset], "test", bit)
        return [got[offset] for offset in sorted(got)], left

    most = (nsource - cut) * kmax
    main = min(most, -(-most * 18 // (25 * LANES)) * LANES)
    widths = [main, min(most, main + 2 * LANES), most]

    order, offsets, basis_a, basis_b = pick(cut, source_counts, source_basis)
    tables = (order, source_counts, offsets)
    test_features, source_features, basis_rows = distance_features(
        ntest_axis, jnp.reshape(me_test, (1,)), test_points, source_points, test_basis
    )

    left_a = left_products(order, test_features, source_features, basis_rows, 0, cut)
    shards_a, left_a = gather("a", basis_a, left_a)
    (tiles_a,) = tiles(nsrc, 0, tables, test_counts, left_a, shards_a, None)
    moved_a = lax.all_to_all(tiles_a, "src", split_axis=0, concat_axis=0, tiled=True)

    rest, _ = lax.optimization_barrier((basis_b, source_features))
    features_b, _ = lax.optimization_barrier((source_features, tiles_a))
    left_b = left_products(order, test_features, features_b, basis_rows, cut, nsource)
    shards_b, left_b = gather("b", rest, left_b)
    tiles_b, packed, beyond = tiles(nsrc, cut, tables, test_counts, left_b, shards_b, main)
    moved_b = lax.all_to_all(packed, "src", split_axis=0, concat_axis=0, tiled=True)

    inner = max(1, nsrc // 4)
    counts, _ = lax.optimization_barrier((source_counts, tiles_a))
    near = [counts] + [exchange(counts, "src", flip) for flip in range(1, inner)]
    sums, joined = project(order, tiles_a, tiles_b, coefficients, near)
    groups = [joined] + [exchange(joined, "src", flip) for flip in range(inner, nsrc, inner)]
    projected = sum_rows(sums, "src")
    me_src, _ = lax.optimization_barrier((jnp.reshape(lax.axis_index("src"), (1,)), packed))
    all_counts, all_order, all_offsets, branch = all_tables(cut, nsource, widths, me_src, groups)
    spread = (all_order, all_counts, all_offsets)

    def finish(width, beyond, moved_a, moved_b, spread):
        if width > main:
            more = lax.all_to_all(
                beyond[..., : width - main], "src", split_axis=0, concat_axis=0, tiled=True
            )
            moved_b = jnp.concatenate([moved_b, more], axis=3)
        return unpack(cut, spread, moved_a, moved_b)

    reduced = lax.switch(
        branch[0],
        [functools.partial(finish, width) for width in widths],
        beyond,
        moved_a,
        moved_b,
        spread,
    )
    return (reduced, projected)


def solution(mesh):
    return jax.shard_map(
        body,
        mesh=mesh,
        in_specs=(
            P("test", None, None),
            P("test", None, None),
            P("test"),
            P("src", None, None),
            P("src", "test", None),
            P("src"),
            P("src", None, None),
        ),
        out_specs=(P("test", "src", None, None), P("test", "src", None)),
        check_vma=False,
    )
```

```python
import functools

import jax
import jax.numpy as jnp
from jax import lax
from jax.experimental import pallas as pl
from jax.experimental.pallas import tpu as pltpu
from jax.sharding import PartitionSpec as P

softening = 0.0025
QBLOCK = 256
LANES = 128
VMEM_LIMIT = 60 * 1024 * 1024


def exchange(x, axis, flip):
    size = lax.axis_size(axis)
    return lax.ppermute(x, axis, [(a, a ^ flip) for a in range(size)])


def bits_down(size):
    bit = size // 2
    while bit >= 1:
        yield bit
        bit //= 2


def sum_rows(total, axis):
    size = lax.axis_size(axis)
    me = lax.axis_index(axis)
    held, bit = total, 1
    while held.shape[0] > 4:
        pairs = held.reshape((held.shape[0] // 2, 2) + held.shape[1:])
        mine = (me // bit) % 2
        keep = lax.dynamic_index_in_dim(pairs, mine, 1, keepdims=False)
        give = lax.dynamic_index_in_dim(pairs, 1 - mine, 1, keepdims=False)
        got = exchange(give, axis, bit)
        held = (keep.astype(jnp.float32) + got.astype(jnp.float32)).astype(held.dtype)
        bit *= 2
    mine = me // bit
    result = lax.dynamic_index_in_dim(held, mine, 0, keepdims=False).astype(jnp.float32)
    for flip in range(1, held.shape[0]):
        give = lax.dynamic_index_in_dim(held, mine ^ flip, 0, keepdims=False)
        result = result + exchange(give, axis, flip * bit).astype(jnp.float32)
    return result.astype(total.dtype)


def rank_blocks(counts, cut):
    ranks = []
    for j, mine in enumerate(counts):
        rank = jnp.int32(0)
        for k, other in enumerate(counts):
            if k != j:
                ahead = other >= mine if k < j else other > mine
                rank += ahead.astype(jnp.int32)
        ranks.append(rank)
    offsets = []
    for j in range(len(counts)):
        offset = jnp.int32(0)
        for k, other in enumerate(counts):
            if k != j:
                offset += jnp.where((ranks[k] >= cut) & (ranks[k] < ranks[j]), other, 0)
        offsets.append(offset)
    return ranks, offsets


def pick_kernel(cut, counts_ref, basis_ref, order_ref, offsets_ref, first_ref, rest_ref):
    nblock = basis_ref.shape[0]
    ranks, offsets = rank_blocks([counts_ref[j] for j in range(nblock)], cut)
    for j in range(nblock):
        order_ref[ranks[j]] = jnp.int32(j)
        offsets_ref[j] = offsets[j]
    for place in range(nblock):
        block = basis_ref[order_ref[place]]
        if place < cut:
            first_ref[place] = block
        else:
            rest_ref[place - cut] = block


def pick(cut, counts, basis):
    nblock = basis.shape[0]
    smem, vmem = pl.BlockSpec(memory_space=pltpu.SMEM), pl.BlockSpec(memory_space=pltpu.VMEM)
    return pl.pallas_call(
        functools.partial(pick_kernel, cut),
        out_shape=(
            jax.ShapeDtypeStruct((nblock,), jnp.int32),
            jax.ShapeDtypeStruct((nblock,), jnp.int32),
            jax.ShapeDtypeStruct((cut,) + basis.shape[1:], basis.dtype),
            jax.ShapeDtypeStruct((nblock - cut,) + basis.shape[1:], basis.dtype),
        ),
        in_specs=[smem, vmem],
        out_specs=(smem, smem, vmem, vmem),
        compiler_params=pltpu.CompilerParams(vmem_limit_bytes=VMEM_LIMIT),
    )(counts, basis)


def tables_kernel(cut, nblock, widths, me_ref, *refs):
    *group_refs, counts_ref, order_ref, offsets_ref, branch_ref, joined_ref = refs
    group = group_refs[0].shape[0]
    for place, group_ref in enumerate(group_refs):
        for k in range(group):
            joined_ref[place * group + k] = group_ref[k]

    def step(source, need):
        base = source * nblock
        theirs = (source ^ me_ref[0]) * nblock
        counts = [joined_ref[theirs + j] for j in range(nblock)]
        ranks, offsets = rank_blocks(counts, cut)
        used = jnp.int32(0)
        for j in range(nblock):
            counts_ref[base + j] = counts[j]
            order_ref[base + ranks[j]] = jnp.int32(j)
            offsets_ref[base + j] = offsets[j]
            used += jnp.where(ranks[j] >= cut, counts[j], 0)
        return jnp.maximum(need, used)

    need = lax.fori_loop(0, counts_ref.shape[0] // nblock, step, jnp.int32(0))
    branch = jnp.int32(0)
    for width in widths[:-1]:
        branch += (need > width).astype(jnp.int32)
    branch_ref[0] = branch


def all_tables(cut, nblock, widths, me, groups):
    smem = pl.BlockSpec(memory_space=pltpu.SMEM)
    total = sum(group.shape[0] for group in groups)
    table = jax.ShapeDtypeStruct((total,), jnp.int32)
    return pl.pallas_call(
        functools.partial(tables_kernel, cut, nblock, widths),
        out_shape=(table, table, table, jax.ShapeDtypeStruct((1,), jnp.int32)),
        in_specs=[smem] * (1 + len(groups)),
        out_specs=(smem,) * 4,
        scratch_shapes=[pltpu.SMEM((total,), jnp.int32)],
    )(me, *groups)


NFEATURE = 128


def fill_features(rows_ref, points, is_test):
    def three_terms(x):
        high = x.astype(jnp.bfloat16).astype(jnp.float32)
        middle = (x - high).astype(jnp.bfloat16).astype(jnp.float32)
        return high, middle, x - high - middle

    centred = points - 0.5
    norm = jnp.sum(centred * centred, axis=0, keepdims=True)
    terms = three_terms(centred)
    norms = three_terms(norm + softening if is_test else norm)
    for a in range(3):
        for b in range(3):
            place = 3 * (3 * a + b)
            rows_ref[place : place + 3, :] = -2.0 * terms[a] if is_test else terms[b]
    for a in range(3):
        rows_ref[27 + a : 28 + a, :] = norms[a] if is_test else jnp.ones_like(norm)
        rows_ref[30 + a : 31 + a, :] = jnp.ones_like(norm) if is_test else norms[a]


def left_kernel(
    nshard, first, me_ref, order_ref, test_ref, source_ref, basis_ref, out_ref,
    rows_ref, features_ref, turned_ref, near_ref,
):
    j = pl.program_id(0)
    ntest = test_ref.shape[1]
    nq = source_ref.shape[2]
    part = nq // nshard
    block = min(QBLOCK, nq)

    @pl.when(j == 0)
    def _():
        rows_ref[...] = jnp.zeros_like(rows_ref)
        for i in range(ntest):
            fill_features(rows_ref, test_ref[:, i, :], True)
            features_ref[i] = rows_ref[...].T.astype(jnp.bfloat16)
            turned_ref[i] = basis_ref[i].T

    source = order_ref[first + j]
    for comp in range(3):
        rows_ref[comp : comp + 1, :] = source_ref[comp, pl.ds(source, 1), :]
    pieces = []
    for offset in range(nshard):
        start = pl.multiple_of((me_ref[0] ^ offset) * part, part)
        pieces.append(rows_ref[0:3, pl.ds(start, part)])
    fill_features(rows_ref, jnp.concatenate(pieces, axis=1), False)
    near_ref[...] = rows_ref[...].astype(jnp.bfloat16)

    steps = [(i, start) for i in range(ntest) for start in range(0, nq, block)]

    def kernel_block(i, start):
        squared = jnp.dot(
            features_ref[i], near_ref[:, start : start + block], preferred_element_type=jnp.float32
        )
        return lax.rsqrt(squared.astype(jnp.bfloat16))

    ready = kernel_block(*steps[0])
    for place, (i, start) in enumerate(steps):
        now = ready
        if place + 1 < len(steps):
            ready = kernel_block(*steps[place + 1])
        out_ref[i, 0, :, start : start + block] = jnp.dot(
            turned_ref[i], now, preferred_element_type=jnp.float32
        ).astype(jnp.bfloat16)


def left_products(nshard, me, order, test_points, source_points, test_basis, first, last):
    _, ntest, npoint = test_points.shape
    nall, nq = source_points.shape[1:]
    kmax = test_basis.shape[2]
    nsource = last - first
    return pl.pallas_call(
        functools.partial(left_kernel, nshard, first),
        grid_spec=pltpu.PrefetchScalarGridSpec(
            num_scalar_prefetch=2,
            grid=(nsource,),
            in_specs=[
                pl.BlockSpec((3, ntest, npoint), lambda j, *_: (0, 0, 0)),
                pl.BlockSpec((3, nall, nq), lambda j, *_: (0, 0, 0)),
                pl.BlockSpec((ntest, npoint, kmax), lambda j, *_: (0, 0, 0)),
            ],
            out_specs=pl.BlockSpec((ntest, 1, kmax, nq), lambda j, *_: (0, j, 0, 0)),
            scratch_shapes=[
                pltpu.VMEM((NFEATURE, npoint), jnp.float32),
                pltpu.VMEM((ntest, npoint, NFEATURE), jnp.bfloat16),
                pltpu.VMEM((ntest, kmax, npoint), jnp.bfloat16),
                pltpu.VMEM((NFEATURE, nq), jnp.bfloat16),
            ],
        ),
        out_shape=jax.ShapeDtypeStruct((ntest, nsource, kmax, nq), jnp.bfloat16),
        compiler_params=pltpu.CompilerParams(vmem_limit_bytes=VMEM_LIMIT),
        cost_estimate=pl.CostEstimate(
            flops=2 * ntest * nsource * npoint * nq * kmax,
            bytes_accessed=2 * ntest * nsource * kmax * nq,
            transcendentals=ntest * nsource * npoint * nq,
        ),
    )(me, order, test_points, source_points, test_basis)


def tile_kernel(nshard, first, packed, *refs):
    order_ref, source_counts_ref, offsets_ref, test_counts_ref, left_ref = refs[:5]
    shard_refs = refs[5 : 5 + nshard]
    if packed:
        tile_ref, main_ref, over_ref, pack_ref = refs[5 + nshard :]
    else:
        (tile_ref,) = refs[5 + nshard :]
    j = pl.program_id(0)
    ntest, _, kmax, _ = left_ref.shape
    ndest, _, _, rows, width = tile_ref.shape
    count = source_counts_ref[order_ref[first + j]]

    def work(wide):
        side = jnp.concatenate([shard_ref[0, :, :wide] for shard_ref in shard_refs], axis=0)
        row_ids = lax.broadcasted_iota(jnp.int32, (kmax, wide), 0)
        column_ids = lax.broadcasted_iota(jnp.int32, (kmax, wide), 1)
        products = [
            jnp.dot(left_ref[i, 0], side, preferred_element_type=jnp.float32) for i in range(ntest)
        ]
        if packed:
            offset = offsets_ref[order_ref[first + j]]
            shift = offset % LANES
            base = offset - shift
            low = lax.broadcasted_iota(jnp.int32, (kmax, LANES), 1) < shift
        for i in range(ntest):
            used = (row_ids < test_counts_ref[i]) & (column_ids < count)
            tile = jnp.where(used, products[i], 0.0)
            for dest in range(ndest):
                tile_ref[dest, i, 0, :, :wide] = tile[dest * rows : (dest + 1) * rows].astype(jnp.bfloat16)
                if wide < width:
                    tile_ref[dest, i, 0, :, wide:] = jnp.zeros((rows, width - wide), jnp.bfloat16)
            if not packed:
                continue
            rolled = [
                pltpu.roll(tile[:, start : start + LANES], shift, axis=1) for start in range(0, wide, LANES)
            ]
            for place in range(len(rolled) + 1):
                here = pl.ds(pl.multiple_of(base + place * LANES, LANES), LANES)
                if place == 0:
                    before = jnp.concatenate(
                        [pack_ref[dest, i, :, here].astype(jnp.float32) for dest in range(ndest)], axis=0
                    )
                else:
                    before = rolled[place - 1]
                after = rolled[place] if place < len(rolled) else jnp.zeros_like(before)
                window = jnp.where(low, before, after)
                for dest in range(ndest):
                    pack_ref[dest, i, :, here] = window[dest * rows : (dest + 1) * rows].astype(jnp.bfloat16)

    narrow = width - LANES
    if narrow > 0:
        pl.when(count <= narrow)(lambda: work(narrow))
        pl.when(count > narrow)(lambda: work(width))
    else:
        work(width)

    if packed:

        @pl.when(j == pl.num_programs(0) - 1)
        def _():
            main = main_ref.shape[3]
            main_ref[...] = pack_ref[:, :, :, :main]
            over_ref[...] = pack_ref[:, :, :, main : main + over_ref.shape[3]]


def tiles(ndest, first, tables, test_counts, left, shards, main):
    ntest, nsource, kmax, nq = left.shape
    nshard = len(shards)
    part, width = shards[0].shape[1:]
    rows = kmax // ndest
    packed = main is not None
    shapes = [jax.ShapeDtypeStruct((ndest, ntest, nsource, rows, width), jnp.bfloat16)]
    specs = [pl.BlockSpec((ndest, ntest, 1, rows, width), lambda j, *_: (0, 0, j, 0, 0))]
    scratch = []
    if packed:
        for columns in (main, nsource * width - main):
            shape = (ndest, ntest, rows, columns)
            shapes.append(jax.ShapeDtypeStruct(shape, jnp.bfloat16))
            specs.append(pl.BlockSpec(shape, lambda j, *_: (0, 0, 0, 0)))
        scratch.append(pltpu.VMEM((ndest, ntest, rows, nsource * width + LANES), jnp.bfloat16))
    return pl.pallas_call(
        functools.partial(tile_kernel, nshard, first, packed),
        grid_spec=pltpu.PrefetchScalarGridSpec(
            num_scalar_prefetch=4,
            grid=(nsource,),
            in_specs=[pl.BlockSpec((ntest, 1, kmax, nq), lambda j, *_: (0, j, 0, 0))]
            + [pl.BlockSpec((1, part, width), lambda j, *_: (j, 0, 0))] * nshard,
            out_specs=specs,
            scratch_shapes=scratch,
        ),
        out_shape=shapes,
        compiler_params=pltpu.CompilerParams(vmem_limit_bytes=VMEM_LIMIT),
        cost_estimate=pl.CostEstimate(
            flops=2 * ntest * nsource * kmax * width * nq,
            bytes_accessed=2 * ntest * nsource * kmax * (nq + width),
            transcendentals=0,
        ),
    )(*tables, test_counts, left, *shards)


def project_kernel(cut, order_ref, first_ref, rest_ref, coeff_ref, *refs):
    *counts_refs, sum_ref, joined_ref, total_ref = refs
    j = pl.program_id(0)
    ndest, ntest, _, rows, width = first_ref.shape

    def add(tile_ref, fresh):
        whole = [tile_ref[dest, i, 0] for i in range(ntest) for dest in range(ndest)]
        term = jnp.dot(jnp.concatenate(whole, axis=0), coeff_ref[0], preferred_element_type=jnp.float32)
        total_ref[...] = term if fresh else total_ref[...] + term

    pl.when(j == 0)(lambda: add(first_ref, True))
    pl.when((j > 0) & (j < cut))(lambda: add(first_ref, False))
    pl.when(j >= cut)(lambda: add(rest_ref, False))

    @pl.when(j == pl.num_programs(0) - 1)
    def _():
        for i in range(ntest):
            for dest in range(ndest):
                top = (i * ndest + dest) * rows
                sum_ref[dest, i] = total_ref[top : top + rows, :].astype(sum_ref.dtype)
        nblock = counts_refs[0].shape[0]
        for place, counts_ref in enumerate(counts_refs):
            for k in range(nblock):
                joined_ref[place * nblock + k] = counts_ref[k]


def project(order, first, rest, coefficients, counts):
    ndest, ntest, cut, rows, width = first.shape
    nsource, _, ncol = coefficients.shape
    block = (ndest, ntest, 1, rows, width)
    smem = pl.BlockSpec(memory_space=pltpu.SMEM)
    return pl.pallas_call(
        functools.partial(project_kernel, cut),
        grid_spec=pltpu.PrefetchScalarGridSpec(
            num_scalar_prefetch=1,
            grid=(nsource,),
            in_specs=[
                pl.BlockSpec(block, lambda j, order: (0, 0, jnp.minimum(j, cut - 1), 0, 0)),
                pl.BlockSpec(block, lambda j, order: (0, 0, jnp.maximum(j - cut, 0), 0, 0)),
                pl.BlockSpec((1, width, ncol), lambda j, order: (order[j], 0, 0)),
            ]
            + [smem] * len(counts),
            out_specs=(pl.BlockSpec((ndest, ntest, rows, ncol), lambda j, order: (0, 0, 0, 0)), smem),
            scratch_shapes=[pltpu.VMEM((ndest * ntest * rows, ncol), jnp.float32)],
        ),
        out_shape=(
            jax.ShapeDtypeStruct((ndest, ntest, rows, ncol), jnp.bfloat16),
            jax.ShapeDtypeStruct((len(counts) * nsource,), jnp.int32),
        ),
        compiler_params=pltpu.CompilerParams(vmem_limit_bytes=VMEM_LIMIT),
        cost_estimate=pl.CostEstimate(
            flops=2 * ndest * ntest * rows * width * ncol * nsource,
            bytes_accessed=2 * ndest * ntest * rows * width * nsource,
            transcendentals=0,
        ),
    )(order, first, rest, coefficients, *counts)


def unpack_kernel(cut, order_ref, counts_ref, offsets_ref, whole_ref, packed_ref, out_ref, rows_ref):
    nsrc, _, _, rows, width = whole_ref.shape
    packed_width = packed_ref.shape[3]
    nall = out_ref.shape[2]
    nblock = nall // nsrc
    ntile = width // LANES
    step = 16 if rows % 16 == 0 else rows
    lanes = lax.broadcasted_iota(jnp.int32, (rows, LANES), 1)

    @pl.loop(0, nsrc)
    def _(source):
        for place in range(nblock):
            block = order_ref[source * nblock + place]
            target = source * nblock + block
            if place < cut:
                rows_ref[target] = whole_ref[source, 0, place].astype(jnp.float32)
                continue
            count = counts_ref[target]
            offset = offsets_ref[target]
            shift = offset % LANES
            base = offset - shift
            back = (LANES - shift) % LANES
            low = lanes < LANES - shift
            rolled = []
            for tile in range(ntile + 1):
                start = pl.multiple_of(jnp.minimum(base + tile * LANES, packed_width - LANES), LANES)
                piece = packed_ref[source, 0, :, pl.ds(start, LANES)].astype(jnp.float32)
                rolled.append(pltpu.roll(piece, back, axis=1))
            for tile in range(ntile):
                value = jnp.where(low, rolled[tile], rolled[tile + 1])
                value = jnp.where(lanes < count - tile * LANES, value, 0.0)
                rows_ref[target, :, tile * LANES : (tile + 1) * LANES] = value

    @pl.loop(0, nall // 16)
    def _(group):
        here = pl.ds(pl.multiple_of(group * 16, 16), 16)
        for top in range(0, rows, step):
            turned = jnp.transpose(rows_ref[here, top : top + step, :], (1, 0, 2))
            out_ref[0, top : top + step, here, :] = turned.astype(out_ref.dtype)


def unpack(cut, tables, whole, packed):
    nsrc, ntest, _, rows, width = whole.shape
    packed_width = packed.shape[3]
    nall = tables[0].shape[0]
    return pl.pallas_call(
        functools.partial(unpack_kernel, cut),
        grid_spec=pltpu.PrefetchScalarGridSpec(
            num_scalar_prefetch=3,
            grid=(ntest,),
            in_specs=[
                pl.BlockSpec((nsrc, 1, cut, rows, width), lambda i, *_: (0, i, 0, 0, 0)),
                pl.BlockSpec((nsrc, 1, rows, packed_width), lambda i, *_: (0, i, 0, 0)),
            ],
            out_specs=pl.BlockSpec((1, rows, nall, width), lambda i, *_: (i, 0, 0, 0)),
            scratch_shapes=[pltpu.VMEM((nall, rows, width), jnp.float32)],
        ),
        out_shape=jax.ShapeDtypeStruct((ntest, rows, nall, width), jnp.bfloat16),
        compiler_params=pltpu.CompilerParams(vmem_limit_bytes=VMEM_LIMIT),
    )(*tables, whole, packed)


def body(
    test_points, test_basis, test_counts, source_points, source_basis, source_counts, coefficients
):
    nsource, part, kmax = source_basis.shape
    ntest = test_points.shape[0]
    nsrc = lax.axis_size("src")
    ntest_axis = lax.axis_size("test")
    me_test = lax.axis_index("test")
    cut = max(1, nsource * 3 // 8)

    held = {}

    def gather(name, shard, left):
        got = {0: shard}
        bits = list(bits_down(ntest_axis))
        for bit in bits:
            if bit == bits[-1]:
                names = [o for o in got if o != 0]
                tied = lax.optimization_barrier(tuple(got[o] for o in names) + (left,))
                got.update(zip(names, tied[:-1]))
                left = tied[-1]
            for offset in list(got):
                got[offset ^ bit] = exchange(got[offset], "test", bit)
            if bit == bits[0]:
                held[name] = got[bit]
        return [got[offset] for offset in sorted(got)], left

    most = (nsource - cut) * kmax
    main = min(most, -(-most * 18 // (25 * LANES)) * LANES)
    widths = [main, min(most, main + 2 * LANES), most]

    order, offsets, basis_a, basis_b = pick(cut, source_counts, source_basis)
    tables = (order, source_counts, offsets)
    me = jnp.reshape(me_test, (1,))
    test_points, source_points = test_points.transpose(1, 0, 2), source_points.transpose(1, 0, 2)

    left_a = left_products(ntest_axis, me, order, test_points, source_points, test_basis, 0, cut)
    shards_a, left_a = gather("a", basis_a, left_a)
    inner = max(1, nsrc // 4)
    near = [exchange(source_counts, "src", flip) for flip in range(1, inner)]
    *near, left_a = lax.optimization_barrier((*near, left_a))
    (tiles_a,) = tiles(nsrc, 0, tables, test_counts, left_a, shards_a, None)
    moved_a = lax.all_to_all(tiles_a, "src", split_axis=0, concat_axis=0, tiled=True)

    rest, _ = lax.optimization_barrier((basis_b, held["a"]))
    later, _ = lax.optimization_barrier((source_points, tiles_a))
    left_b = left_products(ntest_axis, me, order, test_points, later, test_basis, cut, nsource)
    shards_b, left_b = gather("b", rest, left_b)
    tiles_b, packed, beyond = tiles(nsrc, cut, tables, test_counts, left_b, shards_b, main)
    moved_b = lax.all_to_all(packed, "src", split_axis=0, concat_axis=0, tiled=True)

    sums, joined = project(order, tiles_a, tiles_b, coefficients, [source_counts] + near)
    groups = [joined] + [exchange(joined, "src", flip) for flip in range(inner, nsrc, inner)]
    projected = sum_rows(sums, "src")
    me_src, _ = lax.optimization_barrier((jnp.reshape(lax.axis_index("src"), (1,)), packed))
    all_counts, all_order, all_offsets, branch = all_tables(cut, nsource, widths, me_src, groups)
    spread = (all_order, all_counts, all_offsets)

    def finish(width, beyond, moved_a, moved_b, spread):
        if width > main:
            more = lax.all_to_all(
                beyond[..., : width - main], "src", split_axis=0, concat_axis=0, tiled=True
            )
            moved_b = jnp.concatenate([moved_b, more], axis=3)
        return unpack(cut, spread, moved_a, moved_b)

    reduced = lax.switch(
        branch[0],
        [functools.partial(finish, width) for width in widths],
        beyond,
        moved_a,
        moved_b,
        spread,
    )
    return (reduced, projected)


def solution(mesh):
    return jax.shard_map(
        body,
        mesh=mesh,
        in_specs=(
            P("test", None, None),
            P("test", None, None),
            P("test"),
            P("src", None, None),
            P("src", "test", None),
            P("src"),
            P("src", None, None),
        ),
        out_specs=(P("test", "src", None, None), P("test", "src", None)),
        check_vma=False,
    )
```

```python
import functools

import jax
import jax.numpy as jnp
from jax import lax
from jax.experimental import pallas as pl
from jax.experimental.pallas import tpu as pltpu
from jax.sharding import PartitionSpec as P

softening = 0.0025
QBLOCK = 256
LANES = 128
VMEM_LIMIT = 60 * 1024 * 1024
SMALL_VMEM_LIMIT = 32 * 1024 * 1024


def exchange(x, axis, flip):
    size = lax.axis_size(axis)
    return lax.ppermute(x, axis, [(a, a ^ flip) for a in range(size)])


def bits_down(size):
    bit = size // 2
    while bit >= 1:
        yield bit
        bit //= 2


def sum_rows(total, axis):
    size = lax.axis_size(axis)
    me = lax.axis_index(axis)
    held, bit = total, 1
    while held.shape[0] > 4:
        pairs = held.reshape((held.shape[0] // 2, 2) + held.shape[1:])
        mine = (me // bit) % 2
        keep = lax.dynamic_index_in_dim(pairs, mine, 1, keepdims=False)
        give = lax.dynamic_index_in_dim(pairs, 1 - mine, 1, keepdims=False)
        got = exchange(give, axis, bit)
        held = (keep.astype(jnp.float32) + got.astype(jnp.float32)).astype(held.dtype)
        bit *= 2
    mine = me // bit
    result = lax.dynamic_index_in_dim(held, mine, 0, keepdims=False).astype(jnp.float32)
    for flip in range(1, held.shape[0]):
        give = lax.dynamic_index_in_dim(held, mine ^ flip, 0, keepdims=False)
        result = result + exchange(give, axis, flip * bit).astype(jnp.float32)
    return result.astype(total.dtype)


def rank_blocks(counts, cut):
    ranks = []
    for j, mine in enumerate(counts):
        rank = jnp.int32(0)
        for k, other in enumerate(counts):
            if k != j:
                ahead = other >= mine if k < j else other > mine
                rank += ahead.astype(jnp.int32)
        ranks.append(rank)
    offsets = []
    for j in range(len(counts)):
        offset = jnp.int32(0)
        for k, other in enumerate(counts):
            if k != j:
                offset += jnp.where((ranks[k] >= cut) & (ranks[k] < ranks[j]), other, 0)
        offsets.append(offset)
    return ranks, offsets


def pick_kernel(cut, counts_ref, basis_ref, order_ref, offsets_ref, first_ref, rest_ref):
    nblock = basis_ref.shape[0]
    ranks, offsets = rank_blocks([counts_ref[j] for j in range(nblock)], cut)
    for j in range(nblock):
        order_ref[ranks[j]] = jnp.int32(j)
        offsets_ref[j] = offsets[j]
    for place in range(nblock):
        block = basis_ref[order_ref[place]]
        if place < cut:
            first_ref[place] = block
        else:
            rest_ref[place - cut] = block


def pick(cut, counts, basis):
    nblock = basis.shape[0]
    smem, vmem = pl.BlockSpec(memory_space=pltpu.SMEM), pl.BlockSpec(memory_space=pltpu.VMEM)
    return pl.pallas_call(
        functools.partial(pick_kernel, cut),
        out_shape=(
            jax.ShapeDtypeStruct((nblock,), jnp.int32),
            jax.ShapeDtypeStruct((nblock,), jnp.int32),
            jax.ShapeDtypeStruct((cut,) + basis.shape[1:], basis.dtype),
            jax.ShapeDtypeStruct((nblock - cut,) + basis.shape[1:], basis.dtype),
        ),
        in_specs=[smem, vmem],
        out_specs=(smem, smem, vmem, vmem),
        compiler_params=pltpu.CompilerParams(vmem_limit_bytes=VMEM_LIMIT),
    )(counts, basis)


def tables_kernel(cut, nblock, widths, me_ref, *refs):
    *group_refs, counts_ref, order_ref, offsets_ref, branch_ref, joined_ref = refs
    group = group_refs[0].shape[0]
    for place, group_ref in enumerate(group_refs):
        for k in range(group):
            joined_ref[place * group + k] = group_ref[k]

    def step(source, need):
        base = source * nblock
        theirs = (source ^ me_ref[0]) * nblock
        counts = [joined_ref[theirs + j] for j in range(nblock)]
        ranks, offsets = rank_blocks(counts, cut)
        used = jnp.int32(0)
        for j in range(nblock):
            counts_ref[base + j] = counts[j]
            order_ref[base + ranks[j]] = jnp.int32(j)
            offsets_ref[base + j] = offsets[j]
            used += jnp.where(ranks[j] >= cut, counts[j], 0)
        return jnp.maximum(need, used)

    need = lax.fori_loop(0, counts_ref.shape[0] // nblock, step, jnp.int32(0))
    branch = jnp.int32(0)
    for width in widths[:-1]:
        branch += (need > width).astype(jnp.int32)
    branch_ref[0] = branch


def all_tables(cut, nblock, widths, me, groups):
    smem = pl.BlockSpec(memory_space=pltpu.SMEM)
    total = sum(group.shape[0] for group in groups)
    table = jax.ShapeDtypeStruct((total,), jnp.int32)
    return pl.pallas_call(
        functools.partial(tables_kernel, cut, nblock, widths),
        out_shape=(table, table, table, jax.ShapeDtypeStruct((1,), jnp.int32)),
        in_specs=[smem] * (1 + len(groups)),
        out_specs=(smem,) * 4,
        scratch_shapes=[pltpu.SMEM((total,), jnp.int32)],
    )(me, *groups)


NFEATURE = 128


def fill_features(rows_ref, points, is_test):
    def three_terms(x):
        high = x.astype(jnp.bfloat16).astype(jnp.float32)
        middle = (x - high).astype(jnp.bfloat16).astype(jnp.float32)
        return high, middle, x - high - middle

    centred = points - 0.5
    norm = jnp.sum(centred * centred, axis=0, keepdims=True)
    terms = three_terms(centred)
    norms = three_terms(norm + softening if is_test else norm)
    for a in range(3):
        for b in range(3):
            place = 3 * (3 * a + b)
            rows_ref[place : place + 3, :] = -2.0 * terms[a] if is_test else terms[b]
    for a in range(3):
        rows_ref[27 + a : 28 + a, :] = norms[a] if is_test else jnp.ones_like(norm)
        rows_ref[30 + a : 31 + a, :] = jnp.ones_like(norm) if is_test else norms[a]


def left_kernel(
    nshard, first, me_ref, order_ref, test_ref, source_ref, basis_ref, out_ref,
    rows_ref, features_ref, turned_ref, near_ref,
):
    j = pl.program_id(0)
    ntest = test_ref.shape[1]
    nq = source_ref.shape[2]
    part = nq // nshard
    block = min(QBLOCK, nq)

    @pl.when(j == 0)
    def _():
        rows_ref[...] = jnp.zeros_like(rows_ref)
        for i in range(ntest):
            fill_features(rows_ref, test_ref[:, i, :], True)
            features_ref[i] = rows_ref[...].T.astype(jnp.bfloat16)
            turned_ref[i] = basis_ref[i].T

    source = order_ref[first + j]
    for comp in range(3):
        rows_ref[comp : comp + 1, :] = source_ref[comp, pl.ds(source, 1), :]
    pieces = []
    for offset in range(nshard):
        start = pl.multiple_of((me_ref[0] ^ offset) * part, part)
        pieces.append(rows_ref[0:3, pl.ds(start, part)])
    fill_features(rows_ref, jnp.concatenate(pieces, axis=1), False)
    near_ref[...] = rows_ref[...].astype(jnp.bfloat16)

    steps = [(i, start) for i in range(ntest) for start in range(0, nq, block)]

    def kernel_block(i, start):
        squared = jnp.dot(
            features_ref[i], near_ref[:, start : start + block], preferred_element_type=jnp.float32
        )
        return lax.rsqrt(squared.astype(jnp.bfloat16))

    ready = kernel_block(*steps[0])
    for place, (i, start) in enumerate(steps):
        now = ready
        if place + 1 < len(steps):
            ready = kernel_block(*steps[place + 1])
        out_ref[i, 0, :, start : start + block] = jnp.dot(
            turned_ref[i], now, preferred_element_type=jnp.float32
        ).astype(jnp.bfloat16)


def left_products(nshard, me, order, test_points, source_points, test_basis, first, last):
    _, ntest, npoint = test_points.shape
    nall, nq = source_points.shape[1:]
    kmax = test_basis.shape[2]
    nsource = last - first
    return pl.pallas_call(
        functools.partial(left_kernel, nshard, first),
        grid_spec=pltpu.PrefetchScalarGridSpec(
            num_scalar_prefetch=2,
            grid=(nsource,),
            in_specs=[
                pl.BlockSpec((3, ntest, npoint), lambda j, *_: (0, 0, 0)),
                pl.BlockSpec((3, nall, nq), lambda j, *_: (0, 0, 0)),
                pl.BlockSpec((ntest, npoint, kmax), lambda j, *_: (0, 0, 0)),
            ],
            out_specs=pl.BlockSpec((ntest, 1, kmax, nq), lambda j, *_: (0, j, 0, 0)),
            scratch_shapes=[
                pltpu.VMEM((NFEATURE, npoint), jnp.float32),
                pltpu.VMEM((ntest, npoint, NFEATURE), jnp.bfloat16),
                pltpu.VMEM((ntest, kmax, npoint), jnp.bfloat16),
                pltpu.VMEM((NFEATURE, nq), jnp.bfloat16),
            ],
        ),
        out_shape=jax.ShapeDtypeStruct((ntest, nsource, kmax, nq), jnp.bfloat16),
        compiler_params=pltpu.CompilerParams(vmem_limit_bytes=VMEM_LIMIT),
        cost_estimate=pl.CostEstimate(
            flops=2 * ntest * nsource * npoint * nq * kmax,
            bytes_accessed=2 * ntest * nsource * kmax * nq,
            transcendentals=ntest * nsource * npoint * nq,
        ),
    )(me, order, test_points, source_points, test_basis)


def tile_kernel(nshard, first, packed, *refs):
    order_ref, source_counts_ref, offsets_ref, test_counts_ref, left_ref = refs[:5]
    shard_refs = refs[5 : 5 + nshard]
    j = pl.program_id(0)
    if packed:
        tile_ref, main_ref, over_ref, pack_ref = refs[5 + nshard :]
    else:
        *near_refs, tile_ref, joined_ref = refs[5 + nshard :]

        @pl.when(j == 0)
        def _():
            nblock = source_counts_ref.shape[0]
            for place, near_ref in enumerate([source_counts_ref] + near_refs):
                for k in range(nblock):
                    joined_ref[place * nblock + k] = near_ref[k]

    ntest, _, kmax, _ = left_ref.shape
    ndest, _, _, rows, width = tile_ref.shape
    count = source_counts_ref[order_ref[first + j]]

    def work(wide):
        side = jnp.concatenate([shard_ref[0, :, :wide] for shard_ref in shard_refs], axis=0)
        row_ids = lax.broadcasted_iota(jnp.int32, (kmax, wide), 0)
        column_ids = lax.broadcasted_iota(jnp.int32, (kmax, wide), 1)
        products = [
            jnp.dot(left_ref[i, 0], side, preferred_element_type=jnp.float32) for i in range(ntest)
        ]
        if packed:
            offset = offsets_ref[order_ref[first + j]]
            shift = offset % LANES
            base = offset - shift
            low = lax.broadcasted_iota(jnp.int32, (kmax, LANES), 1) < shift
        for i in range(ntest):
            used = (row_ids < test_counts_ref[i]) & (column_ids < count)
            tile = jnp.where(used, products[i], 0.0)
            for dest in range(ndest):
                tile_ref[dest, i, 0, :, :wide] = tile[dest * rows : (dest + 1) * rows].astype(jnp.bfloat16)
                if wide < width:
                    tile_ref[dest, i, 0, :, wide:] = jnp.zeros((rows, width - wide), jnp.bfloat16)
            if not packed:
                continue
            rolled = [
                pltpu.roll(tile[:, start : start + LANES], shift, axis=1) for start in range(0, wide, LANES)
            ]
            for place in range(len(rolled) + 1):
                here = pl.ds(pl.multiple_of(base + place * LANES, LANES), LANES)
                if place == 0:
                    before = jnp.concatenate(
                        [pack_ref[dest, i, :, here].astype(jnp.float32) for dest in range(ndest)], axis=0
                    )
                else:
                    before = rolled[place - 1]
                after = rolled[place] if place < len(rolled) else jnp.zeros_like(before)
                window = jnp.where(low, before, after)
                for dest in range(ndest):
                    pack_ref[dest, i, :, here] = window[dest * rows : (dest + 1) * rows].astype(jnp.bfloat16)

    narrow = width - LANES
    if narrow > 0:
        pl.when(count <= narrow)(lambda: work(narrow))
        pl.when(count > narrow)(lambda: work(width))
    else:
        work(width)

    if packed:

        @pl.when(j == pl.num_programs(0) - 1)
        def _():
            main = main_ref.shape[3]
            main_ref[...] = pack_ref[:, :, :, :main]
            over_ref[...] = pack_ref[:, :, :, main : main + over_ref.shape[3]]


def tiles(ndest, first, tables, test_counts, left, shards, main, near=()):
    ntest, nsource, kmax, nq = left.shape
    nshard = len(shards)
    part, width = shards[0].shape[1:]
    rows = kmax // ndest
    packed = main is not None
    shapes = [jax.ShapeDtypeStruct((ndest, ntest, nsource, rows, width), jnp.bfloat16)]
    specs = [pl.BlockSpec((ndest, ntest, 1, rows, width), lambda j, *_: (0, 0, j, 0, 0))]
    scratch = []
    if packed:
        for columns in (main, nsource * width - main):
            shape = (ndest, ntest, rows, columns)
            shapes.append(jax.ShapeDtypeStruct(shape, jnp.bfloat16))
            specs.append(pl.BlockSpec(shape, lambda j, *_: (0, 0, 0, 0)))
        scratch.append(pltpu.VMEM((ndest, ntest, rows, nsource * width + LANES), jnp.bfloat16))
    else:
        shapes.append(jax.ShapeDtypeStruct(((1 + len(near)) * tables[1].shape[0],), jnp.int32))
        specs.append(pl.BlockSpec(memory_space=pltpu.SMEM))
    return pl.pallas_call(
        functools.partial(tile_kernel, nshard, first, packed),
        grid_spec=pltpu.PrefetchScalarGridSpec(
            num_scalar_prefetch=4,
            grid=(nsource,),
            in_specs=[pl.BlockSpec((ntest, 1, kmax, nq), lambda j, *_: (0, j, 0, 0))]
            + [pl.BlockSpec((1, part, width), lambda j, *_: (j, 0, 0))] * nshard
            + [pl.BlockSpec(memory_space=pltpu.SMEM)] * len(near),
            out_specs=specs,
            scratch_shapes=scratch,
        ),
        out_shape=shapes,
        compiler_params=pltpu.CompilerParams(vmem_limit_bytes=VMEM_LIMIT),
        cost_estimate=pl.CostEstimate(
            flops=2 * ntest * nsource * kmax * width * nq,
            bytes_accessed=2 * ntest * nsource * kmax * (nq + width),
            transcendentals=0,
        ),
    )(*tables, test_counts, left, *shards, *near)


def project_kernel(order_ref, tile_ref, coeff_ref, *refs):
    *start_refs, sum_ref, total_ref = refs
    j = pl.program_id(0)
    ndest, ntest, _, rows, _ = tile_ref.shape
    whole = [tile_ref[dest, i, 0] for i in range(ntest) for dest in range(ndest)]
    term = jnp.dot(jnp.concatenate(whole, axis=0), coeff_ref[0], preferred_element_type=jnp.float32)

    @pl.when(j == 0)
    def _():
        total_ref[...] = term + start_refs[0][...] if start_refs else term

    @pl.when(j > 0)
    def _():
        total_ref[...] += term

    @pl.when(j == pl.num_programs(0) - 1)
    def _():
        if not start_refs:
            sum_ref[...] = total_ref[...]
            return
        for i in range(ntest):
            for dest in range(ndest):
                top = (i * ndest + dest) * rows
                sum_ref[dest, i] = total_ref[top : top + rows, :].astype(sum_ref.dtype)


def project(order, first, tiles, coefficients, start):
    ndest, ntest, nsource, rows, width = tiles.shape
    ncol = coefficients.shape[2]
    total_spec = pl.BlockSpec((ntest * ndest * rows, ncol), lambda j, order: (0, 0))
    if start is None:
        started = []
        sum_spec = total_spec
        sum_shape = jax.ShapeDtypeStruct((ntest * ndest * rows, ncol), jnp.float32)
    else:
        started = [start]
        sum_spec = pl.BlockSpec((ndest, ntest, rows, ncol), lambda j, order: (0, 0, 0, 0))
        sum_shape = jax.ShapeDtypeStruct((ndest, ntest, rows, ncol), jnp.bfloat16)
    return pl.pallas_call(
        project_kernel,
        grid_spec=pltpu.PrefetchScalarGridSpec(
            num_scalar_prefetch=1,
            grid=(nsource,),
            in_specs=[
                pl.BlockSpec((ndest, ntest, 1, rows, width), lambda j, order: (0, 0, j, 0, 0)),
                pl.BlockSpec((1, width, ncol), lambda j, order: (order[first + j], 0, 0)),
            ]
            + [total_spec] * len(started),
            out_specs=sum_spec,
            scratch_shapes=[pltpu.VMEM((ntest * ndest * rows, ncol), jnp.float32)],
        ),
        out_shape=sum_shape,
        compiler_params=pltpu.CompilerParams(vmem_limit_bytes=SMALL_VMEM_LIMIT),
        cost_estimate=pl.CostEstimate(
            flops=2 * ndest * ntest * rows * width * ncol * nsource,
            bytes_accessed=2 * ndest * ntest * rows * width * nsource,
            transcendentals=0,
        ),
    )(order, tiles, coefficients, *started)


def unpack_kernel(cut, order_ref, counts_ref, offsets_ref, whole_ref, packed_ref, out_ref, rows_ref):
    nsrc, _, _, rows, width = whole_ref.shape
    packed_width = packed_ref.shape[3]
    nall = out_ref.shape[2]
    nblock = nall // nsrc
    ntile = width // LANES
    step = 16 if rows % 16 == 0 else rows
    lanes = lax.broadcasted_iota(jnp.int32, (rows, LANES), 1)

    @pl.loop(0, nsrc)
    def _(source):
        for place in range(nblock):
            block = order_ref[source * nblock + place]
            target = source * nblock + block
            if place < cut:
                rows_ref[target] = whole_ref[source, 0, place].astype(jnp.float32)
                continue
            count = counts_ref[target]
            offset = offsets_ref[target]
            shift = offset % LANES
            base = offset - shift
            back = (LANES - shift) % LANES
            low = lanes < LANES - shift
            rolled = []
            for tile in range(ntile + 1):
                start = pl.multiple_of(jnp.minimum(base + tile * LANES, packed_width - LANES), LANES)
                piece = packed_ref[source, 0, :, pl.ds(start, LANES)].astype(jnp.float32)
                rolled.append(pltpu.roll(piece, back, axis=1))
            for tile in range(ntile):
                value = jnp.where(low, rolled[tile], rolled[tile + 1])
                value = jnp.where(lanes < count - tile * LANES, value, 0.0)
                rows_ref[target, :, tile * LANES : (tile + 1) * LANES] = value

    @pl.loop(0, nall // 16)
    def _(group):
        here = pl.ds(pl.multiple_of(group * 16, 16), 16)
        for top in range(0, rows, step):
            turned = jnp.transpose(rows_ref[here, top : top + step, :], (1, 0, 2))
            out_ref[0, top : top + step, here, :] = turned.astype(out_ref.dtype)


def unpack(cut, tables, whole, packed):
    nsrc, ntest, _, rows, width = whole.shape
    packed_width = packed.shape[3]
    nall = tables[0].shape[0]
    return pl.pallas_call(
        functools.partial(unpack_kernel, cut),
        grid_spec=pltpu.PrefetchScalarGridSpec(
            num_scalar_prefetch=3,
            grid=(ntest,),
            in_specs=[
                pl.BlockSpec((nsrc, 1, cut, rows, width), lambda i, *_: (0, i, 0, 0, 0)),
                pl.BlockSpec((nsrc, 1, rows, packed_width), lambda i, *_: (0, i, 0, 0)),
            ],
            out_specs=pl.BlockSpec((1, rows, nall, width), lambda i, *_: (i, 0, 0, 0)),
            scratch_shapes=[pltpu.VMEM((nall, rows, width), jnp.float32)],
        ),
        out_shape=jax.ShapeDtypeStruct((ntest, rows, nall, width), jnp.bfloat16),
        compiler_params=pltpu.CompilerParams(vmem_limit_bytes=SMALL_VMEM_LIMIT),
    )(*tables, whole, packed)


def body(
    test_points, test_basis, test_counts, source_points, source_basis, source_counts, coefficients
):
    nsource, part, kmax = source_basis.shape
    ntest = test_points.shape[0]
    nsrc = lax.axis_size("src")
    ntest_axis = lax.axis_size("test")
    me_test = lax.axis_index("test")
    cut = max(1, nsource * 3 // 8)

    held = {}

    def gather(name, shard, left):
        got = {0: shard}
        bits = list(bits_down(ntest_axis))
        for bit in bits:
            if bit == bits[-1]:
                names = [o for o in got if o != 0]
                tied = lax.optimization_barrier(tuple(got[o] for o in names) + (left,))
                got.update(zip(names, tied[:-1]))
                left = tied[-1]
            for offset in list(got):
                got[offset ^ bit] = exchange(got[offset], "test", bit)
            if bit == bits[0]:
                held[name] = got[bit]
        return [got[offset] for offset in sorted(got)], left

    most = (nsource - cut) * kmax
    main = min(most, -(-most * 18 // (25 * LANES)) * LANES)
    widths = [main, min(most, main + 2 * LANES), most]

    order, offsets, basis_a, basis_b = pick(cut, source_counts, source_basis)
    tables = (order, source_counts, offsets)
    me = jnp.reshape(me_test, (1,))
    test_points, source_points = test_points.transpose(1, 0, 2), source_points.transpose(1, 0, 2)

    left_a = left_products(ntest_axis, me, order, test_points, source_points, test_basis, 0, cut)
    shards_a, left_a = gather("a", basis_a, left_a)
    inner = max(1, nsrc // 4)
    near = [exchange(source_counts, "src", flip) for flip in range(1, inner)]
    *near, left_a = lax.optimization_barrier((*near, left_a))
    tiles_a, joined = tiles(nsrc, 0, tables, test_counts, left_a, shards_a, None, near)
    groups = [joined] + [exchange(joined, "src", flip) for flip in range(inner, nsrc, inner)]
    moved_a = lax.all_to_all(tiles_a, "src", split_axis=0, concat_axis=0, tiled=True)

    rest, _ = lax.optimization_barrier((basis_b, held["a"]))
    later, _ = lax.optimization_barrier((source_points, tiles_a))
    left_b = left_products(ntest_axis, me, order, test_points, later, test_basis, cut, nsource)
    shards_b, left_b = gather("b", rest, left_b)
    tiles_b, packed, beyond = tiles(nsrc, cut, tables, test_counts, left_b, shards_b, main)
    sums_a = project(order, 0, tiles_a, coefficients, None)
    packed, sums_a, *groups = lax.optimization_barrier((packed, sums_a, *groups))
    moved_b = lax.all_to_all(packed, "src", split_axis=0, concat_axis=0, tiled=True)

    sums = project(order, cut, tiles_b, coefficients, sums_a)
    projected = sum_rows(sums, "src")
    me_src, _ = lax.optimization_barrier((jnp.reshape(lax.axis_index("src"), (1,)), packed))
    all_counts, all_order, all_offsets, branch = all_tables(cut, nsource, widths, me_src, groups)
    spread = (all_order, all_counts, all_offsets)

    def finish(width, beyond, moved_a, moved_b, spread):
        if width > main:
            more = lax.all_to_all(
                beyond[..., : width - main], "src", split_axis=0, concat_axis=0, tiled=True
            )
            moved_b = jnp.concatenate([moved_b, more], axis=3)
        return unpack(cut, spread, moved_a, moved_b)

    reduced = lax.switch(
        branch[0],
        [functools.partial(finish, width) for width in widths],
        beyond,
        moved_a,
        moved_b,
        spread,
    )
    return (reduced, projected)


def solution(mesh):
    return jax.shard_map(
        body,
        mesh=mesh,
        in_specs=(
            P("test", None, None),
            P("test", None, None),
            P("test"),
            P("src", None, None),
            P("src", "test", None),
            P("src"),
            P("src", None, None),
        ),
        out_specs=(P("test", "src", None, None), P("test", "src", None)),
        check_vma=False,
    )
```

```python
import functools

import jax
import jax.numpy as jnp
from jax import lax
from jax.experimental import pallas as pl
from jax.experimental.pallas import tpu as pltpu
from jax.sharding import PartitionSpec as P

softening = 0.0025
QBLOCK = 256
LANES = 128
VMEM_LIMIT = 60 * 1024 * 1024
SMALL_VMEM_LIMIT = 32 * 1024 * 1024


def exchange(x, axis, flip):
    size = lax.axis_size(axis)
    return lax.ppermute(x, axis, [(a, a ^ flip) for a in range(size)])


def bits_down(size):
    bit = size // 2
    while bit >= 1:
        yield bit
        bit //= 2


def sum_rows(total, axis):
    size = lax.axis_size(axis)
    me = lax.axis_index(axis)
    held, bit = total, 1
    while held.shape[0] > 4:
        pairs = held.reshape((held.shape[0] // 2, 2) + held.shape[1:])
        mine = (me // bit) % 2
        keep = lax.dynamic_index_in_dim(pairs, mine, 1, keepdims=False)
        give = lax.dynamic_index_in_dim(pairs, 1 - mine, 1, keepdims=False)
        got = exchange(give, axis, bit)
        held = (keep.astype(jnp.float32) + got.astype(jnp.float32)).astype(held.dtype)
        bit *= 2
    mine = me // bit
    result = lax.dynamic_index_in_dim(held, mine, 0, keepdims=False).astype(jnp.float32)
    for flip in range(1, held.shape[0]):
        give = lax.dynamic_index_in_dim(held, mine ^ flip, 0, keepdims=False)
        result = result + exchange(give, axis, flip * bit).astype(jnp.float32)
    return result.astype(total.dtype)


def rank_blocks(counts, cut):
    ranks = []
    for j, mine in enumerate(counts):
        rank = jnp.int32(0)
        for k, other in enumerate(counts):
            if k != j:
                ahead = other >= mine if k < j else other > mine
                rank += ahead.astype(jnp.int32)
        ranks.append(rank)
    offsets = []
    for j in range(len(counts)):
        offset = jnp.int32(0)
        for k, other in enumerate(counts):
            if k != j:
                offset += jnp.where((ranks[k] >= cut) & (ranks[k] < ranks[j]), other, 0)
        offsets.append(offset)
    return ranks, offsets


def pick_kernel(cut, counts_ref, basis_ref, order_ref, offsets_ref, first_ref, rest_ref):
    nblock = basis_ref.shape[0]
    ranks, offsets = rank_blocks([counts_ref[j] for j in range(nblock)], cut)
    for j in range(nblock):
        order_ref[ranks[j]] = jnp.int32(j)
        offsets_ref[j] = offsets[j]
    for place in range(nblock):
        block = basis_ref[order_ref[place]]
        if place < cut:
            first_ref[place] = block
        else:
            rest_ref[place - cut] = block


def pick(cut, counts, basis):
    nblock = basis.shape[0]
    smem, vmem = pl.BlockSpec(memory_space=pltpu.SMEM), pl.BlockSpec(memory_space=pltpu.VMEM)
    return pl.pallas_call(
        functools.partial(pick_kernel, cut),
        out_shape=(
            jax.ShapeDtypeStruct((nblock,), jnp.int32),
            jax.ShapeDtypeStruct((nblock,), jnp.int32),
            jax.ShapeDtypeStruct((cut,) + basis.shape[1:], basis.dtype),
            jax.ShapeDtypeStruct((nblock - cut,) + basis.shape[1:], basis.dtype),
        ),
        in_specs=[smem, vmem],
        out_specs=(smem, smem, vmem, vmem),
        compiler_params=pltpu.CompilerParams(vmem_limit_bytes=VMEM_LIMIT),
    )(counts, basis)


def tables_kernel(cut, nblock, widths, me_ref, *refs):
    *group_refs, counts_ref, order_ref, offsets_ref, branch_ref, joined_ref = refs
    group = group_refs[0].shape[0]
    for place, group_ref in enumerate(group_refs):
        for k in range(group):
            joined_ref[place * group + k] = group_ref[k]

    def step(source, need):
        base = source * nblock
        theirs = (source ^ me_ref[0]) * nblock
        counts = [joined_ref[theirs + j] for j in range(nblock)]
        ranks, offsets = rank_blocks(counts, cut)
        used = jnp.int32(0)
        for j in range(nblock):
            counts_ref[base + j] = counts[j]
            order_ref[base + ranks[j]] = jnp.int32(j)
            offsets_ref[base + j] = offsets[j]
            used += jnp.where(ranks[j] >= cut, counts[j], 0)
        return jnp.maximum(need, used)

    need = lax.fori_loop(0, counts_ref.shape[0] // nblock, step, jnp.int32(0))
    branch = jnp.int32(0)
    for width in widths[:-1]:
        branch += (need > width).astype(jnp.int32)
    branch_ref[0] = branch


def all_tables(cut, nblock, widths, me, groups):
    smem = pl.BlockSpec(memory_space=pltpu.SMEM)
    total = sum(group.shape[0] for group in groups)
    table = jax.ShapeDtypeStruct((total,), jnp.int32)
    return pl.pallas_call(
        functools.partial(tables_kernel, cut, nblock, widths),
        out_shape=(table, table, table, jax.ShapeDtypeStruct((1,), jnp.int32)),
        in_specs=[smem] * (1 + len(groups)),
        out_specs=(smem,) * 4,
        scratch_shapes=[pltpu.SMEM((total,), jnp.int32)],
    )(me, *groups)


NFEATURE = 128


def fill_features(rows_ref, points, is_test):
    def three_terms(x):
        high = x.astype(jnp.bfloat16).astype(jnp.float32)
        middle = (x - high).astype(jnp.bfloat16).astype(jnp.float32)
        return high, middle, x - high - middle

    centred = points - 0.5
    norm = jnp.sum(centred * centred, axis=0, keepdims=True)
    terms = three_terms(centred)
    norms = three_terms(norm + softening if is_test else norm)
    for a in range(3):
        for b in range(3):
            place = 3 * (3 * a + b)
            rows_ref[place : place + 3, :] = -2.0 * terms[a] if is_test else terms[b]
    for a in range(3):
        rows_ref[27 + a : 28 + a, :] = norms[a] if is_test else jnp.ones_like(norm)
        rows_ref[30 + a : 31 + a, :] = jnp.ones_like(norm) if is_test else norms[a]


def left_kernel(
    nshard, first, me_ref, order_ref, test_ref, source_ref, basis_ref, out_ref,
    rows_ref, features_ref, turned_ref, near_ref,
):
    j = pl.program_id(0)
    ntest = test_ref.shape[1]
    nq = source_ref.shape[2]
    part = nq // nshard
    block = min(QBLOCK, nq)

    @pl.when(j == 0)
    def _():
        rows_ref[...] = jnp.zeros_like(rows_ref)
        for i in range(ntest):
            fill_features(rows_ref, test_ref[:, i, :], True)
            features_ref[i] = rows_ref[...].T.astype(jnp.bfloat16)
            turned_ref[i] = basis_ref[i].T

    source = order_ref[first + j]
    for comp in range(3):
        rows_ref[comp : comp + 1, :] = source_ref[comp, pl.ds(source, 1), :]
    pieces = []
    for offset in range(nshard):
        start = pl.multiple_of((me_ref[0] ^ offset) * part, part)
        pieces.append(rows_ref[0:3, pl.ds(start, part)])
    fill_features(rows_ref, jnp.concatenate(pieces, axis=1), False)
    near_ref[...] = rows_ref[...].astype(jnp.bfloat16)

    steps = [(i, start) for i in range(ntest) for start in range(0, nq, block)]

    def kernel_block(i, start):
        squared = jnp.dot(
            features_ref[i], near_ref[:, start : start + block], preferred_element_type=jnp.float32
        )
        return lax.rsqrt(squared.astype(jnp.bfloat16))

    ready = kernel_block(*steps[0])
    for place, (i, start) in enumerate(steps):
        now = ready
        if place + 1 < len(steps):
            ready = kernel_block(*steps[place + 1])
        out_ref[i, 0, :, start : start + block] = jnp.dot(
            turned_ref[i], now, preferred_element_type=jnp.float32
        ).astype(jnp.bfloat16)


def left_products(nshard, me, order, test_points, source_points, test_basis, first, last):
    _, ntest, npoint = test_points.shape
    nall, nq = source_points.shape[1:]
    kmax = test_basis.shape[2]
    nsource = last - first
    return pl.pallas_call(
        functools.partial(left_kernel, nshard, first),
        grid_spec=pltpu.PrefetchScalarGridSpec(
            num_scalar_prefetch=2,
            grid=(nsource,),
            in_specs=[
                pl.BlockSpec((3, ntest, npoint), lambda j, *_: (0, 0, 0)),
                pl.BlockSpec((3, nall, nq), lambda j, *_: (0, 0, 0)),
                pl.BlockSpec((ntest, npoint, kmax), lambda j, *_: (0, 0, 0)),
            ],
            out_specs=pl.BlockSpec((ntest, 1, kmax, nq), lambda j, *_: (0, j, 0, 0)),
            scratch_shapes=[
                pltpu.VMEM((NFEATURE, npoint), jnp.float32),
                pltpu.VMEM((ntest, npoint, NFEATURE), jnp.bfloat16),
                pltpu.VMEM((ntest, kmax, npoint), jnp.bfloat16),
                pltpu.VMEM((NFEATURE, nq), jnp.bfloat16),
            ],
        ),
        out_shape=jax.ShapeDtypeStruct((ntest, nsource, kmax, nq), jnp.bfloat16),
        compiler_params=pltpu.CompilerParams(vmem_limit_bytes=VMEM_LIMIT),
        cost_estimate=pl.CostEstimate(
            flops=2 * ntest * nsource * npoint * nq * kmax,
            bytes_accessed=2 * ntest * nsource * kmax * nq,
            transcendentals=ntest * nsource * npoint * nq,
        ),
    )(me, order, test_points, source_points, test_basis)


def tile_kernel(nshard, first, packed, *refs):
    order_ref, source_counts_ref, offsets_ref, test_counts_ref, left_ref = refs[:5]
    shard_refs = refs[5 : 5 + nshard]
    j = pl.program_id(0)
    if not packed:
        (tile_ref,) = refs[5 + nshard :]
    else:
        *near_refs, tile_ref, main_ref, over_ref, joined_ref, pack_ref = refs[5 + nshard :]

        @pl.when(j == 0)
        def _():
            nblock = source_counts_ref.shape[0]
            for place, near_ref in enumerate([source_counts_ref] + near_refs):
                for k in range(nblock):
                    joined_ref[place * nblock + k] = near_ref[k]

    ntest, _, kmax, _ = left_ref.shape
    ndest, _, _, rows, width = tile_ref.shape
    count = source_counts_ref[order_ref[first + j]]

    def work(wide):
        side = jnp.concatenate([shard_ref[0, :, :wide] for shard_ref in shard_refs], axis=0)
        row_ids = lax.broadcasted_iota(jnp.int32, (kmax, wide), 0)
        column_ids = lax.broadcasted_iota(jnp.int32, (kmax, wide), 1)
        products = [
            jnp.dot(left_ref[i, 0], side, preferred_element_type=jnp.float32) for i in range(ntest)
        ]
        if packed:
            offset = offsets_ref[order_ref[first + j]]
            shift = offset % LANES
            base = offset - shift
            low = lax.broadcasted_iota(jnp.int32, (kmax, LANES), 1) < shift
        for i in range(ntest):
            used = (row_ids < test_counts_ref[i]) & (column_ids < count)
            tile = jnp.where(used, products[i], 0.0)
            for dest in range(ndest):
                tile_ref[dest, i, 0, :, :wide] = tile[dest * rows : (dest + 1) * rows].astype(jnp.bfloat16)
                if wide < width:
                    tile_ref[dest, i, 0, :, wide:] = jnp.zeros((rows, width - wide), jnp.bfloat16)
            if not packed:
                continue
            rolled = [
                pltpu.roll(tile[:, start : start + LANES], shift, axis=1) for start in range(0, wide, LANES)
            ]
            for place in range(len(rolled) + 1):
                here = pl.ds(pl.multiple_of(base + place * LANES, LANES), LANES)
                if place == 0:
                    before = jnp.concatenate(
                        [pack_ref[dest, i, :, here].astype(jnp.float32) for dest in range(ndest)], axis=0
                    )
                else:
                    before = rolled[place - 1]
                after = rolled[place] if place < len(rolled) else jnp.zeros_like(before)
                window = jnp.where(low, before, after)
                for dest in range(ndest):
                    pack_ref[dest, i, :, here] = window[dest * rows : (dest + 1) * rows].astype(jnp.bfloat16)

    narrow = width - LANES
    if narrow > 0:
        pl.when(count <= narrow)(lambda: work(narrow))
        pl.when(count > narrow)(lambda: work(width))
    else:
        work(width)

    if packed:

        @pl.when(j == pl.num_programs(0) - 1)
        def _():
            main = main_ref.shape[3]
            main_ref[...] = pack_ref[:, :, :, :main]
            over_ref[...] = pack_ref[:, :, :, main : main + over_ref.shape[3]]


def tiles(ndest, first, tables, test_counts, left, shards, main, near=()):
    ntest, nsource, kmax, nq = left.shape
    nshard = len(shards)
    part, width = shards[0].shape[1:]
    rows = kmax // ndest
    packed = main is not None
    shapes = [jax.ShapeDtypeStruct((ndest, ntest, nsource, rows, width), jnp.bfloat16)]
    specs = [pl.BlockSpec((ndest, ntest, 1, rows, width), lambda j, *_: (0, 0, j, 0, 0))]
    scratch = []
    if packed:
        for columns in (main, nsource * width - main):
            shape = (ndest, ntest, rows, columns)
            shapes.append(jax.ShapeDtypeStruct(shape, jnp.bfloat16))
            specs.append(pl.BlockSpec(shape, lambda j, *_: (0, 0, 0, 0)))
        scratch.append(pltpu.VMEM((ndest, ntest, rows, nsource * width + LANES), jnp.bfloat16))
        shapes.append(jax.ShapeDtypeStruct(((1 + len(near)) * tables[1].shape[0],), jnp.int32))
        specs.append(pl.BlockSpec(memory_space=pltpu.SMEM))
    return pl.pallas_call(
        functools.partial(tile_kernel, nshard, first, packed),
        grid_spec=pltpu.PrefetchScalarGridSpec(
            num_scalar_prefetch=4,
            grid=(nsource,),
            in_specs=[pl.BlockSpec((ntest, 1, kmax, nq), lambda j, *_: (0, j, 0, 0))]
            + [pl.BlockSpec((1, part, width), lambda j, *_: (j, 0, 0))] * nshard
            + [pl.BlockSpec(memory_space=pltpu.SMEM)] * len(near),
            out_specs=specs,
            scratch_shapes=scratch,
        ),
        out_shape=shapes,
        compiler_params=pltpu.CompilerParams(vmem_limit_bytes=VMEM_LIMIT),
        cost_estimate=pl.CostEstimate(
            flops=2 * ntest * nsource * kmax * width * nq,
            bytes_accessed=2 * ntest * nsource * kmax * (nq + width),
            transcendentals=0,
        ),
    )(*tables, test_counts, left, *shards, *near)


def project_kernel(order_ref, tile_ref, coeff_ref, *refs):
    *start_refs, sum_ref, total_ref = refs
    j = pl.program_id(0)
    ndest, ntest, _, rows, _ = tile_ref.shape
    whole = [tile_ref[dest, i, 0] for i in range(ntest) for dest in range(ndest)]
    term = jnp.dot(jnp.concatenate(whole, axis=0), coeff_ref[0], preferred_element_type=jnp.float32)

    @pl.when(j == 0)
    def _():
        total_ref[...] = term + start_refs[0][...] if start_refs else term

    @pl.when(j > 0)
    def _():
        total_ref[...] += term

    @pl.when(j == pl.num_programs(0) - 1)
    def _():
        if not start_refs:
            sum_ref[...] = total_ref[...]
            return
        for i in range(ntest):
            for dest in range(ndest):
                top = (i * ndest + dest) * rows
                sum_ref[dest, i] = total_ref[top : top + rows, :].astype(sum_ref.dtype)


def project(order, first, tiles, coefficients, start):
    ndest, ntest, nsource, rows, width = tiles.shape
    ncol = coefficients.shape[2]
    total_spec = pl.BlockSpec((ntest * ndest * rows, ncol), lambda j, order: (0, 0))
    if start is None:
        started = []
        sum_spec = total_spec
        sum_shape = jax.ShapeDtypeStruct((ntest * ndest * rows, ncol), jnp.float32)
    else:
        started = [start]
        sum_spec = pl.BlockSpec((ndest, ntest, rows, ncol), lambda j, order: (0, 0, 0, 0))
        sum_shape = jax.ShapeDtypeStruct((ndest, ntest, rows, ncol), jnp.bfloat16)
    return pl.pallas_call(
        project_kernel,
        grid_spec=pltpu.PrefetchScalarGridSpec(
            num_scalar_prefetch=1,
            grid=(nsource,),
            in_specs=[
                pl.BlockSpec((ndest, ntest, 1, rows, width), lambda j, order: (0, 0, j, 0, 0)),
                pl.BlockSpec((1, width, ncol), lambda j, order: (order[first + j], 0, 0)),
            ]
            + [total_spec] * len(started),
            out_specs=sum_spec,
            scratch_shapes=[pltpu.VMEM((ntest * ndest * rows, ncol), jnp.float32)],
        ),
        out_shape=sum_shape,
        compiler_params=pltpu.CompilerParams(vmem_limit_bytes=VMEM_LIMIT),
        cost_estimate=pl.CostEstimate(
            flops=2 * ndest * ntest * rows * width * ncol * nsource,
            bytes_accessed=2 * ndest * ntest * rows * width * nsource,
            transcendentals=0,
        ),
    )(order, tiles, coefficients, *started)


def unpack_kernel(cut, order_ref, counts_ref, offsets_ref, whole_ref, packed_ref, out_ref, rows_ref):
    nsrc, _, _, rows, width = whole_ref.shape
    packed_width = packed_ref.shape[3]
    nall = out_ref.shape[2]
    nblock = nall // nsrc
    ntile = width // LANES
    step = 16 if rows % 16 == 0 else rows
    lanes = lax.broadcasted_iota(jnp.int32, (rows, LANES), 1)

    @pl.loop(0, nsrc)
    def _(source):
        for place in range(nblock):
            block = order_ref[source * nblock + place]
            target = source * nblock + block
            if place < cut:
                rows_ref[target] = whole_ref[source, 0, place].astype(jnp.float32)
                continue
            count = counts_ref[target]
            offset = offsets_ref[target]
            shift = offset % LANES
            base = offset - shift
            back = (LANES - shift) % LANES
            low = lanes < LANES - shift
            rolled = []
            for tile in range(ntile + 1):
                start = pl.multiple_of(jnp.minimum(base + tile * LANES, packed_width - LANES), LANES)
                piece = packed_ref[source, 0, :, pl.ds(start, LANES)].astype(jnp.float32)
                rolled.append(pltpu.roll(piece, back, axis=1))
            for tile in range(ntile):
                value = jnp.where(low, rolled[tile], rolled[tile + 1])
                value = jnp.where(lanes < count - tile * LANES, value, 0.0)
                rows_ref[target, :, tile * LANES : (tile + 1) * LANES] = value

    @pl.loop(0, nall // 16)
    def _(group):
        here = pl.ds(pl.multiple_of(group * 16, 16), 16)
        for top in range(0, rows, step):
            turned = jnp.transpose(rows_ref[here, top : top + step, :], (1, 0, 2))
            out_ref[0, top : top + step, here, :] = turned.astype(out_ref.dtype)


def unpack(cut, tables, whole, packed):
    nsrc, ntest, _, rows, width = whole.shape
    packed_width = packed.shape[3]
    nall = tables[0].shape[0]
    return pl.pallas_call(
        functools.partial(unpack_kernel, cut),
        grid_spec=pltpu.PrefetchScalarGridSpec(
            num_scalar_prefetch=3,
            grid=(ntest,),
            in_specs=[
                pl.BlockSpec((nsrc, 1, cut, rows, width), lambda i, *_: (0, i, 0, 0, 0)),
                pl.BlockSpec((nsrc, 1, rows, packed_width), lambda i, *_: (0, i, 0, 0)),
            ],
            out_specs=pl.BlockSpec((1, rows, nall, width), lambda i, *_: (i, 0, 0, 0)),
            scratch_shapes=[pltpu.VMEM((nall, rows, width), jnp.float32)],
        ),
        out_shape=jax.ShapeDtypeStruct((ntest, rows, nall, width), jnp.bfloat16),
        compiler_params=pltpu.CompilerParams(vmem_limit_bytes=SMALL_VMEM_LIMIT),
    )(*tables, whole, packed)


def body(
    test_points, test_basis, test_counts, source_points, source_basis, source_counts, coefficients
):
    nsource, part, kmax = source_basis.shape
    ntest = test_points.shape[0]
    nsrc = lax.axis_size("src")
    ntest_axis = lax.axis_size("test")
    me_test = lax.axis_index("test")
    cut = max(1, nsource * 3 // 8)

    held = {}

    def gather(name, shard, left):
        got = {0: shard}
        bits = list(bits_down(ntest_axis))
        for bit in bits:
            if bit == bits[-1]:
                names = [o for o in got if o != 0]
                tied = lax.optimization_barrier(tuple(got[o] for o in names) + (left,))
                got.update(zip(names, tied[:-1]))
                left = tied[-1]
            for offset in list(got):
                got[offset ^ bit] = exchange(got[offset], "test", bit)
            if bit == bits[0]:
                held[name] = got[bit]
        return [got[offset] for offset in sorted(got)], left

    most = (nsource - cut) * kmax
    main = min(most, -(-most * 18 // (25 * LANES)) * LANES)
    widths = [main, min(most, main + 2 * LANES), most]

    order, offsets, basis_a, basis_b = pick(cut, source_counts, source_basis)
    tables = (order, source_counts, offsets)
    me = jnp.reshape(me_test, (1,))
    test_points, source_points = test_points.transpose(1, 0, 2), source_points.transpose(1, 0, 2)

    left_a = left_products(ntest_axis, me, order, test_points, source_points, test_basis, 0, cut)
    shards_a, left_a = gather("a", basis_a, left_a)
    (tiles_a,) = tiles(nsrc, 0, tables, test_counts, left_a, shards_a, None)
    moved_a = lax.all_to_all(tiles_a, "src", split_axis=0, concat_axis=0, tiled=True)

    rest, _ = lax.optimization_barrier((basis_b, held["a"]))
    later, _ = lax.optimization_barrier((source_points, tiles_a))
    left_b = left_products(ntest_axis, me, order, test_points, later, test_basis, cut, nsource)
    shards_b, left_b = gather("b", rest, left_b)
    inner = max(1, nsrc // 4)
    counts, _ = lax.optimization_barrier((source_counts, left_b))
    near = [exchange(counts, "src", flip) for flip in range(1, inner)]
    tiles_b, packed, beyond, joined = tiles(
        nsrc, cut, tables, test_counts, left_b, shards_b, main, near
    )
    groups = [joined] + [exchange(joined, "src", flip) for flip in range(inner, nsrc, inner)]
    packed, *groups = lax.optimization_barrier((packed, *groups))
    moved_b = lax.all_to_all(packed, "src", split_axis=0, concat_axis=0, tiled=True)

    sums = project(order, 0, tiles_a, coefficients, None)
    sums = project(order, cut, tiles_b, coefficients, sums)
    projected = sum_rows(sums, "src")
    me_src, _ = lax.optimization_barrier((jnp.reshape(lax.axis_index("src"), (1,)), packed))
    all_counts, all_order, all_offsets, branch = all_tables(cut, nsource, widths, me_src, groups)
    spread = (all_order, all_counts, all_offsets)

    def finish(width, beyond, moved_a, moved_b, spread):
        if width > main:
            more = lax.all_to_all(
                beyond[..., : width - main], "src", split_axis=0, concat_axis=0, tiled=True
            )
            moved_b = jnp.concatenate([moved_b, more], axis=3)
        return unpack(cut, spread, moved_a, moved_b)

    reduced = lax.switch(
        branch[0],
        [functools.partial(finish, width) for width in widths],
        beyond,
        moved_a,
        moved_b,
        spread,
    )
    return (reduced, projected)


def solution(mesh):
    return jax.shard_map(
        body,
        mesh=mesh,
        in_specs=(
            P("test", None, None),
            P("test", None, None),
            P("test"),
            P("src", None, None),
            P("src", "test", None),
            P("src"),
            P("src", None, None),
        ),
        out_specs=(P("test", "src", None, None), P("test", "src", None)),
        check_vma=False,
    )
```

```python
import functools

import jax
import jax.numpy as jnp
from jax import lax
from jax.experimental import pallas as pl
from jax.experimental.pallas import tpu as pltpu
from jax.sharding import PartitionSpec as P

softening = 0.0025
QBLOCK = 256
LANES = 128
VMEM_LIMIT = 60 * 1024 * 1024
SMALL_VMEM_LIMIT = 32 * 1024 * 1024


def exchange(x, axis, flip):
    size = lax.axis_size(axis)
    return lax.ppermute(x, axis, [(a, a ^ flip) for a in range(size)])


def bits_down(size):
    bit = size // 2
    while bit >= 1:
        yield bit
        bit //= 2


def sum_rows(total, axis):
    size = lax.axis_size(axis)
    me = lax.axis_index(axis)
    held, bit = total, 1
    while held.shape[0] > 4:
        pairs = held.reshape((held.shape[0] // 2, 2) + held.shape[1:])
        mine = (me // bit) % 2
        keep = lax.dynamic_index_in_dim(pairs, mine, 1, keepdims=False)
        give = lax.dynamic_index_in_dim(pairs, 1 - mine, 1, keepdims=False)
        got = exchange(give, axis, bit)
        held = (keep.astype(jnp.float32) + got.astype(jnp.float32)).astype(held.dtype)
        bit *= 2
    mine = me // bit
    result = lax.dynamic_index_in_dim(held, mine, 0, keepdims=False).astype(jnp.float32)
    for flip in range(1, held.shape[0]):
        give = lax.dynamic_index_in_dim(held, mine ^ flip, 0, keepdims=False)
        result = result + exchange(give, axis, flip * bit).astype(jnp.float32)
    return result.astype(total.dtype)


def rank_blocks(counts, cut):
    ranks = []
    for j, mine in enumerate(counts):
        rank = jnp.int32(0)
        for k, other in enumerate(counts):
            if k != j:
                ahead = other >= mine if k < j else other > mine
                rank += ahead.astype(jnp.int32)
        ranks.append(rank)
    offsets = []
    for j in range(len(counts)):
        offset = jnp.int32(0)
        for k, other in enumerate(counts):
            if k != j:
                offset += jnp.where((ranks[k] >= cut) & (ranks[k] < ranks[j]), other, 0)
        offsets.append(offset)
    return ranks, offsets


def pick_kernel(cut, counts_ref, basis_ref, order_ref, offsets_ref, first_ref, rest_ref):
    nblock = basis_ref.shape[0]
    ranks, offsets = rank_blocks([counts_ref[j] for j in range(nblock)], cut)
    for j in range(nblock):
        order_ref[ranks[j]] = jnp.int32(j)
        offsets_ref[j] = offsets[j]
    for place in range(nblock):
        block = basis_ref[order_ref[place]]
        if place < cut:
            first_ref[place] = block
        else:
            rest_ref[place - cut] = block


def pick(cut, counts, basis):
    nblock = basis.shape[0]
    smem, vmem = pl.BlockSpec(memory_space=pltpu.SMEM), pl.BlockSpec(memory_space=pltpu.VMEM)
    return pl.pallas_call(
        functools.partial(pick_kernel, cut),
        out_shape=(
            jax.ShapeDtypeStruct((nblock,), jnp.int32),
            jax.ShapeDtypeStruct((nblock,), jnp.int32),
            jax.ShapeDtypeStruct((cut,) + basis.shape[1:], basis.dtype),
            jax.ShapeDtypeStruct((nblock - cut,) + basis.shape[1:], basis.dtype),
        ),
        in_specs=[smem, vmem],
        out_specs=(smem, smem, vmem, vmem),
        compiler_params=pltpu.CompilerParams(vmem_limit_bytes=VMEM_LIMIT),
    )(counts, basis)


def tables_kernel(cut, nblock, widths, me_ref, *refs):
    *group_refs, counts_ref, order_ref, offsets_ref, branch_ref, joined_ref = refs
    group, inner = group_refs[0].shape[0], len(group_refs)
    for place, group_ref in enumerate(group_refs):
        for k in range(group):
            joined_ref[place * group + k] = group_ref[k]

    def step(source, need):
        base = source * nblock
        offset = source ^ me_ref[0]
        theirs = (offset % inner) * group + (offset // inner) * nblock
        counts = [joined_ref[theirs + j] for j in range(nblock)]
        ranks, offsets = rank_blocks(counts, cut)
        used = jnp.int32(0)
        for j in range(nblock):
            counts_ref[base + j] = counts[j]
            order_ref[base + ranks[j]] = jnp.int32(j)
            offsets_ref[base + j] = offsets[j]
            used += jnp.where(ranks[j] >= cut, counts[j], 0)
        return jnp.maximum(need, used)

    need = lax.fori_loop(0, counts_ref.shape[0] // nblock, step, jnp.int32(0))
    branch = jnp.int32(0)
    for width in widths[:-1]:
        branch += (need > width).astype(jnp.int32)
    branch_ref[0] = branch


def all_tables(cut, nblock, widths, me, groups):
    smem = pl.BlockSpec(memory_space=pltpu.SMEM)
    total = sum(group.shape[0] for group in groups)
    table = jax.ShapeDtypeStruct((total,), jnp.int32)
    return pl.pallas_call(
        functools.partial(tables_kernel, cut, nblock, widths),
        out_shape=(table, table, table, jax.ShapeDtypeStruct((1,), jnp.int32)),
        in_specs=[smem] * (1 + len(groups)),
        out_specs=(smem,) * 4,
        scratch_shapes=[pltpu.SMEM((total,), jnp.int32)],
    )(me, *groups)


NFEATURE = 128


def fill_features(rows_ref, points, is_test):
    def three_terms(x):
        high = x.astype(jnp.bfloat16).astype(jnp.float32)
        middle = (x - high).astype(jnp.bfloat16).astype(jnp.float32)
        return high, middle, x - high - middle

    centred = points - 0.5
    norm = jnp.sum(centred * centred, axis=0, keepdims=True)
    terms = three_terms(centred)
    norms = three_terms(norm + softening if is_test else norm)
    for a in range(3):
        for b in range(3):
            place = 3 * (3 * a + b)
            rows_ref[place : place + 3, :] = -2.0 * terms[a] if is_test else terms[b]
    for a in range(3):
        rows_ref[27 + a : 28 + a, :] = norms[a] if is_test else jnp.ones_like(norm)
        rows_ref[30 + a : 31 + a, :] = jnp.ones_like(norm) if is_test else norms[a]


def left_kernel(
    nshard, first, me_ref, order_ref, test_ref, source_ref, basis_ref, out_ref,
    rows_ref, features_ref, turned_ref, near_ref,
):
    j = pl.program_id(0)
    ntest = test_ref.shape[1]
    nq = source_ref.shape[2]
    part = nq // nshard
    block = min(QBLOCK, nq)

    @pl.when(j == 0)
    def _():
        rows_ref[...] = jnp.zeros_like(rows_ref)
        for i in range(ntest):
            fill_features(rows_ref, test_ref[:, i, :], True)
            features_ref[i] = rows_ref[...].T.astype(jnp.bfloat16)
            turned_ref[i] = basis_ref[i].T

    source = order_ref[first + j]
    for comp in range(3):
        rows_ref[comp : comp + 1, :] = source_ref[comp, pl.ds(source, 1), :]
    pieces = []
    for offset in range(nshard):
        start = pl.multiple_of((me_ref[0] ^ offset) * part, part)
        pieces.append(rows_ref[0:3, pl.ds(start, part)])
    fill_features(rows_ref, jnp.concatenate(pieces, axis=1), False)
    near_ref[...] = rows_ref[...].astype(jnp.bfloat16)

    steps = [(i, start) for i in range(ntest) for start in range(0, nq, block)]

    def kernel_block(i, start):
        squared = jnp.dot(
            features_ref[i], near_ref[:, start : start + block], preferred_element_type=jnp.float32
        )
        return lax.rsqrt(squared.astype(jnp.bfloat16))

    ready = kernel_block(*steps[0])
    for place, (i, start) in enumerate(steps):
        now = ready
        if place + 1 < len(steps):
            ready = kernel_block(*steps[place + 1])
        out_ref[i, 0, :, start : start + block] = jnp.dot(
            turned_ref[i], now, preferred_element_type=jnp.float32
        ).astype(jnp.bfloat16)


def left_products(nshard, me, order, test_points, source_points, test_basis, first, last):
    _, ntest, npoint = test_points.shape
    nall, nq = source_points.shape[1:]
    kmax = test_basis.shape[2]
    nsource = last - first
    return pl.pallas_call(
        functools.partial(left_kernel, nshard, first),
        grid_spec=pltpu.PrefetchScalarGridSpec(
            num_scalar_prefetch=2,
            grid=(nsource,),
            in_specs=[
                pl.BlockSpec((3, ntest, npoint), lambda j, *_: (0, 0, 0)),
                pl.BlockSpec((3, nall, nq), lambda j, *_: (0, 0, 0)),
                pl.BlockSpec((ntest, npoint, kmax), lambda j, *_: (0, 0, 0)),
            ],
            out_specs=pl.BlockSpec((ntest, 1, kmax, nq), lambda j, *_: (0, j, 0, 0)),
            scratch_shapes=[
                pltpu.VMEM((NFEATURE, npoint), jnp.float32),
                pltpu.VMEM((ntest, npoint, NFEATURE), jnp.bfloat16),
                pltpu.VMEM((ntest, kmax, npoint), jnp.bfloat16),
                pltpu.VMEM((NFEATURE, nq), jnp.bfloat16),
            ],
        ),
        out_shape=jax.ShapeDtypeStruct((ntest, nsource, kmax, nq), jnp.bfloat16),
        compiler_params=pltpu.CompilerParams(vmem_limit_bytes=VMEM_LIMIT),
        cost_estimate=pl.CostEstimate(
            flops=2 * ntest * nsource * npoint * nq * kmax,
            bytes_accessed=2 * ntest * nsource * kmax * nq,
            transcendentals=ntest * nsource * npoint * nq,
        ),
    )(me, order, test_points, source_points, test_basis)


def tile_kernel(nshard, first, packed, *refs):
    order_ref, source_counts_ref, offsets_ref, test_counts_ref, left_ref = refs[:5]
    shard_refs = refs[5 : 5 + nshard]
    j = pl.program_id(0)
    if packed:
        tile_ref, main_ref, over_ref, pack_ref = refs[5 + nshard :]
    else:
        *far_refs, tile_ref, joined_ref = refs[5 + nshard :]

        @pl.when(j == 0)
        def _():
            nblock = source_counts_ref.shape[0]
            for place, far_ref in enumerate([source_counts_ref] + far_refs):
                for k in range(nblock):
                    joined_ref[place * nblock + k] = far_ref[k]

    ntest, _, kmax, _ = left_ref.shape
    ndest, _, _, rows, width = tile_ref.shape
    count = source_counts_ref[order_ref[first + j]]

    def work(wide):
        side = jnp.concatenate([shard_ref[0, :, :wide] for shard_ref in shard_refs], axis=0)
        row_ids = lax.broadcasted_iota(jnp.int32, (kmax, wide), 0)
        column_ids = lax.broadcasted_iota(jnp.int32, (kmax, wide), 1)
        products = [
            jnp.dot(left_ref[i, 0], side, preferred_element_type=jnp.float32) for i in range(ntest)
        ]
        if packed:
            offset = offsets_ref[order_ref[first + j]]
            shift = offset % LANES
            base = offset - shift
            low = lax.broadcasted_iota(jnp.int32, (kmax, LANES), 1) < shift
        for i in range(ntest):
            used = (row_ids < test_counts_ref[i]) & (column_ids < count)
            tile = jnp.where(used, products[i], 0.0)
            for dest in range(ndest):
                tile_ref[dest, i, 0, :, :wide] = tile[dest * rows : (dest + 1) * rows].astype(jnp.bfloat16)
                if wide < width:
                    tile_ref[dest, i, 0, :, wide:] = jnp.zeros((rows, width - wide), jnp.bfloat16)
            if not packed:
                continue
            rolled = [
                pltpu.roll(tile[:, start : start + LANES], shift, axis=1) for start in range(0, wide, LANES)
            ]
            for place in range(len(rolled) + 1):
                here = pl.ds(pl.multiple_of(base + place * LANES, LANES), LANES)
                if place == 0:
                    before = jnp.concatenate(
                        [pack_ref[dest, i, :, here].astype(jnp.float32) for dest in range(ndest)], axis=0
                    )
                else:
                    before = rolled[place - 1]
                after = rolled[place] if place < len(rolled) else jnp.zeros_like(before)
                window = jnp.where(low, before, after)
                for dest in range(ndest):
                    pack_ref[dest, i, :, here] = window[dest * rows : (dest + 1) * rows].astype(jnp.bfloat16)

    narrow = width - LANES
    if narrow > 0:
        pl.when(count <= narrow)(lambda: work(narrow))
        pl.when(count > narrow)(lambda: work(width))
    else:
        work(width)

    if packed:

        @pl.when(j == pl.num_programs(0) - 1)
        def _():
            main = main_ref.shape[3]
            main_ref[...] = pack_ref[:, :, :, :main]
            over_ref[...] = pack_ref[:, :, :, main : main + over_ref.shape[3]]


def tiles(ndest, first, tables, test_counts, left, shards, main, far=()):
    ntest, nsource, kmax, nq = left.shape
    nshard = len(shards)
    part, width = shards[0].shape[1:]
    rows = kmax // ndest
    packed = main is not None
    shapes = [jax.ShapeDtypeStruct((ndest, ntest, nsource, rows, width), jnp.bfloat16)]
    specs = [pl.BlockSpec((ndest, ntest, 1, rows, width), lambda j, *_: (0, 0, j, 0, 0))]
    scratch = []
    if packed:
        for columns in (main, nsource * width - main):
            shape = (ndest, ntest, rows, columns)
            shapes.append(jax.ShapeDtypeStruct(shape, jnp.bfloat16))
            specs.append(pl.BlockSpec(shape, lambda j, *_: (0, 0, 0, 0)))
        scratch.append(pltpu.VMEM((ndest, ntest, rows, nsource * width + LANES), jnp.bfloat16))
    else:
        shapes.append(jax.ShapeDtypeStruct(((1 + len(far)) * tables[1].shape[0],), jnp.int32))
        specs.append(pl.BlockSpec(memory_space=pltpu.SMEM))
    return pl.pallas_call(
        functools.partial(tile_kernel, nshard, first, packed),
        grid_spec=pltpu.PrefetchScalarGridSpec(
            num_scalar_prefetch=4,
            grid=(nsource,),
            in_specs=[pl.BlockSpec((ntest, 1, kmax, nq), lambda j, *_: (0, j, 0, 0))]
            + [pl.BlockSpec((1, part, width), lambda j, *_: (j, 0, 0))] * nshard
            + [pl.BlockSpec(memory_space=pltpu.SMEM)] * len(far),
            out_specs=specs,
            scratch_shapes=scratch,
        ),
        out_shape=shapes,
        compiler_params=pltpu.CompilerParams(vmem_limit_bytes=VMEM_LIMIT),
        cost_estimate=pl.CostEstimate(
            flops=2 * ntest * nsource * kmax * width * nq,
            bytes_accessed=2 * ntest * nsource * kmax * (nq + width),
            transcendentals=0,
        ),
    )(*tables, test_counts, left, *shards, *far)


def project_kernel(order_ref, tile_ref, coeff_ref, *refs):
    *start_refs, sum_ref, total_ref = refs
    j = pl.program_id(0)
    ndest, ntest, _, rows, _ = tile_ref.shape
    whole = [tile_ref[dest, i, 0] for i in range(ntest) for dest in range(ndest)]
    term = jnp.dot(jnp.concatenate(whole, axis=0), coeff_ref[0], preferred_element_type=jnp.float32)

    @pl.when(j == 0)
    def _():
        total_ref[...] = term + start_refs[0][...] if start_refs else term

    @pl.when(j > 0)
    def _():
        total_ref[...] += term

    @pl.when(j == pl.num_programs(0) - 1)
    def _():
        if not start_refs:
            sum_ref[...] = total_ref[...]
            return
        for i in range(ntest):
            for dest in range(ndest):
                top = (i * ndest + dest) * rows
                sum_ref[dest, i] = total_ref[top : top + rows, :].astype(sum_ref.dtype)


def project(order, first, tiles, coefficients, start):
    ndest, ntest, nsource, rows, width = tiles.shape
    ncol = coefficients.shape[2]
    total_spec = pl.BlockSpec((ntest * ndest * rows, ncol), lambda j, order: (0, 0))
    if start is None:
        started = []
        sum_spec = total_spec
        sum_shape = jax.ShapeDtypeStruct((ntest * ndest * rows, ncol), jnp.float32)
    else:
        started = [start]
        sum_spec = pl.BlockSpec((ndest, ntest, rows, ncol), lambda j, order: (0, 0, 0, 0))
        sum_shape = jax.ShapeDtypeStruct((ndest, ntest, rows, ncol), jnp.bfloat16)
    return pl.pallas_call(
        project_kernel,
        grid_spec=pltpu.PrefetchScalarGridSpec(
            num_scalar_prefetch=1,
            grid=(nsource,),
            in_specs=[
                pl.BlockSpec((ndest, ntest, 1, rows, width), lambda j, order: (0, 0, j, 0, 0)),
                pl.BlockSpec((1, width, ncol), lambda j, order: (order[first + j], 0, 0)),
            ]
            + [total_spec] * len(started),
            out_specs=sum_spec,
            scratch_shapes=[pltpu.VMEM((ntest * ndest * rows, ncol), jnp.float32)],
        ),
        out_shape=sum_shape,
        compiler_params=pltpu.CompilerParams(vmem_limit_bytes=VMEM_LIMIT),
        cost_estimate=pl.CostEstimate(
            flops=2 * ndest * ntest * rows * width * ncol * nsource,
            bytes_accessed=2 * ndest * ntest * rows * width * nsource,
            transcendentals=0,
        ),
    )(order, tiles, coefficients, *started)


def unpack_kernel(cut, order_ref, counts_ref, offsets_ref, whole_ref, packed_ref, out_ref, rows_ref):
    nsrc, _, _, rows, width = whole_ref.shape
    packed_width = packed_ref.shape[3]
    nall = out_ref.shape[2]
    nblock = nall // nsrc
    ntile = width // LANES
    step = 16 if rows % 16 == 0 else rows
    lanes = lax.broadcasted_iota(jnp.int32, (rows, LANES), 1)

    @pl.loop(0, nsrc)
    def _(source):
        for place in range(nblock):
            block = order_ref[source * nblock + place]
            target = source * nblock + block
            if place < cut:
                rows_ref[target] = whole_ref[source, 0, place].astype(jnp.float32)
                continue
            count = counts_ref[target]
            offset = offsets_ref[target]
            shift = offset % LANES
            base = offset - shift
            back = (LANES - shift) % LANES
            low = lanes < LANES - shift
            rolled = []
            for tile in range(ntile + 1):
                start = pl.multiple_of(jnp.minimum(base + tile * LANES, packed_width - LANES), LANES)
                piece = packed_ref[source, 0, :, pl.ds(start, LANES)].astype(jnp.float32)
                rolled.append(pltpu.roll(piece, back, axis=1))
            for tile in range(ntile):
                value = jnp.where(low, rolled[tile], rolled[tile + 1])
                value = jnp.where(lanes < count - tile * LANES, value, 0.0)
                rows_ref[target, :, tile * LANES : (tile + 1) * LANES] = value

    @pl.loop(0, nall // 16)
    def _(group):
        here = pl.ds(pl.multiple_of(group * 16, 16), 16)
        for top in range(0, rows, step):
            turned = jnp.transpose(rows_ref[here, top : top + step, :], (1, 0, 2))
            out_ref[0, top : top + step, here, :] = turned.astype(out_ref.dtype)


def unpack(cut, tables, whole, packed):
    nsrc, ntest, _, rows, width = whole.shape
    packed_width = packed.shape[3]
    nall = tables[0].shape[0]
    return pl.pallas_call(
        functools.partial(unpack_kernel, cut),
        grid_spec=pltpu.PrefetchScalarGridSpec(
            num_scalar_prefetch=3,
            grid=(ntest,),
            in_specs=[
                pl.BlockSpec((nsrc, 1, cut, rows, width), lambda i, *_: (0, i, 0, 0, 0)),
                pl.BlockSpec((nsrc, 1, rows, packed_width), lambda i, *_: (0, i, 0, 0)),
            ],
            out_specs=pl.BlockSpec((1, rows, nall, width), lambda i, *_: (i, 0, 0, 0)),
            scratch_shapes=[pltpu.VMEM((nall, rows, width), jnp.float32)],
        ),
        out_shape=jax.ShapeDtypeStruct((ntest, rows, nall, width), jnp.bfloat16),
        compiler_params=pltpu.CompilerParams(vmem_limit_bytes=SMALL_VMEM_LIMIT),
    )(*tables, whole, packed)


def body(
    test_points, test_basis, test_counts, source_points, source_basis, source_counts, coefficients
):
    nsource, part, kmax = source_basis.shape
    ntest = test_points.shape[0]
    nsrc = lax.axis_size("src")
    ntest_axis = lax.axis_size("test")
    me_test = lax.axis_index("test")
    cut = max(1, nsource * 3 // 8)

    held = {}

    def gather(name, shard, left):
        got = {0: shard}
        bits = list(bits_down(ntest_axis))
        for bit in bits:
            if bit == bits[-1]:
                names = [o for o in got if o != 0]
                tied = lax.optimization_barrier(tuple(got[o] for o in names) + (left,))
                got.update(zip(names, tied[:-1]))
                left = tied[-1]
            for offset in list(got):
                got[offset ^ bit] = exchange(got[offset], "test", bit)
            if bit == bits[0]:
                held[name] = got[bit]
        return [got[offset] for offset in sorted(got)], left

    most = (nsource - cut) * kmax
    main = min(most, -(-most * 18 // (25 * LANES)) * LANES)
    widths = [main, min(most, main + 2 * LANES), most]

    order, offsets, basis_a, basis_b = pick(cut, source_counts, source_basis)
    tables = (order, source_counts, offsets)
    inner = max(1, nsrc // 4)
    far = [exchange(source_counts, "src", flip) for flip in range(inner, nsrc, inner)]
    basis_a, *far = lax.optimization_barrier((basis_a, *far))
    me = jnp.reshape(me_test, (1,))
    test_points, source_points = test_points.transpose(1, 0, 2), source_points.transpose(1, 0, 2)

    left_a = left_products(ntest_axis, me, order, test_points, source_points, test_basis, 0, cut)
    shards_a, left_a = gather("a", basis_a, left_a)
    tiles_a, joined = tiles(nsrc, 0, tables, test_counts, left_a, shards_a, None, far)
    moved_a = lax.all_to_all(tiles_a, "src", split_axis=0, concat_axis=0, tiled=True)

    rest, _ = lax.optimization_barrier((basis_b, held["a"]))
    later, _ = lax.optimization_barrier((source_points, tiles_a))
    left_b = left_products(ntest_axis, me, order, test_points, later, test_basis, cut, nsource)
    shards_b, left_b = gather("b", rest, left_b)
    tiles_b, packed, beyond = tiles(nsrc, cut, tables, test_counts, left_b, shards_b, main)
    moved_b = lax.all_to_all(packed, "src", split_axis=0, concat_axis=0, tiled=True)

    joined, _ = lax.optimization_barrier((joined, packed))
    groups = [joined] + [exchange(joined, "src", flip) for flip in range(1, inner)]
    sums = project(order, 0, tiles_a, coefficients, None)
    sums = project(order, cut, tiles_b, coefficients, sums)
    projected = sum_rows(sums, "src")
    me_src, _ = lax.optimization_barrier((jnp.reshape(lax.axis_index("src"), (1,)), packed))
    all_counts, all_order, all_offsets, branch = all_tables(cut, nsource, widths, me_src, groups)
    spread = (all_order, all_counts, all_offsets)

    def finish(width, beyond, moved_a, moved_b, spread):
        if width > main:
            more = lax.all_to_all(
                beyond[..., : width - main], "src", split_axis=0, concat_axis=0, tiled=True
            )
            moved_b = jnp.concatenate([moved_b, more], axis=3)
        return unpack(cut, spread, moved_a, moved_b)

    reduced = lax.switch(
        branch[0],
        [functools.partial(finish, width) for width in widths],
        beyond,
        moved_a,
        moved_b,
        spread,
    )
    return (reduced, projected)


def solution(mesh):
    return jax.shard_map(
        body,
        mesh=mesh,
        in_specs=(
            P("test", None, None),
            P("test", None, None),
            P("test"),
            P("src", None, None),
            P("src", "test", None),
            P("src"),
            P("src", None, None),
        ),
        out_specs=(P("test", "src", None, None), P("test", "src", None)),
        check_vma=False,
    )
```

```python
import functools

import jax
import jax.numpy as jnp
from jax import lax
from jax.experimental import pallas as pl
from jax.experimental.pallas import tpu as pltpu
from jax.sharding import PartitionSpec as P

softening = 0.0025
QBLOCK = 256
LANES = 128
VMEM_LIMIT = 60 * 1024 * 1024
SMALL_VMEM_LIMIT = 32 * 1024 * 1024


def exchange(x, axis, flip):
    size = lax.axis_size(axis)
    return lax.ppermute(x, axis, [(a, a ^ flip) for a in range(size)])


def bits_down(size):
    bit = size // 2
    while bit >= 1:
        yield bit
        bit //= 2


def sum_rows(total, axis):
    size = lax.axis_size(axis)
    me = lax.axis_index(axis)
    held, bit = total, 1
    while held.shape[0] > 4:
        pairs = held.reshape((held.shape[0] // 2, 2) + held.shape[1:])
        mine = (me // bit) % 2
        keep = lax.dynamic_index_in_dim(pairs, mine, 1, keepdims=False)
        give = lax.dynamic_index_in_dim(pairs, 1 - mine, 1, keepdims=False)
        got = exchange(give, axis, bit)
        held = (keep.astype(jnp.float32) + got.astype(jnp.float32)).astype(held.dtype)
        bit *= 2
    mine = me // bit
    result = lax.dynamic_index_in_dim(held, mine, 0, keepdims=False).astype(jnp.float32)
    for flip in range(1, held.shape[0]):
        give = lax.dynamic_index_in_dim(held, mine ^ flip, 0, keepdims=False)
        result = result + exchange(give, axis, flip * bit).astype(jnp.float32)
    return result.astype(total.dtype)


def rank_blocks(counts, cut):
    ranks = []
    for j, mine in enumerate(counts):
        rank = jnp.int32(0)
        for k, other in enumerate(counts):
            if k != j:
                ahead = other >= mine if k < j else other > mine
                rank += ahead.astype(jnp.int32)
        ranks.append(rank)
    offsets = []
    for j in range(len(counts)):
        offset = jnp.int32(0)
        for k, other in enumerate(counts):
            if k != j:
                offset += jnp.where((ranks[k] >= cut) & (ranks[k] < ranks[j]), other, 0)
        offsets.append(offset)
    return ranks, offsets


def pick_kernel(cut, counts_ref, basis_ref, order_ref, offsets_ref, first_ref, rest_ref):
    nblock = basis_ref.shape[0]
    ranks, offsets = rank_blocks([counts_ref[j] for j in range(nblock)], cut)
    for j in range(nblock):
        order_ref[ranks[j]] = jnp.int32(j)
        offsets_ref[j] = offsets[j]
    for place in range(nblock):
        block = basis_ref[order_ref[place]]
        if place < cut:
            first_ref[place] = block
        else:
            rest_ref[place - cut] = block


def pick(cut, counts, basis):
    nblock = basis.shape[0]
    smem, vmem = pl.BlockSpec(memory_space=pltpu.SMEM), pl.BlockSpec(memory_space=pltpu.VMEM)
    return pl.pallas_call(
        functools.partial(pick_kernel, cut),
        out_shape=(
            jax.ShapeDtypeStruct((nblock,), jnp.int32),
            jax.ShapeDtypeStruct((nblock,), jnp.int32),
            jax.ShapeDtypeStruct((cut,) + basis.shape[1:], basis.dtype),
            jax.ShapeDtypeStruct((nblock - cut,) + basis.shape[1:], basis.dtype),
        ),
        in_specs=[smem, vmem],
        out_specs=(smem, smem, vmem, vmem),
        compiler_params=pltpu.CompilerParams(vmem_limit_bytes=VMEM_LIMIT),
    )(counts, basis)


def tables_kernel(cut, nblock, widths, me_ref, *refs):
    *group_refs, counts_ref, order_ref, offsets_ref, branch_ref, joined_ref = refs
    group, inner = group_refs[0].shape[0], len(group_refs)
    for place, group_ref in enumerate(group_refs):
        for k in range(group):
            joined_ref[place * group + k] = group_ref[k]

    def step(source, need):
        base = source * nblock
        offset = source ^ me_ref[0]
        theirs = (offset % inner) * group + (offset // inner) * nblock
        counts = [joined_ref[theirs + j] for j in range(nblock)]
        ranks, offsets = rank_blocks(counts, cut)
        used = jnp.int32(0)
        for j in range(nblock):
            counts_ref[base + j] = counts[j]
            order_ref[base + ranks[j]] = jnp.int32(j)
            offsets_ref[base + j] = offsets[j]
            used += jnp.where(ranks[j] >= cut, counts[j], 0)
        return jnp.maximum(need, used)

    need = lax.fori_loop(0, counts_ref.shape[0] // nblock, step, jnp.int32(0))
    branch = jnp.int32(0)
    for width in widths[:-1]:
        branch += (need > width).astype(jnp.int32)
    branch_ref[0] = branch


def all_tables(cut, nblock, widths, me, groups):
    smem = pl.BlockSpec(memory_space=pltpu.SMEM)
    total = sum(group.shape[0] for group in groups)
    table = jax.ShapeDtypeStruct((total,), jnp.int32)
    return pl.pallas_call(
        functools.partial(tables_kernel, cut, nblock, widths),
        out_shape=(table, table, table, jax.ShapeDtypeStruct((1,), jnp.int32)),
        in_specs=[smem] * (1 + len(groups)),
        out_specs=(smem,) * 4,
        scratch_shapes=[pltpu.SMEM((total,), jnp.int32)],
    )(me, *groups)


NFEATURE = 128


def fill_features(rows_ref, points, is_test):
    def three_terms(x):
        high = x.astype(jnp.bfloat16).astype(jnp.float32)
        middle = (x - high).astype(jnp.bfloat16).astype(jnp.float32)
        return high, middle, x - high - middle

    centred = points - 0.5
    norm = jnp.sum(centred * centred, axis=0, keepdims=True)
    terms = three_terms(centred)
    norms = three_terms(norm + softening if is_test else norm)
    for a in range(3):
        for b in range(3):
            place = 3 * (3 * a + b)
            rows_ref[place : place + 3, :] = -2.0 * terms[a] if is_test else terms[b]
    for a in range(3):
        rows_ref[27 + a : 28 + a, :] = norms[a] if is_test else jnp.ones_like(norm)
        rows_ref[30 + a : 31 + a, :] = jnp.ones_like(norm) if is_test else norms[a]


def left_kernel(
    nshard, first, me_ref, order_ref, test_ref, source_ref, basis_ref, out_ref,
    rows_ref, features_ref, turned_ref, near_ref,
):
    j = pl.program_id(0)
    ntest = test_ref.shape[1]
    nq = source_ref.shape[2]
    part = nq // nshard
    block = min(QBLOCK, nq)

    @pl.when(j == 0)
    def _():
        rows_ref[...] = jnp.zeros_like(rows_ref)
        for i in range(ntest):
            fill_features(rows_ref, test_ref[:, i, :], True)
            features_ref[i] = rows_ref[...].T.astype(jnp.bfloat16)
            turned_ref[i] = basis_ref[i].T

    source = order_ref[first + j]
    for comp in range(3):
        rows_ref[comp : comp + 1, :] = source_ref[comp, pl.ds(source, 1), :]
    pieces = []
    for offset in range(nshard):
        start = pl.multiple_of((me_ref[0] ^ offset) * part, part)
        pieces.append(rows_ref[0:3, pl.ds(start, part)])
    fill_features(rows_ref, jnp.concatenate(pieces, axis=1), False)
    near_ref[...] = rows_ref[...].astype(jnp.bfloat16)

    steps = [(i, start) for i in range(ntest) for start in range(0, nq, block)]

    def kernel_block(i, start):
        squared = jnp.dot(
            features_ref[i], near_ref[:, start : start + block], preferred_element_type=jnp.float32
        )
        return lax.rsqrt(squared.astype(jnp.bfloat16))

    ready = kernel_block(*steps[0])
    for place, (i, start) in enumerate(steps):
        now = ready
        if place + 1 < len(steps):
            ready = kernel_block(*steps[place + 1])
        out_ref[i, 0, :, start : start + block] = jnp.dot(
            turned_ref[i], now, preferred_element_type=jnp.float32
        ).astype(jnp.bfloat16)


def left_products(nshard, me, order, test_points, source_points, test_basis, first, last):
    _, ntest, npoint = test_points.shape
    nall, nq = source_points.shape[1:]
    kmax = test_basis.shape[2]
    nsource = last - first
    return pl.pallas_call(
        functools.partial(left_kernel, nshard, first),
        grid_spec=pltpu.PrefetchScalarGridSpec(
            num_scalar_prefetch=2,
            grid=(nsource,),
            in_specs=[
                pl.BlockSpec((3, ntest, npoint), lambda j, *_: (0, 0, 0)),
                pl.BlockSpec((3, nall, nq), lambda j, *_: (0, 0, 0)),
                pl.BlockSpec((ntest, npoint, kmax), lambda j, *_: (0, 0, 0)),
            ],
            out_specs=pl.BlockSpec((ntest, 1, kmax, nq), lambda j, *_: (0, j, 0, 0)),
            scratch_shapes=[
                pltpu.VMEM((NFEATURE, npoint), jnp.float32),
                pltpu.VMEM((ntest, npoint, NFEATURE), jnp.bfloat16),
                pltpu.VMEM((ntest, kmax, npoint), jnp.bfloat16),
                pltpu.VMEM((NFEATURE, nq), jnp.bfloat16),
            ],
        ),
        out_shape=jax.ShapeDtypeStruct((ntest, nsource, kmax, nq), jnp.bfloat16),
        compiler_params=pltpu.CompilerParams(vmem_limit_bytes=VMEM_LIMIT),
        cost_estimate=pl.CostEstimate(
            flops=2 * ntest * nsource * npoint * nq * kmax,
            bytes_accessed=2 * ntest * nsource * kmax * nq,
            transcendentals=ntest * nsource * npoint * nq,
        ),
    )(me, order, test_points, source_points, test_basis)


def tile_kernel(nshard, first, packed, *refs):
    order_ref, source_counts_ref, offsets_ref, test_counts_ref, left_ref = refs[:5]
    shard_refs = refs[5 : 5 + nshard]
    j = pl.program_id(0)
    if not packed:
        (tile_ref,) = refs[5 + nshard :]
    else:
        *far_refs, tile_ref, main_ref, over_ref, joined_ref, pack_ref = refs[5 + nshard :]

        @pl.when(j == 0)
        def _():
            nblock = source_counts_ref.shape[0]
            for place, far_ref in enumerate([source_counts_ref] + far_refs):
                for k in range(nblock):
                    joined_ref[place * nblock + k] = far_ref[k]

    ntest, _, kmax, _ = left_ref.shape
    ndest, _, _, rows, width = tile_ref.shape
    count = source_counts_ref[order_ref[first + j]]

    def work(wide):
        side = jnp.concatenate([shard_ref[0, :, :wide] for shard_ref in shard_refs], axis=0)
        row_ids = lax.broadcasted_iota(jnp.int32, (kmax, wide), 0)
        column_ids = lax.broadcasted_iota(jnp.int32, (kmax, wide), 1)
        products = [
            jnp.dot(left_ref[i, 0], side, preferred_element_type=jnp.float32) for i in range(ntest)
        ]
        if packed:
            offset = offsets_ref[order_ref[first + j]]
            shift = offset % LANES
            base = offset - shift
            low = lax.broadcasted_iota(jnp.int32, (kmax, LANES), 1) < shift
        for i in range(ntest):
            used = (row_ids < test_counts_ref[i]) & (column_ids < count)
            tile = jnp.where(used, products[i], 0.0)
            for dest in range(ndest):
                tile_ref[dest, i, 0, :, :wide] = tile[dest * rows : (dest + 1) * rows].astype(jnp.bfloat16)
                if wide < width:
                    tile_ref[dest, i, 0, :, wide:] = jnp.zeros((rows, width - wide), jnp.bfloat16)
            if not packed:
                continue
            rolled = [
                pltpu.roll(tile[:, start : start + LANES], shift, axis=1) for start in range(0, wide, LANES)
            ]
            for place in range(len(rolled) + 1):
                here = pl.ds(pl.multiple_of(base + place * LANES, LANES), LANES)
                if place == 0:
                    before = jnp.concatenate(
                        [pack_ref[dest, i, :, here].astype(jnp.float32) for dest in range(ndest)], axis=0
                    )
                else:
                    before = rolled[place - 1]
                after = rolled[place] if place < len(rolled) else jnp.zeros_like(before)
                window = jnp.where(low, before, after)
                for dest in range(ndest):
                    pack_ref[dest, i, :, here] = window[dest * rows : (dest + 1) * rows].astype(jnp.bfloat16)

    narrow = width - LANES
    if narrow > 0:
        pl.when(count <= narrow)(lambda: work(narrow))
        pl.when(count > narrow)(lambda: work(width))
    else:
        work(width)

    if packed:

        @pl.when(j == pl.num_programs(0) - 1)
        def _():
            main = main_ref.shape[3]
            main_ref[...] = pack_ref[:, :, :, :main]
            over_ref[...] = pack_ref[:, :, :, main : main + over_ref.shape[3]]


def tiles(ndest, first, tables, test_counts, left, shards, main, far=()):
    ntest, nsource, kmax, nq = left.shape
    nshard = len(shards)
    part, width = shards[0].shape[1:]
    rows = kmax // ndest
    packed = main is not None
    shapes = [jax.ShapeDtypeStruct((ndest, ntest, nsource, rows, width), jnp.bfloat16)]
    specs = [pl.BlockSpec((ndest, ntest, 1, rows, width), lambda j, *_: (0, 0, j, 0, 0))]
    scratch = []
    if packed:
        for columns in (main, nsource * width - main):
            shape = (ndest, ntest, rows, columns)
            shapes.append(jax.ShapeDtypeStruct(shape, jnp.bfloat16))
            specs.append(pl.BlockSpec(shape, lambda j, *_: (0, 0, 0, 0)))
        scratch.append(pltpu.VMEM((ndest, ntest, rows, nsource * width + LANES), jnp.bfloat16))
        shapes.append(jax.ShapeDtypeStruct(((1 + len(far)) * tables[1].shape[0],), jnp.int32))
        specs.append(pl.BlockSpec(memory_space=pltpu.SMEM))
    return pl.pallas_call(
        functools.partial(tile_kernel, nshard, first, packed),
        grid_spec=pltpu.PrefetchScalarGridSpec(
            num_scalar_prefetch=4,
            grid=(nsource,),
            in_specs=[pl.BlockSpec((ntest, 1, kmax, nq), lambda j, *_: (0, j, 0, 0))]
            + [pl.BlockSpec((1, part, width), lambda j, *_: (j, 0, 0))] * nshard
            + [pl.BlockSpec(memory_space=pltpu.SMEM)] * len(far),
            out_specs=specs,
            scratch_shapes=scratch,
        ),
        out_shape=shapes,
        compiler_params=pltpu.CompilerParams(vmem_limit_bytes=VMEM_LIMIT),
        cost_estimate=pl.CostEstimate(
            flops=2 * ntest * nsource * kmax * width * nq,
            bytes_accessed=2 * ntest * nsource * kmax * (nq + width),
            transcendentals=0,
        ),
    )(*tables, test_counts, left, *shards, *far)


def project_kernel(order_ref, tile_ref, coeff_ref, *refs):
    *start_refs, sum_ref, total_ref = refs
    j = pl.program_id(0)
    ndest, ntest, _, rows, _ = tile_ref.shape
    whole = [tile_ref[dest, i, 0] for i in range(ntest) for dest in range(ndest)]
    term = jnp.dot(jnp.concatenate(whole, axis=0), coeff_ref[0], preferred_element_type=jnp.float32)

    @pl.when(j == 0)
    def _():
        total_ref[...] = term + start_refs[0][...] if start_refs else term

    @pl.when(j > 0)
    def _():
        total_ref[...] += term

    @pl.when(j == pl.num_programs(0) - 1)
    def _():
        if not start_refs:
            sum_ref[...] = total_ref[...]
            return
        for i in range(ntest):
            for dest in range(ndest):
                top = (i * ndest + dest) * rows
                sum_ref[dest, i] = total_ref[top : top + rows, :].astype(sum_ref.dtype)


def project(order, first, tiles, coefficients, start):
    ndest, ntest, nsource, rows, width = tiles.shape
    ncol = coefficients.shape[2]
    total_spec = pl.BlockSpec((ntest * ndest * rows, ncol), lambda j, order: (0, 0))
    if start is None:
        started = []
        sum_spec = total_spec
        sum_shape = jax.ShapeDtypeStruct((ntest * ndest * rows, ncol), jnp.float32)
    else:
        started = [start]
        sum_spec = pl.BlockSpec((ndest, ntest, rows, ncol), lambda j, order: (0, 0, 0, 0))
        sum_shape = jax.ShapeDtypeStruct((ndest, ntest, rows, ncol), jnp.bfloat16)
    return pl.pallas_call(
        project_kernel,
        grid_spec=pltpu.PrefetchScalarGridSpec(
            num_scalar_prefetch=1,
            grid=(nsource,),
            in_specs=[
                pl.BlockSpec((ndest, ntest, 1, rows, width), lambda j, order: (0, 0, j, 0, 0)),
                pl.BlockSpec((1, width, ncol), lambda j, order: (order[first + j], 0, 0)),
            ]
            + [total_spec] * len(started),
            out_specs=sum_spec,
            scratch_shapes=[pltpu.VMEM((ntest * ndest * rows, ncol), jnp.float32)],
        ),
        out_shape=sum_shape,
        compiler_params=pltpu.CompilerParams(vmem_limit_bytes=VMEM_LIMIT),
        cost_estimate=pl.CostEstimate(
            flops=2 * ndest * ntest * rows * width * ncol * nsource,
            bytes_accessed=2 * ndest * ntest * rows * width * nsource,
            transcendentals=0,
        ),
    )(order, tiles, coefficients, *started)


def unpack_kernel(cut, order_ref, counts_ref, offsets_ref, whole_ref, packed_ref, out_ref, rows_ref):
    nsrc, _, _, rows, width = whole_ref.shape
    packed_width = packed_ref.shape[3]
    nall = out_ref.shape[2]
    nblock = nall // nsrc
    ntile = width // LANES
    step = 16 if rows % 16 == 0 else rows
    lanes = lax.broadcasted_iota(jnp.int32, (rows, LANES), 1)

    @pl.loop(0, nsrc)
    def _(source):
        for place in range(nblock):
            block = order_ref[source * nblock + place]
            target = source * nblock + block
            if place < cut:
                rows_ref[target] = whole_ref[source, 0, place].astype(jnp.float32)
                continue
            count = counts_ref[target]
            offset = offsets_ref[target]
            shift = offset % LANES
            base = offset - shift
            back = (LANES - shift) % LANES
            low = lanes < LANES - shift
            rolled = []
            for tile in range(ntile + 1):
                start = pl.multiple_of(jnp.minimum(base + tile * LANES, packed_width - LANES), LANES)
                piece = packed_ref[source, 0, :, pl.ds(start, LANES)].astype(jnp.float32)
                rolled.append(pltpu.roll(piece, back, axis=1))
            for tile in range(ntile):
                value = jnp.where(low, rolled[tile], rolled[tile + 1])
                value = jnp.where(lanes < count - tile * LANES, value, 0.0)
                rows_ref[target, :, tile * LANES : (tile + 1) * LANES] = value

    @pl.loop(0, nall // 16)
    def _(group):
        here = pl.ds(pl.multiple_of(group * 16, 16), 16)
        for top in range(0, rows, step):
            turned = jnp.transpose(rows_ref[here, top : top + step, :], (1, 0, 2))
            out_ref[0, top : top + step, here, :] = turned.astype(out_ref.dtype)


def unpack(cut, tables, whole, packed):
    nsrc, ntest, _, rows, width = whole.shape
    packed_width = packed.shape[3]
    nall = tables[0].shape[0]
    return pl.pallas_call(
        functools.partial(unpack_kernel, cut),
        grid_spec=pltpu.PrefetchScalarGridSpec(
            num_scalar_prefetch=3,
            grid=(ntest,),
            in_specs=[
                pl.BlockSpec((nsrc, 1, cut, rows, width), lambda i, *_: (0, i, 0, 0, 0)),
                pl.BlockSpec((nsrc, 1, rows, packed_width), lambda i, *_: (0, i, 0, 0)),
            ],
            out_specs=pl.BlockSpec((1, rows, nall, width), lambda i, *_: (i, 0, 0, 0)),
            scratch_shapes=[pltpu.VMEM((nall, rows, width), jnp.float32)],
        ),
        out_shape=jax.ShapeDtypeStruct((ntest, rows, nall, width), jnp.bfloat16),
        compiler_params=pltpu.CompilerParams(vmem_limit_bytes=SMALL_VMEM_LIMIT),
    )(*tables, whole, packed)


def body(
    test_points, test_basis, test_counts, source_points, source_basis, source_counts, coefficients
):
    nsource, part, kmax = source_basis.shape
    ntest = test_points.shape[0]
    nsrc = lax.axis_size("src")
    ntest_axis = lax.axis_size("test")
    me_test = lax.axis_index("test")
    cut = max(1, nsource * 3 // 8)

    held = {}

    def gather(name, shard, left):
        got = {0: shard}
        bits = list(bits_down(ntest_axis))
        for bit in bits:
            if bit == bits[-1]:
                names = [o for o in got if o != 0]
                tied = lax.optimization_barrier(tuple(got[o] for o in names) + (left,))
                got.update(zip(names, tied[:-1]))
                left = tied[-1]
            for offset in list(got):
                got[offset ^ bit] = exchange(got[offset], "test", bit)
            if bit == bits[0]:
                held[name] = got[bit]
        return [got[offset] for offset in sorted(got)], left

    most = (nsource - cut) * kmax
    main = min(most, -(-most * 18 // (25 * LANES)) * LANES)
    widths = [main, min(most, main + 2 * LANES), most]

    order, offsets, basis_a, basis_b = pick(cut, source_counts, source_basis)
    tables = (order, source_counts, offsets)
    me = jnp.reshape(me_test, (1,))
    test_points, source_points = test_points.transpose(1, 0, 2), source_points.transpose(1, 0, 2)

    left_a = left_products(ntest_axis, me, order, test_points, source_points, test_basis, 0, cut)
    shards_a, left_a = gather("a", basis_a, left_a)
    (tiles_a,) = tiles(nsrc, 0, tables, test_counts, left_a, shards_a, None)
    moved_a = lax.all_to_all(tiles_a, "src", split_axis=0, concat_axis=0, tiled=True)

    rest, _ = lax.optimization_barrier((basis_b, held["a"]))
    later, _ = lax.optimization_barrier((source_points, tiles_a))
    left_b = left_products(ntest_axis, me, order, test_points, later, test_basis, cut, nsource)
    shards_b, left_b = gather("b", rest, left_b)
    inner = max(1, nsrc // 4)
    counts, _ = lax.optimization_barrier((source_counts, left_b))
    far = [exchange(counts, "src", flip) for flip in range(inner, nsrc, inner)]
    tiles_b, packed, beyond, joined = tiles(
        nsrc, cut, tables, test_counts, left_b, shards_b, main, far
    )
    moved_b = lax.all_to_all(packed, "src", split_axis=0, concat_axis=0, tiled=True)

    joined, _ = lax.optimization_barrier((joined, packed))
    groups = [joined] + [exchange(joined, "src", flip) for flip in range(1, inner)]
    sums = project(order, 0, tiles_a, coefficients, None)
    sums = project(order, cut, tiles_b, coefficients, sums)
    projected = sum_rows(sums, "src")
    me_src, _ = lax.optimization_barrier((jnp.reshape(lax.axis_index("src"), (1,)), packed))
    all_counts, all_order, all_offsets, branch = all_tables(cut, nsource, widths, me_src, groups)
    spread = (all_order, all_counts, all_offsets)

    def finish(width, beyond, moved_a, moved_b, spread):
        if width > main:
            more = lax.all_to_all(
                beyond[..., : width - main], "src", split_axis=0, concat_axis=0, tiled=True
            )
            moved_b = jnp.concatenate([moved_b, more], axis=3)
        return unpack(cut, spread, moved_a, moved_b)

    reduced = lax.switch(
        branch[0],
        [functools.partial(finish, width) for width in widths],
        beyond,
        moved_a,
        moved_b,
        spread,
    )
    return (reduced, projected)


def solution(mesh):
    return jax.shard_map(
        body,
        mesh=mesh,
        in_specs=(
            P("test", None, None),
            P("test", None, None),
            P("test"),
            P("src", None, None),
            P("src", "test", None),
            P("src"),
            P("src", None, None),
        ),
        out_specs=(P("test", "src", None, None), P("test", "src", None)),
        check_vma=False,
    )
```

```python
import functools

import jax
import jax.numpy as jnp
from jax import lax
from jax.experimental import pallas as pl
from jax.experimental.pallas import tpu as pltpu
from jax.sharding import PartitionSpec as P

softening = 0.0025
QBLOCK = 256
LANES = 128
VMEM_LIMIT = 60 * 1024 * 1024
SMALL_VMEM_LIMIT = 32 * 1024 * 1024


def exchange(x, axis, flip):
    size = lax.axis_size(axis)
    return lax.ppermute(x, axis, [(a, a ^ flip) for a in range(size)])


def bits_down(size):
    bit = size // 2
    while bit >= 1:
        yield bit
        bit //= 2


def sum_rows(total, axis):
    size = lax.axis_size(axis)
    me = lax.axis_index(axis)
    held, bit = total, 1
    while held.shape[0] > 4:
        pairs = held.reshape((held.shape[0] // 2, 2) + held.shape[1:])
        mine = (me // bit) % 2
        keep = lax.dynamic_index_in_dim(pairs, mine, 1, keepdims=False)
        give = lax.dynamic_index_in_dim(pairs, 1 - mine, 1, keepdims=False)
        got = exchange(give, axis, bit)
        held = (keep.astype(jnp.float32) + got.astype(jnp.float32)).astype(held.dtype)
        bit *= 2
    mine = me // bit
    result = lax.dynamic_index_in_dim(held, mine, 0, keepdims=False).astype(jnp.float32)
    for flip in range(1, held.shape[0]):
        give = lax.dynamic_index_in_dim(held, mine ^ flip, 0, keepdims=False)
        result = result + exchange(give, axis, flip * bit).astype(jnp.float32)
    return result.astype(total.dtype)


def rank_blocks(counts, cut):
    ranks = []
    for j, mine in enumerate(counts):
        rank = jnp.int32(0)
        for k, other in enumerate(counts):
            if k != j:
                ahead = other >= mine if k < j else other > mine
                rank += ahead.astype(jnp.int32)
        ranks.append(rank)
    offsets = []
    for j in range(len(counts)):
        offset = jnp.int32(0)
        for k, other in enumerate(counts):
            if k != j:
                offset += jnp.where((ranks[k] >= cut) & (ranks[k] < ranks[j]), other, 0)
        offsets.append(offset)
    return ranks, offsets


def pick_kernel(cut, counts_ref, basis_ref, order_ref, offsets_ref, first_ref, rest_ref):
    nblock = basis_ref.shape[0]
    ranks, offsets = rank_blocks([counts_ref[j] for j in range(nblock)], cut)
    for j in range(nblock):
        order_ref[ranks[j]] = jnp.int32(j)
        offsets_ref[j] = offsets[j]
    for place in range(nblock):
        block = basis_ref[order_ref[place]]
        if place < cut:
            first_ref[place] = block
        else:
            rest_ref[place - cut] = block


def pick(cut, counts, basis):
    nblock = basis.shape[0]
    smem, vmem = pl.BlockSpec(memory_space=pltpu.SMEM), pl.BlockSpec(memory_space=pltpu.VMEM)
    return pl.pallas_call(
        functools.partial(pick_kernel, cut),
        out_shape=(
            jax.ShapeDtypeStruct((nblock,), jnp.int32),
            jax.ShapeDtypeStruct((nblock,), jnp.int32),
            jax.ShapeDtypeStruct((cut,) + basis.shape[1:], basis.dtype),
            jax.ShapeDtypeStruct((nblock - cut,) + basis.shape[1:], basis.dtype),
        ),
        in_specs=[smem, vmem],
        out_specs=(smem, smem, vmem, vmem),
        compiler_params=pltpu.CompilerParams(vmem_limit_bytes=VMEM_LIMIT),
    )(counts, basis)


def tables_kernel(cut, nblock, widths, me_ref, *refs):
    *group_refs, counts_ref, order_ref, offsets_ref, branch_ref, joined_ref = refs
    group, inner = group_refs[0].shape[0], len(group_refs)
    for place, group_ref in enumerate(group_refs):
        for k in range(group):
            joined_ref[place * group + k] = group_ref[k]

    def step(source, need):
        base = source * nblock
        offset = source ^ me_ref[0]
        theirs = (offset % inner) * group + (offset // inner) * nblock
        counts = [joined_ref[theirs + j] for j in range(nblock)]
        ranks, offsets = rank_blocks(counts, cut)
        used = jnp.int32(0)
        for j in range(nblock):
            counts_ref[base + j] = counts[j]
            order_ref[base + ranks[j]] = jnp.int32(j)
            offsets_ref[base + j] = offsets[j]
            used += jnp.where(ranks[j] >= cut, counts[j], 0)
        return jnp.maximum(need, used)

    need = lax.fori_loop(0, counts_ref.shape[0] // nblock, step, jnp.int32(0))
    branch = jnp.int32(0)
    for width in widths[:-1]:
        branch += (need > width).astype(jnp.int32)
    branch_ref[0] = branch


def all_tables(cut, nblock, widths, me, groups):
    smem = pl.BlockSpec(memory_space=pltpu.SMEM)
    total = sum(group.shape[0] for group in groups)
    table = jax.ShapeDtypeStruct((total,), jnp.int32)
    return pl.pallas_call(
        functools.partial(tables_kernel, cut, nblock, widths),
        out_shape=(table, table, table, jax.ShapeDtypeStruct((1,), jnp.int32)),
        in_specs=[smem] * (1 + len(groups)),
        out_specs=(smem,) * 4,
        scratch_shapes=[pltpu.SMEM((total,), jnp.int32)],
    )(me, *groups)


NFEATURE = 128


def fill_features(rows_ref, points, is_test):
    def three_terms(x):
        high = x.astype(jnp.bfloat16).astype(jnp.float32)
        middle = (x - high).astype(jnp.bfloat16).astype(jnp.float32)
        return high, middle, x - high - middle

    centred = points - 0.5
    norm = jnp.sum(centred * centred, axis=0, keepdims=True)
    terms = three_terms(centred)
    norms = three_terms(norm + softening if is_test else norm)
    for a in range(3):
        for b in range(3):
            place = 3 * (3 * a + b)
            rows_ref[place : place + 3, :] = -2.0 * terms[a] if is_test else terms[b]
    for a in range(3):
        rows_ref[27 + a : 28 + a, :] = norms[a] if is_test else jnp.ones_like(norm)
        rows_ref[30 + a : 31 + a, :] = jnp.ones_like(norm) if is_test else norms[a]


def left_kernel(
    nshard, first, me_ref, order_ref, test_ref, source_ref, basis_ref, out_ref,
    rows_ref, features_ref, turned_ref, near_ref,
):
    j = pl.program_id(0)
    ntest = test_ref.shape[1]
    nq = source_ref.shape[2]
    part = nq // nshard
    block = min(QBLOCK, nq)

    @pl.when(j == 0)
    def _():
        rows_ref[...] = jnp.zeros_like(rows_ref)
        for i in range(ntest):
            fill_features(rows_ref, test_ref[:, i, :], True)
            features_ref[i] = rows_ref[...].T.astype(jnp.bfloat16)
            turned_ref[i] = basis_ref[i].T

    source = order_ref[first + j]
    for comp in range(3):
        rows_ref[comp : comp + 1, :] = source_ref[comp, pl.ds(source, 1), :]
    pieces = []
    for offset in range(nshard):
        start = pl.multiple_of((me_ref[0] ^ offset) * part, part)
        pieces.append(rows_ref[0:3, pl.ds(start, part)])
    fill_features(rows_ref, jnp.concatenate(pieces, axis=1), False)
    near_ref[...] = rows_ref[...].astype(jnp.bfloat16)

    steps = [(i, start) for i in range(ntest) for start in range(0, nq, block)]

    def kernel_block(i, start):
        squared = jnp.dot(
            features_ref[i], near_ref[:, start : start + block], preferred_element_type=jnp.float32
        )
        return lax.rsqrt(squared.astype(jnp.bfloat16))

    ready = kernel_block(*steps[0])
    for place, (i, start) in enumerate(steps):
        now = ready
        if place + 1 < len(steps):
            ready = kernel_block(*steps[place + 1])
        out_ref[i, 0, :, start : start + block] = jnp.dot(
            turned_ref[i], now, preferred_element_type=jnp.float32
        ).astype(jnp.bfloat16)


def left_products(nshard, me, order, test_points, source_points, test_basis, first, last):
    _, ntest, npoint = test_points.shape
    nall, nq = source_points.shape[1:]
    kmax = test_basis.shape[2]
    nsource = last - first
    return pl.pallas_call(
        functools.partial(left_kernel, nshard, first),
        grid_spec=pltpu.PrefetchScalarGridSpec(
            num_scalar_prefetch=2,
            grid=(nsource,),
            in_specs=[
                pl.BlockSpec((3, ntest, npoint), lambda j, *_: (0, 0, 0)),
                pl.BlockSpec((3, nall, nq), lambda j, *_: (0, 0, 0)),
                pl.BlockSpec((ntest, npoint, kmax), lambda j, *_: (0, 0, 0)),
            ],
            out_specs=pl.BlockSpec((ntest, 1, kmax, nq), lambda j, *_: (0, j, 0, 0)),
            scratch_shapes=[
                pltpu.VMEM((NFEATURE, npoint), jnp.float32),
                pltpu.VMEM((ntest, npoint, NFEATURE), jnp.bfloat16),
                pltpu.VMEM((ntest, kmax, npoint), jnp.bfloat16),
                pltpu.VMEM((NFEATURE, nq), jnp.bfloat16),
            ],
        ),
        out_shape=jax.ShapeDtypeStruct((ntest, nsource, kmax, nq), jnp.bfloat16),
        compiler_params=pltpu.CompilerParams(vmem_limit_bytes=VMEM_LIMIT),
        cost_estimate=pl.CostEstimate(
            flops=2 * ntest * nsource * npoint * nq * kmax,
            bytes_accessed=2 * ntest * nsource * kmax * nq,
            transcendentals=ntest * nsource * npoint * nq,
        ),
    )(me, order, test_points, source_points, test_basis)


def tile_kernel(nshard, first, packed, *refs):
    order_ref, source_counts_ref, offsets_ref, test_counts_ref, left_ref = refs[:5]
    shard_refs = refs[5 : 5 + nshard]
    j = pl.program_id(0)
    if packed:
        tile_ref, main_ref, over_ref, pack_ref = refs[5 + nshard :]
    else:
        (tile_ref,) = refs[5 + nshard :]
    ntest, _, kmax, _ = left_ref.shape
    ndest, _, _, rows, width = tile_ref.shape
    count = source_counts_ref[order_ref[first + j]]

    def work(wide):
        side = jnp.concatenate([shard_ref[0, :, :wide] for shard_ref in shard_refs], axis=0)
        row_ids = lax.broadcasted_iota(jnp.int32, (kmax, wide), 0)
        column_ids = lax.broadcasted_iota(jnp.int32, (kmax, wide), 1)
        products = [
            jnp.dot(left_ref[i, 0], side, preferred_element_type=jnp.float32) for i in range(ntest)
        ]
        if packed:
            offset = offsets_ref[order_ref[first + j]]
            shift = offset % LANES
            base = offset - shift
            low = lax.broadcasted_iota(jnp.int32, (kmax, LANES), 1) < shift
        for i in range(ntest):
            used = (row_ids < test_counts_ref[i]) & (column_ids < count)
            tile = jnp.where(used, products[i], 0.0)
            for dest in range(ndest):
                tile_ref[dest, i, 0, :, :wide] = tile[dest * rows : (dest + 1) * rows].astype(jnp.bfloat16)
                if wide < width:
                    tile_ref[dest, i, 0, :, wide:] = jnp.zeros((rows, width - wide), jnp.bfloat16)
            if not packed:
                continue
            rolled = [
                pltpu.roll(tile[:, start : start + LANES], shift, axis=1) for start in range(0, wide, LANES)
            ]
            for place in range(len(rolled) + 1):
                here = pl.ds(pl.multiple_of(base + place * LANES, LANES), LANES)
                if place == 0:
                    before = jnp.concatenate(
                        [pack_ref[dest, i, :, here].astype(jnp.float32) for dest in range(ndest)], axis=0
                    )
                else:
                    before = rolled[place - 1]
                after = rolled[place] if place < len(rolled) else jnp.zeros_like(before)
                window = jnp.where(low, before, after)
                for dest in range(ndest):
                    pack_ref[dest, i, :, here] = window[dest * rows : (dest + 1) * rows].astype(jnp.bfloat16)

    narrow = width - LANES
    if narrow > 0:
        pl.when(count <= narrow)(lambda: work(narrow))
        pl.when(count > narrow)(lambda: work(width))
    else:
        work(width)

    if packed:

        @pl.when(j == pl.num_programs(0) - 1)
        def _():
            main = main_ref.shape[3]
            main_ref[...] = pack_ref[:, :, :, :main]
            over_ref[...] = pack_ref[:, :, :, main : main + over_ref.shape[3]]


def tiles(ndest, first, tables, test_counts, left, shards, main):
    ntest, nsource, kmax, nq = left.shape
    nshard = len(shards)
    part, width = shards[0].shape[1:]
    rows = kmax // ndest
    packed = main is not None
    shapes = [jax.ShapeDtypeStruct((ndest, ntest, nsource, rows, width), jnp.bfloat16)]
    specs = [pl.BlockSpec((ndest, ntest, 1, rows, width), lambda j, *_: (0, 0, j, 0, 0))]
    scratch = []
    if packed:
        for columns in (main, nsource * width - main):
            shape = (ndest, ntest, rows, columns)
            shapes.append(jax.ShapeDtypeStruct(shape, jnp.bfloat16))
            specs.append(pl.BlockSpec(shape, lambda j, *_: (0, 0, 0, 0)))
        scratch.append(pltpu.VMEM((ndest, ntest, rows, nsource * width + LANES), jnp.bfloat16))
    return pl.pallas_call(
        functools.partial(tile_kernel, nshard, first, packed),
        grid_spec=pltpu.PrefetchScalarGridSpec(
            num_scalar_prefetch=4,
            grid=(nsource,),
            in_specs=[pl.BlockSpec((ntest, 1, kmax, nq), lambda j, *_: (0, j, 0, 0))]
            + [pl.BlockSpec((1, part, width), lambda j, *_: (j, 0, 0))] * nshard,
            out_specs=specs,
            scratch_shapes=scratch,
        ),
        out_shape=shapes,
        compiler_params=pltpu.CompilerParams(vmem_limit_bytes=VMEM_LIMIT),
        cost_estimate=pl.CostEstimate(
            flops=2 * ntest * nsource * kmax * width * nq,
            bytes_accessed=2 * ntest * nsource * kmax * (nq + width),
            transcendentals=0,
        ),
    )(*tables, test_counts, left, *shards)


def project_kernel(started, order_ref, tile_ref, coeff_ref, *refs):
    if started:
        start_ref, sum_ref, total_ref = refs
    else:
        *counts_refs, sum_ref, joined_ref, total_ref = refs
    j = pl.program_id(0)
    ndest, ntest, _, rows, _ = tile_ref.shape
    whole = [tile_ref[dest, i, 0] for i in range(ntest) for dest in range(ndest)]
    term = jnp.dot(jnp.concatenate(whole, axis=0), coeff_ref[0], preferred_element_type=jnp.float32)

    @pl.when(j == 0)
    def _():
        total_ref[...] = term + start_ref[...] if started else term

    @pl.when(j > 0)
    def _():
        total_ref[...] += term

    @pl.when(j == pl.num_programs(0) - 1)
    def _():
        if not started:
            sum_ref[...] = total_ref[...]
            nblock = counts_refs[0].shape[0]
            for place, counts_ref in enumerate(counts_refs):
                for k in range(nblock):
                    joined_ref[place * nblock + k] = counts_ref[k]
            return
        for i in range(ntest):
            for dest in range(ndest):
                top = (i * ndest + dest) * rows
                sum_ref[dest, i] = total_ref[top : top + rows, :].astype(sum_ref.dtype)


def project(order, first, tiles, coefficients, start=None, counts=()):
    ndest, ntest, nsource, rows, width = tiles.shape
    ncol = coefficients.shape[2]
    smem = pl.BlockSpec(memory_space=pltpu.SMEM)
    total_spec = pl.BlockSpec((ntest * ndest * rows, ncol), lambda j, order: (0, 0))
    started = start is not None
    if started:
        more, more_specs = [start], [total_spec]
        out_specs = pl.BlockSpec((ndest, ntest, rows, ncol), lambda j, order: (0, 0, 0, 0))
        out_shape = jax.ShapeDtypeStruct((ndest, ntest, rows, ncol), jnp.bfloat16)
    else:
        more, more_specs = list(counts), [smem] * len(counts)
        out_specs = (total_spec, smem)
        out_shape = (
            jax.ShapeDtypeStruct((ntest * ndest * rows, ncol), jnp.float32),
            jax.ShapeDtypeStruct((sum(part.shape[0] for part in counts),), jnp.int32),
        )
    return pl.pallas_call(
        functools.partial(project_kernel, started),
        grid_spec=pltpu.PrefetchScalarGridSpec(
            num_scalar_prefetch=1,
            grid=(nsource,),
            in_specs=[
                pl.BlockSpec((ndest, ntest, 1, rows, width), lambda j, order: (0, 0, j, 0, 0)),
                pl.BlockSpec((1, width, ncol), lambda j, order: (order[first + j], 0, 0)),
            ]
            + more_specs,
            out_specs=out_specs,
            scratch_shapes=[pltpu.VMEM((ntest * ndest * rows, ncol), jnp.float32)],
        ),
        out_shape=out_shape,
        compiler_params=pltpu.CompilerParams(vmem_limit_bytes=VMEM_LIMIT),
        cost_estimate=pl.CostEstimate(
            flops=2 * ndest * ntest * rows * width * ncol * nsource,
            bytes_accessed=2 * ndest * ntest * rows * width * nsource,
            transcendentals=0,
        ),
    )(order, tiles, coefficients, *more)


def unpack_kernel(cut, order_ref, counts_ref, offsets_ref, whole_ref, packed_ref, out_ref, rows_ref):
    nsrc, _, _, rows, width = whole_ref.shape
    packed_width = packed_ref.shape[3]
    nall = out_ref.shape[2]
    nblock = nall // nsrc
    ntile = width // LANES
    step = 16 if rows % 16 == 0 else rows
    lanes = lax.broadcasted_iota(jnp.int32, (rows, LANES), 1)

    @pl.loop(0, nsrc)
    def _(source):
        for place in range(nblock):
            block = order_ref[source * nblock + place]
            target = source * nblock + block
            if place < cut:
                rows_ref[target] = whole_ref[source, 0, place].astype(jnp.float32)
                continue
            count = counts_ref[target]
            offset = offsets_ref[target]
            shift = offset % LANES
            base = offset - shift
            back = (LANES - shift) % LANES
            low = lanes < LANES - shift
            rolled = []
            for tile in range(ntile + 1):
                start = pl.multiple_of(jnp.minimum(base + tile * LANES, packed_width - LANES), LANES)
                piece = packed_ref[source, 0, :, pl.ds(start, LANES)].astype(jnp.float32)
                rolled.append(pltpu.roll(piece, back, axis=1))
            for tile in range(ntile):
                value = jnp.where(low, rolled[tile], rolled[tile + 1])
                value = jnp.where(lanes < count - tile * LANES, value, 0.0)
                rows_ref[target, :, tile * LANES : (tile + 1) * LANES] = value

    @pl.loop(0, nall // 16)
    def _(group):
        here = pl.ds(pl.multiple_of(group * 16, 16), 16)
        for top in range(0, rows, step):
            turned = jnp.transpose(rows_ref[here, top : top + step, :], (1, 0, 2))
            out_ref[0, top : top + step, here, :] = turned.astype(out_ref.dtype)


def unpack(cut, tables, whole, packed):
    nsrc, ntest, _, rows, width = whole.shape
    packed_width = packed.shape[3]
    nall = tables[0].shape[0]
    return pl.pallas_call(
        functools.partial(unpack_kernel, cut),
        grid_spec=pltpu.PrefetchScalarGridSpec(
            num_scalar_prefetch=3,
            grid=(ntest,),
            in_specs=[
                pl.BlockSpec((nsrc, 1, cut, rows, width), lambda i, *_: (0, i, 0, 0, 0)),
                pl.BlockSpec((nsrc, 1, rows, packed_width), lambda i, *_: (0, i, 0, 0)),
            ],
            out_specs=pl.BlockSpec((1, rows, nall, width), lambda i, *_: (i, 0, 0, 0)),
            scratch_shapes=[pltpu.VMEM((nall, rows, width), jnp.float32)],
        ),
        out_shape=jax.ShapeDtypeStruct((ntest, rows, nall, width), jnp.bfloat16),
        compiler_params=pltpu.CompilerParams(vmem_limit_bytes=SMALL_VMEM_LIMIT),
    )(*tables, whole, packed)


def body(
    test_points, test_basis, test_counts, source_points, source_basis, source_counts, coefficients
):
    nsource, part, kmax = source_basis.shape
    ntest = test_points.shape[0]
    nsrc = lax.axis_size("src")
    ntest_axis = lax.axis_size("test")
    me_test = lax.axis_index("test")
    cut = max(1, nsource * 3 // 8)

    held = {}

    def gather(name, shard, left):
        got = {0: shard}
        bits = list(bits_down(ntest_axis))
        for bit in bits:
            if bit == bits[-1]:
                names = [o for o in got if o != 0]
                tied = lax.optimization_barrier(tuple(got[o] for o in names) + (left,))
                got.update(zip(names, tied[:-1]))
                left = tied[-1]
            for offset in list(got):
                got[offset ^ bit] = exchange(got[offset], "test", bit)
            if bit == bits[0]:
                held[name] = got[bit]
        return [got[offset] for offset in sorted(got)], left

    most = (nsource - cut) * kmax
    main = min(most, -(-most * 18 // (25 * LANES)) * LANES)
    widths = [main, min(most, main + 2 * LANES), most]

    order, offsets, basis_a, basis_b = pick(cut, source_counts, source_basis)
    tables = (order, source_counts, offsets)
    me = jnp.reshape(me_test, (1,))
    test_points, source_points = test_points.transpose(1, 0, 2), source_points.transpose(1, 0, 2)

    left_a = left_products(ntest_axis, me, order, test_points, source_points, test_basis, 0, cut)
    shards_a, left_a = gather("a", basis_a, left_a)
    (tiles_a,) = tiles(nsrc, 0, tables, test_counts, left_a, shards_a, None)
    moved_a = lax.all_to_all(tiles_a, "src", split_axis=0, concat_axis=0, tiled=True)

    rest, _ = lax.optimization_barrier((basis_b, held["a"]))
    later, _ = lax.optimization_barrier((source_points, tiles_a))
    left_b = left_products(ntest_axis, me, order, test_points, later, test_basis, cut, nsource)
    shards_b, left_b = gather("b", rest, left_b)
    inner = max(1, nsrc // 4)
    counts, _ = lax.optimization_barrier((source_counts, left_b))
    far = [exchange(counts, "src", flip) for flip in range(inner, nsrc, inner)]
    tiles_b, packed, beyond = tiles(nsrc, cut, tables, test_counts, left_b, shards_b, main)
    packed, *far = lax.optimization_barrier((packed, *far))
    moved_b = lax.all_to_all(packed, "src", split_axis=0, concat_axis=0, tiled=True)

    sums, joined = project(order, 0, tiles_a, coefficients, counts=[source_counts] + far)
    groups = [joined] + [exchange(joined, "src", flip) for flip in range(1, inner)]
    sums = project(order, cut, tiles_b, coefficients, sums)
    projected = sum_rows(sums, "src")
    me_src, _ = lax.optimization_barrier((jnp.reshape(lax.axis_index("src"), (1,)), packed))
    all_counts, all_order, all_offsets, branch = all_tables(cut, nsource, widths, me_src, groups)
    spread = (all_order, all_counts, all_offsets)

    def finish(width, beyond, moved_a, moved_b, spread):
        if width > main:
            more = lax.all_to_all(
                beyond[..., : width - main], "src", split_axis=0, concat_axis=0, tiled=True
            )
            moved_b = jnp.concatenate([moved_b, more], axis=3)
        return unpack(cut, spread, moved_a, moved_b)

    reduced = lax.switch(
        branch[0],
        [functools.partial(finish, width) for width in widths],
        beyond,
        moved_a,
        moved_b,
        spread,
    )
    return (reduced, projected)


def solution(mesh):
    return jax.shard_map(
        body,
        mesh=mesh,
        in_specs=(
            P("test", None, None),
            P("test", None, None),
            P("test"),
            P("src", None, None),
            P("src", "test", None),
            P("src"),
            P("src", None, None),
        ),
        out_specs=(P("test", "src", None, None), P("test", "src", None)),
        check_vma=False,
    )
```

```python
import functools

import jax
import jax.numpy as jnp
from jax import lax
from jax.experimental import pallas as pl
from jax.experimental.pallas import tpu as pltpu
from jax.sharding import PartitionSpec as P

softening = 0.0025
QBLOCK = 256
LANES = 128
VMEM_LIMIT = 63 * 1024 * 1024
SMALL_VMEM_LIMIT = 32 * 1024 * 1024


def exchange(x, axis, flip):
    size = lax.axis_size(axis)
    return lax.ppermute(x, axis, [(a, a ^ flip) for a in range(size)])


def bits_down(size):
    bit = size // 2
    while bit >= 1:
        yield bit
        bit //= 2


def sum_rows(total, axis):
    size = lax.axis_size(axis)
    me = lax.axis_index(axis)
    held, bit = total, 1
    while held.shape[0] > 4:
        pairs = held.reshape((held.shape[0] // 2, 2) + held.shape[1:])
        mine = (me // bit) % 2
        keep = lax.dynamic_index_in_dim(pairs, mine, 1, keepdims=False)
        give = lax.dynamic_index_in_dim(pairs, 1 - mine, 1, keepdims=False)
        got = exchange(give, axis, bit)
        held = (keep.astype(jnp.float32) + got.astype(jnp.float32)).astype(held.dtype)
        bit *= 2
    mine = me // bit
    parts = [lax.dynamic_index_in_dim(held, mine, 0, keepdims=False)]
    for flip in range(1, held.shape[0]):
        give = lax.dynamic_index_in_dim(held, mine ^ flip, 0, keepdims=False)
        parts.append(exchange(give, axis, flip * bit))
    return parts


def rank_blocks(counts, cut):
    ranks = []
    for j, mine in enumerate(counts):
        rank = jnp.int32(0)
        for k, other in enumerate(counts):
            if k != j:
                ahead = other >= mine if k < j else other > mine
                rank += ahead.astype(jnp.int32)
        ranks.append(rank)
    offsets = []
    for j in range(len(counts)):
        offset = jnp.int32(0)
        for k, other in enumerate(counts):
            if k != j:
                offset += jnp.where((ranks[k] >= cut) & (ranks[k] < ranks[j]), other, 0)
        offsets.append(offset)
    return ranks, offsets


def pick_kernel(cut, counts_ref, basis_ref, order_ref, offsets_ref, first_ref, rest_ref):
    nblock = basis_ref.shape[0]
    ranks, offsets = rank_blocks([counts_ref[j] for j in range(nblock)], cut)
    for j in range(nblock):
        order_ref[ranks[j]] = jnp.int32(j)
        offsets_ref[j] = offsets[j]
    for place in range(nblock):
        block = basis_ref[order_ref[place]]
        if place < cut:
            first_ref[place] = block
        else:
            rest_ref[place - cut] = block


def pick(cut, counts, basis):
    nblock = basis.shape[0]
    smem, vmem = pl.BlockSpec(memory_space=pltpu.SMEM), pl.BlockSpec(memory_space=pltpu.VMEM)
    return pl.pallas_call(
        functools.partial(pick_kernel, cut),
        out_shape=(
            jax.ShapeDtypeStruct((nblock,), jnp.int32),
            jax.ShapeDtypeStruct((nblock,), jnp.int32),
            jax.ShapeDtypeStruct((cut,) + basis.shape[1:], basis.dtype),
            jax.ShapeDtypeStruct((nblock - cut,) + basis.shape[1:], basis.dtype),
        ),
        in_specs=[smem, vmem],
        out_specs=(smem, smem, vmem, vmem),
        compiler_params=pltpu.CompilerParams(vmem_limit_bytes=VMEM_LIMIT),
    )(counts, basis)


def tables_kernel(cut, nblock, widths, me_ref, *refs):
    *group_refs, counts_ref, order_ref, offsets_ref, branch_ref, joined_ref = refs
    group, inner = group_refs[0].shape[0], len(group_refs)
    for place, group_ref in enumerate(group_refs):
        for k in range(group):
            joined_ref[place * group + k] = group_ref[k]

    def step(source, need):
        base = source * nblock
        offset = source ^ me_ref[0]
        theirs = (offset % inner) * group + (offset // inner) * nblock
        counts = [joined_ref[theirs + j] for j in range(nblock)]
        ranks, offsets = rank_blocks(counts, cut)
        used = jnp.int32(0)
        for j in range(nblock):
            counts_ref[base + j] = counts[j]
            order_ref[base + ranks[j]] = jnp.int32(j)
            offsets_ref[base + j] = offsets[j]
            used += jnp.where(ranks[j] >= cut, counts[j], 0)
        return jnp.maximum(need, used)

    need = lax.fori_loop(0, counts_ref.shape[0] // nblock, step, jnp.int32(0))
    branch = jnp.int32(0)
    for width in widths[:-1]:
        branch += (need > width).astype(jnp.int32)
    branch_ref[0] = branch


def all_tables(cut, nblock, widths, me, groups):
    smem = pl.BlockSpec(memory_space=pltpu.SMEM)
    total = sum(group.shape[0] for group in groups)
    table = jax.ShapeDtypeStruct((total,), jnp.int32)
    return pl.pallas_call(
        functools.partial(tables_kernel, cut, nblock, widths),
        out_shape=(table, table, table, jax.ShapeDtypeStruct((1,), jnp.int32)),
        in_specs=[smem] * (1 + len(groups)),
        out_specs=(smem,) * 4,
        scratch_shapes=[pltpu.SMEM((total,), jnp.int32)],
    )(me, *groups)


NFEATURE = 128


def fill_features(rows_ref, points, is_test):
    def three_terms(x):
        high = x.astype(jnp.bfloat16).astype(jnp.float32)
        middle = (x - high).astype(jnp.bfloat16).astype(jnp.float32)
        return high, middle, x - high - middle

    centred = points - 0.5
    norm = jnp.sum(centred * centred, axis=0, keepdims=True)
    terms = three_terms(centred)
    norms = three_terms(norm + softening if is_test else norm)
    for a in range(3):
        for b in range(3):
            place = 3 * (3 * a + b)
            rows_ref[place : place + 3, :] = -2.0 * terms[a] if is_test else terms[b]
    for a in range(3):
        rows_ref[27 + a : 28 + a, :] = norms[a] if is_test else jnp.ones_like(norm)
        rows_ref[30 + a : 31 + a, :] = jnp.ones_like(norm) if is_test else norms[a]


def left_kernel(
    nshard, first, me_ref, order_ref, test_ref, source_ref, basis_ref, out_ref,
    rows_ref, features_ref, turned_ref, near_ref,
):
    j = pl.program_id(0)
    ntest = test_ref.shape[1]
    nq = source_ref.shape[2]
    part = nq // nshard
    block = min(QBLOCK, nq)

    @pl.when(j == 0)
    def _():
        rows_ref[...] = jnp.zeros_like(rows_ref)
        for i in range(ntest):
            fill_features(rows_ref, test_ref[:, i, :], True)
            features_ref[i] = rows_ref[...].T.astype(jnp.bfloat16)
            turned_ref[i] = basis_ref[i].T

    source = order_ref[first + j]
    for comp in range(3):
        rows_ref[comp : comp + 1, :] = source_ref[comp, pl.ds(source, 1), :]
    pieces = []
    for offset in range(nshard):
        start = pl.multiple_of((me_ref[0] ^ offset) * part, part)
        pieces.append(rows_ref[0:3, pl.ds(start, part)])
    fill_features(rows_ref, jnp.concatenate(pieces, axis=1), False)
    near_ref[...] = rows_ref[...].astype(jnp.bfloat16)

    steps = [(i, start) for i in range(ntest) for start in range(0, nq, block)]

    def kernel_block(i, start):
        squared = jnp.dot(
            features_ref[i], near_ref[:, start : start + block], preferred_element_type=jnp.float32
        )
        return lax.rsqrt(squared.astype(jnp.bfloat16))

    ready = kernel_block(*steps[0])
    for place, (i, start) in enumerate(steps):
        now = ready
        if place + 1 < len(steps):
            ready = kernel_block(*steps[place + 1])
        out_ref[i, 0, :, start : start + block] = jnp.dot(
            turned_ref[i], now, preferred_element_type=jnp.float32
        ).astype(jnp.bfloat16)


def left_products(nshard, me, order, test_points, source_points, test_basis, first, last):
    _, ntest, npoint = test_points.shape
    nall, nq = source_points.shape[1:]
    kmax = test_basis.shape[2]
    nsource = last - first
    return pl.pallas_call(
        functools.partial(left_kernel, nshard, first),
        grid_spec=pltpu.PrefetchScalarGridSpec(
            num_scalar_prefetch=2,
            grid=(nsource,),
            in_specs=[
                pl.BlockSpec((3, ntest, npoint), lambda j, *_: (0, 0, 0)),
                pl.BlockSpec((3, nall, nq), lambda j, *_: (0, 0, 0)),
                pl.BlockSpec((ntest, npoint, kmax), lambda j, *_: (0, 0, 0)),
            ],
            out_specs=pl.BlockSpec((ntest, 1, kmax, nq), lambda j, *_: (0, j, 0, 0)),
            scratch_shapes=[
                pltpu.VMEM((NFEATURE, npoint), jnp.float32),
                pltpu.VMEM((ntest, npoint, NFEATURE), jnp.bfloat16),
                pltpu.VMEM((ntest, kmax, npoint), jnp.bfloat16),
                pltpu.VMEM((NFEATURE, nq), jnp.bfloat16),
            ],
        ),
        out_shape=jax.ShapeDtypeStruct((ntest, nsource, kmax, nq), jnp.bfloat16),
        compiler_params=pltpu.CompilerParams(vmem_limit_bytes=VMEM_LIMIT),
        cost_estimate=pl.CostEstimate(
            flops=2 * ntest * nsource * npoint * nq * kmax,
            bytes_accessed=2 * ntest * nsource * kmax * nq,
            transcendentals=ntest * nsource * npoint * nq,
        ),
    )(me, order, test_points, source_points, test_basis)


def tile_kernel(nshard, first, packed, *refs):
    order_ref, source_counts_ref, offsets_ref, test_counts_ref, left_ref = refs[:5]
    shard_refs = refs[5 : 5 + nshard]
    j = pl.program_id(0)
    if packed:
        tile_ref, main_ref, over_ref, pack_ref = refs[5 + nshard :]
    else:
        (tile_ref,) = refs[5 + nshard :]
    ntest, _, kmax, _ = left_ref.shape
    ndest, _, _, rows, width = tile_ref.shape
    count = source_counts_ref[order_ref[first + j]]

    def work(wide):
        side = jnp.concatenate([shard_ref[0, :, :wide] for shard_ref in shard_refs], axis=0)
        row_ids = lax.broadcasted_iota(jnp.int32, (kmax, wide), 0)
        column_ids = lax.broadcasted_iota(jnp.int32, (kmax, wide), 1)
        products = [
            jnp.dot(left_ref[i, 0], side, preferred_element_type=jnp.float32) for i in range(ntest)
        ]
        if packed:
            offset = offsets_ref[order_ref[first + j]]
            shift = offset % LANES
            base = offset - shift
            low = lax.broadcasted_iota(jnp.int32, (kmax, LANES), 1) < shift
        for i in range(ntest):
            used = (row_ids < test_counts_ref[i]) & (column_ids < count)
            tile = jnp.where(used, products[i], 0.0)
            for dest in range(ndest):
                tile_ref[dest, i, 0, :, :wide] = tile[dest * rows : (dest + 1) * rows].astype(jnp.bfloat16)
                if wide < width:
                    tile_ref[dest, i, 0, :, wide:] = jnp.zeros((rows, width - wide), jnp.bfloat16)
            if not packed:
                continue
            rolled = [
                pltpu.roll(tile[:, start : start + LANES], shift, axis=1) for start in range(0, wide, LANES)
            ]
            for place in range(len(rolled) + 1):
                here = pl.ds(pl.multiple_of(base + place * LANES, LANES), LANES)
                if place == 0:
                    before = jnp.concatenate(
                        [pack_ref[dest, i, :, here].astype(jnp.float32) for dest in range(ndest)], axis=0
                    )
                else:
                    before = rolled[place - 1]
                after = rolled[place] if place < len(rolled) else jnp.zeros_like(before)
                window = jnp.where(low, before, after)
                for dest in range(ndest):
                    pack_ref[dest, i, :, here] = window[dest * rows : (dest + 1) * rows].astype(jnp.bfloat16)

    narrow = width - LANES
    if narrow > 0:
        pl.when(count <= narrow)(lambda: work(narrow))
        pl.when(count > narrow)(lambda: work(width))
    else:
        work(width)

    if packed:

        @pl.when(j == pl.num_programs(0) - 1)
        def _():
            main = main_ref.shape[3]
            main_ref[...] = pack_ref[:, :, :, :main]
            over_ref[...] = pack_ref[:, :, :, main : main + over_ref.shape[3]]


def tiles(ndest, first, tables, test_counts, left, shards, main):
    ntest, nsource, kmax, nq = left.shape
    nshard = len(shards)
    part, width = shards[0].shape[1:]
    rows = kmax // ndest
    packed = main is not None
    shapes = [jax.ShapeDtypeStruct((ndest, ntest, nsource, rows, width), jnp.bfloat16)]
    specs = [pl.BlockSpec((ndest, ntest, 1, rows, width), lambda j, *_: (0, 0, j, 0, 0))]
    scratch = []
    if packed:
        for columns in (main, nsource * width - main):
            shape = (ndest, ntest, rows, columns)
            shapes.append(jax.ShapeDtypeStruct(shape, jnp.bfloat16))
            specs.append(pl.BlockSpec(shape, lambda j, *_: (0, 0, 0, 0)))
        scratch.append(pltpu.VMEM((ndest, ntest, rows, nsource * width + LANES), jnp.bfloat16))
    return pl.pallas_call(
        functools.partial(tile_kernel, nshard, first, packed),
        grid_spec=pltpu.PrefetchScalarGridSpec(
            num_scalar_prefetch=4,
            grid=(nsource,),
            in_specs=[pl.BlockSpec((ntest, 1, kmax, nq), lambda j, *_: (0, j, 0, 0))]
            + [pl.BlockSpec((1, part, width), lambda j, *_: (j, 0, 0))] * nshard,
            out_specs=specs,
            scratch_shapes=scratch,
        ),
        out_shape=shapes,
        compiler_params=pltpu.CompilerParams(vmem_limit_bytes=VMEM_LIMIT),
        cost_estimate=pl.CostEstimate(
            flops=2 * ntest * nsource * kmax * width * nq,
            bytes_accessed=2 * ntest * nsource * kmax * (nq + width),
            transcendentals=0,
        ),
    )(*tables, test_counts, left, *shards)


def project_kernel(started, order_ref, tile_ref, coeff_ref, *refs):
    if started:
        start_ref, sum_ref, total_ref = refs
    else:
        *counts_refs, sum_ref, joined_ref, total_ref = refs
    j = pl.program_id(0)
    ndest, ntest, _, rows, _ = tile_ref.shape
    whole = [tile_ref[dest, i, 0] for i in range(ntest) for dest in range(ndest)]
    term = jnp.dot(jnp.concatenate(whole, axis=0), coeff_ref[0], preferred_element_type=jnp.float32)

    @pl.when(j == 0)
    def _():
        total_ref[...] = term + start_ref[...] if started else term

    @pl.when(j > 0)
    def _():
        total_ref[...] += term

    @pl.when(j == pl.num_programs(0) - 1)
    def _():
        if not started:
            sum_ref[...] = total_ref[...]
            nblock = counts_refs[0].shape[0]
            for place, counts_ref in enumerate(counts_refs):
                for k in range(nblock):
                    joined_ref[place * nblock + k] = counts_ref[k]
            return
        for i in range(ntest):
            for dest in range(ndest):
                top = (i * ndest + dest) * rows
                sum_ref[dest, i] = total_ref[top : top + rows, :].astype(sum_ref.dtype)


def project(order, first, tiles, coefficients, start=None, counts=()):
    ndest, ntest, nsource, rows, width = tiles.shape
    ncol = coefficients.shape[2]
    smem = pl.BlockSpec(memory_space=pltpu.SMEM)
    total_spec = pl.BlockSpec((ntest * ndest * rows, ncol), lambda j, order: (0, 0))
    started = start is not None
    if started:
        more, more_specs = [start], [total_spec]
        out_specs = pl.BlockSpec((ndest, ntest, rows, ncol), lambda j, order: (0, 0, 0, 0))
        out_shape = jax.ShapeDtypeStruct((ndest, ntest, rows, ncol), jnp.bfloat16)
    else:
        more, more_specs = list(counts), [smem] * len(counts)
        out_specs = (total_spec, smem)
        out_shape = (
            jax.ShapeDtypeStruct((ntest * ndest * rows, ncol), jnp.float32),
            jax.ShapeDtypeStruct((sum(part.shape[0] for part in counts),), jnp.int32),
        )
    return pl.pallas_call(
        functools.partial(project_kernel, started),
        grid_spec=pltpu.PrefetchScalarGridSpec(
            num_scalar_prefetch=1,
            grid=(nsource,),
            in_specs=[
                pl.BlockSpec((ndest, ntest, 1, rows, width), lambda j, order: (0, 0, j, 0, 0)),
                pl.BlockSpec((1, width, ncol), lambda j, order: (order[first + j], 0, 0)),
            ]
            + more_specs,
            out_specs=out_specs,
            scratch_shapes=[pltpu.VMEM((ntest * ndest * rows, ncol), jnp.float32)],
        ),
        out_shape=out_shape,
        compiler_params=pltpu.CompilerParams(vmem_limit_bytes=VMEM_LIMIT),
        cost_estimate=pl.CostEstimate(
            flops=2 * ndest * ntest * rows * width * ncol * nsource,
            bytes_accessed=2 * ndest * ntest * rows * width * nsource,
            transcendentals=0,
        ),
    )(order, tiles, coefficients, *more)


def unpack_kernel(cut, order_ref, counts_ref, offsets_ref, whole_ref, packed_ref, *refs):
    *part_refs, out_ref, sum_ref, rows_ref = refs
    sum_ref[...] = sum(part_ref[...].astype(jnp.float32) for part_ref in part_refs).astype(sum_ref.dtype)
    nsrc, _, _, rows, width = whole_ref.shape
    packed_width = packed_ref.shape[3]
    nall = out_ref.shape[2]
    nblock = nall // nsrc
    ntile = width // LANES
    step = 16 if rows % 16 == 0 else rows
    lanes = lax.broadcasted_iota(jnp.int32, (rows, LANES), 1)

    @pl.loop(0, nsrc, unroll=2)
    def _(source):
        for place in range(nblock):
            block = order_ref[source * nblock + place]
            target = source * nblock + block
            if place < cut:
                rows_ref[target] = whole_ref[source, 0, place].astype(jnp.float32)
                continue
            count = counts_ref[target]
            offset = offsets_ref[target]
            shift = offset % LANES
            base = offset - shift
            back = (LANES - shift) % LANES
            low = lanes < LANES - shift
            rolled = []
            for tile in range(ntile + 1):
                start = pl.multiple_of(jnp.minimum(base + tile * LANES, packed_width - LANES), LANES)
                piece = packed_ref[source, 0, :, pl.ds(start, LANES)].astype(jnp.float32)
                rolled.append(pltpu.roll(piece, back, axis=1))
            for tile in range(ntile):
                value = jnp.where(low, rolled[tile], rolled[tile + 1])
                value = jnp.where(lanes < count - tile * LANES, value, 0.0)
                rows_ref[target, :, tile * LANES : (tile + 1) * LANES] = value

    @pl.loop(0, nall // 16)
    def _(group):
        here = pl.ds(pl.multiple_of(group * 16, 16), 16)
        for top in range(0, rows, step):
            turned = jnp.transpose(rows_ref[here, top : top + step, :], (1, 0, 2))
            out_ref[0, top : top + step, here, :] = turned.astype(out_ref.dtype)


def unpack(cut, tables, whole, packed, parts):
    nsrc, ntest, _, rows, width = whole.shape
    packed_width = packed.shape[3]
    nall = tables[0].shape[0]
    sum_spec = pl.BlockSpec((1,) + parts[0].shape[1:], lambda i, *_: (i, 0, 0))
    return pl.pallas_call(
        functools.partial(unpack_kernel, cut),
        grid_spec=pltpu.PrefetchScalarGridSpec(
            num_scalar_prefetch=3,
            grid=(ntest,),
            in_specs=[
                pl.BlockSpec((nsrc, 1, cut, rows, width), lambda i, *_: (0, i, 0, 0, 0)),
                pl.BlockSpec((nsrc, 1, rows, packed_width), lambda i, *_: (0, i, 0, 0)),
            ]
            + [sum_spec] * len(parts),
            out_specs=(pl.BlockSpec((1, rows, nall, width), lambda i, *_: (i, 0, 0, 0)), sum_spec),
            scratch_shapes=[pltpu.VMEM((nall, rows, width), jnp.float32)],
        ),
        out_shape=(
            jax.ShapeDtypeStruct((ntest, rows, nall, width), jnp.bfloat16),
            jax.ShapeDtypeStruct(parts[0].shape, jnp.bfloat16),
        ),
        compiler_params=pltpu.CompilerParams(vmem_limit_bytes=SMALL_VMEM_LIMIT),
    )(*tables, whole, packed, *parts)


def body(
    test_points, test_basis, test_counts, source_points, source_basis, source_counts, coefficients
):
    nsource, part, kmax = source_basis.shape
    ntest = test_points.shape[0]
    nsrc = lax.axis_size("src")
    ntest_axis = lax.axis_size("test")
    me_test = lax.axis_index("test")
    cut = max(1, nsource * 3 // 8)

    held = {}

    def gather(name, shard, left):
        got = {0: shard}
        bits = list(bits_down(ntest_axis))
        for bit in bits:
            if bit == bits[-1]:
                names = [o for o in got if o != 0]
                tied = lax.optimization_barrier(tuple(got[o] for o in names) + (left,))
                got.update(zip(names, tied[:-1]))
                left = tied[-1]
            for offset in list(got):
                got[offset ^ bit] = exchange(got[offset], "test", bit)
            if bit == bits[0]:
                held[name] = got[bit]
        return [got[offset] for offset in sorted(got)], left

    most = (nsource - cut) * kmax
    main = min(most, -(-most * 18 // (25 * LANES)) * LANES)
    widths = [main, min(most, main + LANES), min(most, main + 2 * LANES), most]

    order, offsets, basis_a, basis_b = pick(cut, source_counts, source_basis)
    tables = (order, source_counts, offsets)
    me = jnp.reshape(me_test, (1,))
    test_points, source_points = test_points.transpose(1, 0, 2), source_points.transpose(1, 0, 2)

    left_a = left_products(ntest_axis, me, order, test_points, source_points, test_basis, 0, cut)
    shards_a, left_a = gather("a", basis_a, left_a)
    (tiles_a,) = tiles(nsrc, 0, tables, test_counts, left_a, shards_a, None)
    moved_a = lax.all_to_all(tiles_a, "src", split_axis=0, concat_axis=0, tiled=True)

    rest, _ = lax.optimization_barrier((basis_b, held["a"]))
    later, _ = lax.optimization_barrier((source_points, tiles_a))
    left_b = left_products(ntest_axis, me, order, test_points, later, test_basis, cut, nsource)
    shards_b, left_b = gather("b", rest, left_b)
    inner = max(1, nsrc // 4)
    counts, _ = lax.optimization_barrier((source_counts, left_b))
    far = [exchange(counts, "src", flip) for flip in range(inner, nsrc, inner)]
    tiles_b, packed, beyond = tiles(nsrc, cut, tables, test_counts, left_b, shards_b, main)
    packed, *far = lax.optimization_barrier((packed, *far))
    moved_b = lax.all_to_all(packed, "src", split_axis=0, concat_axis=0, tiled=True)

    sums, joined = project(order, 0, tiles_a, coefficients, counts=[source_counts] + far)
    groups = [joined] + [exchange(joined, "src", flip) for flip in range(1, inner)]
    sums = project(order, cut, tiles_b, coefficients, sums)
    parts = sum_rows(sums, "src")
    me_src, _ = lax.optimization_barrier((jnp.reshape(lax.axis_index("src"), (1,)), packed))
    all_counts, all_order, all_offsets, branch = all_tables(cut, nsource, widths, me_src, groups)
    spread = (all_order, all_counts, all_offsets)

    def finish(width, beyond, moved_a, moved_b, spread, parts):
        if width > main:
            more = lax.all_to_all(
                beyond[..., : width - main], "src", split_axis=0, concat_axis=0, tiled=True
            )
            moved_b = jnp.concatenate([moved_b, more], axis=3)
        return unpack(cut, spread, moved_a, moved_b, parts)

    return lax.switch(
        branch[0],
        [functools.partial(finish, width) for width in widths],
        beyond,
        moved_a,
        moved_b,
        spread,
        parts,
    )


def solution(mesh):
    return jax.shard_map(
        body,
        mesh=mesh,
        in_specs=(
            P("test", None, None),
            P("test", None, None),
            P("test"),
            P("src", None, None),
            P("src", "test", None),
            P("src"),
            P("src", None, None),
        ),
        out_specs=(P("test", "src", None, None), P("test", "src", None)),
        check_vma=False,
    )
```

```python
import functools

import jax
import jax.numpy as jnp
from jax import lax
from jax.experimental import pallas as pl
from jax.experimental.pallas import tpu as pltpu
from jax.sharding import PartitionSpec as P

softening = 0.0025
QBLOCK = 512
LANES = 128
VMEM_LIMIT = 255 * 256 * 1024
SMALL_VMEM_LIMIT = 32 * 1024 * 1024


def exchange(x, axis, flip):
    size = lax.axis_size(axis)
    return lax.ppermute(x, axis, [(a, a ^ flip) for a in range(size)])


def bits_down(size):
    bit = size // 2
    while bit >= 1:
        yield bit
        bit //= 2


def sum_rows(total, axis):
    size = lax.axis_size(axis)
    me = lax.axis_index(axis)
    held, bit = total, 1
    while held.shape[0] > 4:
        pairs = held.reshape((held.shape[0] // 2, 2) + held.shape[1:])
        mine = (me // bit) % 2
        keep = lax.dynamic_index_in_dim(pairs, mine, 1, keepdims=False)
        give = lax.dynamic_index_in_dim(pairs, 1 - mine, 1, keepdims=False)
        got = exchange(give, axis, bit)
        held = (keep.astype(jnp.float32) + got.astype(jnp.float32)).astype(held.dtype)
        bit *= 2
    mine = me // bit
    parts = [lax.dynamic_index_in_dim(held, mine, 0, keepdims=False)]
    for flip in range(1, held.shape[0]):
        give = lax.dynamic_index_in_dim(held, mine ^ flip, 0, keepdims=False)
        parts.append(exchange(give, axis, flip * bit))
    return parts


def rank_blocks(counts, cut):
    ranks = []
    for j, mine in enumerate(counts):
        rank = jnp.int32(0)
        for k, other in enumerate(counts):
            if k != j:
                ahead = other >= mine if k < j else other > mine
                rank += ahead.astype(jnp.int32)
        ranks.append(rank)
    offsets = []
    for j in range(len(counts)):
        offset = jnp.int32(0)
        for k, other in enumerate(counts):
            if k != j:
                offset += jnp.where((ranks[k] >= cut) & (ranks[k] < ranks[j]), other, 0)
        offsets.append(offset)
    return ranks, offsets


def pick_kernel(cut, counts_ref, basis_ref, order_ref, offsets_ref, first_ref, rest_ref):
    nblock = basis_ref.shape[0]
    ranks, offsets = rank_blocks([counts_ref[j] for j in range(nblock)], cut)
    for j in range(nblock):
        order_ref[ranks[j]] = jnp.int32(j)
        offsets_ref[j] = offsets[j]
    for place in range(nblock):
        block = basis_ref[order_ref[place]]
        if place < cut:
            first_ref[place] = block
        else:
            rest_ref[place - cut] = block


def pick(cut, counts, basis):
    nblock = basis.shape[0]
    smem, vmem = pl.BlockSpec(memory_space=pltpu.SMEM), pl.BlockSpec(memory_space=pltpu.VMEM)
    return pl.pallas_call(
        functools.partial(pick_kernel, cut),
        out_shape=(
            jax.ShapeDtypeStruct((nblock,), jnp.int32),
            jax.ShapeDtypeStruct((nblock,), jnp.int32),
            jax.ShapeDtypeStruct((cut,) + basis.shape[1:], basis.dtype),
            jax.ShapeDtypeStruct((nblock - cut,) + basis.shape[1:], basis.dtype),
        ),
        in_specs=[smem, vmem],
        out_specs=(smem, smem, vmem, vmem),
        compiler_params=pltpu.CompilerParams(vmem_limit_bytes=VMEM_LIMIT),
    )(counts, basis)


def tables_kernel(cut, nblock, widths, me_ref, *refs):
    *group_refs, counts_ref, order_ref, offsets_ref, branch_ref, joined_ref = refs
    group, inner = group_refs[0].shape[0], len(group_refs)
    for place, group_ref in enumerate(group_refs):
        for k in range(group):
            joined_ref[place * group + k] = group_ref[k]

    def step(source, need):
        base = source * nblock
        offset = source ^ me_ref[0]
        theirs = (offset % inner) * group + (offset // inner) * nblock
        counts = [joined_ref[theirs + j] for j in range(nblock)]
        ranks, offsets = rank_blocks(counts, cut)
        used = jnp.int32(0)
        for j in range(nblock):
            counts_ref[base + j] = counts[j]
            order_ref[base + ranks[j]] = jnp.int32(j)
            offsets_ref[base + j] = offsets[j]
            used += jnp.where(ranks[j] >= cut, counts[j], 0)
        return jnp.maximum(need, used)

    need = lax.fori_loop(0, counts_ref.shape[0] // nblock, step, jnp.int32(0))
    branch = jnp.int32(0)
    for width in widths[:-1]:
        branch += (need > width).astype(jnp.int32)
    branch_ref[0] = branch


def all_tables(cut, nblock, widths, me, groups):
    smem = pl.BlockSpec(memory_space=pltpu.SMEM)
    total = sum(group.shape[0] for group in groups)
    table = jax.ShapeDtypeStruct((total,), jnp.int32)
    return pl.pallas_call(
        functools.partial(tables_kernel, cut, nblock, widths),
        out_shape=(table, table, table, jax.ShapeDtypeStruct((1,), jnp.int32)),
        in_specs=[smem] * (1 + len(groups)),
        out_specs=(smem,) * 4,
        scratch_shapes=[pltpu.SMEM((total,), jnp.int32)],
    )(me, *groups)


NFEATURE = 128


def fill_features(rows_ref, points, is_test):
    def three_terms(x):
        high = x.astype(jnp.bfloat16).astype(jnp.float32)
        middle = (x - high).astype(jnp.bfloat16).astype(jnp.float32)
        return high, middle, x - high - middle

    centred = points - 0.5
    norm = jnp.sum(centred * centred, axis=0, keepdims=True)
    terms = three_terms(centred)
    norms = three_terms(norm + softening if is_test else norm)
    for a in range(3):
        for b in range(3):
            place = 3 * (3 * a + b)
            rows_ref[place : place + 3, :] = -2.0 * terms[a] if is_test else terms[b]
    for a in range(3):
        rows_ref[27 + a : 28 + a, :] = norms[a] if is_test else jnp.ones_like(norm)
        rows_ref[30 + a : 31 + a, :] = jnp.ones_like(norm) if is_test else norms[a]


def left_kernel(
    nshard, first, me_ref, order_ref, test_ref, source_ref, basis_ref, out_ref,
    rows_ref, features_ref, turned_ref, near_ref,
):
    j = pl.program_id(0)
    ntest = test_ref.shape[1]
    nq = source_ref.shape[2]
    part = nq // nshard
    block = min(QBLOCK, nq)

    @pl.when(j == 0)
    def _():
        rows_ref[...] = jnp.zeros_like(rows_ref)
        for i in range(ntest):
            fill_features(rows_ref, test_ref[:, i, :], True)
            features_ref[i] = rows_ref[...].T.astype(jnp.bfloat16)
            turned_ref[i] = basis_ref[i].T

    source = order_ref[first + j]
    for comp in range(3):
        rows_ref[comp : comp + 1, :] = source_ref[comp, pl.ds(source, 1), :]
    pieces = []
    for offset in range(nshard):
        start = pl.multiple_of((me_ref[0] ^ offset) * part, part)
        pieces.append(rows_ref[0:3, pl.ds(start, part)])
    fill_features(rows_ref, jnp.concatenate(pieces, axis=1), False)
    near_ref[...] = rows_ref[...].astype(jnp.bfloat16)

    steps = [(i, start) for i in range(ntest) for start in range(0, nq, block)]

    def kernel_block(i, start):
        squared = jnp.dot(
            features_ref[i], near_ref[:, start : start + block], preferred_element_type=jnp.float32
        )
        return lax.rsqrt(squared.astype(jnp.bfloat16))

    ready = kernel_block(*steps[0])
    for place, (i, start) in enumerate(steps):
        now = ready
        if place + 1 < len(steps):
            ready = kernel_block(*steps[place + 1])
        out_ref[i, 0, :, start : start + block] = jnp.dot(
            turned_ref[i], now, preferred_element_type=jnp.float32
        ).astype(jnp.bfloat16)


def left_products(nshard, me, order, test_points, source_points, test_basis, first, last):
    _, ntest, npoint = test_points.shape
    nall, nq = source_points.shape[1:]
    kmax = test_basis.shape[2]
    nsource = last - first
    return pl.pallas_call(
        functools.partial(left_kernel, nshard, first),
        grid_spec=pltpu.PrefetchScalarGridSpec(
            num_scalar_prefetch=2,
            grid=(nsource,),
            in_specs=[
                pl.BlockSpec((3, ntest, npoint), lambda j, *_: (0, 0, 0)),
                pl.BlockSpec((3, nall, nq), lambda j, *_: (0, 0, 0)),
                pl.BlockSpec((ntest, npoint, kmax), lambda j, *_: (0, 0, 0)),
            ],
            out_specs=pl.BlockSpec((ntest, 1, kmax, nq), lambda j, *_: (0, j, 0, 0)),
            scratch_shapes=[
                pltpu.VMEM((NFEATURE, npoint), jnp.float32),
                pltpu.VMEM((ntest, npoint, NFEATURE), jnp.bfloat16),
                pltpu.VMEM((ntest, kmax, npoint), jnp.bfloat16),
                pltpu.VMEM((NFEATURE, nq), jnp.bfloat16),
            ],
        ),
        out_shape=jax.ShapeDtypeStruct((ntest, nsource, kmax, nq), jnp.bfloat16),
        compiler_params=pltpu.CompilerParams(vmem_limit_bytes=VMEM_LIMIT),
        cost_estimate=pl.CostEstimate(
            flops=2 * ntest * nsource * npoint * nq * kmax,
            bytes_accessed=2 * ntest * nsource * kmax * nq,
            transcendentals=ntest * nsource * npoint * nq,
        ),
    )(me, order, test_points, source_points, test_basis)


def tile_kernel(nshard, first, packed, *refs):
    order_ref, source_counts_ref, offsets_ref, test_counts_ref, left_ref = refs[:5]
    shard_refs = refs[5 : 5 + nshard]
    j = pl.program_id(0)
    if packed:
        tile_ref, main_ref, over_ref, pack_ref = refs[5 + nshard :]
    else:
        (tile_ref,) = refs[5 + nshard :]
    ntest, _, kmax, _ = left_ref.shape
    ndest, _, _, rows, width = tile_ref.shape
    count = source_counts_ref[order_ref[first + j]]

    def work(wide):
        side = jnp.concatenate([shard_ref[0, :, :wide] for shard_ref in shard_refs], axis=0)
        row_ids = lax.broadcasted_iota(jnp.int32, (kmax, wide), 0)
        column_ids = lax.broadcasted_iota(jnp.int32, (kmax, wide), 1)
        products = [
            jnp.dot(left_ref[i, 0], side, preferred_element_type=jnp.float32) for i in range(ntest)
        ]
        if packed:
            offset = offsets_ref[order_ref[first + j]]
            shift = offset % LANES
            base = offset - shift
            low = lax.broadcasted_iota(jnp.int32, (kmax, LANES), 1) < shift
        for i in range(ntest):
            used = (row_ids < test_counts_ref[i]) & (column_ids < count)
            tile = jnp.where(used, products[i], 0.0)
            for dest in range(ndest):
                tile_ref[dest, i, 0, :, :wide] = tile[dest * rows : (dest + 1) * rows].astype(jnp.bfloat16)
                if wide < width:
                    tile_ref[dest, i, 0, :, wide:] = jnp.zeros((rows, width - wide), jnp.bfloat16)
            if not packed:
                continue
            rolled = [
                pltpu.roll(tile[:, start : start + LANES], shift, axis=1) for start in range(0, wide, LANES)
            ]
            for place in range(len(rolled) + 1):
                here = pl.ds(pl.multiple_of(base + place * LANES, LANES), LANES)
                if place == 0:
                    before = jnp.concatenate(
                        [pack_ref[dest, i, :, here].astype(jnp.float32) for dest in range(ndest)], axis=0
                    )
                else:
                    before = rolled[place - 1]
                after = rolled[place] if place < len(rolled) else jnp.zeros_like(before)
                window = jnp.where(low, before, after)
                for dest in range(ndest):
                    pack_ref[dest, i, :, here] = window[dest * rows : (dest + 1) * rows].astype(jnp.bfloat16)

    narrow = width - LANES
    if narrow > 0:
        pl.when(count <= narrow)(lambda: work(narrow))
        pl.when(count > narrow)(lambda: work(width))
    else:
        work(width)

    if packed:

        @pl.when(j == pl.num_programs(0) - 1)
        def _():
            main = main_ref.shape[3]
            main_ref[...] = pack_ref[:, :, :, :main]
            over_ref[...] = pack_ref[:, :, :, main : main + over_ref.shape[3]]


def tiles(ndest, first, tables, test_counts, left, shards, main):
    ntest, nsource, kmax, nq = left.shape
    nshard = len(shards)
    part, width = shards[0].shape[1:]
    rows = kmax // ndest
    packed = main is not None
    shapes = [jax.ShapeDtypeStruct((ndest, ntest, nsource, rows, width), jnp.bfloat16)]
    specs = [pl.BlockSpec((ndest, ntest, 1, rows, width), lambda j, *_: (0, 0, j, 0, 0))]
    scratch = []
    if packed:
        for columns in (main, nsource * width - main):
            shape = (ndest, ntest, rows, columns)
            shapes.append(jax.ShapeDtypeStruct(shape, jnp.bfloat16))
            specs.append(pl.BlockSpec(shape, lambda j, *_: (0, 0, 0, 0)))
        scratch.append(pltpu.VMEM((ndest, ntest, rows, nsource * width + LANES), jnp.bfloat16))
    return pl.pallas_call(
        functools.partial(tile_kernel, nshard, first, packed),
        grid_spec=pltpu.PrefetchScalarGridSpec(
            num_scalar_prefetch=4,
            grid=(nsource,),
            in_specs=[pl.BlockSpec((ntest, 1, kmax, nq), lambda j, *_: (0, j, 0, 0))]
            + [pl.BlockSpec((1, part, width), lambda j, *_: (j, 0, 0))] * nshard,
            out_specs=specs,
            scratch_shapes=scratch,
        ),
        out_shape=shapes,
        compiler_params=pltpu.CompilerParams(vmem_limit_bytes=VMEM_LIMIT),
        cost_estimate=pl.CostEstimate(
            flops=2 * ntest * nsource * kmax * width * nq,
            bytes_accessed=2 * ntest * nsource * kmax * (nq + width),
            transcendentals=0,
        ),
    )(*tables, test_counts, left, *shards)


def project_kernel(started, order_ref, tile_ref, coeff_ref, *refs):
    if started:
        start_ref, sum_ref, total_ref = refs
    else:
        *counts_refs, sum_ref, joined_ref, total_ref = refs
    j = pl.program_id(0)
    ndest, ntest, _, rows, _ = tile_ref.shape
    whole = [tile_ref[dest, i, 0] for i in range(ntest) for dest in range(ndest)]
    term = jnp.dot(jnp.concatenate(whole, axis=0), coeff_ref[0], preferred_element_type=jnp.float32)

    @pl.when(j == 0)
    def _():
        total_ref[...] = term + start_ref[...] if started else term

    @pl.when(j > 0)
    def _():
        total_ref[...] += term

    @pl.when(j == pl.num_programs(0) - 1)
    def _():
        if not started:
            sum_ref[...] = total_ref[...]
            nblock = counts_refs[0].shape[0]
            for place, counts_ref in enumerate(counts_refs):
                for k in range(nblock):
                    joined_ref[place * nblock + k] = counts_ref[k]
            return
        for i in range(ntest):
            for dest in range(ndest):
                top = (i * ndest + dest) * rows
                sum_ref[dest, i] = total_ref[top : top + rows, :].astype(sum_ref.dtype)


def project(order, first, tiles, coefficients, start=None, counts=()):
    ndest, ntest, nsource, rows, width = tiles.shape
    ncol = coefficients.shape[2]
    smem = pl.BlockSpec(memory_space=pltpu.SMEM)
    total_spec = pl.BlockSpec((ntest * ndest * rows, ncol), lambda j, order: (0, 0))
    started = start is not None
    if started:
        more, more_specs = [start], [total_spec]
        out_specs = pl.BlockSpec((ndest, ntest, rows, ncol), lambda j, order: (0, 0, 0, 0))
        out_shape = jax.ShapeDtypeStruct((ndest, ntest, rows, ncol), jnp.bfloat16)
    else:
        more, more_specs = list(counts), [smem] * len(counts)
        out_specs = (total_spec, smem)
        out_shape = (
            jax.ShapeDtypeStruct((ntest * ndest * rows, ncol), jnp.float32),
            jax.ShapeDtypeStruct((sum(part.shape[0] for part in counts),), jnp.int32),
        )
    return pl.pallas_call(
        functools.partial(project_kernel, started),
        grid_spec=pltpu.PrefetchScalarGridSpec(
            num_scalar_prefetch=1,
            grid=(nsource,),
            in_specs=[
                pl.BlockSpec((ndest, ntest, 1, rows, width), lambda j, order: (0, 0, j, 0, 0)),
                pl.BlockSpec((1, width, ncol), lambda j, order: (order[first + j], 0, 0)),
            ]
            + more_specs,
            out_specs=out_specs,
            scratch_shapes=[pltpu.VMEM((ntest * ndest * rows, ncol), jnp.float32)],
        ),
        out_shape=out_shape,
        compiler_params=pltpu.CompilerParams(vmem_limit_bytes=VMEM_LIMIT),
        cost_estimate=pl.CostEstimate(
            flops=2 * ndest * ntest * rows * width * ncol * nsource,
            bytes_accessed=2 * ndest * ntest * rows * width * nsource,
            transcendentals=0,
        ),
    )(order, tiles, coefficients, *more)


def unpack_kernel(cut, order_ref, counts_ref, offsets_ref, whole_ref, packed_ref, *refs):
    *part_refs, out_ref, sum_ref, rows_ref = refs
    sum_ref[...] = sum(part_ref[...].astype(jnp.float32) for part_ref in part_refs).astype(sum_ref.dtype)
    nsrc, _, _, rows, width = whole_ref.shape
    packed_width = packed_ref.shape[3]
    nall = out_ref.shape[2]
    nblock = nall // nsrc
    ntile = width // LANES
    step = 16 if rows % 16 == 0 else rows
    lanes = lax.broadcasted_iota(jnp.int32, (rows, LANES), 1)

    @pl.loop(0, nsrc, unroll=2)
    def _(source):
        for place in range(nblock):
            block = order_ref[source * nblock + place]
            target = source * nblock + block
            if place < cut:
                rows_ref[target] = whole_ref[source, 0, place].astype(jnp.float32)
                continue
            count = counts_ref[target]
            offset = offsets_ref[target]
            shift = offset % LANES
            base = offset - shift
            back = (LANES - shift) % LANES
            low = lanes < LANES - shift
            rolled = []
            for tile in range(ntile + 1):
                start = pl.multiple_of(jnp.minimum(base + tile * LANES, packed_width - LANES), LANES)
                piece = packed_ref[source, 0, :, pl.ds(start, LANES)].astype(jnp.float32)
                rolled.append(pltpu.roll(piece, back, axis=1))
            for tile in range(ntile):
                value = jnp.where(low, rolled[tile], rolled[tile + 1])
                value = jnp.where(lanes < count - tile * LANES, value, 0.0)
                rows_ref[target, :, tile * LANES : (tile + 1) * LANES] = value

    @pl.loop(0, nall // 16)
    def _(group):
        here = pl.ds(pl.multiple_of(group * 16, 16), 16)
        for top in range(0, rows, step):
            turned = jnp.transpose(rows_ref[here, top : top + step, :], (1, 0, 2))
            out_ref[0, top : top + step, here, :] = turned.astype(out_ref.dtype)


def unpack(cut, tables, whole, packed, parts):
    nsrc, ntest, _, rows, width = whole.shape
    packed_width = packed.shape[3]
    nall = tables[0].shape[0]
    sum_spec = pl.BlockSpec((1,) + parts[0].shape[1:], lambda i, *_: (i, 0, 0))
    return pl.pallas_call(
        functools.partial(unpack_kernel, cut),
        grid_spec=pltpu.PrefetchScalarGridSpec(
            num_scalar_prefetch=3,
            grid=(ntest,),
            in_specs=[
                pl.BlockSpec((nsrc, 1, cut, rows, width), lambda i, *_: (0, i, 0, 0, 0)),
                pl.BlockSpec((nsrc, 1, rows, packed_width), lambda i, *_: (0, i, 0, 0)),
            ]
            + [sum_spec] * len(parts),
            out_specs=(pl.BlockSpec((1, rows, nall, width), lambda i, *_: (i, 0, 0, 0)), sum_spec),
            scratch_shapes=[pltpu.VMEM((nall, rows, width), jnp.float32)],
        ),
        out_shape=(
            jax.ShapeDtypeStruct((ntest, rows, nall, width), jnp.bfloat16),
            jax.ShapeDtypeStruct(parts[0].shape, jnp.bfloat16),
        ),
        compiler_params=pltpu.CompilerParams(vmem_limit_bytes=SMALL_VMEM_LIMIT),
    )(*tables, whole, packed, *parts)


def body(
    test_points, test_basis, test_counts, source_points, source_basis, source_counts, coefficients
):
    nsource, part, kmax = source_basis.shape
    ntest = test_points.shape[0]
    nsrc = lax.axis_size("src")
    ntest_axis = lax.axis_size("test")
    me_test = lax.axis_index("test")
    cut = max(1, nsource * 3 // 8)

    held = {}

    def gather(name, shard, left):
        got = {0: shard}
        bits = list(bits_down(ntest_axis))
        for bit in bits:
            if bit == bits[-1]:
                names = [o for o in got if o != 0]
                tied = lax.optimization_barrier(tuple(got[o] for o in names) + (left,))
                got.update(zip(names, tied[:-1]))
                left = tied[-1]
            for offset in list(got):
                got[offset ^ bit] = exchange(got[offset], "test", bit)
            if bit == bits[0]:
                held[name] = got[bit]
        return [got[offset] for offset in sorted(got)], left

    most = (nsource - cut) * kmax
    main = min(most, -(-most * 18 // (25 * LANES)) * LANES)
    widths = [main, min(most, main + LANES), min(most, main + 2 * LANES), most]

    order, offsets, basis_a, basis_b = pick(cut, source_counts, source_basis)
    tables = (order, source_counts, offsets)
    me = jnp.reshape(me_test, (1,))
    test_points, source_points = test_points.transpose(1, 0, 2), source_points.transpose(1, 0, 2)

    left_a = left_products(ntest_axis, me, order, test_points, source_points, test_basis, 0, cut)
    shards_a, left_a = gather("a", basis_a, left_a)
    (tiles_a,) = tiles(nsrc, 0, tables, test_counts, left_a, shards_a, None)
    moved_a = lax.all_to_all(tiles_a, "src", split_axis=0, concat_axis=0, tiled=True)

    rest, _ = lax.optimization_barrier((basis_b, held["a"]))
    later, _ = lax.optimization_barrier((source_points, tiles_a))
    left_b = left_products(ntest_axis, me, order, test_points, later, test_basis, cut, nsource)
    shards_b, left_b = gather("b", rest, left_b)
    inner = max(1, nsrc // 4)
    counts, _ = lax.optimization_barrier((source_counts, left_b))
    far = [exchange(counts, "src", flip) for flip in range(inner, nsrc, inner)]
    tiles_b, packed, beyond = tiles(nsrc, cut, tables, test_counts, left_b, shards_b, main)
    packed, *far = lax.optimization_barrier((packed, *far))
    moved_b = lax.all_to_all(packed, "src", split_axis=0, concat_axis=0, tiled=True)

    sums, joined = project(order, 0, tiles_a, coefficients, counts=[source_counts] + far)
    groups = [joined] + [exchange(joined, "src", flip) for flip in range(1, inner)]
    sums = project(order, cut, tiles_b, coefficients, sums)
    parts = sum_rows(sums, "src")
    me_src, _ = lax.optimization_barrier((jnp.reshape(lax.axis_index("src"), (1,)), packed))
    all_counts, all_order, all_offsets, branch = all_tables(cut, nsource, widths, me_src, groups)
    spread = (all_order, all_counts, all_offsets)

    def finish(width, beyond, moved_a, moved_b, spread, parts):
        if width > main:
            more = lax.all_to_all(
                beyond[..., : width - main], "src", split_axis=0, concat_axis=0, tiled=True
            )
            moved_b = jnp.concatenate([moved_b, more], axis=3)
        return unpack(cut, spread, moved_a, moved_b, parts)

    return lax.switch(
        branch[0],
        [functools.partial(finish, width) for width in widths],
        beyond,
        moved_a,
        moved_b,
        spread,
        parts,
    )


def solution(mesh):
    return jax.shard_map(
        body,
        mesh=mesh,
        in_specs=(
            P("test", None, None),
            P("test", None, None),
            P("test"),
            P("src", None, None),
            P("src", "test", None),
            P("src"),
            P("src", None, None),
        ),
        out_specs=(P("test", "src", None, None), P("test", "src", None)),
        check_vma=False,
    )
```

```python
import functools

import jax
import jax.numpy as jnp
from jax import lax
from jax.experimental import pallas as pl
from jax.experimental.pallas import tpu as pltpu
from jax.sharding import PartitionSpec as P

softening = 0.0025
QBLOCK = 256
LANES = 128
VMEM_LIMIT = 255 * 256 * 1024
SMALL_VMEM_LIMIT = 32 * 1024 * 1024


def exchange(x, axis, flip):
    size = lax.axis_size(axis)
    return lax.ppermute(x, axis, [(a, a ^ flip) for a in range(size)])


def bits_down(size):
    bit = size // 2
    while bit >= 1:
        yield bit
        bit //= 2


def sum_rows(total, axis):
    size = lax.axis_size(axis)
    me = lax.axis_index(axis)
    held, bit = total, 1
    while held.shape[0] > 4:
        pairs = held.reshape((held.shape[0] // 2, 2) + held.shape[1:])
        mine = (me // bit) % 2
        keep = lax.dynamic_index_in_dim(pairs, mine, 1, keepdims=False)
        give = lax.dynamic_index_in_dim(pairs, 1 - mine, 1, keepdims=False)
        got = exchange(give, axis, bit)
        held = (keep.astype(jnp.float32) + got.astype(jnp.float32)).astype(held.dtype)
        bit *= 2
    mine = me // bit
    parts = [lax.dynamic_index_in_dim(held, mine, 0, keepdims=False)]
    for flip in range(1, held.shape[0]):
        give = lax.dynamic_index_in_dim(held, mine ^ flip, 0, keepdims=False)
        parts.append(exchange(give, axis, flip * bit))
    return parts


def rank_blocks(counts, cut):
    ranks = []
    for j, mine in enumerate(counts):
        rank = jnp.int32(0)
        for k, other in enumerate(counts):
            if k != j:
                ahead = other >= mine if k < j else other > mine
                rank += ahead.astype(jnp.int32)
        ranks.append(rank)
    offsets = []
    for j in range(len(counts)):
        offset = jnp.int32(0)
        for k, other in enumerate(counts):
            if k != j:
                offset += jnp.where((ranks[k] >= cut) & (ranks[k] < ranks[j]), other, 0)
        offsets.append(offset)
    return ranks, offsets


def copy_blocks(order_ref, first, source_ref, target_ref, sems):
    copies = [
        pltpu.make_async_copy(source_ref.at[order_ref[first + place]], target_ref.at[place], sems.at[place])
        for place in range(target_ref.shape[0])
    ]
    for copy in copies:
        copy.start()
    for copy in copies:
        copy.wait()


def pick_kernel(cut, counts_ref, basis_ref, order_ref, offsets_ref, out_ref, sems):
    nblock = basis_ref.shape[0]
    ranks, offsets = rank_blocks([counts_ref[j] for j in range(nblock)], cut)
    for j in range(nblock):
        order_ref[ranks[j]] = jnp.int32(j)
        offsets_ref[j] = offsets[j]
    copy_blocks(order_ref, 0, basis_ref, out_ref, sems)


def pick(cut, counts, basis):
    nblock = basis.shape[0]
    smem, vmem = pl.BlockSpec(memory_space=pltpu.SMEM), pl.BlockSpec(memory_space=pltpu.VMEM)
    return pl.pallas_call(
        functools.partial(pick_kernel, cut),
        out_shape=(
            jax.ShapeDtypeStruct((nblock,), jnp.int32),
            jax.ShapeDtypeStruct((nblock,), jnp.int32),
            jax.ShapeDtypeStruct((cut,) + basis.shape[1:], basis.dtype),
        ),
        in_specs=[smem, pl.BlockSpec(memory_space=pl.ANY)],
        out_specs=(smem, smem, vmem),
        scratch_shapes=[pltpu.SemaphoreType.DMA((cut,))],
        compiler_params=pltpu.CompilerParams(vmem_limit_bytes=VMEM_LIMIT),
    )(counts, basis)


def take_kernel(first, order_ref, basis_ref, out_ref, sems):
    copy_blocks(order_ref, first, basis_ref, out_ref, sems)


def take(first, order, basis):
    shape = (basis.shape[0] - first,) + basis.shape[1:]
    return pl.pallas_call(
        functools.partial(take_kernel, first),
        out_shape=jax.ShapeDtypeStruct(shape, basis.dtype),
        in_specs=[pl.BlockSpec(memory_space=pltpu.SMEM), pl.BlockSpec(memory_space=pl.ANY)],
        out_specs=pl.BlockSpec(memory_space=pltpu.VMEM),
        scratch_shapes=[pltpu.SemaphoreType.DMA((shape[0],))],
        compiler_params=pltpu.CompilerParams(vmem_limit_bytes=VMEM_LIMIT),
    )(order, basis)


def tables_kernel(cut, nblock, widths, me_ref, *refs):
    *group_refs, counts_ref, order_ref, offsets_ref, branch_ref, joined_ref = refs
    group, inner = group_refs[0].shape[0], len(group_refs)
    for place, group_ref in enumerate(group_refs):
        for k in range(group):
            joined_ref[place * group + k] = group_ref[k]

    def step(source, need):
        base = source * nblock
        offset = source ^ me_ref[0]
        theirs = (offset % inner) * group + (offset // inner) * nblock
        counts = [joined_ref[theirs + j] for j in range(nblock)]
        ranks, offsets = rank_blocks(counts, cut)
        used = jnp.int32(0)
        for j in range(nblock):
            counts_ref[base + j] = counts[j]
            order_ref[base + ranks[j]] = jnp.int32(j)
            offsets_ref[base + j] = offsets[j]
            used += jnp.where(ranks[j] >= cut, counts[j], 0)
        return jnp.maximum(need, used)

    need = lax.fori_loop(0, counts_ref.shape[0] // nblock, step, jnp.int32(0))
    branch = jnp.int32(0)
    for width in widths[:-1]:
        branch += (need > width).astype(jnp.int32)
    branch_ref[0] = branch


def all_tables(cut, nblock, widths, me, groups):
    smem = pl.BlockSpec(memory_space=pltpu.SMEM)
    total = sum(group.shape[0] for group in groups)
    table = jax.ShapeDtypeStruct((total,), jnp.int32)
    return pl.pallas_call(
        functools.partial(tables_kernel, cut, nblock, widths),
        out_shape=(table, table, table, jax.ShapeDtypeStruct((1,), jnp.int32)),
        in_specs=[smem] * (1 + len(groups)),
        out_specs=(smem,) * 4,
        scratch_shapes=[pltpu.SMEM((total,), jnp.int32)],
    )(me, *groups)


NFEATURE = 64


def fill_features(rows_ref, points, is_test):
    def three_terms(x):
        high = x.astype(jnp.bfloat16).astype(jnp.float32)
        middle = (x - high).astype(jnp.bfloat16).astype(jnp.float32)
        return high, middle, x - high - middle

    centred = points - 0.5
    norm = jnp.sum(centred * centred, axis=0, keepdims=True)
    terms = three_terms(centred)
    norms = three_terms(norm + softening if is_test else norm)
    for a in range(3):
        for b in range(3):
            place = 3 * (3 * a + b)
            rows_ref[place : place + 3, :] = -2.0 * terms[a] if is_test else terms[b]
    for a in range(3):
        rows_ref[27 + a : 28 + a, :] = norms[a] if is_test else jnp.ones_like(norm)
        rows_ref[30 + a : 31 + a, :] = jnp.ones_like(norm) if is_test else norms[a]


def left_kernel(
    nshard, first, me_ref, order_ref, test_ref, source_ref, basis_ref, out_ref,
    rows_ref, features_ref, turned_ref, near_ref,
):
    j = pl.program_id(0)
    ntest = test_ref.shape[1]
    nq = source_ref.shape[2]
    part = nq // nshard
    block = min(QBLOCK, nq)

    @pl.when(j == 0)
    def _():
        rows_ref[...] = jnp.zeros_like(rows_ref)
        for i in range(ntest):
            fill_features(rows_ref, test_ref[:, i, :], True)
            features_ref[i] = rows_ref[...].T.astype(jnp.bfloat16)
            turned_ref[i] = basis_ref[i].T

    source = order_ref[first + j]
    for comp in range(3):
        rows_ref[comp : comp + 1, :] = source_ref[comp, pl.ds(source, 1), :]
    pieces = []
    for offset in range(nshard):
        start = pl.multiple_of((me_ref[0] ^ offset) * part, part)
        pieces.append(rows_ref[0:3, pl.ds(start, part)])
    fill_features(rows_ref, jnp.concatenate(pieces, axis=1), False)
    near_ref[...] = rows_ref[...].astype(jnp.bfloat16)

    steps = [(i, start) for i in range(ntest) for start in range(0, nq, block)]

    def kernel_block(i, start):
        squared = jnp.dot(
            features_ref[i], near_ref[:, start : start + block], preferred_element_type=jnp.float32
        )
        return lax.rsqrt(squared.astype(jnp.bfloat16))

    ready = kernel_block(*steps[0])
    for place, (i, start) in enumerate(steps):
        now = ready
        if place + 1 < len(steps):
            ready = kernel_block(*steps[place + 1])
        out_ref[i, 0, :, start : start + block] = jnp.dot(
            turned_ref[i], now, preferred_element_type=jnp.float32
        ).astype(jnp.bfloat16)


def left_products(nshard, me, order, test_points, source_points, test_basis, first, last):
    _, ntest, npoint = test_points.shape
    nall, nq = source_points.shape[1:]
    kmax = test_basis.shape[2]
    nsource = last - first
    return pl.pallas_call(
        functools.partial(left_kernel, nshard, first),
        grid_spec=pltpu.PrefetchScalarGridSpec(
            num_scalar_prefetch=2,
            grid=(nsource,),
            in_specs=[
                pl.BlockSpec((3, ntest, npoint), lambda j, *_: (0, 0, 0)),
                pl.BlockSpec((3, nall, nq), lambda j, *_: (0, 0, 0)),
                pl.BlockSpec((ntest, npoint, kmax), lambda j, *_: (0, 0, 0)),
            ],
            out_specs=pl.BlockSpec((ntest, 1, kmax, nq), lambda j, *_: (0, j, 0, 0)),
            scratch_shapes=[
                pltpu.VMEM((NFEATURE, npoint), jnp.float32),
                pltpu.VMEM((ntest, npoint, NFEATURE), jnp.bfloat16),
                pltpu.VMEM((ntest, kmax, npoint), jnp.bfloat16),
                pltpu.VMEM((NFEATURE, nq), jnp.bfloat16),
            ],
        ),
        out_shape=jax.ShapeDtypeStruct((ntest, nsource, kmax, nq), jnp.bfloat16),
        compiler_params=pltpu.CompilerParams(vmem_limit_bytes=VMEM_LIMIT),
        cost_estimate=pl.CostEstimate(
            flops=2 * ntest * nsource * npoint * nq * kmax,
            bytes_accessed=2 * ntest * nsource * kmax * nq,
            transcendentals=ntest * nsource * npoint * nq,
        ),
    )(me, order, test_points, source_points, test_basis)


def tile_kernel(nshard, first, packed, *refs):
    order_ref, source_counts_ref, offsets_ref, test_counts_ref, left_ref = refs[:5]
    shard_refs = refs[5 : 5 + nshard]
    j = pl.program_id(0)
    if packed:
        tile_ref, main_ref, over_ref, pack_ref = refs[5 + nshard :]
    else:
        (tile_ref,) = refs[5 + nshard :]
    ntest, _, kmax, _ = left_ref.shape
    ndest, _, _, rows, width = tile_ref.shape
    count = source_counts_ref[order_ref[first + j]]

    def work(wide):
        side = jnp.concatenate([shard_ref[0, :, :wide] for shard_ref in shard_refs], axis=0)
        row_ids = lax.broadcasted_iota(jnp.int32, (kmax, wide), 0)
        column_ids = lax.broadcasted_iota(jnp.int32, (kmax, wide), 1)
        products = [
            jnp.dot(left_ref[i, 0], side, preferred_element_type=jnp.float32) for i in range(ntest)
        ]
        if packed:
            offset = offsets_ref[order_ref[first + j]]
            shift = offset % LANES
            base = offset - shift
            low = lax.broadcasted_iota(jnp.int32, (kmax, LANES), 1) < shift
        for i in range(ntest):
            used = (row_ids < test_counts_ref[i]) & (column_ids < count)
            tile = jnp.where(used, products[i], 0.0)
            for dest in range(ndest):
                tile_ref[dest, i, 0, :, :wide] = tile[dest * rows : (dest + 1) * rows].astype(jnp.bfloat16)
                if wide < width:
                    tile_ref[dest, i, 0, :, wide:] = jnp.zeros((rows, width - wide), jnp.bfloat16)
            if not packed:
                continue
            rolled = [
                pltpu.roll(tile[:, start : start + LANES], shift, axis=1) for start in range(0, wide, LANES)
            ]
            for place in range(len(rolled) + 1):
                here = pl.ds(pl.multiple_of(base + place * LANES, LANES), LANES)
                if place == 0:
                    before = jnp.concatenate(
                        [pack_ref[dest, i, :, here].astype(jnp.float32) for dest in range(ndest)], axis=0
                    )
                else:
                    before = rolled[place - 1]
                after = rolled[place] if place < len(rolled) else jnp.zeros_like(before)
                window = jnp.where(low, before, after)
                for dest in range(ndest):
                    pack_ref[dest, i, :, here] = window[dest * rows : (dest + 1) * rows].astype(jnp.bfloat16)

    narrow = width - LANES
    if narrow > 0:
        pl.when(count <= narrow)(lambda: work(narrow))
        pl.when(count > narrow)(lambda: work(width))
    else:
        work(width)

    if packed:

        @pl.when(j == pl.num_programs(0) - 1)
        def _():
            main = main_ref.shape[3]
            main_ref[...] = pack_ref[:, :, :, :main]
            over_ref[...] = pack_ref[:, :, :, main : main + over_ref.shape[3]]


def tiles(ndest, first, tables, test_counts, left, shards, main):
    ntest, nsource, kmax, nq = left.shape
    nshard = len(shards)
    part, width = shards[0].shape[1:]
    rows = kmax // ndest
    packed = main is not None
    shapes = [jax.ShapeDtypeStruct((ndest, ntest, nsource, rows, width), jnp.bfloat16)]
    specs = [pl.BlockSpec((ndest, ntest, 1, rows, width), lambda j, *_: (0, 0, j, 0, 0))]
    scratch = []
    if packed:
        for columns in (main, nsource * width - main):
            shape = (ndest, ntest, rows, columns)
            shapes.append(jax.ShapeDtypeStruct(shape, jnp.bfloat16))
            specs.append(pl.BlockSpec(shape, lambda j, *_: (0, 0, 0, 0)))
        scratch.append(pltpu.VMEM((ndest, ntest, rows, nsource * width + LANES), jnp.bfloat16))
    return pl.pallas_call(
        functools.partial(tile_kernel, nshard, first, packed),
        grid_spec=pltpu.PrefetchScalarGridSpec(
            num_scalar_prefetch=4,
            grid=(nsource,),
            in_specs=[pl.BlockSpec((ntest, 1, kmax, nq), lambda j, *_: (0, j, 0, 0))]
            + [pl.BlockSpec((1, part, width), lambda j, *_: (j, 0, 0))] * nshard,
            out_specs=specs,
            scratch_shapes=scratch,
        ),
        out_shape=shapes,
        compiler_params=pltpu.CompilerParams(vmem_limit_bytes=VMEM_LIMIT),
        cost_estimate=pl.CostEstimate(
            flops=2 * ntest * nsource * kmax * width * nq,
            bytes_accessed=2 * ntest * nsource * kmax * (nq + width),
            transcendentals=0,
        ),
    )(*tables, test_counts, left, *shards)


def project_kernel(started, order_ref, tile_ref, coeff_ref, *refs):
    if started:
        start_ref, sum_ref, total_ref = refs
    else:
        *counts_refs, sum_ref, joined_ref, total_ref = refs
    j = pl.program_id(0)
    ndest, ntest, _, rows, _ = tile_ref.shape
    whole = [tile_ref[dest, i, 0] for i in range(ntest) for dest in range(ndest)]
    term = jnp.dot(jnp.concatenate(whole, axis=0), coeff_ref[0], preferred_element_type=jnp.float32)

    @pl.when(j == 0)
    def _():
        total_ref[...] = term + start_ref[...] if started else term

    @pl.when(j > 0)
    def _():
        total_ref[...] += term

    @pl.when(j == pl.num_programs(0) - 1)
    def _():
        if not started:
            sum_ref[...] = total_ref[...]
            nblock = counts_refs[0].shape[0]
            for place, counts_ref in enumerate(counts_refs):
                for k in range(nblock):
                    joined_ref[place * nblock + k] = counts_ref[k]
            return
        for i in range(ntest):
            for dest in range(ndest):
                top = (i * ndest + dest) * rows
                sum_ref[dest, i] = total_ref[top : top + rows, :].astype(sum_ref.dtype)


def project(order, first, tiles, coefficients, start=None, counts=()):
    ndest, ntest, nsource, rows, width = tiles.shape
    ncol = coefficients.shape[2]
    smem = pl.BlockSpec(memory_space=pltpu.SMEM)
    total_spec = pl.BlockSpec((ntest * ndest * rows, ncol), lambda j, order: (0, 0))
    started = start is not None
    if started:
        more, more_specs = [start], [total_spec]
        out_specs = pl.BlockSpec((ndest, ntest, rows, ncol), lambda j, order: (0, 0, 0, 0))
        out_shape = jax.ShapeDtypeStruct((ndest, ntest, rows, ncol), jnp.bfloat16)
    else:
        more, more_specs = list(counts), [smem] * len(counts)
        out_specs = (total_spec, smem)
        out_shape = (
            jax.ShapeDtypeStruct((ntest * ndest * rows, ncol), jnp.float32),
            jax.ShapeDtypeStruct((sum(part.shape[0] for part in counts),), jnp.int32),
        )
    return pl.pallas_call(
        functools.partial(project_kernel, started),
        grid_spec=pltpu.PrefetchScalarGridSpec(
            num_scalar_prefetch=1,
            grid=(nsource,),
            in_specs=[
                pl.BlockSpec((ndest, ntest, 1, rows, width), lambda j, order: (0, 0, j, 0, 0)),
                pl.BlockSpec((1, width, ncol), lambda j, order: (order[first + j], 0, 0)),
            ]
            + more_specs,
            out_specs=out_specs,
            scratch_shapes=[pltpu.VMEM((ntest * ndest * rows, ncol), jnp.float32)],
        ),
        out_shape=out_shape,
        compiler_params=pltpu.CompilerParams(vmem_limit_bytes=VMEM_LIMIT),
        cost_estimate=pl.CostEstimate(
            flops=2 * ndest * ntest * rows * width * ncol * nsource,
            bytes_accessed=2 * ndest * ntest * rows * width * nsource,
            transcendentals=0,
        ),
    )(order, tiles, coefficients, *more)


def unpack_kernel(cut, order_ref, counts_ref, offsets_ref, whole_ref, packed_ref, *refs):
    *part_refs, out_ref, sum_ref, rows_ref = refs
    sum_ref[...] = sum(part_ref[...].astype(jnp.float32) for part_ref in part_refs).astype(sum_ref.dtype)
    nsrc, _, _, rows, width = whole_ref.shape
    packed_width = packed_ref.shape[3]
    nall = out_ref.shape[2]
    nblock = nall // nsrc
    ntile = width // LANES
    step = 16 if rows % 16 == 0 else rows
    lanes = lax.broadcasted_iota(jnp.int32, (rows, LANES), 1)

    @pl.loop(0, nsrc, unroll=2)
    def _(source):
        for place in range(nblock):
            block = order_ref[source * nblock + place]
            target = source * nblock + block
            if place < cut:
                rows_ref[target] = whole_ref[source, 0, place].astype(jnp.float32)
                continue
            count = counts_ref[target]
            offset = offsets_ref[target]
            shift = offset % LANES
            base = offset - shift
            back = (LANES - shift) % LANES
            low = lanes < LANES - shift
            rolled = []
            for tile in range(ntile + 1):
                start = pl.multiple_of(jnp.minimum(base + tile * LANES, packed_width - LANES), LANES)
                piece = packed_ref[source, 0, :, pl.ds(start, LANES)].astype(jnp.float32)
                rolled.append(pltpu.roll(piece, back, axis=1))
            for tile in range(ntile):
                value = jnp.where(low, rolled[tile], rolled[tile + 1])
                value = jnp.where(lanes < count - tile * LANES, value, 0.0)
                rows_ref[target, :, tile * LANES : (tile + 1) * LANES] = value

    @pl.loop(0, nall // 16)
    def _(group):
        here = pl.ds(pl.multiple_of(group * 16, 16), 16)
        for top in range(0, rows, step):
            turned = jnp.transpose(rows_ref[here, top : top + step, :], (1, 0, 2))
            out_ref[0, top : top + step, here, :] = turned.astype(out_ref.dtype)


def unpack(cut, tables, whole, packed, parts):
    nsrc, ntest, _, rows, width = whole.shape
    packed_width = packed.shape[3]
    nall = tables[0].shape[0]
    sum_spec = pl.BlockSpec((1,) + parts[0].shape[1:], lambda i, *_: (i, 0, 0))
    return pl.pallas_call(
        functools.partial(unpack_kernel, cut),
        grid_spec=pltpu.PrefetchScalarGridSpec(
            num_scalar_prefetch=3,
            grid=(ntest,),
            in_specs=[
                pl.BlockSpec((nsrc, 1, cut, rows, width), lambda i, *_: (0, i, 0, 0, 0)),
                pl.BlockSpec((nsrc, 1, rows, packed_width), lambda i, *_: (0, i, 0, 0)),
            ]
            + [sum_spec] * len(parts),
            out_specs=(pl.BlockSpec((1, rows, nall, width), lambda i, *_: (i, 0, 0, 0)), sum_spec),
            scratch_shapes=[pltpu.VMEM((nall, rows, width), jnp.float32)],
        ),
        out_shape=(
            jax.ShapeDtypeStruct((ntest, rows, nall, width), jnp.bfloat16),
            jax.ShapeDtypeStruct(parts[0].shape, jnp.bfloat16),
        ),
        compiler_params=pltpu.CompilerParams(vmem_limit_bytes=SMALL_VMEM_LIMIT),
    )(*tables, whole, packed, *parts)


def body(
    test_points, test_basis, test_counts, source_points, source_basis, source_counts, coefficients
):
    nsource, part, kmax = source_basis.shape
    ntest = test_points.shape[0]
    nsrc = lax.axis_size("src")
    ntest_axis = lax.axis_size("test")
    me_test = lax.axis_index("test")
    cut = max(1, nsource * 3 // 8)

    held = {}

    def gather(name, shard, left):
        got = {0: shard}
        bits = list(bits_down(ntest_axis))
        for bit in bits:
            if bit == bits[-1]:
                names = [o for o in got if o != 0]
                tied = lax.optimization_barrier(tuple(got[o] for o in names) + (left,))
                got.update(zip(names, tied[:-1]))
                left = tied[-1]
            for offset in list(got):
                got[offset ^ bit] = exchange(got[offset], "test", bit)
            if bit == bits[0]:
                held[name] = got[bit]
        return [got[offset] for offset in sorted(got)], left

    most = (nsource - cut) * kmax
    main = min(most, -(-most * 18 // (25 * LANES)) * LANES)
    widths = [main, min(most, main + LANES), min(most, main + 2 * LANES), most]

    order, offsets, basis_a = pick(cut, source_counts, source_basis)
    tables = (order, source_counts, offsets)
    me = jnp.reshape(me_test, (1,))
    test_points, source_points = test_points.transpose(1, 0, 2), source_points.transpose(1, 0, 2)

    left_a = left_products(ntest_axis, me, order, test_points, source_points, test_basis, 0, cut)
    shards_a, left_a = gather("a", basis_a, left_a)
    (tiles_a,) = tiles(nsrc, 0, tables, test_counts, left_a, shards_a, None)
    moved_a = lax.all_to_all(tiles_a, "src", split_axis=0, concat_axis=0, tiled=True)

    later_basis, _ = lax.optimization_barrier((source_basis, tiles_a))
    rest, _ = lax.optimization_barrier((take(cut, order, later_basis), held["a"]))
    later, _ = lax.optimization_barrier((source_points, tiles_a))
    left_b = left_products(ntest_axis, me, order, test_points, later, test_basis, cut, nsource)
    shards_b, left_b = gather("b", rest, left_b)
    inner = max(1, nsrc // 4)
    counts, _ = lax.optimization_barrier((source_counts, left_b))
    far = [exchange(counts, "src", flip) for flip in range(inner, nsrc, inner)]
    tiles_b, packed, beyond = tiles(nsrc, cut, tables, test_counts, left_b, shards_b, main)
    packed, *far = lax.optimization_barrier((packed, *far))
    moved_b = lax.all_to_all(packed, "src", split_axis=0, concat_axis=0, tiled=True)

    sums, joined = project(order, 0, tiles_a, coefficients, counts=[source_counts] + far)
    groups = [joined] + [exchange(joined, "src", flip) for flip in range(1, inner)]
    sums = project(order, cut, tiles_b, coefficients, sums)
    parts = sum_rows(sums, "src")
    me_src, _ = lax.optimization_barrier((jnp.reshape(lax.axis_index("src"), (1,)), packed))
    all_counts, all_order, all_offsets, branch = all_tables(cut, nsource, widths, me_src, groups)
    spread = (all_order, all_counts, all_offsets)

    def finish(width, beyond, moved_a, moved_b, spread, parts):
        if width > main:
            more = lax.all_to_all(
                beyond[..., : width - main], "src", split_axis=0, concat_axis=0, tiled=True
            )
            moved_b = jnp.concatenate([moved_b, more], axis=3)
        return unpack(cut, spread, moved_a, moved_b, parts)

    return lax.switch(
        branch[0],
        [functools.partial(finish, width) for width in widths],
        beyond,
        moved_a,
        moved_b,
        spread,
        parts,
    )


def solution(mesh):
    return jax.shard_map(
        body,
        mesh=mesh,
        in_specs=(
            P("test", None, None),
            P("test", None, None),
            P("test"),
            P("src", None, None),
            P("src", "test", None),
            P("src"),
            P("src", None, None),
        ),
        out_specs=(P("test", "src", None, None), P("test", "src", None)),
        check_vma=False,
    )
```

```python
import functools

import jax
import jax.numpy as jnp
from jax import lax
from jax.experimental import pallas as pl
from jax.experimental.pallas import tpu as pltpu
from jax.sharding import PartitionSpec as P

softening = 0.0025
QBLOCK = 256
LANES = 128
VMEM_LIMIT = 255 * 256 * 1024
SMALL_VMEM_LIMIT = 32 * 1024 * 1024


def exchange(x, axis, flip):
    size = lax.axis_size(axis)
    return lax.ppermute(x, axis, [(a, a ^ flip) for a in range(size)])


def bits_down(size):
    bit = size // 2
    while bit >= 1:
        yield bit
        bit //= 2


def sum_rows(total, axis):
    size = lax.axis_size(axis)
    me = lax.axis_index(axis)
    held, bit = total, 1
    while held.shape[0] > 2:
        pairs = held.reshape((held.shape[0] // 2, 2) + held.shape[1:])
        mine = (me // bit) % 2
        keep = lax.dynamic_index_in_dim(pairs, mine, 1, keepdims=False)
        give = lax.dynamic_index_in_dim(pairs, 1 - mine, 1, keepdims=False)
        got = exchange(give, axis, bit)
        held = (keep.astype(jnp.float32) + got.astype(jnp.float32)).astype(held.dtype)
        bit *= 2
    mine = me // bit
    parts = [lax.dynamic_index_in_dim(held, mine, 0, keepdims=False)]
    for flip in range(1, held.shape[0]):
        give = lax.dynamic_index_in_dim(held, mine ^ flip, 0, keepdims=False)
        parts.append(exchange(give, axis, flip * bit))
    return parts


def rank_blocks(counts, cut):
    ranks = []
    for j, mine in enumerate(counts):
        rank = jnp.int32(0)
        for k, other in enumerate(counts):
            if k != j:
                ahead = other >= mine if k < j else other > mine
                rank += ahead.astype(jnp.int32)
        ranks.append(rank)
    offsets = []
    for j in range(len(counts)):
        offset = jnp.int32(0)
        for k, other in enumerate(counts):
            if k != j:
                offset += jnp.where((ranks[k] >= cut) & (ranks[k] < ranks[j]), other, 0)
        offsets.append(offset)
    return ranks, offsets


def pick_kernel(cut, counts_ref, basis_ref, order_ref, offsets_ref, first_ref, rest_ref):
    nblock = basis_ref.shape[0]
    ranks, offsets = rank_blocks([counts_ref[j] for j in range(nblock)], cut)
    for j in range(nblock):
        order_ref[ranks[j]] = jnp.int32(j)
        offsets_ref[j] = offsets[j]
    for place in range(nblock):
        block = basis_ref[order_ref[place]]
        if place < cut:
            first_ref[place] = block
        else:
            rest_ref[place - cut] = block


def pick(cut, counts, basis):
    nblock = basis.shape[0]
    smem, vmem = pl.BlockSpec(memory_space=pltpu.SMEM), pl.BlockSpec(memory_space=pltpu.VMEM)
    return pl.pallas_call(
        functools.partial(pick_kernel, cut),
        out_shape=(
            jax.ShapeDtypeStruct((nblock,), jnp.int32),
            jax.ShapeDtypeStruct((nblock,), jnp.int32),
            jax.ShapeDtypeStruct((cut,) + basis.shape[1:], basis.dtype),
            jax.ShapeDtypeStruct((nblock - cut,) + basis.shape[1:], basis.dtype),
        ),
        in_specs=[smem, vmem],
        out_specs=(smem, smem, vmem, vmem),
        compiler_params=pltpu.CompilerParams(vmem_limit_bytes=VMEM_LIMIT),
    )(counts, basis)


def tables_kernel(cut, nblock, widths, me_ref, *refs):
    *group_refs, counts_ref, order_ref, offsets_ref, branch_ref, joined_ref = refs
    group, inner = group_refs[0].shape[0], len(group_refs)
    for place, group_ref in enumerate(group_refs):
        for k in range(group):
            joined_ref[place * group + k] = group_ref[k]

    def step(source, need):
        base = source * nblock
        offset = source ^ me_ref[0]
        theirs = (offset % inner) * group + (offset // inner) * nblock
        counts = [joined_ref[theirs + j] for j in range(nblock)]
        ranks, offsets = rank_blocks(counts, cut)
        used = jnp.int32(0)
        for j in range(nblock):
            counts_ref[base + j] = counts[j]
            order_ref[base + ranks[j]] = jnp.int32(j)
            offsets_ref[base + j] = offsets[j]
            used += jnp.where(ranks[j] >= cut, counts[j], 0)
        return jnp.maximum(need, used)

    need = lax.fori_loop(0, counts_ref.shape[0] // nblock, step, jnp.int32(0))
    branch = jnp.int32(0)
    for width in widths[:-1]:
        branch += (need > width).astype(jnp.int32)
    branch_ref[0] = branch


def all_tables(cut, nblock, widths, me, groups):
    smem = pl.BlockSpec(memory_space=pltpu.SMEM)
    total = sum(group.shape[0] for group in groups)
    table = jax.ShapeDtypeStruct((total,), jnp.int32)
    return pl.pallas_call(
        functools.partial(tables_kernel, cut, nblock, widths),
        out_shape=(table, table, table, jax.ShapeDtypeStruct((1,), jnp.int32)),
        in_specs=[smem] * (1 + len(groups)),
        out_specs=(smem,) * 4,
        scratch_shapes=[pltpu.SMEM((total,), jnp.int32)],
    )(me, *groups)


NFEATURE = 128


def fill_features(rows_ref, points, is_test):
    def three_terms(x):
        high = x.astype(jnp.bfloat16).astype(jnp.float32)
        middle = (x - high).astype(jnp.bfloat16).astype(jnp.float32)
        return high, middle, x - high - middle

    centred = points - 0.5
    norm = jnp.sum(centred * centred, axis=0, keepdims=True)
    terms = three_terms(centred)
    norms = three_terms(norm + softening if is_test else norm)
    for a in range(3):
        for b in range(3):
            place = 3 * (3 * a + b)
            rows_ref[place : place + 3, :] = -2.0 * terms[a] if is_test else terms[b]
    for a in range(3):
        rows_ref[27 + a : 28 + a, :] = norms[a] if is_test else jnp.ones_like(norm)
        rows_ref[30 + a : 31 + a, :] = jnp.ones_like(norm) if is_test else norms[a]


def left_kernel(
    nshard, first, me_ref, order_ref, test_ref, source_ref, basis_ref, out_ref,
    rows_ref, features_ref, turned_ref, near_ref,
):
    j = pl.program_id(0)
    ntest = test_ref.shape[1]
    nq = source_ref.shape[2]
    part = nq // nshard
    block = min(QBLOCK, nq)

    @pl.when(j == 0)
    def _():
        rows_ref[...] = jnp.zeros_like(rows_ref)
        for i in range(ntest):
            fill_features(rows_ref, test_ref[:, i, :], True)
            features_ref[i] = rows_ref[...].T.astype(jnp.bfloat16)
            turned_ref[i] = basis_ref[i].T

    source = order_ref[first + j]
    for comp in range(3):
        rows_ref[comp : comp + 1, :] = source_ref[comp, pl.ds(source, 1), :]
    pieces = []
    for offset in range(nshard):
        start = pl.multiple_of((me_ref[0] ^ offset) * part, part)
        pieces.append(rows_ref[0:3, pl.ds(start, part)])
    fill_features(rows_ref, jnp.concatenate(pieces, axis=1), False)
    near_ref[...] = rows_ref[...].astype(jnp.bfloat16)

    steps = [(i, start) for i in range(ntest) for start in range(0, nq, block)]

    def kernel_block(i, start):
        squared = jnp.dot(
            features_ref[i], near_ref[:, start : start + block], preferred_element_type=jnp.float32
        )
        return lax.rsqrt(squared.astype(jnp.bfloat16))

    ready = kernel_block(*steps[0])
    for place, (i, start) in enumerate(steps):
        now = ready
        if place + 1 < len(steps):
            ready = kernel_block(*steps[place + 1])
        out_ref[i, 0, :, start : start + block] = jnp.dot(
            turned_ref[i], now, preferred_element_type=jnp.float32
        ).astype(jnp.bfloat16)


def left_products(nshard, me, order, test_points, source_points, test_basis, first, last):
    _, ntest, npoint = test_points.shape
    nall, nq = source_points.shape[1:]
    kmax = test_basis.shape[2]
    nsource = last - first
    return pl.pallas_call(
        functools.partial(left_kernel, nshard, first),
        grid_spec=pltpu.PrefetchScalarGridSpec(
            num_scalar_prefetch=2,
            grid=(nsource,),
            in_specs=[
                pl.BlockSpec((3, ntest, npoint), lambda j, *_: (0, 0, 0)),
                pl.BlockSpec((3, nall, nq), lambda j, *_: (0, 0, 0)),
                pl.BlockSpec((ntest, npoint, kmax), lambda j, *_: (0, 0, 0)),
            ],
            out_specs=pl.BlockSpec((ntest, 1, kmax, nq), lambda j, *_: (0, j, 0, 0)),
            scratch_shapes=[
                pltpu.VMEM((NFEATURE, npoint), jnp.float32),
                pltpu.VMEM((ntest, npoint, NFEATURE), jnp.bfloat16),
                pltpu.VMEM((ntest, kmax, npoint), jnp.bfloat16),
                pltpu.VMEM((NFEATURE, nq), jnp.bfloat16),
            ],
        ),
        out_shape=jax.ShapeDtypeStruct((ntest, nsource, kmax, nq), jnp.bfloat16),
        compiler_params=pltpu.CompilerParams(vmem_limit_bytes=VMEM_LIMIT),
        cost_estimate=pl.CostEstimate(
            flops=2 * ntest * nsource * npoint * nq * kmax,
            bytes_accessed=2 * ntest * nsource * kmax * nq,
            transcendentals=ntest * nsource * npoint * nq,
        ),
    )(me, order, test_points, source_points, test_basis)


def tile_kernel(nshard, first, packed, *refs):
    order_ref, source_counts_ref, offsets_ref, test_counts_ref, left_ref = refs[:5]
    shard_refs = refs[5 : 5 + nshard]
    j = pl.program_id(0)
    if packed:
        tile_ref, main_ref, over_ref, pack_ref = refs[5 + nshard :]
    else:
        (tile_ref,) = refs[5 + nshard :]
    ntest, _, kmax, _ = left_ref.shape
    ndest, _, _, rows, width = tile_ref.shape
    count = source_counts_ref[order_ref[first + j]]

    def work(wide):
        side = jnp.concatenate([shard_ref[0, :, :wide] for shard_ref in shard_refs], axis=0)
        row_ids = lax.broadcasted_iota(jnp.int32, (kmax, wide), 0)
        column_ids = lax.broadcasted_iota(jnp.int32, (kmax, wide), 1)
        products = [
            jnp.dot(left_ref[i, 0], side, preferred_element_type=jnp.float32) for i in range(ntest)
        ]
        if packed:
            offset = offsets_ref[order_ref[first + j]]
            shift = offset % LANES
            base = offset - shift
            low = lax.broadcasted_iota(jnp.int32, (kmax, LANES), 1) < shift
        for i in range(ntest):
            used = (row_ids < test_counts_ref[i]) & (column_ids < count)
            tile = jnp.where(used, products[i], 0.0)
            for dest in range(ndest):
                tile_ref[dest, i, 0, :, :wide] = tile[dest * rows : (dest + 1) * rows].astype(jnp.bfloat16)
                if wide < width:
                    tile_ref[dest, i, 0, :, wide:] = jnp.zeros((rows, width - wide), jnp.bfloat16)
            if not packed:
                continue
            rolled = [
                pltpu.roll(tile[:, start : start + LANES], shift, axis=1) for start in range(0, wide, LANES)
            ]
            for place in range(len(rolled) + 1):
                here = pl.ds(pl.multiple_of(base + place * LANES, LANES), LANES)
                if place == 0:
                    before = jnp.concatenate(
                        [pack_ref[dest, i, :, here].astype(jnp.float32) for dest in range(ndest)], axis=0
                    )
                else:
                    before = rolled[place - 1]
                after = rolled[place] if place < len(rolled) else jnp.zeros_like(before)
                window = jnp.where(low, before, after)
                for dest in range(ndest):
                    pack_ref[dest, i, :, here] = window[dest * rows : (dest + 1) * rows].astype(jnp.bfloat16)

    narrow = width - LANES
    if narrow > 0:
        pl.when(count <= narrow)(lambda: work(narrow))
        pl.when(count > narrow)(lambda: work(width))
    else:
        work(width)

    if packed:

        @pl.when(j == pl.num_programs(0) - 1)
        def _():
            main = main_ref.shape[3]
            main_ref[...] = pack_ref[:, :, :, :main]
            over_ref[...] = pack_ref[:, :, :, main : main + over_ref.shape[3]]


def tiles(ndest, first, tables, test_counts, left, shards, main):
    ntest, nsource, kmax, nq = left.shape
    nshard = len(shards)
    part, width = shards[0].shape[1:]
    rows = kmax // ndest
    packed = main is not None
    shapes = [jax.ShapeDtypeStruct((ndest, ntest, nsource, rows, width), jnp.bfloat16)]
    specs = [pl.BlockSpec((ndest, ntest, 1, rows, width), lambda j, *_: (0, 0, j, 0, 0))]
    scratch = []
    if packed:
        for columns in (main, nsource * width - main):
            shape = (ndest, ntest, rows, columns)
            shapes.append(jax.ShapeDtypeStruct(shape, jnp.bfloat16))
            specs.append(pl.BlockSpec(shape, lambda j, *_: (0, 0, 0, 0)))
        scratch.append(pltpu.VMEM((ndest, ntest, rows, nsource * width + LANES), jnp.bfloat16))
    return pl.pallas_call(
        functools.partial(tile_kernel, nshard, first, packed),
        grid_spec=pltpu.PrefetchScalarGridSpec(
            num_scalar_prefetch=4,
            grid=(nsource,),
            in_specs=[pl.BlockSpec((ntest, 1, kmax, nq), lambda j, *_: (0, j, 0, 0))]
            + [pl.BlockSpec((1, part, width), lambda j, *_: (j, 0, 0))] * nshard,
            out_specs=specs,
            scratch_shapes=scratch,
        ),
        out_shape=shapes,
        compiler_params=pltpu.CompilerParams(vmem_limit_bytes=VMEM_LIMIT),
        cost_estimate=pl.CostEstimate(
            flops=2 * ntest * nsource * kmax * width * nq,
            bytes_accessed=2 * ntest * nsource * kmax * (nq + width),
            transcendentals=0,
        ),
    )(*tables, test_counts, left, *shards)


def project_kernel(started, order_ref, tile_ref, coeff_ref, *refs):
    if started:
        start_ref, sum_ref, total_ref = refs
    else:
        *counts_refs, sum_ref, joined_ref, total_ref = refs
    j = pl.program_id(0)
    ndest, ntest, _, rows, _ = tile_ref.shape
    whole = [tile_ref[dest, i, 0] for i in range(ntest) for dest in range(ndest)]
    term = jnp.dot(jnp.concatenate(whole, axis=0), coeff_ref[0], preferred_element_type=jnp.float32)

    @pl.when(j == 0)
    def _():
        total_ref[...] = term + start_ref[...] if started else term

    @pl.when(j > 0)
    def _():
        total_ref[...] += term

    @pl.when(j == pl.num_programs(0) - 1)
    def _():
        if not started:
            sum_ref[...] = total_ref[...]
            nblock = counts_refs[0].shape[0]
            for place, counts_ref in enumerate(counts_refs):
                for k in range(nblock):
                    joined_ref[place * nblock + k] = counts_ref[k]
            return
        for i in range(ntest):
            for dest in range(ndest):
                top = (i * ndest + dest) * rows
                sum_ref[dest, i] = total_ref[top : top + rows, :].astype(sum_ref.dtype)


def project(order, first, tiles, coefficients, start=None, counts=()):
    ndest, ntest, nsource, rows, width = tiles.shape
    ncol = coefficients.shape[2]
    smem = pl.BlockSpec(memory_space=pltpu.SMEM)
    total_spec = pl.BlockSpec((ntest * ndest * rows, ncol), lambda j, order: (0, 0))
    started = start is not None
    if started:
        more, more_specs = [start], [total_spec]
        out_specs = pl.BlockSpec((ndest, ntest, rows, ncol), lambda j, order: (0, 0, 0, 0))
        out_shape = jax.ShapeDtypeStruct((ndest, ntest, rows, ncol), jnp.bfloat16)
    else:
        more, more_specs = list(counts), [smem] * len(counts)
        out_specs = (total_spec, smem)
        out_shape = (
            jax.ShapeDtypeStruct((ntest * ndest * rows, ncol), jnp.float32),
            jax.ShapeDtypeStruct((sum(part.shape[0] for part in counts),), jnp.int32),
        )
    return pl.pallas_call(
        functools.partial(project_kernel, started),
        grid_spec=pltpu.PrefetchScalarGridSpec(
            num_scalar_prefetch=1,
            grid=(nsource,),
            in_specs=[
                pl.BlockSpec((ndest, ntest, 1, rows, width), lambda j, order: (0, 0, j, 0, 0)),
                pl.BlockSpec((1, width, ncol), lambda j, order: (order[first + j], 0, 0)),
            ]
            + more_specs,
            out_specs=out_specs,
            scratch_shapes=[pltpu.VMEM((ntest * ndest * rows, ncol), jnp.float32)],
        ),
        out_shape=out_shape,
        compiler_params=pltpu.CompilerParams(vmem_limit_bytes=VMEM_LIMIT),
        cost_estimate=pl.CostEstimate(
            flops=2 * ndest * ntest * rows * width * ncol * nsource,
            bytes_accessed=2 * ndest * ntest * rows * width * nsource,
            transcendentals=0,
        ),
    )(order, tiles, coefficients, *more)


def unpack_kernel(cut, order_ref, counts_ref, offsets_ref, whole_ref, packed_ref, *refs):
    *part_refs, out_ref, sum_ref, rows_ref = refs
    sum_ref[...] = sum(part_ref[...].astype(jnp.float32) for part_ref in part_refs).astype(sum_ref.dtype)
    nsrc, _, _, rows, width = whole_ref.shape
    packed_width = packed_ref.shape[3]
    nall = out_ref.shape[2]
    nblock = nall // nsrc
    ntile = width // LANES
    step = 16 if rows % 16 == 0 else rows
    lanes = lax.broadcasted_iota(jnp.int32, (rows, LANES), 1)

    @pl.loop(0, nsrc, unroll=2)
    def _(source):
        for place in range(nblock):
            block = order_ref[source * nblock + place]
            target = source * nblock + block
            if place < cut:
                rows_ref[target] = whole_ref[source, 0, place].astype(jnp.float32)
                continue
            count = counts_ref[target]
            offset = offsets_ref[target]
            shift = offset % LANES
            base = offset - shift
            back = (LANES - shift) % LANES
            low = lanes < LANES - shift
            rolled = []
            for tile in range(ntile + 1):
                start = pl.multiple_of(jnp.minimum(base + tile * LANES, packed_width - LANES), LANES)
                piece = packed_ref[source, 0, :, pl.ds(start, LANES)].astype(jnp.float32)
                rolled.append(pltpu.roll(piece, back, axis=1))
            for tile in range(ntile):
                value = jnp.where(low, rolled[tile], rolled[tile + 1])
                value = jnp.where(lanes < count - tile * LANES, value, 0.0)
                rows_ref[target, :, tile * LANES : (tile + 1) * LANES] = value

    @pl.loop(0, nall // 16)
    def _(group):
        here = pl.ds(pl.multiple_of(group * 16, 16), 16)
        for top in range(0, rows, step):
            turned = jnp.transpose(rows_ref[here, top : top + step, :], (1, 0, 2))
            out_ref[0, top : top + step, here, :] = turned.astype(out_ref.dtype)


def unpack(cut, tables, whole, packed, parts):
    nsrc, ntest, _, rows, width = whole.shape
    packed_width = packed.shape[3]
    nall = tables[0].shape[0]
    sum_spec = pl.BlockSpec((1,) + parts[0].shape[1:], lambda i, *_: (i, 0, 0))
    return pl.pallas_call(
        functools.partial(unpack_kernel, cut),
        grid_spec=pltpu.PrefetchScalarGridSpec(
            num_scalar_prefetch=3,
            grid=(ntest,),
            in_specs=[
                pl.BlockSpec((nsrc, 1, cut, rows, width), lambda i, *_: (0, i, 0, 0, 0)),
                pl.BlockSpec((nsrc, 1, rows, packed_width), lambda i, *_: (0, i, 0, 0)),
            ]
            + [sum_spec] * len(parts),
            out_specs=(pl.BlockSpec((1, rows, nall, width), lambda i, *_: (i, 0, 0, 0)), sum_spec),
            scratch_shapes=[pltpu.VMEM((nall, rows, width), jnp.float32)],
        ),
        out_shape=(
            jax.ShapeDtypeStruct((ntest, rows, nall, width), jnp.bfloat16),
            jax.ShapeDtypeStruct(parts[0].shape, jnp.bfloat16),
        ),
        compiler_params=pltpu.CompilerParams(vmem_limit_bytes=SMALL_VMEM_LIMIT),
    )(*tables, whole, packed, *parts)


def body(
    test_points, test_basis, test_counts, source_points, source_basis, source_counts, coefficients
):
    nsource, part, kmax = source_basis.shape
    ntest = test_points.shape[0]
    nsrc = lax.axis_size("src")
    ntest_axis = lax.axis_size("test")
    me_test = lax.axis_index("test")
    cut = max(1, nsource * 3 // 8)

    held = {}

    def gather(name, shard, left):
        got = {0: shard}
        bits = list(bits_down(ntest_axis))
        for bit in bits:
            if bit == bits[-1]:
                names = [o for o in got if o != 0]
                tied = lax.optimization_barrier(tuple(got[o] for o in names) + (left,))
                got.update(zip(names, tied[:-1]))
                left = tied[-1]
            for offset in list(got):
                got[offset ^ bit] = exchange(got[offset], "test", bit)
            if bit == bits[0]:
                held[name] = got[bit]
        return [got[offset] for offset in sorted(got)], left

    most = (nsource - cut) * kmax
    main = min(most, -(-most * 18 // (25 * LANES)) * LANES)
    widths = [main, min(most, main + LANES), min(most, main + 2 * LANES), most]

    order, offsets, basis_a, basis_b = pick(cut, source_counts, source_basis)
    tables = (order, source_counts, offsets)
    me = jnp.reshape(me_test, (1,))
    test_points, source_points = test_points.transpose(1, 0, 2), source_points.transpose(1, 0, 2)

    left_a = left_products(ntest_axis, me, order, test_points, source_points, test_basis, 0, cut)
    shards_a, left_a = gather("a", basis_a, left_a)
    (tiles_a,) = tiles(nsrc, 0, tables, test_counts, left_a, shards_a, None)
    moved_a = lax.all_to_all(tiles_a, "src", split_axis=0, concat_axis=0, tiled=True)

    rest, _ = lax.optimization_barrier((basis_b, held["a"]))
    later, _ = lax.optimization_barrier((source_points, tiles_a))
    left_b = left_products(ntest_axis, me, order, test_points, later, test_basis, cut, nsource)
    shards_b, left_b = gather("b", rest, left_b)
    inner = max(1, nsrc // 4)
    counts, _ = lax.optimization_barrier((source_counts, left_b))
    far = [exchange(counts, "src", flip) for flip in range(inner, nsrc, inner)]
    tiles_b, packed, beyond = tiles(nsrc, cut, tables, test_counts, left_b, shards_b, main)
    packed, *far = lax.optimization_barrier((packed, *far))
    moved_b = lax.all_to_all(packed, "src", split_axis=0, concat_axis=0, tiled=True)

    sums, joined = project(order, 0, tiles_a, coefficients, counts=[source_counts] + far)
    groups = [joined] + [exchange(joined, "src", flip) for flip in range(1, inner)]
    sums = project(order, cut, tiles_b, coefficients, sums)
    parts = sum_rows(sums, "src")
    me_src, _ = lax.optimization_barrier((jnp.reshape(lax.axis_index("src"), (1,)), packed))
    all_counts, all_order, all_offsets, branch = all_tables(cut, nsource, widths, me_src, groups)
    spread = (all_order, all_counts, all_offsets)

    def finish(width, beyond, moved_a, moved_b, spread, parts):
        if width > main:
            more = lax.all_to_all(
                beyond[..., : width - main], "src", split_axis=0, concat_axis=0, tiled=True
            )
            moved_b = jnp.concatenate([moved_b, more], axis=3)
        return unpack(cut, spread, moved_a, moved_b, parts)

    return lax.switch(
        branch[0],
        [functools.partial(finish, width) for width in widths],
        beyond,
        moved_a,
        moved_b,
        spread,
        parts,
    )


def solution(mesh):
    return jax.shard_map(
        body,
        mesh=mesh,
        in_specs=(
            P("test", None, None),
            P("test", None, None),
            P("test"),
            P("src", None, None),
            P("src", "test", None),
            P("src"),
            P("src", None, None),
        ),
        out_specs=(P("test", "src", None, None), P("test", "src", None)),
        check_vma=False,
    )
```

```python
import functools

import jax
import jax.numpy as jnp
from jax import lax
from jax.experimental import pallas as pl
from jax.experimental.pallas import tpu as pltpu
from jax.sharding import PartitionSpec as P

softening = 0.0025
QBLOCK = 256
LANES = 128
VMEM_LIMIT = 255 * 256 * 1024
SMALL_VMEM_LIMIT = 32 * 1024 * 1024


def exchange(x, axis, flip):
    size = lax.axis_size(axis)
    return lax.ppermute(x, axis, [(a, a ^ flip) for a in range(size)])


def bits_down(size):
    bit = size // 2
    while bit >= 1:
        yield bit
        bit //= 2


def sum_rows(total, axis):
    size = lax.axis_size(axis)
    me = lax.axis_index(axis)
    held, bit = total, 1
    while held.shape[0] > 4:
        pairs = held.reshape((held.shape[0] // 2, 2) + held.shape[1:])
        mine = (me // bit) % 2
        keep = lax.dynamic_index_in_dim(pairs, mine, 1, keepdims=False)
        give = lax.dynamic_index_in_dim(pairs, 1 - mine, 1, keepdims=False)
        got = exchange(give, axis, bit)
        held = (keep.astype(jnp.float32) + got.astype(jnp.float32)).astype(held.dtype)
        bit *= 2
    mine = me // bit
    parts = [lax.dynamic_index_in_dim(held, mine, 0, keepdims=False)]
    for flip in range(1, held.shape[0]):
        give = lax.dynamic_index_in_dim(held, mine ^ flip, 0, keepdims=False)
        parts.append(exchange(give, axis, flip * bit))
    return parts


def rank_blocks(counts, cut):
    ranks = []
    for j, mine in enumerate(counts):
        rank = jnp.int32(0)
        for k, other in enumerate(counts):
            if k != j:
                ahead = other >= mine if k < j else other > mine
                rank += ahead.astype(jnp.int32)
        ranks.append(rank)
    offsets = []
    for j in range(len(counts)):
        offset = jnp.int32(0)
        for k, other in enumerate(counts):
            if k != j:
                offset += jnp.where((ranks[k] >= cut) & (ranks[k] < ranks[j]), other, 0)
        offsets.append(offset)
    return ranks, offsets


def pick_kernel(cut, counts_ref, basis_ref, order_ref, offsets_ref, first_ref, rest_ref):
    nblock = basis_ref.shape[0]
    ranks, offsets = rank_blocks([counts_ref[j] for j in range(nblock)], cut)
    for j in range(nblock):
        order_ref[ranks[j]] = jnp.int32(j)
        offsets_ref[j] = offsets[j]
    for place in range(nblock):
        block = basis_ref[order_ref[place]]
        if place < cut:
            first_ref[place] = block
        else:
            rest_ref[place - cut] = block


def pick(cut, counts, basis):
    nblock = basis.shape[0]
    smem, vmem = pl.BlockSpec(memory_space=pltpu.SMEM), pl.BlockSpec(memory_space=pltpu.VMEM)
    return pl.pallas_call(
        functools.partial(pick_kernel, cut),
        out_shape=(
            jax.ShapeDtypeStruct((nblock,), jnp.int32),
            jax.ShapeDtypeStruct((nblock,), jnp.int32),
            jax.ShapeDtypeStruct((cut,) + basis.shape[1:], basis.dtype),
            jax.ShapeDtypeStruct((nblock - cut,) + basis.shape[1:], basis.dtype),
        ),
        in_specs=[smem, vmem],
        out_specs=(smem, smem, vmem, vmem),
        compiler_params=pltpu.CompilerParams(vmem_limit_bytes=VMEM_LIMIT),
    )(counts, basis)


def tables_kernel(cut, nblock, widths, me_ref, *refs):
    *group_refs, counts_ref, order_ref, offsets_ref, branch_ref, joined_ref = refs
    group, inner = group_refs[0].shape[0], len(group_refs)
    for place, group_ref in enumerate(group_refs):
        for k in range(group):
            joined_ref[place * group + k] = group_ref[k]

    def step(source, need):
        base = source * nblock
        offset = source ^ me_ref[0]
        theirs = (offset % inner) * group + (offset // inner) * nblock
        counts = [joined_ref[theirs + j] for j in range(nblock)]
        ranks, offsets = rank_blocks(counts, cut)
        used = jnp.int32(0)
        for j in range(nblock):
            counts_ref[base + j] = counts[j]
            order_ref[base + ranks[j]] = jnp.int32(j)
            offsets_ref[base + j] = offsets[j]
            used += jnp.where(ranks[j] >= cut, counts[j], 0)
        return jnp.maximum(need, used)

    need = lax.fori_loop(0, counts_ref.shape[0] // nblock, step, jnp.int32(0))
    branch = jnp.int32(0)
    for width in widths[:-1]:
        branch += (need > width).astype(jnp.int32)
    branch_ref[0] = branch


def all_tables(cut, nblock, widths, me, groups):
    smem = pl.BlockSpec(memory_space=pltpu.SMEM)
    total = sum(group.shape[0] for group in groups)
    table = jax.ShapeDtypeStruct((total,), jnp.int32)
    return pl.pallas_call(
        functools.partial(tables_kernel, cut, nblock, widths),
        out_shape=(table, table, table, jax.ShapeDtypeStruct((1,), jnp.int32)),
        in_specs=[smem] * (1 + len(groups)),
        out_specs=(smem,) * 4,
        scratch_shapes=[pltpu.SMEM((total,), jnp.int32)],
    )(me, *groups)


NFEATURE = 128


def fill_features(rows_ref, points, is_test):
    def three_terms(x):
        high = x.astype(jnp.bfloat16).astype(jnp.float32)
        middle = (x - high).astype(jnp.bfloat16).astype(jnp.float32)
        return high, middle, x - high - middle

    centred = points - 0.5
    norm = jnp.sum(centred * centred, axis=0, keepdims=True)
    terms = three_terms(centred)
    norms = three_terms(norm + softening if is_test else norm)
    for a in range(3):
        for b in range(3):
            place = 3 * (3 * a + b)
            rows_ref[place : place + 3, :] = -2.0 * terms[a] if is_test else terms[b]
    for a in range(3):
        rows_ref[27 + a : 28 + a, :] = norms[a] if is_test else jnp.ones_like(norm)
        rows_ref[30 + a : 31 + a, :] = jnp.ones_like(norm) if is_test else norms[a]


def left_kernel(
    nshard, first, me_ref, order_ref, test_ref, source_ref, basis_ref, out_ref,
    rows_ref, features_ref, turned_ref, near_ref,
):
    j = pl.program_id(0)
    ntest = test_ref.shape[1]
    nq = source_ref.shape[2]
    part = nq // nshard
    block = min(QBLOCK, nq)

    @pl.when(j == 0)
    def _():
        rows_ref[...] = jnp.zeros_like(rows_ref)
        for i in range(ntest):
            fill_features(rows_ref, test_ref[:, i, :], True)
            features_ref[i] = rows_ref[...].T.astype(jnp.bfloat16)
            turned_ref[i] = basis_ref[i].T

    source = order_ref[first + j]
    for comp in range(3):
        rows_ref[comp : comp + 1, :] = source_ref[comp, pl.ds(source, 1), :]
    pieces = []
    for offset in range(nshard):
        start = pl.multiple_of((me_ref[0] ^ offset) * part, part)
        pieces.append(rows_ref[0:3, pl.ds(start, part)])
    fill_features(rows_ref, jnp.concatenate(pieces, axis=1), False)
    near_ref[...] = rows_ref[...].astype(jnp.bfloat16)

    steps = [(i, start) for i in range(ntest) for start in range(0, nq, block)]

    def kernel_block(i, start):
        squared = jnp.dot(
            features_ref[i], near_ref[:, start : start + block], preferred_element_type=jnp.float32
        )
        return lax.rsqrt(squared.astype(jnp.bfloat16))

    ready = kernel_block(*steps[0])
    for place, (i, start) in enumerate(steps):
        now = ready
        if place + 1 < len(steps):
            ready = kernel_block(*steps[place + 1])
        out_ref[i, 0, :, start : start + block] = jnp.dot(
            turned_ref[i], now, preferred_element_type=jnp.float32
        ).astype(jnp.bfloat16)


def left_products(nshard, me, order, test_points, source_points, test_basis, first, last):
    _, ntest, npoint = test_points.shape
    nall, nq = source_points.shape[1:]
    kmax = test_basis.shape[2]
    nsource = last - first
    return pl.pallas_call(
        functools.partial(left_kernel, nshard, first),
        grid_spec=pltpu.PrefetchScalarGridSpec(
            num_scalar_prefetch=2,
            grid=(nsource,),
            in_specs=[
                pl.BlockSpec((3, ntest, npoint), lambda j, *_: (0, 0, 0)),
                pl.BlockSpec((3, nall, nq), lambda j, *_: (0, 0, 0)),
                pl.BlockSpec((ntest, npoint, kmax), lambda j, *_: (0, 0, 0)),
            ],
            out_specs=pl.BlockSpec((ntest, 1, kmax, nq), lambda j, *_: (0, j, 0, 0)),
            scratch_shapes=[
                pltpu.VMEM((NFEATURE, npoint), jnp.float32),
                pltpu.VMEM((ntest, npoint, NFEATURE), jnp.bfloat16),
                pltpu.VMEM((ntest, kmax, npoint), jnp.bfloat16),
                pltpu.VMEM((NFEATURE, nq), jnp.bfloat16),
            ],
        ),
        out_shape=jax.ShapeDtypeStruct((ntest, nsource, kmax, nq), jnp.bfloat16),
        compiler_params=pltpu.CompilerParams(vmem_limit_bytes=VMEM_LIMIT),
        cost_estimate=pl.CostEstimate(
            flops=2 * ntest * nsource * npoint * nq * kmax,
            bytes_accessed=2 * ntest * nsource * kmax * nq,
            transcendentals=ntest * nsource * npoint * nq,
        ),
    )(me, order, test_points, source_points, test_basis)


def tile_kernel(nshard, first, packed, *refs):
    order_ref, source_counts_ref, offsets_ref, test_counts_ref, left_ref = refs[:5]
    shard_refs = refs[5 : 5 + nshard]
    j = pl.program_id(0)
    if packed:
        tile_ref, main_ref, over_ref, pack_ref = refs[5 + nshard :]
    else:
        (tile_ref,) = refs[5 + nshard :]
    ntest, _, kmax, _ = left_ref.shape
    ndest, _, _, rows, width = tile_ref.shape
    count = source_counts_ref[order_ref[first + j]]

    def work(wide):
        side = jnp.concatenate([shard_ref[0, :, :wide] for shard_ref in shard_refs], axis=0)
        row_ids = lax.broadcasted_iota(jnp.int32, (kmax, wide), 0)
        column_ids = lax.broadcasted_iota(jnp.int32, (kmax, wide), 1)
        products = [
            jnp.dot(left_ref[i, 0], side, preferred_element_type=jnp.float32) for i in range(ntest)
        ]
        if packed:
            offset = offsets_ref[order_ref[first + j]]
            shift = offset % LANES
            base = offset - shift
            low = lax.broadcasted_iota(jnp.int32, (kmax, LANES), 1) < shift
        for i in range(ntest):
            used = (row_ids < test_counts_ref[i]) & (column_ids < count)
            tile = jnp.where(used, products[i], 0.0)
            for dest in range(ndest):
                tile_ref[dest, i, 0, :, :wide] = tile[dest * rows : (dest + 1) * rows].astype(jnp.bfloat16)
                if wide < width:
                    tile_ref[dest, i, 0, :, wide:] = jnp.zeros((rows, width - wide), jnp.bfloat16)
            if not packed:
                continue
            rolled = [
                pltpu.roll(tile[:, start : start + LANES], shift, axis=1) for start in range(0, wide, LANES)
            ]
            for place in range(len(rolled) + 1):
                here = pl.ds(pl.multiple_of(base + place * LANES, LANES), LANES)
                if place == 0:
                    before = jnp.concatenate(
                        [pack_ref[dest, i, :, here].astype(jnp.float32) for dest in range(ndest)], axis=0
                    )
                else:
                    before = rolled[place - 1]
                after = rolled[place] if place < len(rolled) else jnp.zeros_like(before)
                window = jnp.where(low, before, after)
                for dest in range(ndest):
                    pack_ref[dest, i, :, here] = window[dest * rows : (dest + 1) * rows].astype(jnp.bfloat16)

    narrow = width - LANES
    if narrow > 0:
        pl.when(count <= narrow)(lambda: work(narrow))
        pl.when(count > narrow)(lambda: work(width))
    else:
        work(width)

    if packed:

        @pl.when(j == pl.num_programs(0) - 1)
        def _():
            main = main_ref.shape[3]
            main_ref[...] = pack_ref[:, :, :, :main]
            over_ref[...] = pack_ref[:, :, :, main : main + over_ref.shape[3]]


def tiles(ndest, first, tables, test_counts, left, shards, main):
    ntest, nsource, kmax, nq = left.shape
    nshard = len(shards)
    part, width = shards[0].shape[1:]
    rows = kmax // ndest
    packed = main is not None
    shapes = [jax.ShapeDtypeStruct((ndest, ntest, nsource, rows, width), jnp.bfloat16)]
    specs = [pl.BlockSpec((ndest, ntest, 1, rows, width), lambda j, *_: (0, 0, j, 0, 0))]
    scratch = []
    if packed:
        for columns in (main, nsource * width - main):
            shape = (ndest, ntest, rows, columns)
            shapes.append(jax.ShapeDtypeStruct(shape, jnp.bfloat16))
            specs.append(pl.BlockSpec(shape, lambda j, *_: (0, 0, 0, 0)))
        scratch.append(pltpu.VMEM((ndest, ntest, rows, nsource * width + LANES), jnp.bfloat16))
    return pl.pallas_call(
        functools.partial(tile_kernel, nshard, first, packed),
        grid_spec=pltpu.PrefetchScalarGridSpec(
            num_scalar_prefetch=4,
            grid=(nsource,),
            in_specs=[pl.BlockSpec((ntest, 1, kmax, nq), lambda j, *_: (0, j, 0, 0))]
            + [pl.BlockSpec((1, part, width), lambda j, *_: (j, 0, 0))] * nshard,
            out_specs=specs,
            scratch_shapes=scratch,
        ),
        out_shape=shapes,
        compiler_params=pltpu.CompilerParams(vmem_limit_bytes=VMEM_LIMIT),
        cost_estimate=pl.CostEstimate(
            flops=2 * ntest * nsource * kmax * width * nq,
            bytes_accessed=2 * ntest * nsource * kmax * (nq + width),
            transcendentals=0,
        ),
    )(*tables, test_counts, left, *shards)


def project_kernel(started, order_ref, tile_ref, coeff_ref, *refs):
    if started:
        start_ref, sum_ref, total_ref = refs
    else:
        *counts_refs, sum_ref, joined_ref, total_ref = refs
    j = pl.program_id(0)
    ndest, ntest, _, rows, _ = tile_ref.shape
    whole = [tile_ref[dest, i, 0] for i in range(ntest) for dest in range(ndest)]
    term = jnp.dot(jnp.concatenate(whole, axis=0), coeff_ref[0], preferred_element_type=jnp.float32)

    @pl.when(j == 0)
    def _():
        total_ref[...] = term + start_ref[...] if started else term

    @pl.when(j > 0)
    def _():
        total_ref[...] += term

    @pl.when(j == pl.num_programs(0) - 1)
    def _():
        if not started:
            sum_ref[...] = total_ref[...]
            nblock = counts_refs[0].shape[0]
            for place, counts_ref in enumerate(counts_refs):
                for k in range(nblock):
                    joined_ref[place * nblock + k] = counts_ref[k]
            return
        for i in range(ntest):
            for dest in range(ndest):
                top = (i * ndest + dest) * rows
                sum_ref[dest, i] = total_ref[top : top + rows, :].astype(sum_ref.dtype)


def project(order, first, tiles, coefficients, start=None, counts=()):
    ndest, ntest, nsource, rows, width = tiles.shape
    ncol = coefficients.shape[2]
    smem = pl.BlockSpec(memory_space=pltpu.SMEM)
    total_spec = pl.BlockSpec((ntest * ndest * rows, ncol), lambda j, order: (0, 0))
    started = start is not None
    if started:
        more, more_specs = [start], [total_spec]
        out_specs = pl.BlockSpec((ndest, ntest, rows, ncol), lambda j, order: (0, 0, 0, 0))
        out_shape = jax.ShapeDtypeStruct((ndest, ntest, rows, ncol), jnp.bfloat16)
    else:
        more, more_specs = list(counts), [smem] * len(counts)
        out_specs = (total_spec, smem)
        out_shape = (
            jax.ShapeDtypeStruct((ntest * ndest * rows, ncol), jnp.float32),
            jax.ShapeDtypeStruct((sum(part.shape[0] for part in counts),), jnp.int32),
        )
    return pl.pallas_call(
        functools.partial(project_kernel, started),
        grid_spec=pltpu.PrefetchScalarGridSpec(
            num_scalar_prefetch=1,
            grid=(nsource,),
            in_specs=[
                pl.BlockSpec((ndest, ntest, 1, rows, width), lambda j, order: (0, 0, j, 0, 0)),
                pl.BlockSpec((1, width, ncol), lambda j, order: (order[first + j], 0, 0)),
            ]
            + more_specs,
            out_specs=out_specs,
            scratch_shapes=[pltpu.VMEM((ntest * ndest * rows, ncol), jnp.float32)],
        ),
        out_shape=out_shape,
        compiler_params=pltpu.CompilerParams(vmem_limit_bytes=VMEM_LIMIT),
        cost_estimate=pl.CostEstimate(
            flops=2 * ndest * ntest * rows * width * ncol * nsource,
            bytes_accessed=2 * ndest * ntest * rows * width * nsource,
            transcendentals=0,
        ),
    )(order, tiles, coefficients, *more)


def unpack_kernel(cut, order_ref, counts_ref, offsets_ref, whole_ref, packed_ref, *refs):
    *part_refs, out_ref, sum_ref, rows_ref = refs
    sum_ref[...] = sum(part_ref[...].astype(jnp.float32) for part_ref in part_refs).astype(sum_ref.dtype)
    nsrc, _, _, rows, width = whole_ref.shape
    packed_width = packed_ref.shape[3]
    nall = out_ref.shape[2]
    nblock = nall // nsrc
    ntile = width // LANES
    step = 16 if rows % 16 == 0 else rows
    lanes = lax.broadcasted_iota(jnp.int32, (rows, LANES), 1)

    @pl.loop(0, nsrc, unroll=2)
    def _(source):
        for place in range(nblock):
            block = order_ref[source * nblock + place]
            target = source * nblock + block
            if place < cut:
                rows_ref[target] = whole_ref[source, 0, place].astype(jnp.float32)
                continue
            count = counts_ref[target]
            offset = offsets_ref[target]
            shift = offset % LANES
            base = offset - shift
            back = (LANES - shift) % LANES
            low = lanes < LANES - shift
            rolled = []
            for tile in range(ntile + 1):
                start = pl.multiple_of(jnp.minimum(base + tile * LANES, packed_width - LANES), LANES)
                piece = packed_ref[source, 0, :, pl.ds(start, LANES)].astype(jnp.float32)
                rolled.append(pltpu.roll(piece, back, axis=1))
            for tile in range(ntile):
                value = jnp.where(low, rolled[tile], rolled[tile + 1])
                value = jnp.where(lanes < count - tile * LANES, value, 0.0)
                rows_ref[target, :, tile * LANES : (tile + 1) * LANES] = value

    @pl.loop(0, nall // 16)
    def _(group):
        here = pl.ds(pl.multiple_of(group * 16, 16), 16)
        for top in range(0, rows, step):
            turned = jnp.transpose(rows_ref[here, top : top + step, :], (1, 0, 2))
            out_ref[0, top : top + step, here, :] = turned.astype(out_ref.dtype)


def unpack(cut, tables, whole, packed, parts):
    nsrc, ntest, _, rows, width = whole.shape
    packed_width = packed.shape[3]
    nall = tables[0].shape[0]
    sum_spec = pl.BlockSpec((1,) + parts[0].shape[1:], lambda i, *_: (i, 0, 0))
    return pl.pallas_call(
        functools.partial(unpack_kernel, cut),
        grid_spec=pltpu.PrefetchScalarGridSpec(
            num_scalar_prefetch=3,
            grid=(ntest,),
            in_specs=[
                pl.BlockSpec((nsrc, 1, cut, rows, width), lambda i, *_: (0, i, 0, 0, 0)),
                pl.BlockSpec((nsrc, 1, rows, packed_width), lambda i, *_: (0, i, 0, 0)),
            ]
            + [sum_spec] * len(parts),
            out_specs=(pl.BlockSpec((1, rows, nall, width), lambda i, *_: (i, 0, 0, 0)), sum_spec),
            scratch_shapes=[pltpu.VMEM((nall, rows, width), jnp.float32)],
        ),
        out_shape=(
            jax.ShapeDtypeStruct((ntest, rows, nall, width), jnp.bfloat16),
            jax.ShapeDtypeStruct(parts[0].shape, jnp.bfloat16),
        ),
        compiler_params=pltpu.CompilerParams(vmem_limit_bytes=SMALL_VMEM_LIMIT),
    )(*tables, whole, packed, *parts)


def body(
    test_points, test_basis, test_counts, source_points, source_basis, source_counts, coefficients
):
    nsource, part, kmax = source_basis.shape
    ntest = test_points.shape[0]
    nsrc = lax.axis_size("src")
    ntest_axis = lax.axis_size("test")
    me_test = lax.axis_index("test")
    cut = max(1, nsource * 3 // 8)

    held = {}

    def gather(name, shard, left):
        got = {0: shard}
        bits = list(bits_down(ntest_axis))
        for bit in bits:
            if bit == bits[-1]:
                names = [o for o in got if o != 0]
                tied = lax.optimization_barrier(tuple(got[o] for o in names) + (left,))
                got.update(zip(names, tied[:-1]))
                left = tied[-1]
            for offset in list(got):
                got[offset ^ bit] = exchange(got[offset], "test", bit)
            if bit == bits[0]:
                held[name] = got[bit]
        return [got[offset] for offset in sorted(got)], left

    most = (nsource - cut) * kmax
    main = min(most, -(-most * 18 // (25 * LANES)) * LANES)
    widths = [main, min(most, main + LANES), min(most, main + 2 * LANES), most]

    order, offsets, basis_a, basis_b = pick(cut, source_counts, source_basis)
    tables = (order, source_counts, offsets)
    me = jnp.reshape(me_test, (1,))
    test_points, source_points = test_points.transpose(1, 0, 2), source_points.transpose(1, 0, 2)

    left_a = left_products(ntest_axis, me, order, test_points, source_points, test_basis, 0, cut)
    shards_a, left_a = gather("a", basis_a, left_a)
    (tiles_a,) = tiles(nsrc, 0, tables, test_counts, left_a, shards_a, None)
    moved_a = lax.all_to_all(tiles_a, "src", split_axis=0, concat_axis=0, tiled=True)

    rest, _ = lax.optimization_barrier((basis_b, held["a"]))
    later, _ = lax.optimization_barrier((source_points, tiles_a))
    left_b = left_products(ntest_axis, me, order, test_points, later, test_basis, cut, nsource)
    shards_b, left_b = gather("b", rest, left_b)
    inner = max(1, nsrc // 4)
    counts, _ = lax.optimization_barrier((source_counts, left_b))
    far = [exchange(counts, "src", flip) for flip in range(inner, nsrc, inner)]
    tiles_b, packed, beyond = tiles(nsrc, cut, tables, test_counts, left_b, shards_b, main)
    packed, *far = lax.optimization_barrier((packed, *far))
    moved_b = lax.all_to_all(packed, "src", split_axis=0, concat_axis=0, tiled=True)

    sums, joined = project(order, 0, tiles_a, coefficients, counts=[source_counts] + far)
    groups = [joined] + [exchange(joined, "src", flip) for flip in range(1, inner)]
    sums = project(order, cut, tiles_b, coefficients, sums)
    parts = sum_rows(sums, "src")
    me_src, _ = lax.optimization_barrier((jnp.reshape(lax.axis_index("src"), (1,)), packed))
    all_counts, all_order, all_offsets, branch = all_tables(cut, nsource, widths, me_src, groups)
    spread = (all_order, all_counts, all_offsets)

    def finish(width, beyond, moved_a, moved_b, spread, parts):
        if width > main:
            more = lax.all_to_all(
                beyond[..., : width - main], "src", split_axis=0, concat_axis=0, tiled=True
            )
            moved_b = jnp.concatenate([moved_b, more], axis=3)
        return unpack(cut, spread, moved_a, moved_b, parts)

    return lax.switch(
        branch[0],
        [functools.partial(finish, width) for width in widths],
        beyond,
        moved_a,
        moved_b,
        spread,
        parts,
    )


def solution(mesh):
    return jax.shard_map(
        body,
        mesh=mesh,
        in_specs=(
            P("test", None, None),
            P("test", None, None),
            P("test"),
            P("src", None, None),
            P("src", "test", None),
            P("src"),
            P("src", None, None),
        ),
        out_specs=(P("test", "src", None, None), P("test", "src", None)),
        check_vma=False,
    )
```

```python
import functools

import jax
import jax.numpy as jnp
from jax import lax
from jax.experimental import pallas as pl
from jax.experimental.pallas import tpu as pltpu
from jax.sharding import PartitionSpec as P

softening = 0.0025
QBLOCK = 256
LANES = 128
VMEM_LIMIT = 255 * 256 * 1024
SMALL_VMEM_LIMIT = 32 * 1024 * 1024


def exchange(x, axis, flip):
    size = lax.axis_size(axis)
    return lax.ppermute(x, axis, [(a, a ^ flip) for a in range(size)])


def bits_down(size):
    bit = size // 2
    while bit >= 1:
        yield bit
        bit //= 2


def sum_rows(total, axis):
    size = lax.axis_size(axis)
    me = lax.axis_index(axis)
    held, bit = total, 1
    while held.shape[0] > 4:
        pairs = held.reshape((held.shape[0] // 2, 2) + held.shape[1:])
        mine = (me // bit) % 2
        keep = lax.dynamic_index_in_dim(pairs, mine, 1, keepdims=False)
        give = lax.dynamic_index_in_dim(pairs, 1 - mine, 1, keepdims=False)
        got = exchange(give, axis, bit)
        held = (keep.astype(jnp.float32) + got.astype(jnp.float32)).astype(held.dtype)
        bit *= 2
    mine = me // bit
    parts = [lax.dynamic_index_in_dim(held, mine, 0, keepdims=False)]
    for flip in range(1, held.shape[0]):
        give = lax.dynamic_index_in_dim(held, mine ^ flip, 0, keepdims=False)
        parts.append(exchange(give, axis, flip * bit))
    return parts


def rank_blocks(counts, cut):
    ranks = []
    for j, mine in enumerate(counts):
        rank = jnp.int32(0)
        for k, other in enumerate(counts):
            if k != j:
                ahead = other >= mine if k < j else other > mine
                rank += ahead.astype(jnp.int32)
        ranks.append(rank)
    offsets = []
    for j in range(len(counts)):
        offset = jnp.int32(0)
        for k, other in enumerate(counts):
            if k != j:
                offset += jnp.where((ranks[k] >= cut) & (ranks[k] < ranks[j]), other, 0)
        offsets.append(offset)
    return ranks, offsets


def pick_kernel(cut, counts_ref, basis_ref, order_ref, offsets_ref, first_ref, rest_ref):
    nblock = basis_ref.shape[0]
    ranks, offsets = rank_blocks([counts_ref[j] for j in range(nblock)], cut)
    for j in range(nblock):
        order_ref[ranks[j]] = jnp.int32(j)
        offsets_ref[j] = offsets[j]
    for place in range(nblock):
        block = basis_ref[order_ref[place]]
        if place < cut:
            first_ref[place] = block
        else:
            rest_ref[place - cut] = block


def pick(cut, counts, basis):
    nblock = basis.shape[0]
    smem, vmem = pl.BlockSpec(memory_space=pltpu.SMEM), pl.BlockSpec(memory_space=pltpu.VMEM)
    return pl.pallas_call(
        functools.partial(pick_kernel, cut),
        out_shape=(
            jax.ShapeDtypeStruct((nblock,), jnp.int32),
            jax.ShapeDtypeStruct((nblock,), jnp.int32),
            jax.ShapeDtypeStruct((cut,) + basis.shape[1:], basis.dtype),
            jax.ShapeDtypeStruct((nblock - cut,) + basis.shape[1:], basis.dtype),
        ),
        in_specs=[smem, vmem],
        out_specs=(smem, smem, vmem, vmem),
        compiler_params=pltpu.CompilerParams(vmem_limit_bytes=VMEM_LIMIT),
    )(counts, basis)


def tables_kernel(cut, nblock, widths, me_ref, *refs):
    *group_refs, counts_ref, order_ref, offsets_ref, branch_ref, joined_ref = refs
    group, inner = group_refs[0].shape[0], len(group_refs)
    for place, group_ref in enumerate(group_refs):
        for k in range(group):
            joined_ref[place * group + k] = group_ref[k]

    def step(source, need):
        base = source * nblock
        offset = source ^ me_ref[0]
        theirs = (offset % inner) * group + (offset // inner) * nblock
        counts = [joined_ref[theirs + j] for j in range(nblock)]
        ranks, offsets = rank_blocks(counts, cut)
        used = jnp.int32(0)
        for j in range(nblock):
            counts_ref[base + j] = counts[j]
            order_ref[base + ranks[j]] = jnp.int32(j)
            offsets_ref[base + j] = offsets[j]
            used += jnp.where(ranks[j] >= cut, counts[j], 0)
        return jnp.maximum(need, used)

    need = lax.fori_loop(0, counts_ref.shape[0] // nblock, step, jnp.int32(0))
    branch = jnp.int32(0)
    for width in widths[:-1]:
        branch += (need > width).astype(jnp.int32)
    branch_ref[0] = branch


def all_tables(cut, nblock, widths, me, groups):
    smem = pl.BlockSpec(memory_space=pltpu.SMEM)
    total = sum(group.shape[0] for group in groups)
    table = jax.ShapeDtypeStruct((total,), jnp.int32)
    return pl.pallas_call(
        functools.partial(tables_kernel, cut, nblock, widths),
        out_shape=(table, table, table, jax.ShapeDtypeStruct((1,), jnp.int32)),
        in_specs=[smem] * (1 + len(groups)),
        out_specs=(smem,) * 4,
        scratch_shapes=[pltpu.SMEM((total,), jnp.int32)],
    )(me, *groups)


NFEATURE = 64


def fill_features(rows_ref, points, is_test):
    def three_terms(x):
        high = x.astype(jnp.bfloat16).astype(jnp.float32)
        middle = (x - high).astype(jnp.bfloat16).astype(jnp.float32)
        return high, middle, x - high - middle

    centred = points - 0.5
    norm = jnp.sum(centred * centred, axis=0, keepdims=True)
    terms = three_terms(centred)
    norms = three_terms(norm + softening if is_test else norm)
    for a in range(3):
        for b in range(3):
            place = 3 * (3 * a + b)
            rows_ref[place : place + 3, :] = -2.0 * terms[a] if is_test else terms[b]
    for a in range(3):
        rows_ref[27 + a : 28 + a, :] = norms[a] if is_test else jnp.ones_like(norm)
        rows_ref[30 + a : 31 + a, :] = jnp.ones_like(norm) if is_test else norms[a]


def left_kernel(
    nshard, first, me_ref, order_ref, test_ref, source_ref, basis_ref, out_ref,
    rows_ref, features_ref, turned_ref, near_ref,
):
    j = pl.program_id(0)
    ntest = test_ref.shape[1]
    nq = source_ref.shape[2]
    part = nq // nshard
    block = min(QBLOCK, nq)

    @pl.when(j == 0)
    def _():
        rows_ref[...] = jnp.zeros_like(rows_ref)
        for i in range(ntest):
            fill_features(rows_ref, test_ref[:, i, :], True)
            features_ref[i] = rows_ref[...].T.astype(jnp.bfloat16)
            turned_ref[i] = basis_ref[i].T

    source = order_ref[first + j]
    for comp in range(3):
        rows_ref[comp : comp + 1, :] = source_ref[comp, pl.ds(source, 1), :]
    pieces = []
    for offset in range(nshard):
        start = pl.multiple_of((me_ref[0] ^ offset) * part, part)
        pieces.append(rows_ref[0:3, pl.ds(start, part)])
    fill_features(rows_ref, jnp.concatenate(pieces, axis=1), False)
    near_ref[...] = rows_ref[...].astype(jnp.bfloat16)

    steps = [(i, start) for i in range(ntest) for start in range(0, nq, block)]

    def kernel_block(i, start):
        squared = jnp.dot(
            features_ref[i], near_ref[:, start : start + block], preferred_element_type=jnp.float32
        )
        return lax.rsqrt(squared.astype(jnp.bfloat16))

    ready = kernel_block(*steps[0])
    for place, (i, start) in enumerate(steps):
        now = ready
        if place + 1 < len(steps):
            ready = kernel_block(*steps[place + 1])
        out_ref[i, 0, :, start : start + block] = jnp.dot(
            turned_ref[i], now, preferred_element_type=jnp.float32
        ).astype(jnp.bfloat16)


def left_products(nshard, me, order, test_points, source_points, test_basis, first, last):
    _, ntest, npoint = test_points.shape
    nall, nq = source_points.shape[1:]
    kmax = test_basis.shape[2]
    nsource = last - first
    return pl.pallas_call(
        functools.partial(left_kernel, nshard, first),
        grid_spec=pltpu.PrefetchScalarGridSpec(
            num_scalar_prefetch=2,
            grid=(nsource,),
            in_specs=[
                pl.BlockSpec((3, ntest, npoint), lambda j, *_: (0, 0, 0)),
                pl.BlockSpec((3, nall, nq), lambda j, *_: (0, 0, 0)),
                pl.BlockSpec((ntest, npoint, kmax), lambda j, *_: (0, 0, 0)),
            ],
            out_specs=pl.BlockSpec((ntest, 1, kmax, nq), lambda j, *_: (0, j, 0, 0)),
            scratch_shapes=[
                pltpu.VMEM((NFEATURE, npoint), jnp.float32),
                pltpu.VMEM((ntest, npoint, NFEATURE), jnp.bfloat16),
                pltpu.VMEM((ntest, kmax, npoint), jnp.bfloat16),
                pltpu.VMEM((NFEATURE, nq), jnp.bfloat16),
            ],
        ),
        out_shape=jax.ShapeDtypeStruct((ntest, nsource, kmax, nq), jnp.bfloat16),
        compiler_params=pltpu.CompilerParams(vmem_limit_bytes=VMEM_LIMIT),
        cost_estimate=pl.CostEstimate(
            flops=2 * ntest * nsource * npoint * nq * kmax,
            bytes_accessed=2 * ntest * nsource * kmax * nq,
            transcendentals=ntest * nsource * npoint * nq,
        ),
    )(me, order, test_points, source_points, test_basis)


def tile_kernel(nshard, first, packed, *refs):
    order_ref, source_counts_ref, offsets_ref, test_counts_ref, left_ref = refs[:5]
    shard_refs = refs[5 : 5 + nshard]
    j = pl.program_id(0)
    if packed:
        tile_ref, main_ref, over_ref, pack_ref = refs[5 + nshard :]
    else:
        (tile_ref,) = refs[5 + nshard :]
    ntest, _, kmax, _ = left_ref.shape
    ndest, _, _, rows, width = tile_ref.shape
    count = source_counts_ref[order_ref[first + j]]

    def work(wide):
        side = jnp.concatenate([shard_ref[0, :, :wide] for shard_ref in shard_refs], axis=0)
        row_ids = lax.broadcasted_iota(jnp.int32, (kmax, wide), 0)
        column_ids = lax.broadcasted_iota(jnp.int32, (kmax, wide), 1)
        products = [
            jnp.dot(left_ref[i, 0], side, preferred_element_type=jnp.float32) for i in range(ntest)
        ]
        if packed:
            offset = offsets_ref[order_ref[first + j]]
            shift = offset % LANES
            base = offset - shift
            low = lax.broadcasted_iota(jnp.int32, (kmax, LANES), 1) < shift
        for i in range(ntest):
            used = (row_ids < test_counts_ref[i]) & (column_ids < count)
            tile = jnp.where(used, products[i], 0.0)
            for dest in range(ndest):
                tile_ref[dest, i, 0, :, :wide] = tile[dest * rows : (dest + 1) * rows].astype(jnp.bfloat16)
                if wide < width:
                    tile_ref[dest, i, 0, :, wide:] = jnp.zeros((rows, width - wide), jnp.bfloat16)
            if not packed:
                continue
            rolled = [
                pltpu.roll(tile[:, start : start + LANES], shift, axis=1) for start in range(0, wide, LANES)
            ]
            for place in range(len(rolled) + 1):
                here = pl.ds(pl.multiple_of(base + place * LANES, LANES), LANES)
                if place == 0:
                    before = jnp.concatenate(
                        [pack_ref[dest, i, :, here].astype(jnp.float32) for dest in range(ndest)], axis=0
                    )
                else:
                    before = rolled[place - 1]
                after = rolled[place] if place < len(rolled) else jnp.zeros_like(before)
                window = jnp.where(low, before, after)
                for dest in range(ndest):
                    pack_ref[dest, i, :, here] = window[dest * rows : (dest + 1) * rows].astype(jnp.bfloat16)

    narrow = width - LANES
    if narrow > 0:
        pl.when(count <= narrow)(lambda: work(narrow))
        pl.when(count > narrow)(lambda: work(width))
    else:
        work(width)

    if packed:

        @pl.when(j == pl.num_programs(0) - 1)
        def _():
            main = main_ref.shape[3]
            main_ref[...] = pack_ref[:, :, :, :main]
            over_ref[...] = pack_ref[:, :, :, main : main + over_ref.shape[3]]


def tiles(ndest, first, tables, test_counts, left, shards, main):
    ntest, nsource, kmax, nq = left.shape
    nshard = len(shards)
    part, width = shards[0].shape[1:]
    rows = kmax // ndest
    packed = main is not None
    shapes = [jax.ShapeDtypeStruct((ndest, ntest, nsource, rows, width), jnp.bfloat16)]
    specs = [pl.BlockSpec((ndest, ntest, 1, rows, width), lambda j, *_: (0, 0, j, 0, 0))]
    scratch = []
    if packed:
        for columns in (main, nsource * width - main):
            shape = (ndest, ntest, rows, columns)
            shapes.append(jax.ShapeDtypeStruct(shape, jnp.bfloat16))
            specs.append(pl.BlockSpec(shape, lambda j, *_: (0, 0, 0, 0)))
        scratch.append(pltpu.VMEM((ndest, ntest, rows, nsource * width + LANES), jnp.bfloat16))
    return pl.pallas_call(
        functools.partial(tile_kernel, nshard, first, packed),
        grid_spec=pltpu.PrefetchScalarGridSpec(
            num_scalar_prefetch=4,
            grid=(nsource,),
            in_specs=[pl.BlockSpec((ntest, 1, kmax, nq), lambda j, *_: (0, j, 0, 0))]
            + [pl.BlockSpec((1, part, width), lambda j, *_: (j, 0, 0))] * nshard,
            out_specs=specs,
            scratch_shapes=scratch,
        ),
        out_shape=shapes,
        compiler_params=pltpu.CompilerParams(vmem_limit_bytes=VMEM_LIMIT),
        cost_estimate=pl.CostEstimate(
            flops=2 * ntest * nsource * kmax * width * nq,
            bytes_accessed=2 * ntest * nsource * kmax * (nq + width),
            transcendentals=0,
        ),
    )(*tables, test_counts, left, *shards)


def project_kernel(started, order_ref, tile_ref, coeff_ref, *refs):
    if started:
        start_ref, sum_ref, total_ref = refs
    else:
        *counts_refs, sum_ref, joined_ref, total_ref = refs
    j = pl.program_id(0)
    ndest, ntest, _, rows, _ = tile_ref.shape
    whole = [tile_ref[dest, i, 0] for i in range(ntest) for dest in range(ndest)]
    term = jnp.dot(jnp.concatenate(whole, axis=0), coeff_ref[0], preferred_element_type=jnp.float32)

    @pl.when(j == 0)
    def _():
        total_ref[...] = term + start_ref[...] if started else term

    @pl.when(j > 0)
    def _():
        total_ref[...] += term

    @pl.when(j == pl.num_programs(0) - 1)
    def _():
        if not started:
            sum_ref[...] = total_ref[...]
            nblock = counts_refs[0].shape[0]
            for place, counts_ref in enumerate(counts_refs):
                for k in range(nblock):
                    joined_ref[place * nblock + k] = counts_ref[k]
            return
        for i in range(ntest):
            for dest in range(ndest):
                top = (i * ndest + dest) * rows
                sum_ref[dest, i] = total_ref[top : top + rows, :].astype(sum_ref.dtype)


def project(order, first, tiles, coefficients, start=None, counts=()):
    ndest, ntest, nsource, rows, width = tiles.shape
    ncol = coefficients.shape[2]
    smem = pl.BlockSpec(memory_space=pltpu.SMEM)
    total_spec = pl.BlockSpec((ntest * ndest * rows, ncol), lambda j, order: (0, 0))
    started = start is not None
    if started:
        more, more_specs = [start], [total_spec]
        out_specs = pl.BlockSpec((ndest, ntest, rows, ncol), lambda j, order: (0, 0, 0, 0))
        out_shape = jax.ShapeDtypeStruct((ndest, ntest, rows, ncol), jnp.bfloat16)
    else:
        more, more_specs = list(counts), [smem] * len(counts)
        out_specs = (total_spec, smem)
        out_shape = (
            jax.ShapeDtypeStruct((ntest * ndest * rows, ncol), jnp.float32),
            jax.ShapeDtypeStruct((sum(part.shape[0] for part in counts),), jnp.int32),
        )
    return pl.pallas_call(
        functools.partial(project_kernel, started),
        grid_spec=pltpu.PrefetchScalarGridSpec(
            num_scalar_prefetch=1,
            grid=(nsource,),
            in_specs=[
                pl.BlockSpec((ndest, ntest, 1, rows, width), lambda j, order: (0, 0, j, 0, 0)),
                pl.BlockSpec((1, width, ncol), lambda j, order: (order[first + j], 0, 0)),
            ]
            + more_specs,
            out_specs=out_specs,
            scratch_shapes=[pltpu.VMEM((ntest * ndest * rows, ncol), jnp.float32)],
        ),
        out_shape=out_shape,
        compiler_params=pltpu.CompilerParams(vmem_limit_bytes=VMEM_LIMIT),
        cost_estimate=pl.CostEstimate(
            flops=2 * ndest * ntest * rows * width * ncol * nsource,
            bytes_accessed=2 * ndest * ntest * rows * width * nsource,
            transcendentals=0,
        ),
    )(order, tiles, coefficients, *more)


def unpack_kernel(cut, order_ref, counts_ref, offsets_ref, whole_ref, packed_ref, *refs):
    *part_refs, out_ref, sum_ref, rows_ref = refs
    sum_ref[...] = sum(part_ref[...].astype(jnp.float32) for part_ref in part_refs).astype(sum_ref.dtype)
    nsrc, _, _, rows, width = whole_ref.shape
    packed_width = packed_ref.shape[3]
    nall = out_ref.shape[2]
    nblock = nall // nsrc
    ntile = width // LANES
    step = 16 if rows % 16 == 0 else rows
    lanes = lax.broadcasted_iota(jnp.int32, (rows, LANES), 1)

    @pl.loop(0, nsrc, unroll=4)
    def _(source):
        for place in range(nblock):
            block = order_ref[source * nblock + place]
            target = source * nblock + block
            if place < cut:
                rows_ref[target] = whole_ref[source, 0, place].astype(jnp.float32)
                continue
            count = counts_ref[target]
            offset = offsets_ref[target]
            shift = offset % LANES
            base = offset - shift
            back = (LANES - shift) % LANES
            low = lanes < LANES - shift
            rolled = []
            for tile in range(ntile + 1):
                start = pl.multiple_of(jnp.minimum(base + tile * LANES, packed_width - LANES), LANES)
                piece = packed_ref[source, 0, :, pl.ds(start, LANES)].astype(jnp.float32)
                rolled.append(pltpu.roll(piece, back, axis=1))
            for tile in range(ntile):
                value = jnp.where(low, rolled[tile], rolled[tile + 1])
                value = jnp.where(lanes < count - tile * LANES, value, 0.0)
                rows_ref[target, :, tile * LANES : (tile + 1) * LANES] = value

    @pl.loop(0, nall // 16)
    def _(group):
        here = pl.ds(pl.multiple_of(group * 16, 16), 16)
        for top in range(0, rows, step):
            turned = jnp.transpose(rows_ref[here, top : top + step, :], (1, 0, 2))
            out_ref[0, top : top + step, here, :] = turned.astype(out_ref.dtype)


def unpack(cut, tables, whole, packed, parts):
    nsrc, ntest, _, rows, width = whole.shape
    packed_width = packed.shape[3]
    nall = tables[0].shape[0]
    sum_spec = pl.BlockSpec((1,) + parts[0].shape[1:], lambda i, *_: (i, 0, 0))
    return pl.pallas_call(
        functools.partial(unpack_kernel, cut),
        grid_spec=pltpu.PrefetchScalarGridSpec(
            num_scalar_prefetch=3,
            grid=(ntest,),
            in_specs=[
                pl.BlockSpec((nsrc, 1, cut, rows, width), lambda i, *_: (0, i, 0, 0, 0)),
                pl.BlockSpec((nsrc, 1, rows, packed_width), lambda i, *_: (0, i, 0, 0)),
            ]
            + [sum_spec] * len(parts),
            out_specs=(pl.BlockSpec((1, rows, nall, width), lambda i, *_: (i, 0, 0, 0)), sum_spec),
            scratch_shapes=[pltpu.VMEM((nall, rows, width), jnp.float32)],
        ),
        out_shape=(
            jax.ShapeDtypeStruct((ntest, rows, nall, width), jnp.bfloat16),
            jax.ShapeDtypeStruct(parts[0].shape, jnp.bfloat16),
        ),
        compiler_params=pltpu.CompilerParams(vmem_limit_bytes=SMALL_VMEM_LIMIT),
    )(*tables, whole, packed, *parts)


def body(
    test_points, test_basis, test_counts, source_points, source_basis, source_counts, coefficients
):
    nsource, part, kmax = source_basis.shape
    ntest = test_points.shape[0]
    nsrc = lax.axis_size("src")
    ntest_axis = lax.axis_size("test")
    me_test = lax.axis_index("test")
    cut = max(1, nsource * 3 // 8)

    held = {}

    def gather(name, shard, left):
        got = {0: shard}
        bits = list(bits_down(ntest_axis))
        for bit in bits:
            if bit == bits[-1]:
                names = [o for o in got if o != 0]
                tied = lax.optimization_barrier(tuple(got[o] for o in names) + (left,))
                got.update(zip(names, tied[:-1]))
                left = tied[-1]
            for offset in list(got):
                got[offset ^ bit] = exchange(got[offset], "test", bit)
            if bit == bits[0]:
                held[name] = got[bit]
        return [got[offset] for offset in sorted(got)], left

    most = (nsource - cut) * kmax
    main = min(most, -(-most * 18 // (25 * LANES)) * LANES)
    widths = [main, min(most, main + LANES), min(most, main + 2 * LANES), most]

    order, offsets, basis_a, basis_b = pick(cut, source_counts, source_basis)
    tables = (order, source_counts, offsets)
    me = jnp.reshape(me_test, (1,))
    test_points, source_points = test_points.transpose(1, 0, 2), source_points.transpose(1, 0, 2)

    left_a = left_products(ntest_axis, me, order, test_points, source_points, test_basis, 0, cut)
    shards_a, left_a = gather("a", basis_a, left_a)
    (tiles_a,) = tiles(nsrc, 0, tables, test_counts, left_a, shards_a, None)
    moved_a = lax.all_to_all(tiles_a, "src", split_axis=0, concat_axis=0, tiled=True)

    rest, _ = lax.optimization_barrier((basis_b, held["a"]))
    later, _ = lax.optimization_barrier((source_points, tiles_a))
    left_b = left_products(ntest_axis, me, order, test_points, later, test_basis, cut, nsource)
    shards_b, left_b = gather("b", rest, left_b)
    inner = max(1, nsrc // 4)
    counts, _ = lax.optimization_barrier((source_counts, left_b))
    far = [exchange(counts, "src", flip) for flip in range(inner, nsrc, inner)]
    tiles_b, packed, beyond = tiles(nsrc, cut, tables, test_counts, left_b, shards_b, main)
    packed, *far = lax.optimization_barrier((packed, *far))
    moved_b = lax.all_to_all(packed, "src", split_axis=0, concat_axis=0, tiled=True)

    sums, joined = project(order, 0, tiles_a, coefficients, counts=[source_counts] + far)
    groups = [joined] + [exchange(joined, "src", flip) for flip in range(1, inner)]
    sums = project(order, cut, tiles_b, coefficients, sums)
    parts = sum_rows(sums, "src")
    me_src, _ = lax.optimization_barrier((jnp.reshape(lax.axis_index("src"), (1,)), packed))
    all_counts, all_order, all_offsets, branch = all_tables(cut, nsource, widths, me_src, groups)
    spread = (all_order, all_counts, all_offsets)

    def finish(width, beyond, moved_a, moved_b, spread, parts):
        if width > main:
            more = lax.all_to_all(
                beyond[..., : width - main], "src", split_axis=0, concat_axis=0, tiled=True
            )
            moved_b = jnp.concatenate([moved_b, more], axis=3)
        return unpack(cut, spread, moved_a, moved_b, parts)

    return lax.switch(
        branch[0],
        [functools.partial(finish, width) for width in widths],
        beyond,
        moved_a,
        moved_b,
        spread,
        parts,
    )


def solution(mesh):
    return jax.shard_map(
        body,
        mesh=mesh,
        in_specs=(
            P("test", None, None),
            P("test", None, None),
            P("test"),
            P("src", None, None),
            P("src", "test", None),
            P("src"),
            P("src", None, None),
        ),
        out_specs=(P("test", "src", None, None), P("test", "src", None)),
        check_vma=False,
    )
```
